32 devices in a mesh: head: 4 (over x, core), seq: 8 (over z, y).
Axes of the slice: x: 2, y: 2, z: 4, core: 2. Of those that a mesh axis runs over, the one named last changes fastest.
Arguments:
- frames: bfloat16 [8, 2048, 1024], P('seq', 'head'), may hold values from -6 to 6
- time_embed: bfloat16 [8, 2, 1024], P('seq'), may hold values from -6 to 6
- segment_ids: int32 [8, 2048], P('seq', 'head'), may hold values from 0 to 1, as said below
- frame_mask: int32 [8, 2048], P('seq', 'head'), may hold values from 0 to 1, as said below
- positions: int32 [8, 2048], P('seq', 'head'), may hold values from 0 to 3582, as said below
- w_ada: bfloat16 [1024, 6144], P(('head', 'seq')), may hold values from -0.1875 to 0.1875
- b_ada: bfloat16 [6144], P(('head', 'seq')), may hold values from -3 to 3
- w_qkv: bfloat16 [1024, 3072], P(('head', 'seq')), may hold values from -0.1875 to 0.1875
- b_qkv: bfloat16 [3072], P(('head', 'seq')), may hold values from -2 to 2
- w_out: bfloat16 [1024, 1024], P(('head', 'seq')), may hold values from -2 to 2
- b_out: bfloat16 [1024], P(('head', 'seq')), may hold values from -2 to 2
- w_up: bfloat16 [1024, 2048], P(('head', 'seq')), may hold values from -0.1875 to 0.1875
- b_up: bfloat16 [2048], P(('head', 'seq')), may hold values from -2 to 2
- w_down: bfloat16 [2048, 1024], P(('head', 'seq')), may hold values from -0.25 to 0.25
- b_down: bfloat16 [1024], P(('head', 'seq')), may hold values from -2 to 2
- cotangent: bfloat16 [8, 2048, 1024], P('seq', 'head'), may hold values from -6 to 6
Outputs:
- out_frames: bfloat16 [8, 2048, 1024], P('seq', 'head')
- grad_frames: float32 [8, 2048, 1024], P('seq', 'head')
- grad_time: float32 [8, 2, 1024], P('seq')
- grad_w_ada: float32 [1024, 6144], P(('head', 'seq'))
- grad_b_ada: float32 [6144], P(('head', 'seq'))
- grad_w_qkv: float32 [1024, 3072], P(('head', 'seq'))
- grad_b_qkv: float32 [3072], P(('head', 'seq'))
- grad_w_out: float32 [1024, 1024], P(('head', 'seq'))
- grad_b_out: float32 [1024], P(('head', 'seq'))
- grad_w_up: float32 [1024, 2048], P(('head', 'seq'))
- grad_b_up: float32 [2048], P(('head', 'seq'))
- grad_w_down: float32 [2048, 1024], P(('head', 'seq'))
- grad_b_down: float32 [1024], P(('head', 'seq'))
The draws below stay inside these ranges and needn't reach their ends.
Inputs may be any that keep to these rules, and one draw needn't show every extreme that they name: `segment_ids`: every row holds two utterances, segment 0 in one run of frames and then segment 1 to the row's end; the longer one has 1024 frames or more; padding frames lie at the end of the row, inside segment 1. `frame_mask`: in every row 1 for the frames before a run of 1 to 256 padding frames at its end, 0 on that run; each utterance keeps real frames. `positions`: 0 at the first frame of each utterance, then rising by 1 or 2 from one frame to the next within it.
All inputs are finite; a program needn't handle non-finite values.
Results may differ from the reference program's by a relative error of at most 0.017.
The reference program's roundings to bfloat16 on the way count: a program that leaves them out, or rounds other values in their place, can miss the bound.
Values may be sent and summed in bfloat16 or wider, within the bound.
A program may use at most 256 MiB of HBM per device.

```python
import jax
import jax.numpy as jnp
from jax import lax

D = 1024
HEAD_DIM = 64
FF = 2048
SEGS = 2
ROWS = 8
LEN = 2048


def row_labels(key):
    base_key = jax.random.fold_in(key, 11)
    key_long, key_pad, key_order, key_step = jax.random.split(base_key, 4)
    first_row = jnp.arange(ROWS, dtype=jnp.int32) == 0
    long_len = jax.random.randint(key_long, (ROWS,), LEN // 2, 3 * LEN // 4 + 1)
    long_len = jnp.where(first_row, 3 * LEN // 4, long_len)
    pad_len = jax.random.randint(key_pad, (ROWS,), 1, LEN // 8 + 1)
    pad_len = jnp.where(first_row, LEN // 8, pad_len)
    swap_order = jax.random.randint(key_order, (ROWS,), 0, 2)
    swap_order = jnp.where(first_row, 1, swap_order)
    short_len = LEN - long_len - pad_len
    first_len = jnp.where(swap_order == 1, short_len, long_len)
    place = jnp.arange(LEN, dtype=jnp.int32)[None, :]
    segment = (place >= first_len[:, None]).astype(jnp.int32)
    live_frame = (place < (LEN - pad_len)[:, None]).astype(jnp.int32)
    stride = jax.random.randint(key_step, (ROWS, LEN), 1, 3)
    stride = jnp.where(first_row[:, None], 2, stride)
    before = jnp.cumsum(stride, axis=1) - stride
    offset = jnp.take_along_axis(before, first_len[:, None].astype(jnp.int32), axis=1)
    position = jnp.where(segment == 1, before - offset, before)
    return (segment.astype(jnp.int32), live_frame.astype(jnp.int32), position.astype(jnp.int32))


def draw_segment_ids(key, part):
    return row_labels(key)[0]


def draw_frame_mask(key, part):
    return row_labels(key)[1]


def draw_positions(key, part):
    return row_labels(key)[2]


def steps_of(key, shape, cuts, least, high):
    gain, own = 1.0, jax.random.fold_in(key, 6)
    for axis_at, parts in cuts:
        draws = jnp.exp(jax.random.uniform(jax.random.fold_in(own, axis_at), (parts,), jnp.float32, least / len(cuts), high / len(cuts)))
        gain = gain * jnp.repeat(draws, shape[axis_at] // parts).reshape([-1 if axis == axis_at else 1 for axis in range(len(shape))])
    return gain


def bell_draw(own_key, dims, scale, reach, cuts=(), kind=jnp.bfloat16):
    drawn = jax.random.normal(own_key, dims, jnp.float32) * scale
    if len(cuts) > 0:
        drawn = steps_of(own_key, dims, cuts, -0.22, 0.18) * drawn
    return jnp.clip(drawn, min=-reach, max=reach).astype(kind)


def setup_inputs(seed: int = 0) -> dict:
    splits = jax.random.split(jax.random.key(seed), 17)
    return {
        "frames": bell_draw(splits[0], (ROWS, LEN, D), 1.0, 6.0, ((0, 8), (1, 4))),
        "time_embed": bell_draw(splits[1], (ROWS, SEGS, D), 1.0, 6.0, ((0, 8),)),
        "segment_ids": draw_segment_ids(jax.random.fold_in(splits[16], 71), 0),
        "frame_mask": draw_frame_mask(jax.random.fold_in(splits[16], 71), 0),
        "positions": draw_positions(jax.random.fold_in(splits[16], 71), 0),
        "w_ada": bell_draw(splits[5], (D, 6 * D), D ** -0.5, 0.1875, ((0, 32),)),
        "b_ada": bell_draw(splits[6], (6 * D,), 0.5, 3.0, ((0, 32),)),
        "w_qkv": bell_draw(splits[7], (D, 3 * D), D ** -0.5, 0.1875, ((0, 32),)),
        "b_qkv": bell_draw(splits[8], (3 * D,), 0.3, 2.0, ((0, 32),)),
        "w_out": bell_draw(splits[9], (D, D), (D // 128) ** -0.5, 2.0, ((0, 32),)),
        "b_out": bell_draw(splits[10], (D,), 0.3, 2.0, ((0, 32),)),
        "w_up": bell_draw(splits[11], (D, FF), D ** -0.5, 0.1875, ((0, 32),)),
        "b_up": bell_draw(splits[12], (FF,), 0.3, 2.0, ((0, 32),)),
        "w_down": bell_draw(splits[13], (FF, D), (FF // 4) ** -0.5, 0.25, ((0, 32),)),
        "b_down": bell_draw(splits[14], (D,), 0.3, 2.0, ((0, 32),)),
        "cotangent": bell_draw(splits[15], (ROWS, LEN, D), 1.0, 6.0, ((0, 8), (1, 4))),
    }


norm_eps = 1e-06
masked_score = -1e+30

@jax.custom_vjp
def low(v):
    return lax.optimization_barrier(v.astype(jnp.bfloat16)).astype(jnp.float32)

@jax.custom_vjp
def low_back(v):
    return v

def low_keep(v):
    return (low(v), None)

def low_pass(kept, grad):
    return (grad,)

def back_keep(v):
    return (v, None)

def back_low(kept, grad):
    return (low(grad),)
low.defvjp(low_keep, low_pass)
low_back.defvjp(back_keep, back_low)

def product(left, right):
    return jnp.dot(left, right, precision=lax.Precision.HIGHEST, preferred_element_type=jnp.float32)

def normalize(inputs):
    centre = lax.optimization_barrier(jnp.mean(inputs, -1, keepdims=True))
    centred = inputs - centre
    spread = lax.optimization_barrier(jnp.mean(centred * centred, -1, keepdims=True))
    return centred * lax.rsqrt(spread + norm_eps)

def modulate(inputs, shift_in, scale_in):
    return normalize(inputs) * (1.0 + scale_in) + shift_in

def rotary_angles(positions, model_width, head_size):
    column = lax.iota(jnp.int32, model_width)
    pair_index = (column % head_size // 2).astype(jnp.float32)
    inverse = 10000.0 ** (-(2.0 * pair_index) / head_size)
    return positions.astype(jnp.float32)[..., None] * inverse

def rotate(inputs, angles):
    column = lax.iota(jnp.int32, inputs.shape[-1])
    following = jnp.roll(inputs, -1, axis=-1)
    preceding = jnp.roll(inputs, 1, axis=-1)
    partner = jnp.where(column % 2 == 0, -following, preceding)
    return inputs * jnp.cos(angles) + partner * jnp.sin(angles)

def row_layer(source, time_row, seg_row, mask_row, angles, params):
    w_ada, b_ada, w_qkv, b_qkv, w_out, b_out, w_up, b_up, w_down, b_down = params
    total_frames, model_width = source.shape
    head_count = model_width // HEAD_DIM
    time_act = low(jax.nn.silu(time_row))
    embedding = low_back(product(time_act, w_ada) + b_ada)
    member = (seg_row[:, None] == lax.iota(jnp.int32, time_row.shape[0])[None, :]).astype(jnp.float32)
    modulation = product(member, embedding)
    shift_one, scale_one, gate_one, shift_two, scale_two, gate_two = jnp.split(modulation, 6, axis=1)
    normed_one = low(modulate(source, shift_one, scale_one))
    projected = low_back(product(normed_one, w_qkv) + b_qkv)
    query_rot = low(low_back(rotate(projected[:, :model_width], angles)))
    key_part = low(low_back(rotate(projected[:, model_width:2 * model_width], angles)))
    value_part = low(low_back(projected[:, 2 * model_width:]))
    block_rows = min(512, total_frames)
    col_place = lax.iota(jnp.int32, total_frames)
    key_heads = key_part.reshape(total_frames, head_count, HEAD_DIM)
    value_heads = value_part.reshape(total_frames, head_count, HEAD_DIM)

    def one_block(first_row):
        query_block = lax.dynamic_slice_in_dim(query_rot, first_row, block_rows, 0).reshape(block_rows, head_count, HEAD_DIM)
        seg_query = lax.dynamic_slice_in_dim(seg_row, first_row, block_rows, 0)
        scores = jnp.einsum('qhd,khd->hqk', query_block, key_heads, precision=lax.Precision.HIGHEST) * HEAD_DIM ** (-0.5)
        scores = low_back(scores)
        row_place = first_row + lax.iota(jnp.int32, block_rows)
        allowed = (seg_query[:, None] == seg_row[None, :]) & (mask_row[None, :] == 1) | (row_place[:, None] == col_place[None, :])
        scores = jnp.where(allowed[None], scores, masked_score)
        row_max = lax.optimization_barrier(jnp.max(scores, axis=2, keepdims=True))
        exp_sum = lax.optimization_barrier(jnp.sum(jnp.where(allowed[None], jnp.exp(scores - row_max), 0.0), axis=2, keepdims=True))
        log_total = row_max + jnp.log(exp_sum)
        probability = jnp.where(allowed[None], jnp.exp(scores - log_total), 0.0)
        mixed_heads = jnp.einsum('hqk,khd->qhd', low(probability), value_heads, precision=lax.Precision.HIGHEST)
        return mixed_heads.reshape(block_rows, model_width)
    starts = lax.iota(jnp.int32, total_frames // block_rows) * block_rows
    mixed_all = lax.map(jax.checkpoint(one_block), starts).reshape(total_frames, model_width)
    attended = low(low_back(mixed_all))
    branch = low_back(product(attended, w_out) + b_out) * mask_row.astype(jnp.float32)[:, None]
    middle = source + gate_one * branch
    normed_two = low(modulate(middle, shift_two, scale_two))
    hidden = low_back(product(normed_two, w_up) + b_up)
    activated = low(jax.nn.gelu(hidden, approximate=True))
    feed_out = low_back(product(activated, w_down) + b_down)
    return middle + gate_two * feed_out

def reference(frames, time_embed, segment_ids, frame_mask, positions, w_ada, b_ada, w_qkv, b_qkv, w_out, b_out, w_up, b_up, w_down, b_down, cotangent):
    weights = tuple((matrix.astype(jnp.float32) for matrix in (w_ada, b_ada, w_qkv, b_qkv, w_out, b_out, w_up, b_up, w_down, b_down)))
    model_width = frames.shape[2]

    def row_step(running, row_items):
        source, time_row, seg_row, mask_row, pos_row, cot_row = row_items
        angles = rotary_angles(pos_row, model_width, HEAD_DIM)

        def layer_fn(source_in, time_in, *params):
            return row_layer(source_in, time_in, seg_row, mask_row, angles, params)
        result, pullback = jax.vjp(layer_fn, source.astype(jnp.float32), time_row.astype(jnp.float32), *weights)
        gradients = pullback(cot_row.astype(jnp.float32))
        running = tuple((summed + addend for summed, addend in zip(running, gradients[2:])))
        return (running, (result.astype(jnp.bfloat16), gradients[0], gradients[1]))
    zero_grads = tuple((jnp.zeros(matrix.shape, jnp.float32) for matrix in weights))
    grad_totals, (out_rows, grad_frames, grad_time) = lax.scan(row_step, zero_grads, (frames, time_embed, segment_ids, frame_mask, positions, cotangent))
    return (out_rows, grad_frames, grad_time, grad_totals[0], grad_totals[1], grad_totals[2], grad_totals[3], grad_totals[4], grad_totals[5], grad_totals[6], grad_totals[7], grad_totals[8], grad_totals[9])
```

```python
import functools
import math

import jax
import jax.numpy as jnp
from jax import lax
from jax.experimental import pallas as pl
from jax.experimental.pallas import tpu as pltpu
from jax.sharding import PartitionSpec as P

HD=64
LOG2E=math.log2(math.e)
NEG=-1e30
bf=jnp.bfloat16; f32=jnp.float32
NT=(((1,),(1,)),((),()))
NN=(((1,),(0,)),((),()))
def dot(a,b,dims=NN): return lax.dot_general(a,b,dims,preferred_element_type=f32)

def fwd_kernel(lo_ref,hi_ref,qkv_ref,auxq_ref,auxk_ref,o_ref,lse_ref,k2,vx,q2,s_scr,m_scr,acc,*,T,nh):
    qt=pl.program_id(0)
    W=nh*HD
    L=qkv_ref.shape[0]
    nk=L//T
    lane=lax.broadcasted_iota(jnp.int32,(T,128),1)
    @pl.when(qt==0)
    def _():
        @pl.loop(0,nk)
        def _(t):
            r=pl.ds(pl.multiple_of(t*T,T),T)
            for h in range(nh):
                k=qkv_ref[r,W+h*HD:W+(h+1)*HD]
                k2[h,t]=jnp.concatenate([k,k],axis=1)
                v=qkv_ref[r,2*W+h*HD:2*W+(h+1)*HD]
                one=jnp.where(lax.broadcasted_iota(jnp.int32,(T,HD),1)==0,1.0,0.0).astype(bf)
                vx[h,t]=jnp.concatenate([v,one],axis=1)
    lo=lo_ref[qt]; hi=hi_ref[qt]
    r=pl.ds(pl.multiple_of(qt*T,T),T)
    for h in range(nh):
        q=qkv_ref[r,h*HD:(h+1)*HD].astype(f32)*(HD**-0.5*LOG2E)
        qh=q.astype(bf)
        ql=(q-qh.astype(f32)).astype(bf)
        q2[h]=jnp.concatenate([qh,ql],axis=1)
    auxq=auxq_ref[r,:]
    eye=lax.broadcasted_iota(jnp.int32,(T,T),0)==lax.broadcasted_iota(jnp.int32,(T,T),1)
    def mx(s):
        m=s[:,:128]
        for j in range(1,T//128): m=jnp.maximum(m,s[:,j*128:(j+1)*128])
        return m
    ak=auxk_ref[r,:]
    for h in range(nh):
        raw=dot(q2[h],k2[h,qt],NT)
        s=dot(jnp.concatenate([q2[h],auxq],axis=1),jnp.concatenate([k2[h,qt],ak],axis=1),NT)
        s=jnp.where(eye,raw,s)
        s_scr[h,qt]=s
        m_scr[h]=mx(s)
    @pl.loop(lo,hi-1)
    def _(t):
        kt=jnp.where(t>=qt,t+1,t)
        ak=auxk_ref[pl.ds(pl.multiple_of(kt*T,T),T),:]
        for h in range(nh):
            s=dot(jnp.concatenate([q2[h],auxq],axis=1),jnp.concatenate([k2[h,kt],ak],axis=1),NT)
            s_scr[h,kt]=s
            m_scr[h]=jnp.maximum(m_scr[h],mx(s))
    for h in range(nh):
        m_scr[h]=jnp.broadcast_to(jnp.max(m_scr[h],axis=1,keepdims=True),(T,128))
        acc[h]=jnp.zeros((T,128),f32)
    @pl.loop(lo,hi)
    def _(kt):
        for h in range(nh):
            s=s_scr[h,kt]; m=m_scr[h]
            p=jnp.exp2(s-jnp.concatenate([m]*(T//128),axis=1)).astype(bf)
            acc[h]+=dot(p,vx[h,kt])
    lse=jnp.zeros((T,128),f32)
    for h in range(nh):
        a=acc[h]
        l=a[:,HD:HD+1]
        o_ref[:,h*HD:(h+1)*HD]=(a[:,:HD]/l).astype(bf)
        lse=jnp.where(lane==h,m_scr[h]+jnp.log2(l),lse)
    lse_ref[...]=lse

def attn_fwd(qkv,lo,hi,auxq,auxk,T):
    L,W3=qkv.shape; W=W3//3; nh=W//HD; nk=L//T
    return pl.pallas_call(
        functools.partial(fwd_kernel,T=T,nh=nh),
        out_shape=(jax.ShapeDtypeStruct((L,W),bf),jax.ShapeDtypeStruct((L,128),f32)),
        grid_spec=pltpu.PrefetchScalarGridSpec(num_scalar_prefetch=2,grid=(nk,),
            in_specs=[pl.BlockSpec((L,W3),lambda i,*_:(0,0)),pl.BlockSpec((L,128),lambda i,*_:(0,0)),pl.BlockSpec((L,128),lambda i,*_:(0,0))],
            out_specs=[pl.BlockSpec((T,W),lambda i,*_:(i,0)),pl.BlockSpec((T,128),lambda i,*_:(i,0))],
            scratch_shapes=[pltpu.VMEM((nh,nk,T,128),bf),pltpu.VMEM((nh,nk,T,128),bf),pltpu.VMEM((nh,T,128),bf),
                pltpu.VMEM((nh,nk,T,T),f32),pltpu.VMEM((nh,T,128),f32),pltpu.VMEM((nh,T,128),f32)]),
        compiler_params=pltpu.CompilerParams(vmem_limit_bytes=60*2**20),
        name="attn_fwd",
    )(lo,hi,qkv,auxq,auxk)

def bwd_kernel(lo_ref,hi_ref,qkv_ref,o_ref,do_ref,lse_ref,auxq_ref,auxk_ref,dqkv_ref,q2,qa,k2,dox,vx,kT,dqT,dk,dv,*,T,nh):
    kt=pl.program_id(0)
    W=nh*HD
    L=qkv_ref.shape[0]
    nk=L//T
    lane=lax.broadcasted_iota(jnp.int32,(T,128),1)
    lane64=lax.broadcasted_iota(jnp.int32,(T,HD),1)
    @pl.when(kt==0)
    def _():
        dqT[...]=jnp.zeros_like(dqT)
        @pl.loop(0,nk)
        def _(t):
            r=pl.ds(pl.multiple_of(t*T,T),T)
            lse=lse_ref[r,:]
            aq=auxq_ref[r,:].astype(f32)
            kT[t]=qkv_ref[r,W:2*W].T
            for h in range(nh):
                q=qkv_ref[r,h*HD:(h+1)*HD].astype(f32)*(HD**-0.5*LOG2E)
                qh=q.astype(bf)
                ql=(q-qh.astype(f32)).astype(bf)
                q2[h,t]=jnp.concatenate([qh,ql],axis=1)
                k=qkv_ref[r,W+h*HD:W+(h+1)*HD]
                k2[h,t]=jnp.concatenate([k,k],axis=1)
                v=qkv_ref[r,2*W+h*HD:2*W+(h+1)*HD]
                vx[h,t]=jnp.concatenate([v,jnp.where(lane64<2,1.0,0.0).astype(bf)],axis=1)
                nl=-lse[:,h:h+1]
                l1=nl.astype(bf).astype(f32); l2=(nl-l1).astype(bf).astype(f32); l3=nl-l1-l2
                qa[h,t]=jnp.where(lane==0,l1,jnp.where(lane==1,l2,jnp.where(lane==2,l3,aq))).astype(bf)
                do=do_ref[r,h*HD:(h+1)*HD]
                nd=-jnp.sum(do.astype(f32)*o_ref[r,h*HD:(h+1)*HD].astype(f32),axis=1,keepdims=True)
                d1=nd.astype(bf).astype(f32); d2=nd-d1
                dox[h,t]=jnp.concatenate([do,jnp.where(lane64==0,d1,jnp.where(lane64==1,d2,0.0)).astype(bf)],axis=1)
    r=pl.ds(pl.multiple_of(kt*T,T),T)
    ak=auxk_ref[r,:]
    lo=lo_ref[kt]; hi=hi_ref[kt]
    def tile(qt,diag):
        rq=pl.ds(pl.multiple_of(qt*T,T),T)
        for h in range(nh):
            kx=jnp.concatenate([k2[h,kt],ak],axis=1)
            s=dot(kx,jnp.concatenate([q2[h,qt],qa[h,qt]],axis=1),NT)
            if diag:
                eye=lax.broadcasted_iota(jnp.int32,(T,T),0)==lax.broadcasted_iota(jnp.int32,(T,T),1)
                qr=jnp.where(lane<3,qa[h,qt].astype(f32),0.0).astype(bf)
                raw=dot(kx,jnp.concatenate([q2[h,qt],qr],axis=1),NT)
                s=jnp.where(eye,raw,s)
            p=jnp.exp2(s)
            dp=dot(vx[h,kt],dox[h,qt],NT)
            ds=(p*dp).astype(bf)
            pb=p.astype(bf)
            g=h//2
            rv=dot(pb,do_ref[rq,g*128:(g+1)*128])
            rk=dot(ds,qkv_ref[rq,g*128:(g+1)*128])
            dv[h]+=rv
            dk[h]+=rk
            dqT[qt,h*HD:(h+1)*HD,:]+=dot(kT[kt,h*HD:(h+1)*HD,:],ds)
    dk[...]=jnp.zeros_like(dk); dv[...]=jnp.zeros_like(dv)
    tile(kt,True)
    @pl.loop(lo,hi-1)
    def _(t):
        tile(jnp.where(t>=kt,t+1,t),False)
    for g in range(nh//2):
        dqkv_ref[r,W+g*128:W+(g+1)*128]=(jnp.where(lane<HD,dk[2*g],dk[2*g+1])*HD**-0.5).astype(bf)
        dqkv_ref[r,2*W+g*128:2*W+(g+1)*128]=jnp.where(lane<HD,dv[2*g],dv[2*g+1]).astype(bf)
    @pl.when(kt==nk-1)
    def _():
        @pl.loop(0,nk)
        def _(t):
            dqkv_ref[pl.ds(pl.multiple_of(t*T,T),T),0:W]=(dqT[t].T*HD**-0.5).astype(bf)

def attn_bwd(qkv,o,do,lse,lo,hi,auxq,auxk,T):
    L,W3=qkv.shape; W=W3//3; nh=W//HD; nk=L//T
    full=lambda w: pl.BlockSpec((L,w),lambda i,*_:(0,0))
    return pl.pallas_call(
        functools.partial(bwd_kernel,T=T,nh=nh),
        out_shape=jax.ShapeDtypeStruct((L,W3),bf),
        grid_spec=pltpu.PrefetchScalarGridSpec(num_scalar_prefetch=2,grid=(nk,),
            in_specs=[full(W3),full(W),full(W),full(128),full(128),full(128)],
            out_specs=full(W3),
            scratch_shapes=[pltpu.VMEM((nh,nk,T,128),bf)]*5+[pltpu.VMEM((nk,W,T),bf),pltpu.VMEM((nk,W,T),f32),
                pltpu.VMEM((nh,T,128),f32),pltpu.VMEM((nh,T,128),f32)]),
        compiler_params=pltpu.CompilerParams(vmem_limit_bytes=60*2**20),
        name="attn_bwd",
    )(lo,hi,qkv,o,do,lse,auxq,auxk)

def tables(seg,mask,T):
    L=seg.shape[0]; nk=L//T
    s=seg.reshape(nk,T); m=mask.reshape(nk,T)
    has=jnp.stack([jnp.any(s==c,axis=1) for c in (0,1)],1)
    real=jnp.stack([jnp.any((s==c)&(m==1),axis=1) for c in (0,1)],1)
    use=jnp.any(has[:,None,:]&real[None,:,:],axis=2)|jnp.eye(nk,dtype=bool)
    idx=jnp.arange(nk,dtype=jnp.int32)
    qlo=jnp.min(jnp.where(use,idx[None,:],nk),axis=1); qhi=jnp.max(jnp.where(use,idx[None,:],-1),axis=1)+1
    klo=jnp.min(jnp.where(use,idx[:,None],nk),axis=0); khi=jnp.max(jnp.where(use,idx[:,None],-1),axis=0)+1
    return [a.astype(jnp.int32) for a in (qlo,qhi,klo,khi)]
def aux(seg,mask):
    L=seg.shape[0]
    lane=lax.broadcasted_iota(jnp.int32,(L,128),1)
    sg=seg[:,None]; pad=(mask==0)[:,None]
    aq=jnp.where(lane==3,jnp.where(sg!=0,NEG,0.),jnp.where(lane==4,jnp.where(sg!=1,NEG,0.),jnp.where(lane==5,NEG,0.))).astype(bf)
    ak=jnp.where(lane<3,1.,jnp.where(lane==3,(sg==0).astype(f32),jnp.where(lane==4,(sg==1).astype(f32),jnp.where(lane==5,pad.astype(f32),0.)))).astype(bf)
    return aq,ak

bf=jnp.bfloat16; f32=jnp.float32
EPS=1e-6
NN=(((1,),(0,)),((),()))
NT=(((1,),(1,)),((),()))
TN=(((0,),(0,)),((),()))
def dot(a,b,dims=NN): return lax.dot_general(a,b,dims,preferred_element_type=f32)
V=pl.BlockSpec(memory_space=pltpu.VMEM)

def moments(x):
    c=jnp.mean(x,-1,keepdims=True)
    xc=x-c
    rs=lax.rsqrt(jnp.mean(xc*xc,-1,keepdims=True)+EPS)
    return xc*rs, rs
def pick(seg,emb,i,D):
    return jnp.where(seg==0,emb[0:1,i*D:(i+1)*D],emb[1:2,i*D:(i+1)*D])
def sums(x,seg):
    a=jnp.sum(jnp.where(seg==0,x,0.0),0,keepdims=True); b=jnp.sum(jnp.where(seg==1,x,0.0),0,keepdims=True)
    return a,b
def partner(v):
    w=v.shape[1]
    lane=lax.broadcasted_iota(jnp.int32,v.shape,1)
    return jnp.where(lane%2==0,pltpu.roll(v,w-1,1),pltpu.roll(v,1,1))
def gelu_both(v):
    c=math.sqrt(2/math.pi)
    v2=v*v
    t=jnp.tanh(c*v*(1.0+0.044715*v2))
    h=0.5*(1.0+t)
    return v*h, h+0.5*v*(1.0-t*t)*(c*(1.0+3*0.044715*v2))

def qkv_kernel(x_ref,seg_ref,emb_ref,w_ref,b_ref,cos_ref,sin_ref,n_ref,p_ref,*,R,nd,W):
    F,D=x_ref.shape
    @pl.loop(0,F//R)
    def _(i):
        r=pl.ds(pl.multiple_of(i*R,R),R)
        seg=seg_ref[r,:]
        n,_=moments(x_ref[r,:].astype(f32))
        y=(n*(1.0+pick(seg,emb_ref,1,D))+pick(seg,emb_ref,0,D)).astype(bf)
        n_ref[r,:]=y
        cos=jnp.concatenate([cos_ref[r,:]]*(W//128),1); sin=jnp.concatenate([sin_ref[r,:]]*(W//128),1)
        for d in range(nd):
            for j in range(3):
                c=(d*3+j)*W
                v=dot(y,w_ref[:,c:c+W])+b_ref[0:1,c:c+W]
                if j<2: v=v*cos+partner(v)*sin
                p_ref[d,r,j*W:(j+1)*W]=v.astype(bf)

def qkv_proj(x,seg,emb,w,b,cos,sin,nd,R=128):
    F,D=x.shape; W=D//nd
    return pl.pallas_call(functools.partial(qkv_kernel,R=R,nd=nd,W=W),
        out_shape=(jax.ShapeDtypeStruct((F,D),bf),jax.ShapeDtypeStruct((nd,F,3*W),bf)),
        in_specs=[V]*7,out_specs=(V,V),
        compiler_params=pltpu.CompilerParams(vmem_limit_bytes=60*2**20),name="qkv_proj",
        cost_estimate=pl.CostEstimate(flops=2*F*D*3*D,bytes_accessed=14*2**20,transcendentals=0))(x,seg,emb,w,b,cos,sin)

def mid_kernel(x_ref,a_ref,c_ref,seg_ref,msk_ref,emb_ref,wo_ref,bo_ref,wu_ref,bu_ref,wd_ref,bd_ref,
               out_ref,dm_ref,da_ref,go_ref,gu_ref,gd_ref,gb_ref,ge_ref,
               n2s,acts,dhs,dfs,dps,dgelu,*,R):
    F,D=x_ref.shape; H=wu_ref.shape[1]; CH=512
    gb_ref[...]=jnp.zeros_like(gb_ref); ge_ref[...]=jnp.zeros_like(ge_ref)
    @pl.loop(0,F//R)
    def _(i):
        r=pl.ds(pl.multiple_of(i*R,R),R)
        seg=seg_ref[r,:]; msk=msk_ref[r,:]
        def acc(k,x):
            a,b=sums(x,seg)
            ge_ref[0:1,k*D:(k+1)*D]+=a; ge_ref[1:2,k*D:(k+1)*D]+=b
        branch=(dot(a_ref[r,:],wo_ref[...])+bo_ref[0:1,:])*msk
        g1=pick(seg,emb_ref,2,D)
        middle=x_ref[r,:].astype(f32)+g1*branch
        n,rs=moments(middle)
        sc2=1.0+pick(seg,emb_ref,4,D)
        n2=(n*sc2+pick(seg,emb_ref,3,D)).astype(bf)
        n2s[r,:]=n2
        feed=jnp.broadcast_to(bd_ref[0:1,:],(R,D))
        for j in range(H//CH):
            c=slice(j*CH,(j+1)*CH)
            h=dot(n2,wu_ref[:,c])+bu_ref[0:1,c]
            a,g=gelu_both(h)
            a=a.astype(bf)
            acts[r,c]=a; dgelu[:,c]=g
            feed+=dot(a,wd_ref[c,:])
        up=c_ref[r,:].astype(f32)
        g2=pick(seg,emb_ref,5,D)
        out_ref[r,:]=(middle+g2*feed).astype(bf)
        df=(up*g2).astype(bf)
        dfs[r,:]=df
        acc(3,up*feed)
        gb_ref[2:3,0:D]+=jnp.sum(df.astype(f32),0,keepdims=True)
        dn=jnp.zeros((R,D),f32)
        for j in range(H//CH):
            c=slice(j*CH,(j+1)*CH)
            dh=(dot(df,wd_ref[c,:],NT)*dgelu[:,c]).astype(bf)
            dhs[r,c]=dh
            gb_ref[1:2,c]+=jnp.sum(dh.astype(f32),0,keepdims=True)
            dn+=dot(dh,wu_ref[:,c],NT)
        acc(1,dn); acc(2,dn*n)
        dn=dn*sc2
        dmid=up+(dn-jnp.mean(dn,-1,keepdims=True)-n*jnp.mean(dn*n,-1,keepdims=True))*rs
        dm_ref[r,:]=dmid
        acc(0,dmid*branch)
        dp=(dmid*g1*msk).astype(bf)
        dps[r,:]=dp
        gb_ref[0:1,0:D]+=jnp.sum(dp.astype(f32),0,keepdims=True)
        da_ref[r,:]=dot(dp,wo_ref[...],NT).astype(bf)
    @pl.loop(0,D//256)
    def _(i):
        c=pl.ds(pl.multiple_of(i*256,256),256)
        go_ref[c,:]=dot(a_ref[:,c],dps[...],TN).astype(bf)
        gu_ref[c,:]=dot(n2s[:,c],dhs[...],TN).astype(bf)
    @pl.loop(0,H//256)
    def _(i):
        c=pl.ds(pl.multiple_of(i*256,256),256)
        gd_ref[c,:]=dot(acts[:,c],dfs[...],TN).astype(bf)

def mid(x,a,c,seg,msk,emb,wo,bo,wu,bu,wd,bd,R=128):
    F,D=x.shape; H=wu.shape[1]
    S=jax.ShapeDtypeStruct
    return pl.pallas_call(functools.partial(mid_kernel,R=R),
        out_shape=(S((F,D),bf),S((F,D),f32),S((F,D),bf),S((D,D),bf),S((D,H),bf),S((H,D),bf),S((8,H),f32),S((8,4*D),f32)),
        in_specs=[V]*12,out_specs=(V,)*8,
        scratch_shapes=[pltpu.VMEM((F,D),bf),pltpu.VMEM((F,H),bf),pltpu.VMEM((F,H),bf),pltpu.VMEM((F,D),bf),pltpu.VMEM((F,D),bf),pltpu.VMEM((R,H),f32)],
        compiler_params=pltpu.CompilerParams(vmem_limit_bytes=62*2**20),name="mid",
        cost_estimate=pl.CostEstimate(flops=6*F*D*(D+2*H),bytes_accessed=30*2**20,transcendentals=F*H))(x,a,c,seg,msk,emb,wo,bo,wu,bu,wd,bd)

def tail_kernel(x_ref,n1_ref,dm_ref,g_ref,seg_ref,emb_ref,w_ref,cos_ref,sin_ref,gf_ref,gw_ref,gb_ref,ge_ref,dps,*,R,nd,W):
    F,D=x_ref.shape
    gb_ref[...]=jnp.zeros_like(gb_ref); ge_ref[...]=jnp.zeros_like(ge_ref)
    @pl.loop(0,F//R)
    def _(i):
        r=pl.ds(pl.multiple_of(i*R,R),R)
        seg=seg_ref[r,:]
        cos=jnp.concatenate([cos_ref[r,:]]*(W//128),1); sin=jnp.concatenate([sin_ref[r,:]]*(W//128),1)
        dn=jnp.zeros((R,D),f32)
        for d in range(nd):
            for j in range(3):
                c=(d*3+j)*W
                v=g_ref[d,r,j*W:(j+1)*W]
                if j<2:
                    v=v.astype(f32)
                    v=(v*cos-partner(v)*sin).astype(bf)
                dps[r,c:c+W]=v
                gb_ref[0:1,c:c+W]+=jnp.sum(v.astype(f32),0,keepdims=True)
        for j in range(3*D//512):
            dn+=dot(dps[r,j*512:(j+1)*512],w_ref[:,j*512:(j+1)*512],NT)
        n,rs=moments(x_ref[r,:].astype(f32))
        for k,x in ((0,dn),(1,dn*n)):
            a,b=sums(x,seg)
            ge_ref[0:1,k*D:(k+1)*D]+=a; ge_ref[1:2,k*D:(k+1)*D]+=b
        dn=dn*(1.0+pick(seg,emb_ref,1,D))
        gf_ref[r,:]=dm_ref[r,:]+(dn-jnp.mean(dn,-1,keepdims=True)-n*jnp.mean(dn*n,-1,keepdims=True))*rs
    @pl.loop(0,D//256)
    def _(i):
        c=pl.ds(pl.multiple_of(i*256,256),256)
        for j in range(3):
            gw_ref[c,j*D:(j+1)*D]=dot(n1_ref[:,c],dps[:,j*D:(j+1)*D],TN).astype(bf)

def tail(x,n1,dm,g,seg,emb,w,cos,sin,R=128):
    F,D=x.shape; nd=g.shape[0]; W=D//nd
    S=jax.ShapeDtypeStruct
    return pl.pallas_call(functools.partial(tail_kernel,R=R,nd=nd,W=W),
        out_shape=(S((F,D),f32),S((D,3*D),bf),S((8,3*D),f32),S((8,2*D),f32)),
        in_specs=[V]*9,out_specs=(V,)*4,
        scratch_shapes=[pltpu.VMEM((F,3*D),bf)],
        compiler_params=pltpu.CompilerParams(vmem_limit_bytes=60*2**20),name="tail",
        cost_estimate=pl.CostEstimate(flops=4*F*D*3*D,bytes_accessed=20*2**20,transcendentals=0))(x,n1,dm,g,seg,emb,w,cos,sin)

HS=("head","seq")

def body(frames,time_embed,segment_ids,frame_mask,positions,w_ada,b_ada,w_qkv,b_qkv,w_out,b_out,w_up,b_up,w_down,b_down,cotangent):
    _,F,D=frames.shape
    nd=lax.axis_size("head"); ns=lax.axis_size("seq"); dev=lax.axis_index("head")*ns+lax.axis_index("seq")
    W=D//nd
    E=b_ada.shape[0]; E6=w_ada.shape[1]; K=w_ada.shape[0]
    x=frames[0]; cot=cotangent[0]; seg=segment_ids[0]; msk=frame_mask[0]
    def reorder(w): return w.reshape(-1,3,nd,W).transpose(0,2,1,3).reshape(-1,3*D)
    def restore(w): return w.reshape(-1,nd,3,W).transpose(0,2,1,3).reshape(-1,3*D)
    g=lambda w: lax.all_gather(w,HS,axis=0,tiled=True)
    wq=g(reorder(w_qkv))
    bias=g(jnp.concatenate([b_qkv,b_out,b_up,b_down])[None,:]).astype(f32)
    n0,n1,n2,n3=b_qkv.shape[0],b_out.shape[0],b_up.shape[0],b_down.shape[0]
    bq=reorder(bias[:,:n0].reshape(1,-1))
    bo=bias[:,n0:n0+n1].reshape(1,-1); bu=bias[:,n0+n1:n0+n1+n2].reshape(1,-1); bd=bias[:,n0+n1+n2:].reshape(1,-1)
    wo=g(w_out); wu=g(w_up); wd=g(w_down)
    time_all=lax.all_gather(time_embed,"seq",axis=0,tiled=True).astype(f32)
    act_all=jax.nn.silu(time_all).astype(bf)
    act_own=lax.dynamic_slice_in_dim(act_all,dev*K,K,2)
    part=jnp.einsum("rsd,de->rse",act_own,w_ada,preferred_element_type=f32)
    part=part+lax.dynamic_update_slice(jnp.zeros((E6,),f32),b_ada.astype(f32),(dev*E,))
    emb=lax.psum(lax.psum_scatter(part,"seq",scatter_dimension=0,tiled=True),"head")[0]
    column=lax.iota(jnp.int32,128)
    pair=(column%HD//2).astype(f32)
    angles=positions[0].astype(f32)[:,None]*(10000.0**(-(2.0*pair)/HD))
    cos=jnp.cos(angles); sin=jnp.where(column%2==0,-jnp.sin(angles),jnp.sin(angles))
    segc=seg[:,None]; mskc=msk.astype(f32)[:,None]
    normed,packed=qkv_proj(x,segc,emb,wq,bq,cos,sin,nd)
    qkv=lax.all_to_all(packed,"head",split_axis=0,concat_axis=0,tiled=True).reshape(nd*F,3*W)
    seg_row=lax.all_gather(seg,"head",axis=0,tiled=True); msk_row=lax.all_gather(msk,"head",axis=0,tiled=True)
    T=256
    qlo,qhi,klo,khi=tables(seg_row,msk_row,T)
    aq,ak=aux(seg_row,msk_row)
    o,lse=attn_fwd(qkv,qlo,qhi,aq,ak,T)
    def back(a):
        return lax.all_to_all(a.reshape(nd,F,-1),"head",split_axis=0,concat_axis=0,tiled=True)
    att=back(o).transpose(1,0,2).reshape(F,D)
    out,dmid,datt,gout,gup,gdown,gb,ge=mid(x,att,cot,segc,mskc,emb,wo,bo,wu,bu,wd,bd)
    do=lax.all_to_all(datt.reshape(F,nd,W).transpose(1,0,2),"head",split_axis=0,concat_axis=0,tiled=True).reshape(nd*F,W)
    dqkv=attn_bwd(qkv,o,do,lse,klo,khi,aq,ak,T)
    gx,gqkv,gbq,ge1=tail(x,normed,dmid,back(dqkv),segc,emb,wq,cos,sin)
    rs=lambda w: lax.psum_scatter(w,HS,scatter_dimension=0,tiled=True).astype(f32)
    demb=lax.psum(jnp.concatenate([ge1[:2],ge[:2]],axis=1),"head").astype(bf)
    demb_all=lax.all_gather(demb[None],"seq",axis=0,tiled=True)
    gada=jnp.einsum("rsd,rse->de",act_own,demb_all,preferred_element_type=f32)
    gbada=jnp.sum(lax.dynamic_slice_in_dim(demb_all,dev*E,E,2).astype(f32),(0,1))
    dact=jnp.einsum("rse,de->rsd",demb_all,w_ada,preferred_element_type=f32)
    dact=lax.all_to_all(dact,"seq",split_axis=0,concat_axis=0,tiled=True)
    dact=lax.all_gather(dact,"head",axis=0,tiled=True).transpose(1,0,2).reshape(2,D)
    _,pull=jax.vjp(jax.nn.silu,time_embed[0].astype(f32))
    gtime=pull(dact)[0][None]
    gbias=jnp.concatenate([restore(gbq[0:1]).reshape(-1,n0),gb[0,:D].reshape(-1,n1),gb[1].reshape(-1,n2),gb[2,:D].reshape(-1,n3)],axis=1)
    gbias=lax.psum_scatter(gbias,HS,scatter_dimension=0,tiled=True)[0]
    return (out[None],gx[None],gtime,gada,gbada,restore(rs(gqkv)),gbias[:n0],rs(gout),gbias[n0:n0+n1],rs(gup),gbias[n0+n1:n0+n1+n2],rs(gdown),gbias[n0+n1+n2:])


def solution(mesh):
    row=P("seq","head",None); ids=P("seq","head"); mat=P(HS,None); vec=P(HS); tim=P("seq",None,None)
    in_specs=(row,tim,ids,ids,ids)+(mat,vec)*5+(row,)
    out_specs=(row,row,tim)+(mat,vec)*5
    return jax.shard_map(body,mesh=mesh,in_specs=in_specs,out_specs=out_specs,check_vma=False)
```

```python
import functools
import math

import jax
import jax.numpy as jnp
from jax import lax
from jax.experimental import pallas as pl
from jax.experimental.pallas import tpu as pltpu
from jax.sharding import PartitionSpec as P

bf = jnp.bfloat16
f32 = jnp.float32
HS = ("head", "seq")
ANY = pl.BlockSpec(memory_space=pl.ANY)
V = pl.BlockSpec(memory_space=pltpu.VMEM)
NN = (((1,), (0,)), ((), ()))
NT = (((1,), (1,)), ((), ()))
TN = (((0,), (0,)), ((), ()))


def dot(a, b, dims=NN):
    return lax.dot_general(a, b, dims, preferred_element_type=f32)


HD=64
LOG2E=math.log2(math.e)
NEG=-1e30

def fwd_kernel(lo_ref,hi_ref,qkv_ref,auxq_ref,auxk_ref,o_ref,lse_ref,k2,vx,q2,s_scr,m_scr,acc,*,T,nh):
    qt=pl.program_id(0)
    W=nh*HD
    L=qkv_ref.shape[0]
    nk=L//T
    lane=lax.broadcasted_iota(jnp.int32,(T,128),1)
    @pl.when(qt==0)
    def _():
        @pl.loop(0,nk)
        def _(t):
            r=pl.ds(pl.multiple_of(t*T,T),T)
            for h in range(nh):
                k=qkv_ref[r,W+h*HD:W+(h+1)*HD]
                k2[h,t]=jnp.concatenate([k,k],axis=1)
                v=qkv_ref[r,2*W+h*HD:2*W+(h+1)*HD]
                one=jnp.where(lax.broadcasted_iota(jnp.int32,(T,HD),1)==0,1.0,0.0).astype(bf)
                vx[h,t]=jnp.concatenate([v,one],axis=1)
    lo=lo_ref[qt]; hi=hi_ref[qt]
    r=pl.ds(pl.multiple_of(qt*T,T),T)
    for h in range(nh):
        q=qkv_ref[r,h*HD:(h+1)*HD].astype(f32)*(HD**-0.5*LOG2E)
        qh=q.astype(bf)
        ql=(q-qh.astype(f32)).astype(bf)
        q2[h]=jnp.concatenate([qh,ql],axis=1)
    auxq=auxq_ref[r,:]
    eye=lax.broadcasted_iota(jnp.int32,(T,T),0)==lax.broadcasted_iota(jnp.int32,(T,T),1)
    def mx(s):
        m=s[:,:128]
        for j in range(1,T//128): m=jnp.maximum(m,s[:,j*128:(j+1)*128])
        return m
    ak=auxk_ref[r,:]
    for h in range(nh):
        raw=dot(q2[h],k2[h,qt],NT)
        s=dot(jnp.concatenate([q2[h],auxq],axis=1),jnp.concatenate([k2[h,qt],ak],axis=1),NT)
        s=jnp.where(eye,raw,s)
        s_scr[h,qt]=s
        m_scr[h]=mx(s)
    @pl.loop(lo,hi-1)
    def _(t):
        kt=jnp.where(t>=qt,t+1,t)
        ak=auxk_ref[pl.ds(pl.multiple_of(kt*T,T),T),:]
        for h in range(nh):
            s=dot(jnp.concatenate([q2[h],auxq],axis=1),jnp.concatenate([k2[h,kt],ak],axis=1),NT)
            s_scr[h,kt]=s
            m_scr[h]=jnp.maximum(m_scr[h],mx(s))
    for h in range(nh):
        m_scr[h]=jnp.broadcast_to(jnp.max(m_scr[h],axis=1,keepdims=True),(T,128))
        acc[h]=jnp.zeros((T,128),f32)
    @pl.loop(lo,hi)
    def _(kt):
        for h in range(nh):
            s=s_scr[h,kt]; m=m_scr[h]
            p=jnp.exp2(s-jnp.concatenate([m]*(T//128),axis=1)).astype(bf)
            acc[h]+=dot(p,vx[h,kt])
    lse=jnp.zeros((T,128),f32)
    for h in range(nh):
        a=acc[h]
        l=a[:,HD:HD+1]
        o_ref[:,h*HD:(h+1)*HD]=(a[:,:HD]/l).astype(bf)
        lse=jnp.where(lane==h,m_scr[h]+jnp.log2(l),lse)
    lse_ref[...]=lse

def attn_fwd(qkv,lo,hi,auxq,auxk,T):
    L,W3=qkv.shape; W=W3//3; nh=W//HD; nk=L//T
    return pl.pallas_call(
        functools.partial(fwd_kernel,T=T,nh=nh),
        out_shape=(jax.ShapeDtypeStruct((L,W),bf),jax.ShapeDtypeStruct((L,128),f32)),
        grid_spec=pltpu.PrefetchScalarGridSpec(num_scalar_prefetch=2,grid=(nk,),
            in_specs=[pl.BlockSpec((L,W3),lambda i,*_:(0,0)),pl.BlockSpec((L,128),lambda i,*_:(0,0)),pl.BlockSpec((L,128),lambda i,*_:(0,0))],
            out_specs=[pl.BlockSpec((T,W),lambda i,*_:(i,0)),pl.BlockSpec((T,128),lambda i,*_:(i,0))],
            scratch_shapes=[pltpu.VMEM((nh,nk,T,128),bf),pltpu.VMEM((nh,nk,T,128),bf),pltpu.VMEM((nh,T,128),bf),
                pltpu.VMEM((nh,nk,T,T),f32),pltpu.VMEM((nh,T,128),f32),pltpu.VMEM((nh,T,128),f32)]),
        compiler_params=pltpu.CompilerParams(vmem_limit_bytes=60*2**20),
        name="attn_fwd",
    )(lo,hi,qkv,auxq,auxk)

def bwd_kernel(lo_ref,hi_ref,qkv_ref,o_ref,do_ref,lse_ref,auxq_ref,auxk_ref,dqkv_ref,q2,qa,k2,dox,vx,kT,dqT,dk,dv,*,T,nh):
    kt=pl.program_id(0)
    W=nh*HD
    L=qkv_ref.shape[0]
    nk=L//T
    lane=lax.broadcasted_iota(jnp.int32,(T,128),1)
    lane64=lax.broadcasted_iota(jnp.int32,(T,HD),1)
    @pl.when(kt==0)
    def _():
        dqT[...]=jnp.zeros_like(dqT)
        @pl.loop(0,nk)
        def _(t):
            r=pl.ds(pl.multiple_of(t*T,T),T)
            lse=lse_ref[r,:]
            aq=auxq_ref[r,:].astype(f32)
            kT[t]=qkv_ref[r,W:2*W].T
            for h in range(nh):
                q=qkv_ref[r,h*HD:(h+1)*HD].astype(f32)*(HD**-0.5*LOG2E)
                qh=q.astype(bf)
                ql=(q-qh.astype(f32)).astype(bf)
                q2[h,t]=jnp.concatenate([qh,ql],axis=1)
                k=qkv_ref[r,W+h*HD:W+(h+1)*HD]
                k2[h,t]=jnp.concatenate([k,k],axis=1)
                v=qkv_ref[r,2*W+h*HD:2*W+(h+1)*HD]
                vx[h,t]=jnp.concatenate([v,jnp.where(lane64<2,1.0,0.0).astype(bf)],axis=1)
                nl=-lse[:,h:h+1]
                l1=nl.astype(bf).astype(f32); l2=(nl-l1).astype(bf).astype(f32); l3=nl-l1-l2
                qa[h,t]=jnp.where(lane==0,l1,jnp.where(lane==1,l2,jnp.where(lane==2,l3,aq))).astype(bf)
                do=do_ref[r,h*HD:(h+1)*HD]
                nd=-jnp.sum(do.astype(f32)*o_ref[r,h*HD:(h+1)*HD].astype(f32),axis=1,keepdims=True)
                d1=nd.astype(bf).astype(f32); d2=nd-d1
                dox[h,t]=jnp.concatenate([do,jnp.where(lane64==0,d1,jnp.where(lane64==1,d2,0.0)).astype(bf)],axis=1)
    r=pl.ds(pl.multiple_of(kt*T,T),T)
    ak=auxk_ref[r,:]
    lo=lo_ref[kt]; hi=hi_ref[kt]
    def tile(qt,diag):
        rq=pl.ds(pl.multiple_of(qt*T,T),T)
        for h in range(nh):
            kx=jnp.concatenate([k2[h,kt],ak],axis=1)
            s=dot(kx,jnp.concatenate([q2[h,qt],qa[h,qt]],axis=1),NT)
            if diag:
                eye=lax.broadcasted_iota(jnp.int32,(T,T),0)==lax.broadcasted_iota(jnp.int32,(T,T),1)
                qr=jnp.where(lane<3,qa[h,qt].astype(f32),0.0).astype(bf)
                raw=dot(kx,jnp.concatenate([q2[h,qt],qr],axis=1),NT)
                s=jnp.where(eye,raw,s)
            p=jnp.exp2(s)
            dp=dot(vx[h,kt],dox[h,qt],NT)
            ds=(p*dp).astype(bf)
            pb=p.astype(bf)
            g=h//2
            rv=dot(pb,do_ref[rq,g*128:(g+1)*128])
            rk=dot(ds,qkv_ref[rq,g*128:(g+1)*128])
            dv[h]+=rv
            dk[h]+=rk
            dqT[qt,h*HD:(h+1)*HD,:]+=dot(kT[kt,h*HD:(h+1)*HD,:],ds)
    dk[...]=jnp.zeros_like(dk); dv[...]=jnp.zeros_like(dv)
    tile(kt,True)
    @pl.loop(lo,hi-1)
    def _(t):
        tile(jnp.where(t>=kt,t+1,t),False)
    for g in range(nh//2):
        dqkv_ref[r,W+g*128:W+(g+1)*128]=(jnp.where(lane<HD,dk[2*g],dk[2*g+1])*HD**-0.5).astype(bf)
        dqkv_ref[r,2*W+g*128:2*W+(g+1)*128]=jnp.where(lane<HD,dv[2*g],dv[2*g+1]).astype(bf)
    @pl.when(kt==nk-1)
    def _():
        @pl.loop(0,nk)
        def _(t):
            dqkv_ref[pl.ds(pl.multiple_of(t*T,T),T),0:W]=(dqT[t].T*HD**-0.5).astype(bf)

def attn_bwd(qkv,o,do,lse,lo,hi,auxq,auxk,T):
    L,W3=qkv.shape; W=W3//3; nh=W//HD; nk=L//T
    full=lambda w: pl.BlockSpec((L,w),lambda i,*_:(0,0))
    return pl.pallas_call(
        functools.partial(bwd_kernel,T=T,nh=nh),
        out_shape=jax.ShapeDtypeStruct((L,W3),bf),
        grid_spec=pltpu.PrefetchScalarGridSpec(num_scalar_prefetch=2,grid=(nk,),
            in_specs=[full(W3),full(W),full(W),full(128),full(128),full(128)],
            out_specs=full(W3),
            scratch_shapes=[pltpu.VMEM((nh,nk,T,128),bf)]*5+[pltpu.VMEM((nk,W,T),bf),pltpu.VMEM((nk,W,T),f32),
                pltpu.VMEM((nh,T,128),f32),pltpu.VMEM((nh,T,128),f32)]),
        compiler_params=pltpu.CompilerParams(vmem_limit_bytes=60*2**20),
        name="attn_bwd",
    )(lo,hi,qkv,o,do,lse,auxq,auxk)

def tables(seg,mask,T):
    L=seg.shape[0]; nk=L//T
    s=seg.reshape(nk,T); m=mask.reshape(nk,T)
    has=jnp.stack([jnp.any(s==c,axis=1) for c in (0,1)],1)
    real=jnp.stack([jnp.any((s==c)&(m==1),axis=1) for c in (0,1)],1)
    use=jnp.any(has[:,None,:]&real[None,:,:],axis=2)|jnp.eye(nk,dtype=bool)
    idx=jnp.arange(nk,dtype=jnp.int32)
    qlo=jnp.min(jnp.where(use,idx[None,:],nk),axis=1); qhi=jnp.max(jnp.where(use,idx[None,:],-1),axis=1)+1
    klo=jnp.min(jnp.where(use,idx[:,None],nk),axis=0); khi=jnp.max(jnp.where(use,idx[:,None],-1),axis=0)+1
    return [a.astype(jnp.int32) for a in (qlo,qhi,klo,khi)]
def aux(seg,mask):
    L=seg.shape[0]
    lane=lax.broadcasted_iota(jnp.int32,(L,128),1)
    sg=seg[:,None]; pad=(mask==0)[:,None]
    aq=jnp.where(lane==3,jnp.where(sg!=0,NEG,0.),jnp.where(lane==4,jnp.where(sg!=1,NEG,0.),jnp.where(lane==5,NEG,0.))).astype(bf)
    ak=jnp.where(lane<3,1.,jnp.where(lane==3,(sg==0).astype(f32),jnp.where(lane==4,(sg==1).astype(f32),jnp.where(lane==5,pad.astype(f32),0.)))).astype(bf)
    return aq,ak

EPS=1e-6

def moments(x):
    c=jnp.mean(x,-1,keepdims=True)
    xc=x-c
    rs=lax.rsqrt(jnp.mean(xc*xc,-1,keepdims=True)+EPS)
    return xc*rs, rs
def pick(seg,emb,i,D):
    return jnp.where(seg==0,emb[0:1,i*D:(i+1)*D],emb[1:2,i*D:(i+1)*D])
def sums(x,seg):
    a=jnp.sum(jnp.where(seg==0,x,0.0),0,keepdims=True); b=jnp.sum(jnp.where(seg==1,x,0.0),0,keepdims=True)
    return a,b
def partner(v):
    w=v.shape[1]
    lane=lax.broadcasted_iota(jnp.int32,v.shape,1)
    return jnp.where(lane%2==0,pltpu.roll(v,w-1,1),pltpu.roll(v,1,1))
def gelu_both(v):
    c=math.sqrt(2/math.pi)
    v2=v*v
    t=jnp.tanh(c*v*(1.0+0.044715*v2))
    h=0.5*(1.0+t)
    return v*h, h+0.5*v*(1.0-t*t)*(c*(1.0+3*0.044715*v2))

def qkv_kernel(x_ref,seg_ref,emb_ref,w_ref,b_ref,cos_ref,sin_ref,n_ref,p_ref,*,R,nd,W):
    F,D=x_ref.shape
    @pl.loop(0,F//R)
    def _(i):
        r=pl.ds(pl.multiple_of(i*R,R),R)
        seg=seg_ref[r,:]
        n,_=moments(x_ref[r,:].astype(f32))
        y=(n*(1.0+pick(seg,emb_ref,1,D))+pick(seg,emb_ref,0,D)).astype(bf)
        n_ref[r,:]=y
        cos=jnp.concatenate([cos_ref[r,:]]*(W//128),1); sin=jnp.concatenate([sin_ref[r,:]]*(W//128),1)
        for d in range(nd):
            for j in range(3):
                c=(d*3+j)*W
                v=dot(y,w_ref[:,c:c+W])+b_ref[0:1,c:c+W]
                if j<2: v=v*cos+partner(v)*sin
                p_ref[d,r,j*W:(j+1)*W]=v.astype(bf)

def qkv_proj(x,seg,emb,w,b,cos,sin,nd,R=128):
    F,D=x.shape; W=D//nd
    return pl.pallas_call(functools.partial(qkv_kernel,R=R,nd=nd,W=W),
        out_shape=(jax.ShapeDtypeStruct((F,D),bf),jax.ShapeDtypeStruct((nd,F,3*W),bf)),
        in_specs=[V]*7,out_specs=(V,V),
        compiler_params=pltpu.CompilerParams(vmem_limit_bytes=60*2**20),name="qkv_proj",
        cost_estimate=pl.CostEstimate(flops=2*F*D*3*D,bytes_accessed=14*2**20,transcendentals=0))(x,seg,emb,w,b,cos,sin)

def mid_kernel(x_ref,a_ref,c_ref,seg_ref,msk_ref,emb_ref,w_ref,bo_ref,bu_ref,bd_ref,
               out_ref,dm_ref,da_ref,gw_ref,gb_ref,ge_ref,
               wo_ref,wu_ref,wd_ref,n2s,acts,dhs,dfs,dps,dgelu,sem,*,R):
    F,D=x_ref.shape; H=bu_ref.shape[1]; CH=512
    loads=[pltpu.make_async_copy(w_ref.at[:,pl.ds(o,n)],r,sem.at[i]) for i,(o,n,r) in enumerate(((2*H,D,wo_ref),(0,H,wu_ref),(H,H,wd_ref)))]
    for l in loads: l.start()
    gb_ref[...]=jnp.zeros_like(gb_ref); ge_ref[...]=jnp.zeros_like(ge_ref)
    for l in loads: l.wait()
    def down(j):
        t,o=divmod(j*CH,D)
        return slice(o,o+CH),slice(t*D,(t+1)*D)
    @pl.loop(0,F//R)
    def _(i):
        r=pl.ds(pl.multiple_of(i*R,R),R)
        seg=seg_ref[r,:]; msk=msk_ref[r,:]
        def acc(k,x):
            a,b=sums(x,seg)
            ge_ref[0:1,k*D:(k+1)*D]+=a; ge_ref[1:2,k*D:(k+1)*D]+=b
        branch=(dot(a_ref[r,:],wo_ref[...])+bo_ref[0:1,:])*msk
        g1=pick(seg,emb_ref,2,D)
        middle=x_ref[r,:].astype(f32)+g1*branch
        n,rs=moments(middle)
        sc2=1.0+pick(seg,emb_ref,4,D)
        n2=(n*sc2+pick(seg,emb_ref,3,D)).astype(bf)
        n2s[r,:]=n2
        feed=jnp.broadcast_to(bd_ref[0:1,:],(R,D))
        for j in range(H//CH):
            c=slice(j*CH,(j+1)*CH)
            h=dot(n2,wu_ref[:,c])+bu_ref[0:1,c]
            a,g=gelu_both(h)
            a=a.astype(bf)
            acts[r,c]=a; dgelu[:,c]=g
            feed+=dot(a,wd_ref[down(j)])
        up=c_ref[r,:].astype(f32)
        g2=pick(seg,emb_ref,5,D)
        out_ref[r,:]=(middle+g2*feed).astype(bf)
        df=(up*g2).astype(bf)
        dfs[r,:]=df
        acc(3,up*feed)
        gb_ref[2:3,0:D]+=jnp.sum(df.astype(f32),0,keepdims=True)
        dn=jnp.zeros((R,D),f32)
        for j in range(H//CH):
            c=slice(j*CH,(j+1)*CH)
            dh=(dot(df,wd_ref[down(j)],NT)*dgelu[:,c]).astype(bf)
            dhs[r,c]=dh
            gb_ref[1:2,c]+=jnp.sum(dh.astype(f32),0,keepdims=True)
            dn+=dot(dh,wu_ref[:,c],NT)
        acc(1,dn); acc(2,dn*n)
        dn=dn*sc2
        dmid=up+(dn-jnp.mean(dn,-1,keepdims=True)-n*jnp.mean(dn*n,-1,keepdims=True))*rs
        dm_ref[r,:]=dmid
        acc(0,dmid*branch)
        dp=(dmid*g1*msk).astype(bf)
        dps[r,:]=dp
        gb_ref[0:1,0:D]+=jnp.sum(dp.astype(f32),0,keepdims=True)
        da_ref[r,:]=dot(dp,wo_ref[...],NT).astype(bf)
    @pl.loop(0,D//256)
    def _(i):
        c=pl.ds(pl.multiple_of(i*256,256),256)
        gw_ref[c,2*H:2*H+D]=dot(a_ref[:,c],dps[...],TN).astype(bf)
        gw_ref[c,0:H]=dot(n2s[:,c],dhs[...],TN).astype(bf)
        for t in range(H//D):
            e=pl.ds(pl.multiple_of(t*D+i*256,256),256)
            gw_ref[c,H+t*D:H+(t+1)*D]=dot(acts[:,e],dfs[...],TN).astype(bf)

def mid(x,a,c,seg,msk,emb,w,bo,bu,bd,R=128):
    F,D=x.shape; H=bu.shape[1]
    S=jax.ShapeDtypeStruct; M=pltpu.VMEM
    return pl.pallas_call(functools.partial(mid_kernel,R=R),
        out_shape=(S((F,D),bf),S((F,D),f32),S((F,D),bf),S((D,2*H+D),bf),S((8,H),f32),S((8,4*D),f32)),
        in_specs=[V]*6+[ANY]+[V]*3,out_specs=(V,)*6,
        scratch_shapes=[M((D,D),bf),M((D,H),bf),M((D,H),bf),M((F,D),bf),M((F,H),bf),M((F,H),bf),M((F,D),bf),M((F,D),bf),M((R,H),f32),pltpu.SemaphoreType.DMA((3,))],
        compiler_params=pltpu.CompilerParams(vmem_limit_bytes=62*2**20),name="mid",
        cost_estimate=pl.CostEstimate(flops=6*F*D*(D+2*H),bytes_accessed=30*2**20,transcendentals=F*H))(x,a,c,seg,msk,emb,w,bo,bu,bd)

def tail_kernel(x_ref,n1_ref,dm_ref,g_ref,seg_ref,emb_ref,w_ref,cos_ref,sin_ref,gf_ref,gw_ref,gb_ref,ge_ref,dps,*,R,nd,W):
    F,D=x_ref.shape
    gb_ref[...]=jnp.zeros_like(gb_ref); ge_ref[...]=jnp.zeros_like(ge_ref)
    @pl.loop(0,F//R)
    def _(i):
        r=pl.ds(pl.multiple_of(i*R,R),R)
        seg=seg_ref[r,:]
        cos=jnp.concatenate([cos_ref[r,:]]*(W//128),1); sin=jnp.concatenate([sin_ref[r,:]]*(W//128),1)
        dn=jnp.zeros((R,D),f32)
        for d in range(nd):
            for j in range(3):
                c=(d*3+j)*W
                v=g_ref[d,r,j*W:(j+1)*W]
                if j<2:
                    v=v.astype(f32)
                    v=(v*cos-partner(v)*sin).astype(bf)
                dps[r,c:c+W]=v
                gb_ref[0:1,c:c+W]+=jnp.sum(v.astype(f32),0,keepdims=True)
        for j in range(3*D//512):
            dn+=dot(dps[r,j*512:(j+1)*512],w_ref[:,j*512:(j+1)*512],NT)
        n,rs=moments(x_ref[r,:].astype(f32))
        for k,x in ((0,dn),(1,dn*n)):
            a,b=sums(x,seg)
            ge_ref[0:1,k*D:(k+1)*D]+=a; ge_ref[1:2,k*D:(k+1)*D]+=b
        dn=dn*(1.0+pick(seg,emb_ref,1,D))
        gf_ref[r,:]=dm_ref[r,:]+(dn-jnp.mean(dn,-1,keepdims=True)-n*jnp.mean(dn*n,-1,keepdims=True))*rs
    @pl.loop(0,D//256)
    def _(i):
        c=pl.ds(pl.multiple_of(i*256,256),256)
        for j in range(3):
            gw_ref[c,j*D:(j+1)*D]=dot(n1_ref[:,c],dps[:,j*D:(j+1)*D],TN).astype(bf)

def tail(x,n1,dm,g,seg,emb,w,cos,sin,R=128):
    F,D=x.shape; nd=g.shape[0]; W=D//nd
    S=jax.ShapeDtypeStruct
    return pl.pallas_call(functools.partial(tail_kernel,R=R,nd=nd,W=W),
        out_shape=(S((F,D),f32),S((D,3*D),bf),S((8,3*D),f32),S((8,2*D),f32)),
        in_specs=[V]*9,out_specs=(V,)*4,
        scratch_shapes=[pltpu.VMEM((F,3*D),bf)],
        compiler_params=pltpu.CompilerParams(vmem_limit_bytes=60*2**20),name="tail",
        cost_estimate=pl.CostEstimate(flops=4*F*D*3*D,bytes_accessed=20*2**20,transcendentals=0))(x,n1,dm,g,seg,emb,w,cos,sin)

def sizes(nd,ns):
    Y=2**((ns.bit_length()-1)//2)
    return nd//2,Y,ns//Y

class Place:
    def __init__(self,nd,ns):
        self.nd,self.ns=nd,ns
        self.X,self.Y,self.Z=sizes(nd,ns)
        self.h=lax.axis_index("head"); self.s=lax.axis_index("seq")
        self.x,self.c=self.h//2,self.h%2
        self.z,self.y=self.s//self.Y,self.s%self.Y
    def at(self,x=None,c=None,z=None,y=None):
        x=self.x if x is None else x; c=self.c if c is None else c
        z=self.z if z is None else z; y=self.y if y is None else y
        return (x*2+c,z*self.Y+y)

def near_first(n):
    out=[]
    for d in range(1,n//2+1):
        out.append(d)
        if n-d!=d: out.append(n-d)
    return out

def remote(src,dst,ss,rs,dev):
    cp=pltpu.make_async_remote_copy(src_ref=src,dst_ref=dst,send_sem=ss,recv_sem=rs,device_id=dev,device_id_type=pl.DeviceIdType.MESH)
    cp.start()
    return cp

def greet_all(p):
    b=pltpu.get_barrier_semaphore()
    @pl.loop(0,p.nd)
    def _(dh):
        @pl.loop(0,p.ns)
        def _(ds):
            @pl.when(dh+ds>0)
            def _():
                pl.semaphore_signal(b,inc=1,device_id=(lax.rem(p.h+dh,p.nd),lax.rem(p.s+ds,p.ns)),device_id_type=pl.DeviceIdType.MESH)
    pl.semaphore_wait(b,p.nd*p.ns-1)

class Gather:
    @staticmethod
    def sems(nd,ns):
        X,Y,Z=sizes(nd,ns)
        D=pltpu.SemaphoreType.DMA
        one=[D((Z,)),D((Z,X)),D((Z,Y)),D((Z,X,Y)),D((Z,X,Y)),D((Z,)),D((2,Z,X,Y))]
        return one+one+[D(())]
    def __init__(self,p,shard,out,sems):
        self.p,self.shard,self.out=p,shard,out
        self.ss,self.rs,self.ls=sems[:7],sems[7:14],sems[14]
        self.all=[]; self.half=shard.shape[-1]//2
        self.two={}; self.three={}
    def send(self,k,idx,src,dst,dev):
        cp=remote(src,dst,self.ss[k].at[idx],self.rs[k].at[idx],dev)
        self.all.append(cp); return cp
    def cols(self,part): return pl.ds(part*self.half,self.half)
    def loc(self,x,z,y,part=None):
        r=self.out.at[x,self.p.c,z,y]
        return r if part is None else r.at[:,self.cols(part)]
    def start(self):
        p=self.p
        self.zc={}
        for dz in near_first(p.Z):
            self.zc[dz]=self.send(0,(dz,),self.shard,self.loc(p.x,p.z,p.y),p.at(z=lax.rem(p.z+dz,p.Z)))
        self.local=pltpu.make_async_copy(self.shard,self.loc(p.x,p.z,p.y),self.ls)
        self.local.start()
        self.second(0)
    def second(self,dz):
        p=self.p; zz=lax.rem(p.z+p.Z-dz,p.Z)
        if dz: self.zc[dz].wait_recv()
        def src(part=None):
            if dz: return self.loc(p.x,zz,p.y,part)
            return self.shard if part is None else self.shard.at[:,self.cols(part)]
        for dx in near_first(p.X):
            self.two[0,dz,dx]=self.send(1,(dz,dx),src(0),self.loc(p.x,zz,p.y,0),p.at(x=lax.rem(p.x+dx,p.X)))
        for dy in near_first(p.Y):
            self.two[1,dz,dy]=self.send(2,(dz,dy),src(1),self.loc(p.x,zz,p.y,1),p.at(y=lax.rem(p.y+dy,p.Y)))
        self.send(5,(dz,),src(),self.loc(p.x,zz,p.y),p.at(c=1-p.c))
        for dy in near_first(p.Y):
            self.three[0,dz,0,dy]=self.send(3,(dz,0,dy),src(0),self.loc(p.x,zz,p.y,0),p.at(y=lax.rem(p.y+dy,p.Y)))
        for dx in near_first(p.X):
            self.three[1,dz,dx,0]=self.send(4,(dz,dx,0),src(1),self.loc(p.x,zz,p.y,1),p.at(x=lax.rem(p.x+dx,p.X)))
    def third(self,dz):
        p=self.p; zz=lax.rem(p.z+p.Z-dz,p.Z)
        for dx in near_first(p.X):
            self.two[0,dz,dx].wait_recv()
            l=self.loc(lax.rem(p.x+p.X-dx,p.X),zz,p.y,0)
            for dy in near_first(p.Y):
                self.three[0,dz,dx,dy]=self.send(3,(dz,dx,dy),l,l,p.at(y=lax.rem(p.y+dy,p.Y)))
            self.send(6,(0,dz,dx,0),l,l,p.at(c=1-p.c))
        for dy in near_first(p.Y):
            self.two[1,dz,dy].wait_recv()
            l=self.loc(p.x,zz,lax.rem(p.y+p.Y-dy,p.Y),1)
            for dx in near_first(p.X):
                self.three[1,dz,dx,dy]=self.send(4,(dz,dx,dy),l,l,p.at(x=lax.rem(p.x+dx,p.X)))
            self.send(6,(1,dz,0,dy),l,l,p.at(c=1-p.c))
    def fourth(self,dz):
        p=self.p; zz=lax.rem(p.z+p.Z-dz,p.Z)
        for part in (0,1):
            for dx in range(p.X):
                for dy in range(p.Y):
                    if (part,dz,dx,dy) not in self.three: continue
                    self.three[part,dz,dx,dy].wait_recv()
                    l=self.loc(lax.rem(p.x+p.X-dx,p.X),zz,lax.rem(p.y+p.Y-dy,p.Y),part)
                    self.send(6,(part,dz,dx,dy),l,l,p.at(c=1-p.c))
    def finish(self):
        waited=set()
        for cp in self.zc.values(): waited.add(id(cp))
        for d in (self.two,self.three):
            for cp in d.values(): waited.add(id(cp))
        for cp in self.all:
            if id(cp) not in waited: cp.wait_recv()
            cp.wait_send()
        self.local.wait()

def entry_kernel(nd,ns,nw,*refs):
    shards=refs[:nw]; bias,time,ids,wada=refs[nw:nw+4]
    outs=refs[nw+4:2*nw+4]; bias_all,ids_all,emb,act=refs[2*nw+4:2*nw+8]
    time_all,part,r1,r2,bs,br,isd,ir,ts,tr,e1s,e1r,e2s,e2r=refs[2*nw+8:2*nw+22]
    gs=refs[2*nw+22:]
    p=Place(nd,ns); n=len(Gather.sems(nd,ns))
    greet_all(p)
    tail=[]
    first=[]
    for ds in range(1,ns):
        first.append(remote(time,time_all.at[p.s],ts.at[ds],tr.at[ds],(p.h,lax.rem(p.s+ds,ns))))
    g=[Gather(p,shards[i],outs[i],gs[i*n:(i+1)*n]) for i in range(nw)]
    for a in g: a.start()
    me=p.h*ns+p.s
    for dh in range(1,nd):
        tail.append(remote(ids,ids_all.at[p.h],isd.at[dh],ir.at[dh],(lax.rem(p.h+dh,nd),p.s)))
    @pl.loop(0,nd)
    def _(dh):
        @pl.loop(0,ns)
        def _(ds):
            @pl.when(dh+ds>0)
            def _():
                remote(bias,bias_all.at[me],bs.at[dh,ds],br.at[dh,ds],(lax.rem(p.h+dh,nd),lax.rem(p.s+ds,ns)))
    l1=pltpu.make_async_copy(bias,bias_all.at[me],bs.at[0,0]); l1.start()
    l2=pltpu.make_async_copy(ids,ids_all.at[p.h],isd.at[0]); l2.start()
    time_all[p.s]=time[...]
    for cp in first: cp.wait()
    D=time.shape[1]; K=wada.shape[0]; E=wada.shape[1]//8
    v=time_all[...].reshape(ns*8,D)
    low=(v/(1.0+jnp.exp(-v))).astype(bf)
    kk=D//(nd*ns)
    row=lax.broadcasted_iota(jnp.int32,(D,128),0); col=lax.broadcasted_iota(jnp.int32,(D,128),1)
    pickm=jnp.where((row==me*kk+col)&(col<kk),1.0,0.0).astype(bf)
    own=dot(low,pickm).astype(bf)
    act[...]=own
    for j in range(8):
        pj=dot(own[:,:K],wada[:,j*E:(j+1)*E])
        for s in range(ns):
            part[s,2*j:2*j+2,:]=pj[8*s:8*s+2,:]
    one=[remote(part.at[lax.rem(p.s+ds,ns)],r1.at[ds],e1s.at[ds],e1r.at[ds],(p.h,lax.rem(p.s+ds,ns))) for ds in range(1,ns)]
    order=[0]+near_first(p.Z)
    for a in g:
        for i,dz in enumerate(order):
            if dz: a.second(dz)
            if i: a.third(order[i-1])
        a.third(order[-1])
    tot=part[p.s]
    for ds in range(1,ns):
        one[ds-1].wait()
        tot=tot+r1[ds]
    r2[p.h]=tot
    two=[remote(r2.at[p.h],r2.at[p.h],e2s.at[dh],e2r.at[dh],(lax.rem(p.h+dh,nd),p.s)) for dh in range(1,nd)]
    for a in g:
        for dz in order: a.fourth(dz)
    for cp in two: cp.wait()
    tot=r2[0]
    for i in range(1,nd): tot=tot+r2[i]
    emb[...]=tot
    for a in g: a.finish()
    for cp in tail: cp.wait()
    l1.wait(); l2.wait()
    @pl.loop(0,nd)
    def _(dh):
        @pl.loop(0,ns)
        def _(ds):
            @pl.when(dh+ds>0)
            def _():
                pltpu.make_async_remote_copy(src_ref=bias,dst_ref=bias_all.at[me],send_sem=bs.at[dh,ds],recv_sem=br.at[dh,ds],device_id=(lax.rem(p.h+dh,nd),lax.rem(p.s+ds,ns)),device_id_type=pl.DeviceIdType.MESH).wait()

def entry(nd,ns,shards,bias,time,ids,wada):
    X,Y,Z=sizes(nd,ns)
    S=jax.ShapeDtypeStruct
    D=pltpu.SemaphoreType.DMA
    nw=len(shards); E=wada.shape[1]//8
    outs=[S((X,2,Z,Y)+a.shape,a.dtype) for a in shards]+[S((nd*ns,)+bias.shape,bias.dtype),S((nd,)+ids.shape,ids.dtype),S((16,E),f32),S((ns*8,128),bf)]
    scr=[pltpu.VMEM((ns,8,time.shape[1]),f32),pltpu.VMEM((ns,16,E),f32),pltpu.VMEM((ns,16,E),f32),pltpu.VMEM((nd,16,E),f32),
         D((nd,ns)),D((nd,ns)),D((nd,)),D((nd,)),D((ns,)),D((ns,)),D((ns,)),D((ns,)),D((nd,)),D((nd,))]
    for _ in shards: scr+=Gather.sems(nd,ns)
    return pl.pallas_call(functools.partial(entry_kernel,nd,ns,nw),out_shape=tuple(outs),
        in_specs=[ANY]*(nw+1)+[V,ANY,V],out_specs=tuple([ANY]*(nw+2)+[V,V]),scratch_shapes=scr,
        compiler_params=pltpu.CompilerParams(collective_id=0,has_side_effects=True,vmem_limit_bytes=40*2**20),name="entry")(*shards,bias,time,ids,wada)

class Scatter:
    @staticmethod
    def scratch(nd,ns,k,w,dt):
        X,Y,Z=sizes(nd,ns); M=pltpu.VMEM; D=pltpu.SemaphoreType.DMA
        h=w//2
        return [M((X,Z,Y,k,w),dt),M((X,Z,Y,k,w),dt),M((Y,X,Z,k,h),dt),M((X,Z,Y,k,h),dt),M((X,Z,k,h),dt),M((Y,Z,k,h),dt),M((Z,k,w),dt)]+\
            [D((X,)),D((X,)),D((X,)),D((Y,)),D((Y,)),D((X,)),D((X,)),D((X,)),D((X,)),D((Y,)),D((Y,)),D((Z,)),D((Z,))]
    count=20
    def __init__(self,p,src,col,w,scr):
        self.p,self.src,self.w=p,src,w
        self.cs=pl.ds(col,w); self.h=w//2
        self.own,self.cin,self.ya,self.xb,self.xa,self.yb,self.zr=scr[:7]
        self.ls,self.c1,self.c2,self.a1,self.a2,self.b1,self.b2,self.d1,self.d2,self.e1,self.e2,self.z1,self.z2=scr[7:]
        self.A=pl.ds(0,self.h); self.B=pl.ds(self.h,self.h); self.sent=[]
    def start(self):
        p=self.p
        self.l=[];self.cc=[]
        for x in range(p.X):
            self.cc.append(remote(self.src.at[x,1-p.c,:,:,:,self.cs],self.cin.at[x],self.c1.at[x],self.c2.at[x],p.at(c=1-p.c)))
            l=pltpu.make_async_copy(self.src.at[x,p.c,:,:,:,self.cs],self.own.at[x],self.ls.at[x]); l.start(); self.l.append(l)
        self.sent+=self.cc
    def add(self,i,x,cols):
        self.own[i+(slice(None),cols)]=(self.own[i+(slice(None),cols)].astype(f32)+x.astype(f32)).astype(self.own.dtype)
    def second(self):
        p=self.p
        for x in range(p.X):
            self.l[x].wait(); self.cc[x].wait_recv()
            @pl.loop(0,p.Z)
            def _(z):
                for y in range(p.Y):
                    self.add((x,z,y),self.cin[x,z,y],slice(None))
        self.a=[];self.b=[]
        for dy in near_first(p.Y):
            y=lax.rem(p.y+dy,p.Y)
            self.a.append((dy,remote(self.own.at[:,:,y,:,self.A],self.ya.at[dy],self.a1.at[dy],self.a2.at[dy],p.at(y=y))))
        for dx in near_first(p.X):
            x=lax.rem(p.x+dx,p.X)
            self.b.append((dx,remote(self.own.at[x,:,:,:,self.B],self.xb.at[dx],self.b1.at[dx],self.b2.at[dx],p.at(x=x))))
        self.sent+=[c for _,c in self.a+self.b]
    def third(self):
        p=self.p
        for dy,c in self.a:
            c.wait_recv()
            @pl.loop(0,p.Z)
            def _(z):
                for x in range(p.X): self.add((x,z,p.y),self.ya[dy,x,z],slice(0,self.h))
        for dx,c in self.b:
            c.wait_recv()
            @pl.loop(0,p.Z)
            def _(z):
                for y in range(p.Y): self.add((p.x,z,y),self.xb[dx,z,y],slice(self.h,self.w))
        self.a=[];self.b=[]
        for dx in near_first(p.X):
            x=lax.rem(p.x+dx,p.X)
            self.a.append((dx,remote(self.own.at[x,:,p.y,:,self.A],self.xa.at[dx],self.d1.at[dx],self.d2.at[dx],p.at(x=x))))
        for dy in near_first(p.Y):
            y=lax.rem(p.y+dy,p.Y)
            self.b.append((dy,remote(self.own.at[p.x,:,y,:,self.B],self.yb.at[dy],self.e1.at[dy],self.e2.at[dy],p.at(y=y))))
        self.sent+=[c for _,c in self.a+self.b]
    def fourth(self):
        p=self.p
        for dx,c in self.a:
            c.wait_recv()
            for z in range(p.Z): self.add((p.x,z,p.y),self.xa[dx,z],slice(0,self.h))
        for dy,c in self.b:
            c.wait_recv()
            for z in range(p.Z): self.add((p.x,z,p.y),self.yb[dy,z],slice(self.h,self.w))
        self.zc=[]
        for dz in near_first(p.Z):
            z=lax.rem(p.z+dz,p.Z)
            self.zc.append((dz,remote(self.own.at[p.x,z,p.y],self.zr.at[dz],self.z1.at[dz],self.z2.at[dz],p.at(z=z))))
        self.sent+=[c for _,c in self.zc]
    def last(self,out,cols):
        p=self.p
        t=self.own[p.x,p.z,p.y].astype(f32)
        for dz,c in self.zc:
            c.wait_recv()
            t=t+self.zr[dz].astype(f32)
        out[:,cols]=t
    def finish(self):
        for c in self.sent: c.wait_send()

def exit_kernel(nd,ns,plan,*refs):
    na=max(a for a,_,_ in plan)+1
    srcs=refs[:na]; ge,act,wada=refs[na:na+3]
    outs=refs[na+3:2*na+3]; gada,gbada,dact=refs[2*na+3:2*na+6]
    hsum,demb,dscr,hs,hr,qs,qr,ds_,dr=refs[2*na+6:2*na+15]
    sc=refs[2*na+15:]
    p=Place(nd,ns); me=p.h*ns+p.s
    greet_all(p)
    hsum[p.h]=ge[...]
    hc=[remote(hsum.at[p.h],hsum.at[p.h],hs.at[dh],hr.at[dh],(lax.rem(p.h+dh,nd),p.s)) for dh in range(1,nd)]
    it=[Scatter(p,srcs[a],c,w,sc[i*Scatter.count:(i+1)*Scatter.count]) for i,(a,c,w) in enumerate(plan)]
    for s in it: s.start()
    n=len(it); E=ge.shape[1]; K=wada.shape[0]; R=ns*16
    qc=[]
    for t in range(n+3):
        if t<n: it[t].second()
        if 0<=t-1<n: it[t-1].third()
        if 0<=t-2<n: it[t-2].fourth()
        if 0<=t-3<n: it[t-3].last(outs[plan[t-3][0]],slice(plan[t-3][1],plan[t-3][1]+plan[t-3][2]))
        if t==0:
            for c in hc: c.wait()
            tot=hsum[0]
            for i in range(1,nd): tot=tot+hsum[i]
            demb[p.s]=tot.astype(bf)
            qc=[remote(demb.at[p.s],demb.at[p.s],qs.at[d],qr.at[d],(p.h,lax.rem(p.s+d,ns))) for d in range(1,ns)]
        if t==1:
            for c in qc: c.wait()
            flat=demb[...].reshape(R,E)
            r0=lax.broadcasted_iota(jnp.int32,(R,ns*8),0); c0=lax.broadcasted_iota(jnp.int32,(R,ns*8),1)
            spread=dot(jnp.where((r0//16==c0//8)&(r0%2==c0%8),1.0,0.0).astype(bf),act[...])
            rr=lax.broadcasted_iota(jnp.int32,(R,128),0)%16//2
            rk=lax.broadcasted_iota(jnp.int32,(R,K),0)%16//2
            tot=jnp.zeros((R,K),f32)
            for j in range(8):
                m=jnp.where(rr==j,spread,0.0).astype(bf)
                gada[:,j*E:(j+1)*E]=dot(m,flat,TN)[:K,:]
                tot=jnp.where(rk==j,dot(flat,wada[:,j*E:(j+1)*E],NT),tot)
            r8=lax.broadcasted_iota(jnp.int32,(8,R),0); c8=lax.broadcasted_iota(jnp.int32,(8,R),1)
            gbada[...]=dot(jnp.where(c8%16//2==r8,1.0,0.0).astype(bf),flat)
            dscr[...]=jnp.concatenate([tot,jnp.zeros((R,128-K),f32)],1).reshape(ns,16,128)
            dact[me]=dscr[p.s]
            @pl.loop(0,nd)
            def _(dh):
                @pl.loop(0,ns)
                def _(d):
                    @pl.when(dh+d>0)
                    def _():
                        s=lax.rem(p.s+d,ns)
                        remote(dscr.at[s],dact.at[me],ds_.at[dh,d],dr.at[dh,d],(lax.rem(p.h+dh,nd),s))
    for s in it: s.finish()
    @pl.loop(0,nd)
    def _(dh):
        @pl.loop(0,ns)
        def _(d):
            @pl.when(dh+d>0)
            def _():
                s=lax.rem(p.s+d,ns)
                pltpu.make_async_remote_copy(src_ref=dscr.at[s],dst_ref=dact.at[me],send_sem=ds_.at[dh,d],recv_sem=dr.at[dh,d],device_id=(lax.rem(p.h+dh,nd),s),device_id_type=pl.DeviceIdType.MESH).wait()

def exit_(nd,ns,srcs,plan,ge,act,wada):
    S=jax.ShapeDtypeStruct; D=pltpu.SemaphoreType.DMA
    E=ge.shape[1]; K,E6=wada.shape
    outs=[S(a.shape[-2:],f32) for a in srcs]+[S((K,E6),f32),S((8,E),f32),S((nd*ns,16,128),f32)]
    scr=[pltpu.VMEM((nd,16,E),f32),pltpu.VMEM((ns,16,E),bf),pltpu.VMEM((ns,16,128),f32),D((nd,)),D((nd,)),D((ns,)),D((ns,)),D((nd,ns)),D((nd,ns))]
    for a,c,w in plan: scr+=Scatter.scratch(nd,ns,srcs[a].shape[-2],w,srcs[a].dtype)
    return pl.pallas_call(functools.partial(exit_kernel,nd,ns,tuple(plan)),out_shape=tuple(outs),
        in_specs=[ANY]*len(srcs)+[V]*3,out_specs=tuple([V]*len(outs)),scratch_shapes=scr,
        compiler_params=pltpu.CompilerParams(collective_id=1,has_side_effects=True,vmem_limit_bytes=60*2**20),name="exit")(*srcs,ge,act,wada)


def body(frames,time_embed,segment_ids,frame_mask,positions,w_ada,b_ada,w_qkv,b_qkv,w_out,b_out,w_up,b_up,w_down,b_down,cotangent):
    _,F,D=frames.shape
    nd=lax.axis_size("head"); ns=lax.axis_size("seq"); dev=lax.axis_index("head")*ns+lax.axis_index("seq")
    X,Y,Z=sizes(nd,ns); N=nd*ns
    W=D//nd
    E=b_ada.shape[0]; E6=w_ada.shape[1]; K=w_ada.shape[0]; H=w_up.shape[1]; nt=H//D
    x=frames[0]; cot=cotangent[0]
    def reorder(w): return w.reshape(-1,3,nd,W).transpose(0,2,1,3).reshape(-1,3*D)
    def restore(w): return w.reshape(-1,nd,3,W).transpose(0,2,1,3).reshape(-1,3*D)
    def hide(w): return w.reshape(-1,N,nt,K).transpose(0,2,1,3).reshape(-1,H)
    def unhide(w): return w.reshape(-1,nt,N,K).transpose(0,2,1,3).reshape(-1,H)
    rest=jnp.concatenate([hide(w_up),w_down.reshape(nt,K,D).transpose(1,0,2).reshape(K,H),w_out],axis=1)
    bs=(b_qkv,b_out,b_up,b_down,b_ada); ends=[0]
    for b in bs: ends.append(ends[-1]+b.shape[0])
    wide=-(-ends[-1]//256)*256
    bias=jnp.zeros((16,wide),bf).at[0,:ends[-1]].set(jnp.concatenate(bs))
    time8=jnp.zeros((8,D),f32).at[:2].set(time_embed[0].astype(f32))
    ids=jnp.zeros((8,F),jnp.int32).at[0].set(segment_ids[0]).at[1].set(frame_mask[0])
    wq,bias_all,ids_all,emb,act=entry(nd,ns,[reorder(w_qkv)],bias,time8,ids,w_ada)
    rest_all=lax.all_gather(rest,HS,axis=0,tiled=True)
    wq=wq.reshape(D,3*D)
    bias_all=bias_all[:,0,:].astype(f32)
    bq,bo,bu,bd,ba=[bias_all[:,ends[i]:ends[i+1]].reshape(1,-1) for i in range(5)]
    bq=reorder(bq); bu=hide(bu)
    emb=emb.reshape(8,2,-1).transpose(1,0,2).reshape(2,E6)+ba
    seg_row=ids_all[:,0,:].reshape(-1); msk_row=ids_all[:,1,:].reshape(-1)
    column=lax.iota(jnp.int32,128)
    pair=(column%HD//2).astype(f32)
    angles=positions[0].astype(f32)[:,None]*(10000.0**(-(2.0*pair)/HD))
    cos=jnp.cos(angles); sin=jnp.where(column%2==0,-jnp.sin(angles),jnp.sin(angles))
    segc=segment_ids[0][:,None]; mskc=frame_mask[0].astype(f32)[:,None]
    normed,packed=qkv_proj(x,segc,emb,wq,bq,cos,sin,nd)
    qkv=lax.all_to_all(packed,"head",split_axis=0,concat_axis=0,tiled=True).reshape(nd*F,3*W)
    T=256
    qlo,qhi,klo,khi=tables(seg_row,msk_row,T)
    aq,ak=aux(seg_row,msk_row)
    o,lse=attn_fwd(qkv,qlo,qhi,aq,ak,T)
    def back(a):
        return lax.all_to_all(a.reshape(nd,F,-1),"head",split_axis=0,concat_axis=0,tiled=True)
    att=back(o).transpose(1,0,2).reshape(F,D)
    out,dmid,datt,grest,gb,ge=mid(x,att,cot,segc,mskc,emb,rest_all,bo,bu,bd)
    do=lax.all_to_all(datt.reshape(F,nd,W).transpose(1,0,2),"head",split_axis=0,concat_axis=0,tiled=True).reshape(nd*F,W)
    dqkv=attn_bwd(qkv,o,do,lse,klo,khi,aq,ak,T)
    gx,gqkv,gbq,ge1=tail(x,normed,dmid,back(dqkv),segc,emb,wq,cos,sin)
    shape=(X,2,Z,Y,K)
    gbias=jnp.concatenate([restore(gbq[0:1]).reshape(N,-1),gb[0,:D].reshape(N,-1),unhide(gb[1:2]).reshape(N,-1),gb[2,:D].reshape(N,-1)],axis=1)
    wide=-(-ends[4]//256)*256
    gbias=jnp.zeros((N,8,wide),f32).at[:,0,:ends[4]].set(gbias).reshape(X,2,Z,Y,8,wide)
    ge=jnp.concatenate([ge1[:2],ge[:2]],axis=1).reshape(2,8,-1).transpose(1,0,2).reshape(16,-1)
    plan=[(0,j*D,D) for j in range(2*nt+1)]+[(2,0,wide)]+[(1,j*D,D) for j in range(3)]
    grest,gqkv,gbias,gada,gbada,dact=exit_(nd,ns,[grest.reshape(shape+(2*H+D,)),gqkv.reshape(shape+(3*D,)),gbias],plan,ge,act,w_ada)
    dact=dact[:,:,:K].reshape(N,8,2,K).sum(1).transpose(1,0,2).reshape(2,D)
    _,pull=jax.vjp(jax.nn.silu,time_embed[0].astype(f32))
    gtime=pull(dact)[0][None]
    gbada=lax.dynamic_slice_in_dim(gbada.reshape(-1),dev*E,E,0)
    gbs=[gbias[0,ends[i]:ends[i+1]] for i in range(4)]
    gdown=grest[:,H:2*H].reshape(K,nt,D).transpose(1,0,2).reshape(nt*K,D)
    return (out[None],gx[None],gtime,gada,gbada,restore(gqkv),gbs[0],grest[:,2*H:],gbs[1],unhide(grest[:,:H]),gbs[2],gdown,gbs[3])


def solution(mesh):
    row=P("seq","head",None); ids=P("seq","head"); mat=P(HS,None); vec=P(HS); tim=P("seq",None,None)
    in_specs=(row,tim,ids,ids,ids)+(mat,vec)*5+(row,)
    out_specs=(row,row,tim)+(mat,vec)*5
    return jax.shard_map(body,mesh=mesh,in_specs=in_specs,out_specs=out_specs,check_vma=False)
```

```python
import functools
import math

import jax
import jax.numpy as jnp
from jax import lax
from jax.experimental import pallas as pl
from jax.experimental.pallas import tpu as pltpu
from jax.sharding import PartitionSpec as P

bf = jnp.bfloat16
f32 = jnp.float32
HS = ("head", "seq")
ANY = pl.BlockSpec(memory_space=pl.ANY)
V = pl.BlockSpec(memory_space=pltpu.VMEM)
NN = (((1,), (0,)), ((), ()))
NT = (((1,), (1,)), ((), ()))
TN = (((0,), (0,)), ((), ()))


def dot(a, b, dims=NN):
    return lax.dot_general(a, b, dims, preferred_element_type=f32)


HD=64
LOG2E=math.log2(math.e)
NEG=-1e30

def fwd_kernel(lo_ref,hi_ref,qkv_ref,auxq_ref,auxk_ref,o_ref,lse_ref,k2,vx,q2,s_scr,m_scr,acc,*,T,nh):
    qt=pl.program_id(0)
    W=nh*HD
    L=qkv_ref.shape[0]
    nk=L//T
    lane=lax.broadcasted_iota(jnp.int32,(T,128),1)
    @pl.when(qt==0)
    def _():
        @pl.loop(0,nk)
        def _(t):
            r=pl.ds(pl.multiple_of(t*T,T),T)
            for h in range(nh):
                k=qkv_ref[r,W+h*HD:W+(h+1)*HD]
                k2[h,t]=jnp.concatenate([k,k],axis=1)
                v=qkv_ref[r,2*W+h*HD:2*W+(h+1)*HD]
                one=jnp.where(lax.broadcasted_iota(jnp.int32,(T,HD),1)==0,1.0,0.0).astype(bf)
                vx[h,t]=jnp.concatenate([v,one],axis=1)
    lo=lo_ref[qt]; hi=hi_ref[qt]
    r=pl.ds(pl.multiple_of(qt*T,T),T)
    for h in range(nh):
        q=qkv_ref[r,h*HD:(h+1)*HD].astype(f32)*(HD**-0.5*LOG2E)
        qh=q.astype(bf)
        ql=(q-qh.astype(f32)).astype(bf)
        q2[h]=jnp.concatenate([qh,ql],axis=1)
    auxq=auxq_ref[r,:]
    eye=lax.broadcasted_iota(jnp.int32,(T,T),0)==lax.broadcasted_iota(jnp.int32,(T,T),1)
    def mx(s):
        m=s[:,:128]
        for j in range(1,T//128): m=jnp.maximum(m,s[:,j*128:(j+1)*128])
        return m
    ak=auxk_ref[r,:]
    for h in range(nh):
        raw=dot(q2[h],k2[h,qt],NT)
        s=dot(jnp.concatenate([q2[h],auxq],axis=1),jnp.concatenate([k2[h,qt],ak],axis=1),NT)
        s=jnp.where(eye,raw,s)
        s_scr[h,qt]=s
        m_scr[h]=mx(s)
    @pl.loop(lo,hi-1)
    def _(t):
        kt=jnp.where(t>=qt,t+1,t)
        ak=auxk_ref[pl.ds(pl.multiple_of(kt*T,T),T),:]
        for h in range(nh):
            s=dot(jnp.concatenate([q2[h],auxq],axis=1),jnp.concatenate([k2[h,kt],ak],axis=1),NT)
            s_scr[h,kt]=s
            m_scr[h]=jnp.maximum(m_scr[h],mx(s))
    for h in range(nh):
        m_scr[h]=jnp.broadcast_to(jnp.max(m_scr[h],axis=1,keepdims=True),(T,128))
        acc[h]=jnp.zeros((T,128),f32)
    @pl.loop(lo,hi)
    def _(kt):
        for h in range(nh):
            s=s_scr[h,kt]; m=m_scr[h]
            p=jnp.exp2(s-jnp.concatenate([m]*(T//128),axis=1)).astype(bf)
            acc[h]+=dot(p,vx[h,kt])
    lse=jnp.zeros((T,128),f32)
    for h in range(nh):
        a=acc[h]
        l=a[:,HD:HD+1]
        o_ref[:,h*HD:(h+1)*HD]=(a[:,:HD]/l).astype(bf)
        lse=jnp.where(lane==h,m_scr[h]+jnp.log2(l),lse)
    lse_ref[...]=lse

def attn_fwd(qkv,lo,hi,auxq,auxk,T):
    L,W3=qkv.shape; W=W3//3; nh=W//HD; nk=L//T
    return pl.pallas_call(
        functools.partial(fwd_kernel,T=T,nh=nh),
        out_shape=(jax.ShapeDtypeStruct((L,W),bf),jax.ShapeDtypeStruct((L,128),f32)),
        grid_spec=pltpu.PrefetchScalarGridSpec(num_scalar_prefetch=2,grid=(nk,),
            in_specs=[pl.BlockSpec((L,W3),lambda i,*_:(0,0)),pl.BlockSpec((L,128),lambda i,*_:(0,0)),pl.BlockSpec((L,128),lambda i,*_:(0,0))],
            out_specs=[pl.BlockSpec((T,W),lambda i,*_:(i,0)),pl.BlockSpec((T,128),lambda i,*_:(i,0))],
            scratch_shapes=[pltpu.VMEM((nh,nk,T,128),bf),pltpu.VMEM((nh,nk,T,128),bf),pltpu.VMEM((nh,T,128),bf),
                pltpu.VMEM((nh,nk,T,T),f32),pltpu.VMEM((nh,T,128),f32),pltpu.VMEM((nh,T,128),f32)]),
        compiler_params=pltpu.CompilerParams(vmem_limit_bytes=60*2**20),
        name="attn_fwd",
    )(lo,hi,qkv,auxq,auxk)

def bwd_kernel(lo_ref,hi_ref,qkv_ref,o_ref,do_ref,lse_ref,auxq_ref,auxk_ref,dqkv_ref,q2,qa,k2,dox,vx,kT,dqT,dk,dv,*,T,nh):
    kt=pl.program_id(0)
    W=nh*HD
    L=qkv_ref.shape[0]
    nk=L//T
    lane=lax.broadcasted_iota(jnp.int32,(T,128),1)
    lane64=lax.broadcasted_iota(jnp.int32,(T,HD),1)
    @pl.when(kt==0)
    def _():
        dqT[...]=jnp.zeros_like(dqT)
        @pl.loop(0,nk)
        def _(t):
            r=pl.ds(pl.multiple_of(t*T,T),T)
            lse=lse_ref[r,:]
            aq=auxq_ref[r,:].astype(f32)
            kT[t]=qkv_ref[r,W:2*W].T
            for h in range(nh):
                q=qkv_ref[r,h*HD:(h+1)*HD].astype(f32)*(HD**-0.5*LOG2E)
                qh=q.astype(bf)
                ql=(q-qh.astype(f32)).astype(bf)
                q2[h,t]=jnp.concatenate([qh,ql],axis=1)
                k=qkv_ref[r,W+h*HD:W+(h+1)*HD]
                k2[h,t]=jnp.concatenate([k,k],axis=1)
                v=qkv_ref[r,2*W+h*HD:2*W+(h+1)*HD]
                vx[h,t]=jnp.concatenate([v,jnp.where(lane64<2,1.0,0.0).astype(bf)],axis=1)
                nl=-lse[:,h:h+1]
                l1=nl.astype(bf).astype(f32); l2=(nl-l1).astype(bf).astype(f32); l3=nl-l1-l2
                qa[h,t]=jnp.where(lane==0,l1,jnp.where(lane==1,l2,jnp.where(lane==2,l3,aq))).astype(bf)
                do=do_ref[r,h*HD:(h+1)*HD]
                nd=-jnp.sum(do.astype(f32)*o_ref[r,h*HD:(h+1)*HD].astype(f32),axis=1,keepdims=True)
                d1=nd.astype(bf).astype(f32); d2=nd-d1
                dox[h,t]=jnp.concatenate([do,jnp.where(lane64==0,d1,jnp.where(lane64==1,d2,0.0)).astype(bf)],axis=1)
    r=pl.ds(pl.multiple_of(kt*T,T),T)
    ak=auxk_ref[r,:]
    lo=lo_ref[kt]; hi=hi_ref[kt]
    def tile(qt,diag):
        rq=pl.ds(pl.multiple_of(qt*T,T),T)
        for h in range(nh):
            kx=jnp.concatenate([k2[h,kt],ak],axis=1)
            s=dot(kx,jnp.concatenate([q2[h,qt],qa[h,qt]],axis=1),NT)
            if diag:
                eye=lax.broadcasted_iota(jnp.int32,(T,T),0)==lax.broadcasted_iota(jnp.int32,(T,T),1)
                qr=jnp.where(lane<3,qa[h,qt].astype(f32),0.0).astype(bf)
                raw=dot(kx,jnp.concatenate([q2[h,qt],qr],axis=1),NT)
                s=jnp.where(eye,raw,s)
            p=jnp.exp2(s)
            dp=dot(vx[h,kt],dox[h,qt],NT)
            ds=(p*dp).astype(bf)
            pb=p.astype(bf)
            g=h//2
            rv=dot(pb,do_ref[rq,g*128:(g+1)*128])
            rk=dot(ds,qkv_ref[rq,g*128:(g+1)*128])
            dv[h]+=rv
            dk[h]+=rk
            dqT[qt,h*HD:(h+1)*HD,:]+=dot(kT[kt,h*HD:(h+1)*HD,:],ds)
    dk[...]=jnp.zeros_like(dk); dv[...]=jnp.zeros_like(dv)
    tile(kt,True)
    @pl.loop(lo,hi-1)
    def _(t):
        tile(jnp.where(t>=kt,t+1,t),False)
    for g in range(nh//2):
        dqkv_ref[r,W+g*128:W+(g+1)*128]=(jnp.where(lane<HD,dk[2*g],dk[2*g+1])*HD**-0.5).astype(bf)
        dqkv_ref[r,2*W+g*128:2*W+(g+1)*128]=jnp.where(lane<HD,dv[2*g],dv[2*g+1]).astype(bf)
    @pl.when(kt==nk-1)
    def _():
        @pl.loop(0,nk)
        def _(t):
            dqkv_ref[pl.ds(pl.multiple_of(t*T,T),T),0:W]=(dqT[t].T*HD**-0.5).astype(bf)

def attn_bwd(qkv,o,do,lse,lo,hi,auxq,auxk,T):
    L,W3=qkv.shape; W=W3//3; nh=W//HD; nk=L//T
    full=lambda w: pl.BlockSpec((L,w),lambda i,*_:(0,0))
    return pl.pallas_call(
        functools.partial(bwd_kernel,T=T,nh=nh),
        out_shape=jax.ShapeDtypeStruct((L,W3),bf),
        grid_spec=pltpu.PrefetchScalarGridSpec(num_scalar_prefetch=2,grid=(nk,),
            in_specs=[full(W3),full(W),full(W),full(128),full(128),full(128)],
            out_specs=full(W3),
            scratch_shapes=[pltpu.VMEM((nh,nk,T,128),bf)]*5+[pltpu.VMEM((nk,W,T),bf),pltpu.VMEM((nk,W,T),f32),
                pltpu.VMEM((nh,T,128),f32),pltpu.VMEM((nh,T,128),f32)]),
        compiler_params=pltpu.CompilerParams(vmem_limit_bytes=60*2**20),
        name="attn_bwd",
    )(lo,hi,qkv,o,do,lse,auxq,auxk)

def tables(seg,mask,T):
    L=seg.shape[0]; nk=L//T
    s=seg.reshape(nk,T); m=mask.reshape(nk,T)
    has=jnp.stack([jnp.any(s==c,axis=1) for c in (0,1)],1)
    real=jnp.stack([jnp.any((s==c)&(m==1),axis=1) for c in (0,1)],1)
    use=jnp.any(has[:,None,:]&real[None,:,:],axis=2)|jnp.eye(nk,dtype=bool)
    idx=jnp.arange(nk,dtype=jnp.int32)
    qlo=jnp.min(jnp.where(use,idx[None,:],nk),axis=1); qhi=jnp.max(jnp.where(use,idx[None,:],-1),axis=1)+1
    klo=jnp.min(jnp.where(use,idx[:,None],nk),axis=0); khi=jnp.max(jnp.where(use,idx[:,None],-1),axis=0)+1
    return [a.astype(jnp.int32) for a in (qlo,qhi,klo,khi)]
def aux(seg,mask):
    L=seg.shape[0]
    lane=lax.broadcasted_iota(jnp.int32,(L,128),1)
    sg=seg[:,None]; pad=(mask==0)[:,None]
    aq=jnp.where(lane==3,jnp.where(sg!=0,NEG,0.),jnp.where(lane==4,jnp.where(sg!=1,NEG,0.),jnp.where(lane==5,NEG,0.))).astype(bf)
    ak=jnp.where(lane<3,1.,jnp.where(lane==3,(sg==0).astype(f32),jnp.where(lane==4,(sg==1).astype(f32),jnp.where(lane==5,pad.astype(f32),0.)))).astype(bf)
    return aq,ak

EPS=1e-6

def moments(x):
    c=jnp.mean(x,-1,keepdims=True)
    xc=x-c
    rs=lax.rsqrt(jnp.mean(xc*xc,-1,keepdims=True)+EPS)
    return xc*rs, rs
def pick(seg,emb,i,D):
    return jnp.where(seg==0,emb[0:1,i*D:(i+1)*D],emb[1:2,i*D:(i+1)*D])
def sums(x,seg):
    a=jnp.sum(jnp.where(seg==0,x,0.0),0,keepdims=True); b=jnp.sum(jnp.where(seg==1,x,0.0),0,keepdims=True)
    return a,b
def partner(v):
    w=v.shape[1]
    lane=lax.broadcasted_iota(jnp.int32,v.shape,1)
    return jnp.where(lane%2==0,pltpu.roll(v,w-1,1),pltpu.roll(v,1,1))
def gelu_both(v):
    c=math.sqrt(2/math.pi)
    v2=v*v
    t=jnp.tanh(c*v*(1.0+0.044715*v2))
    h=0.5*(1.0+t)
    return v*h, h+0.5*v*(1.0-t*t)*(c*(1.0+3*0.044715*v2))

def qkv_kernel(x_ref,seg_ref,emb_ref,w_ref,b_ref,cos_ref,sin_ref,n_ref,p_ref,*,R,nd,W):
    F,D=x_ref.shape
    @pl.loop(0,F//R)
    def _(i):
        r=pl.ds(pl.multiple_of(i*R,R),R)
        seg=seg_ref[r,:]
        n,_=moments(x_ref[r,:].astype(f32))
        y=(n*(1.0+pick(seg,emb_ref,1,D))+pick(seg,emb_ref,0,D)).astype(bf)
        n_ref[r,:]=y
        cos=jnp.concatenate([cos_ref[r,:]]*(W//128),1); sin=jnp.concatenate([sin_ref[r,:]]*(W//128),1)
        for d in range(nd):
            for j in range(3):
                c=(d*3+j)*W
                v=dot(y,w_ref[:,c:c+W])+b_ref[0:1,c:c+W]
                if j<2: v=v*cos+partner(v)*sin
                p_ref[d,r,j*W:(j+1)*W]=v.astype(bf)

def qkv_proj(x,seg,emb,w,b,cos,sin,nd,R=128):
    F,D=x.shape; W=D//nd
    return pl.pallas_call(functools.partial(qkv_kernel,R=R,nd=nd,W=W),
        out_shape=(jax.ShapeDtypeStruct((F,D),bf),jax.ShapeDtypeStruct((nd,F,3*W),bf)),
        in_specs=[V]*7,out_specs=(V,V),
        compiler_params=pltpu.CompilerParams(vmem_limit_bytes=60*2**20),name="qkv_proj",
        cost_estimate=pl.CostEstimate(flops=2*F*D*3*D,bytes_accessed=14*2**20,transcendentals=0))(x,seg,emb,w,b,cos,sin)

def mid_kernel(x_ref,a_ref,c_ref,seg_ref,msk_ref,emb_ref,w_ref,bo_ref,bu_ref,bd_ref,
               out_ref,dm_ref,da_ref,gw_ref,gb_ref,ge_ref,
               wo_ref,wu_ref,wd_ref,n2s,acts,dhs,dfs,dps,dgelu,sem,*,R):
    F,D=x_ref.shape; H=bu_ref.shape[1]; CH=512
    loads=[pltpu.make_async_copy(w_ref.at[:,pl.ds(o,n)],r,sem.at[i]) for i,(o,n,r) in enumerate(((2*H,D,wo_ref),(0,H,wu_ref),(H,H,wd_ref)))]
    for l in loads: l.start()
    gb_ref[...]=jnp.zeros_like(gb_ref); ge_ref[...]=jnp.zeros_like(ge_ref)
    for l in loads: l.wait()
    def down(j):
        t,o=divmod(j*CH,D)
        return slice(o,o+CH),slice(t*D,(t+1)*D)
    @pl.loop(0,F//R)
    def _(i):
        r=pl.ds(pl.multiple_of(i*R,R),R)
        seg=seg_ref[r,:]; msk=msk_ref[r,:]
        def acc(k,x):
            a,b=sums(x,seg)
            ge_ref[0:1,k*D:(k+1)*D]+=a; ge_ref[1:2,k*D:(k+1)*D]+=b
        branch=(dot(a_ref[r,:],wo_ref[...])+bo_ref[0:1,:])*msk
        g1=pick(seg,emb_ref,2,D)
        middle=x_ref[r,:].astype(f32)+g1*branch
        n,rs=moments(middle)
        sc2=1.0+pick(seg,emb_ref,4,D)
        n2=(n*sc2+pick(seg,emb_ref,3,D)).astype(bf)
        n2s[r,:]=n2
        feed=jnp.broadcast_to(bd_ref[0:1,:],(R,D))
        for j in range(H//CH):
            c=slice(j*CH,(j+1)*CH)
            h=dot(n2,wu_ref[:,c])+bu_ref[0:1,c]
            a,g=gelu_both(h)
            a=a.astype(bf)
            acts[r,c]=a; dgelu[:,c]=g
            feed+=dot(a,wd_ref[down(j)])
        up=c_ref[r,:].astype(f32)
        g2=pick(seg,emb_ref,5,D)
        out_ref[r,:]=(middle+g2*feed).astype(bf)
        df=(up*g2).astype(bf)
        dfs[r,:]=df
        acc(3,up*feed)
        gb_ref[2:3,0:D]+=jnp.sum(df.astype(f32),0,keepdims=True)
        dn=jnp.zeros((R,D),f32)
        for j in range(H//CH):
            c=slice(j*CH,(j+1)*CH)
            dh=(dot(df,wd_ref[down(j)],NT)*dgelu[:,c]).astype(bf)
            dhs[r,c]=dh
            gb_ref[1:2,c]+=jnp.sum(dh.astype(f32),0,keepdims=True)
            dn+=dot(dh,wu_ref[:,c],NT)
        acc(1,dn); acc(2,dn*n)
        dn=dn*sc2
        dmid=up+(dn-jnp.mean(dn,-1,keepdims=True)-n*jnp.mean(dn*n,-1,keepdims=True))*rs
        dm_ref[r,:]=dmid
        acc(0,dmid*branch)
        dp=(dmid*g1*msk).astype(bf)
        dps[r,:]=dp
        gb_ref[0:1,0:D]+=jnp.sum(dp.astype(f32),0,keepdims=True)
        da_ref[r,:]=dot(dp,wo_ref[...],NT).astype(bf)
    @pl.loop(0,D//256)
    def _(i):
        c=pl.ds(pl.multiple_of(i*256,256),256)
        gw_ref[c,2*H:2*H+D]=dot(a_ref[:,c],dps[...],TN).astype(bf)
        gw_ref[c,0:H]=dot(n2s[:,c],dhs[...],TN).astype(bf)
        for t in range(H//D):
            e=pl.ds(pl.multiple_of(t*D+i*256,256),256)
            gw_ref[c,H+t*D:H+(t+1)*D]=dot(acts[:,e],dfs[...],TN).astype(bf)

def mid(x,a,c,seg,msk,emb,w,bo,bu,bd,R=128):
    F,D=x.shape; H=bu.shape[1]
    S=jax.ShapeDtypeStruct; M=pltpu.VMEM
    return pl.pallas_call(functools.partial(mid_kernel,R=R),
        out_shape=(S((F,D),bf),S((F,D),f32),S((F,D),bf),S((D,2*H+D),bf),S((8,H),f32),S((8,4*D),f32)),
        in_specs=[V]*6+[ANY]+[V]*3,out_specs=(V,)*6,
        scratch_shapes=[M((D,D),bf),M((D,H),bf),M((D,H),bf),M((F,D),bf),M((F,H),bf),M((F,H),bf),M((F,D),bf),M((F,D),bf),M((R,H),f32),pltpu.SemaphoreType.DMA((3,))],
        compiler_params=pltpu.CompilerParams(vmem_limit_bytes=62*2**20),name="mid",
        cost_estimate=pl.CostEstimate(flops=6*F*D*(D+2*H),bytes_accessed=30*2**20,transcendentals=F*H))(x,a,c,seg,msk,emb,w,bo,bu,bd)

def tail_kernel(x_ref,n1_ref,dm_ref,g_ref,seg_ref,emb_ref,w_ref,cos_ref,sin_ref,gf_ref,gw_ref,gb_ref,ge_ref,dps,*,R,nd,W):
    F,D=x_ref.shape
    gb_ref[...]=jnp.zeros_like(gb_ref); ge_ref[...]=jnp.zeros_like(ge_ref)
    @pl.loop(0,F//R)
    def _(i):
        r=pl.ds(pl.multiple_of(i*R,R),R)
        seg=seg_ref[r,:]
        cos=jnp.concatenate([cos_ref[r,:]]*(W//128),1); sin=jnp.concatenate([sin_ref[r,:]]*(W//128),1)
        dn=jnp.zeros((R,D),f32)
        for d in range(nd):
            for j in range(3):
                c=(d*3+j)*W
                v=g_ref[d,r,j*W:(j+1)*W]
                if j<2:
                    v=v.astype(f32)
                    v=(v*cos-partner(v)*sin).astype(bf)
                dps[r,c:c+W]=v
                gb_ref[0:1,c:c+W]+=jnp.sum(v.astype(f32),0,keepdims=True)
        for j in range(3*D//512):
            dn+=dot(dps[r,j*512:(j+1)*512],w_ref[:,j*512:(j+1)*512],NT)
        n,rs=moments(x_ref[r,:].astype(f32))
        for k,x in ((0,dn),(1,dn*n)):
            a,b=sums(x,seg)
            ge_ref[0:1,k*D:(k+1)*D]+=a; ge_ref[1:2,k*D:(k+1)*D]+=b
        dn=dn*(1.0+pick(seg,emb_ref,1,D))
        gf_ref[r,:]=dm_ref[r,:]+(dn-jnp.mean(dn,-1,keepdims=True)-n*jnp.mean(dn*n,-1,keepdims=True))*rs
    @pl.loop(0,D//256)
    def _(i):
        c=pl.ds(pl.multiple_of(i*256,256),256)
        for j in range(3):
            gw_ref[c,j*D:(j+1)*D]=dot(n1_ref[:,c],dps[:,j*D:(j+1)*D],TN).astype(bf)

def tail(x,n1,dm,g,seg,emb,w,cos,sin,R=128):
    F,D=x.shape; nd=g.shape[0]; W=D//nd
    S=jax.ShapeDtypeStruct
    return pl.pallas_call(functools.partial(tail_kernel,R=R,nd=nd,W=W),
        out_shape=(S((F,D),f32),S((D,3*D),bf),S((8,3*D),f32),S((8,2*D),f32)),
        in_specs=[V]*9,out_specs=(V,)*4,
        scratch_shapes=[pltpu.VMEM((F,3*D),bf)],
        compiler_params=pltpu.CompilerParams(vmem_limit_bytes=60*2**20),name="tail",
        cost_estimate=pl.CostEstimate(flops=4*F*D*3*D,bytes_accessed=20*2**20,transcendentals=0))(x,n1,dm,g,seg,emb,w,cos,sin)

def sizes(nd,ns):
    Y=2**((ns.bit_length()-1)//2)
    return nd//2,Y,ns//Y

class Place:
    def __init__(self,nd,ns):
        self.nd,self.ns=nd,ns
        self.X,self.Y,self.Z=sizes(nd,ns)
        self.h=lax.axis_index("head"); self.s=lax.axis_index("seq")
        self.x,self.c=self.h//2,self.h%2
        self.z,self.y=self.s//self.Y,self.s%self.Y
    def at(self,x=None,c=None,z=None,y=None):
        x=self.x if x is None else x; c=self.c if c is None else c
        z=self.z if z is None else z; y=self.y if y is None else y
        return (x*2+c,z*self.Y+y)

def near_first(n):
    out=[]
    for d in range(1,n//2+1):
        out.append(d)
        if n-d!=d: out.append(n-d)
    return out

def remote(src,dst,ss,rs,dev):
    cp=pltpu.make_async_remote_copy(src_ref=src,dst_ref=dst,send_sem=ss,recv_sem=rs,device_id=dev,device_id_type=pl.DeviceIdType.MESH)
    cp.start()
    return cp

def greet_all(p):
    b=pltpu.get_barrier_semaphore()
    @pl.loop(0,p.nd)
    def _(dh):
        @pl.loop(0,p.ns)
        def _(ds):
            @pl.when(dh+ds>0)
            def _():
                pl.semaphore_signal(b,inc=1,device_id=(lax.rem(p.h+dh,p.nd),lax.rem(p.s+ds,p.ns)),device_id_type=pl.DeviceIdType.MESH)
    pl.semaphore_wait(b,p.nd*p.ns-1)

class Gather:
    @staticmethod
    def sems(nd,ns):
        X,Y,Z=sizes(nd,ns)
        D=pltpu.SemaphoreType.DMA
        one=[D((Z,)),D((Z,X)),D((Z,Y)),D((Z,X,Y)),D((Z,X,Y)),D((Z,)),D((2,Z,X,Y))]
        return one+one+[D(())]
    def __init__(self,p,shard,out,sems):
        self.p,self.shard,self.out=p,shard,out
        self.ss,self.rs,self.ls=sems[:7],sems[7:14],sems[14]
        self.all=[]; self.half=shard.shape[-1]//2
        self.two={}; self.three={}
    def send(self,k,idx,src,dst,dev):
        cp=remote(src,dst,self.ss[k].at[idx],self.rs[k].at[idx],dev)
        self.all.append(cp); return cp
    def cols(self,part): return pl.ds(part*self.half,self.half)
    def loc(self,x,z,y,part=None):
        r=self.out.at[x,self.p.c,z,y]
        return r if part is None else r.at[:,self.cols(part)]
    def start(self):
        p=self.p
        self.zc={}
        for dz in near_first(p.Z):
            self.zc[dz]=self.send(0,(dz,),self.shard,self.loc(p.x,p.z,p.y),p.at(z=lax.rem(p.z+dz,p.Z)))
        self.local=pltpu.make_async_copy(self.shard,self.loc(p.x,p.z,p.y),self.ls)
        self.local.start()
        self.second(0)
    def second(self,dz):
        p=self.p; zz=lax.rem(p.z+p.Z-dz,p.Z)
        if dz: self.zc[dz].wait_recv()
        def src(part=None):
            if dz: return self.loc(p.x,zz,p.y,part)
            return self.shard if part is None else self.shard.at[:,self.cols(part)]
        for dx in near_first(p.X):
            self.two[0,dz,dx]=self.send(1,(dz,dx),src(0),self.loc(p.x,zz,p.y,0),p.at(x=lax.rem(p.x+dx,p.X)))
        for dy in near_first(p.Y):
            self.two[1,dz,dy]=self.send(2,(dz,dy),src(1),self.loc(p.x,zz,p.y,1),p.at(y=lax.rem(p.y+dy,p.Y)))
        self.send(5,(dz,),src(),self.loc(p.x,zz,p.y),p.at(c=1-p.c))
        for dy in near_first(p.Y):
            self.three[0,dz,0,dy]=self.send(3,(dz,0,dy),src(0),self.loc(p.x,zz,p.y,0),p.at(y=lax.rem(p.y+dy,p.Y)))
        for dx in near_first(p.X):
            self.three[1,dz,dx,0]=self.send(4,(dz,dx,0),src(1),self.loc(p.x,zz,p.y,1),p.at(x=lax.rem(p.x+dx,p.X)))
    def third(self,dz):
        p=self.p; zz=lax.rem(p.z+p.Z-dz,p.Z)
        for dx in near_first(p.X):
            self.two[0,dz,dx].wait_recv()
            l=self.loc(lax.rem(p.x+p.X-dx,p.X),zz,p.y,0)
            for dy in near_first(p.Y):
                self.three[0,dz,dx,dy]=self.send(3,(dz,dx,dy),l,l,p.at(y=lax.rem(p.y+dy,p.Y)))
            self.send(6,(0,dz,dx,0),l,l,p.at(c=1-p.c))
        for dy in near_first(p.Y):
            self.two[1,dz,dy].wait_recv()
            l=self.loc(p.x,zz,lax.rem(p.y+p.Y-dy,p.Y),1)
            for dx in near_first(p.X):
                self.three[1,dz,dx,dy]=self.send(4,(dz,dx,dy),l,l,p.at(x=lax.rem(p.x+dx,p.X)))
            self.send(6,(1,dz,0,dy),l,l,p.at(c=1-p.c))
    def fourth(self,dz):
        p=self.p; zz=lax.rem(p.z+p.Z-dz,p.Z)
        for part in (0,1):
            for dx in range(p.X):
                for dy in range(p.Y):
                    if (part,dz,dx,dy) not in self.three: continue
                    self.three[part,dz,dx,dy].wait_recv()
                    l=self.loc(lax.rem(p.x+p.X-dx,p.X),zz,lax.rem(p.y+p.Y-dy,p.Y),part)
                    self.send(6,(part,dz,dx,dy),l,l,p.at(c=1-p.c))
    def finish(self):
        waited=set()
        for cp in self.zc.values(): waited.add(id(cp))
        for d in (self.two,self.three):
            for cp in d.values(): waited.add(id(cp))
        for cp in self.all:
            if id(cp) not in waited: cp.wait_recv()
            cp.wait_send()
        self.local.wait()

def entry_kernel(nd,ns,nw,*refs):
    shards=refs[:nw]; bias,time,ids,wada=refs[nw:nw+4]
    outs=refs[nw+4:2*nw+4]; bias_all,ids_all,emb,act=refs[2*nw+4:2*nw+8]
    time_all,part,r1,r2,bs,br,isd,ir,ts,tr,e1s,e1r,e2s,e2r=refs[2*nw+8:2*nw+22]
    gs=refs[2*nw+22:]
    p=Place(nd,ns); n=len(Gather.sems(nd,ns))
    greet_all(p)
    tail=[]
    first=[]
    for ds in range(1,ns):
        first.append(remote(time,time_all.at[p.s],ts.at[ds],tr.at[ds],(p.h,lax.rem(p.s+ds,ns))))
    g=[Gather(p,shards[i],outs[i],gs[i*n:(i+1)*n]) for i in range(nw)]
    for a in g: a.start()
    me=p.h*ns+p.s
    for dh in range(1,nd):
        tail.append(remote(ids,ids_all.at[p.h],isd.at[dh],ir.at[dh],(lax.rem(p.h+dh,nd),p.s)))
    @pl.loop(0,nd)
    def _(dh):
        @pl.loop(0,ns)
        def _(ds):
            @pl.when(dh+ds>0)
            def _():
                remote(bias,bias_all.at[me],bs.at[dh,ds],br.at[dh,ds],(lax.rem(p.h+dh,nd),lax.rem(p.s+ds,ns)))
    l1=pltpu.make_async_copy(bias,bias_all.at[me],bs.at[0,0]); l1.start()
    l2=pltpu.make_async_copy(ids,ids_all.at[p.h],isd.at[0]); l2.start()
    time_all[p.s]=time[...]
    for cp in first: cp.wait()
    D=time.shape[1]; K=wada.shape[0]; E=wada.shape[1]//8
    v=time_all[...].reshape(ns*8,D)
    low=(v/(1.0+jnp.exp(-v))).astype(bf)
    kk=D//(nd*ns)
    row=lax.broadcasted_iota(jnp.int32,(D,128),0); col=lax.broadcasted_iota(jnp.int32,(D,128),1)
    pickm=jnp.where((row==me*kk+col)&(col<kk),1.0,0.0).astype(bf)
    own=dot(low,pickm).astype(bf)
    act[...]=own
    for j in range(8):
        pj=dot(own[:,:K],wada[:,j*E:(j+1)*E])
        for s in range(ns):
            part[s,2*j:2*j+2,:]=pj[8*s:8*s+2,:]
    one=[remote(part.at[lax.rem(p.s+ds,ns)],r1.at[ds],e1s.at[ds],e1r.at[ds],(p.h,lax.rem(p.s+ds,ns))) for ds in range(1,ns)]
    order=[0]+near_first(p.Z)
    for a in g:
        for i,dz in enumerate(order):
            if dz: a.second(dz)
            if i: a.third(order[i-1])
        a.third(order[-1])
    tot=part[p.s]
    for ds in range(1,ns):
        one[ds-1].wait()
        tot=tot+r1[ds]
    r2[p.h]=tot
    two=[remote(r2.at[p.h],r2.at[p.h],e2s.at[dh],e2r.at[dh],(lax.rem(p.h+dh,nd),p.s)) for dh in range(1,nd)]
    for a in g:
        for dz in order: a.fourth(dz)
    for cp in two: cp.wait()
    tot=r2[0]
    for i in range(1,nd): tot=tot+r2[i]
    emb[...]=tot
    for a in g: a.finish()
    for cp in tail: cp.wait()
    l1.wait(); l2.wait()
    @pl.loop(0,nd)
    def _(dh):
        @pl.loop(0,ns)
        def _(ds):
            @pl.when(dh+ds>0)
            def _():
                pltpu.make_async_remote_copy(src_ref=bias,dst_ref=bias_all.at[me],send_sem=bs.at[dh,ds],recv_sem=br.at[dh,ds],device_id=(lax.rem(p.h+dh,nd),lax.rem(p.s+ds,ns)),device_id_type=pl.DeviceIdType.MESH).wait()

def entry(nd,ns,shards,bias,time,ids,wada):
    X,Y,Z=sizes(nd,ns)
    S=jax.ShapeDtypeStruct
    D=pltpu.SemaphoreType.DMA
    nw=len(shards); E=wada.shape[1]//8
    outs=[S((X,2,Z,Y)+a.shape,a.dtype) for a in shards]+[S((nd*ns,)+bias.shape,bias.dtype),S((nd,)+ids.shape,ids.dtype),S((16,E),f32),S((ns*8,128),bf)]
    scr=[pltpu.VMEM((ns,8,time.shape[1]),f32),pltpu.VMEM((ns,16,E),f32),pltpu.VMEM((ns,16,E),f32),pltpu.VMEM((nd,16,E),f32),
         D((nd,ns)),D((nd,ns)),D((nd,)),D((nd,)),D((ns,)),D((ns,)),D((ns,)),D((ns,)),D((nd,)),D((nd,))]
    for _ in shards: scr+=Gather.sems(nd,ns)
    return pl.pallas_call(functools.partial(entry_kernel,nd,ns,nw),out_shape=tuple(outs),
        in_specs=[ANY]*(nw+1)+[V,ANY,V],out_specs=tuple([ANY]*(nw+2)+[V,V]),scratch_shapes=scr,
        compiler_params=pltpu.CompilerParams(collective_id=0,has_side_effects=True,vmem_limit_bytes=40*2**20),name="entry")(*shards,bias,time,ids,wada)

class Reduce:
    def __init__(self,p,parts,scr,own=None,src=None,col=0):
        self.p,self.parts,self.src=p,parts,src
        it=iter(scr)
        self.own=own if own is not None else next(it)
        self.c=p.c if own is not None else 0
        self.w=self.own.shape[-1]; self.cs=pl.ds(col,self.w)
        self.cin=next(it); self.c1,self.c2,self.ls=next(it),next(it),next(it)
        self.bufs=[[(next(it),next(it),next(it)) for _ in o] for _,_,o in parts]
        self.sent=[]; self.stage=0
    @staticmethod
    def scratch(nd,ns,k,w,dt,parts,own):
        X,Y,Z=sizes(nd,ns); M=pltpu.VMEM; D=pltpu.SemaphoreType.DMA; n={"x":X,"y":Y,"z":Z}
        out=[] if own else [M((X,1,Z,Y,k,w),dt)]
        out+=[M((X,Z,Y,k,w),dt),D((X,)),D((X,)),D((X,))]
        for lo,hi,order in parts:
            for i,a in enumerate(order):
                left=tuple(n[b] for b in "xzy" if b in order[i+1:])
                out+=[M((max(n[a]-1,1),)+left+(k,hi-lo),dt),D((n[a],)),D((n[a],))]
        return out
    def start(self):
        p=self.p; self.l=[]; self.cc=[]
        for x in range(p.X):
            s=self.own.at[x,1-p.c] if self.src is None else self.src.at[x,1-p.c,:,:,:,self.cs]
            self.cc.append(remote(s,self.cin.at[x],self.c1.at[x],self.c2.at[x],p.at(c=1-p.c)))
            if self.src is not None:
                l=pltpu.make_async_copy(self.src.at[x,p.c,:,:,:,self.cs],self.own.at[x,0],self.ls.at[x]); l.start(); self.l.append(l)
        self.sent+=self.cc
    def place(self,order,i,v):
        p=self.p; mine={"x":p.x,"y":p.y,"z":p.z}
        ix={b:(mine[b] if b in order[:i] else v if b==order[i] else slice(None)) for b in "xyz"}
        return (ix["x"],self.c,ix["z"],ix["y"])
    def add(self,i,x,cols):
        i=i+(slice(None),slice(*cols))
        self.own[i]=(self.own[i].astype(f32)+x.astype(f32)).astype(self.own.dtype)
    def send(self,part,i):
        p=self.p; lo,hi,order=self.parts[part]; a=order[i]
        n={"x":p.X,"y":p.Y,"z":p.Z}[a]; me={"x":p.x,"y":p.y,"z":p.z}[a]
        buf,s1,s2=self.bufs[part][i]; out=[]
        for d in near_first(n):
            v=lax.rem(me+d,n)
            out.append((d,remote(self.own.at[self.place(order,i,v)+(slice(None),pl.ds(lo,hi-lo))],buf.at[d-1],s1.at[d],s2.at[d],p.at(**{a:v}))))
        self.sent+=[c for _,c in out]
        return out
    def step(self):
        p=self.p; st=self.stage; self.stage+=1
        if st==0:
            for x in range(p.X):
                if self.src is not None: self.l[x].wait()
                self.cc[x].wait_recv()
                @pl.loop(0,p.Z)
                def _(z):
                    for y in range(p.Y): self.add((x,self.c,z,y),self.cin[x,z,y],(0,self.w))
            self.go=[self.send(k,0) for k in range(len(self.parts))]
            return
        go=[]
        for k,(lo,hi,order) in enumerate(self.parts):
            buf=self.bufs[k][st-1][0]; left=[b for b in "xzy" if b in order[st:]]
            n={"x":p.X,"y":p.Y,"z":p.Z}; mine={"x":p.x,"y":p.y,"z":p.z}
            for d,c in self.go[k]:
                c.wait_recv()
                def one(at,d=d):
                    ix={**mine,**at}
                    self.add((ix["x"],self.c,ix["z"],ix["y"]),buf[(d-1,)+tuple(at[b] for b in left)],(lo,hi))
                if len(left)==2:
                    @pl.loop(0,n[left[0]])
                    def _(u):
                        for v in range(n[left[1]]): one({left[0]:u,left[1]:v})
                else:
                    @pl.loop(0,n[left[0]])
                    def _(u): one({left[0]:u})
            go.append(self.send(k,st))
        self.go=go
    def last(self,out,col=0):
        p=self.p
        for k,(lo,hi,order) in enumerate(self.parts):
            buf=self.bufs[k][2][0]
            t=self.own[p.x,self.c,p.z,p.y,:,lo:hi].astype(f32)
            for d,c in self.go[k]:
                c.wait_recv()
                t=t+buf[d-1].astype(f32)
            out[:,col+lo:col+hi]=t
    def finish(self):
        for c in self.sent: c.wait_send()

def everyone(p,f):
    @pl.loop(0,p.nd)
    def _(dh):
        @pl.loop(0,p.ns)
        def _(d):
            @pl.when(dh+d>0)
            def _(): f(dh,d,(lax.rem(p.h+dh,p.nd),lax.rem(p.s+d,p.ns)))

def make_remote(src,dst,ss,rs,dev):
    return pltpu.make_async_remote_copy(src_ref=src,dst_ref=dst,send_sem=ss,recv_sem=rs,device_id=dev,device_id_type=pl.DeviceIdType.MESH)

REST=(lambda w:((0,w,"yzx"),)); QKV=(lambda w:((0,w//2,"yxz"),(w//2,w,"xyz")))

def final_kernel(nd,ns,R,refs,scr):
    (g_ref,rest_ref,x_hbm,n1_hbm,dm_hbm,wq_hbm,cos_ref,sin_ref,seg_ref,emb_ref,gbm_ref,gem_ref,act,wada)=refs[:14]
    (gf_ref,rest_out,qkv_out,bias_all,gada,gbada,dact)=refs[14:]
    (g,x_ref,n1_ref,dm_ref,w_ref,dps,gw,gbv,gev,bsc,bout,hsum,demb,dscr)=scr[:14]
    (gs,gr,gl,ld,hs,hr,qs,qr,ds_,dr,bs,br)=scr[14:26]
    pools=scr[26:]
    p=Place(nd,ns); me=p.h*ns+p.s
    F,D=x_ref.shape; W=D//nd; E=D*6//8; K=wada.shape[0]; H=gbm_ref.shape[1]; NR=F//R
    nr=(2*H+D)//D
    greet_all(p)
    loads=[pltpu.make_async_copy(a,b,ld.at[i]) for i,(a,b) in enumerate(((x_hbm,x_ref),(wq_hbm,w_ref),(dm_hbm,dm_ref),(n1_hbm,n1_ref)))]
    sends=[]; own=[]
    for i in range(NR):
        r=pl.ds(i*R,R)
        sends.append([remote(g_ref.at[lax.rem(p.h+d,nd),r],g.at[p.h,r],gs.at[i,d],gr.at[i,d],(lax.rem(p.h+d,nd),p.s)) for d in range(1,nd)])
        c=pltpu.make_async_copy(g_ref.at[p.h,r],g.at[p.h,r],gl.at[i]); c.start(); own.append(c)
    for l in loads: l.start()
    it=iter(pools)
    take=lambda n: [next(it) for _ in range(n)]
    rest=[]
    for j in range(nr):
        rest.append(Reduce(p,REST(D),take(len(Reduce.scratch(nd,ns,K,D,bf,REST(D),False))),src=rest_ref,col=j*D))
        rest[-1].start()
    qkv=[Reduce(p,QKV(D),take(len(Reduce.scratch(nd,ns,K,D,bf,QKV(D),True))),own=gw.at[j]) for j in range(3)]
    bias=Reduce(p,QKV(256),take(len(Reduce.scratch(nd,ns,8,256,f32,QKV(256),True))),own=bsc)
    gbv[...]=jnp.zeros_like(gbv); gev[...]=jnp.zeros_like(gev); bsc[...]=jnp.zeros_like(bsc)
    for a in rest: a.step()
    for l in loads: l.wait()
    def tile(i):
        for c in sends[i]: c.wait_recv()
        own[i].wait()
        r=slice(i*R,(i+1)*R)
        seg=seg_ref[r,:]
        cos=jnp.concatenate([cos_ref[r,:]]*(W//128),1); sin=jnp.concatenate([sin_ref[r,:]]*(W//128),1)
        dn=jnp.zeros((R,D),f32)
        for d in range(nd):
            for j in range(3):
                c=(d*3+j)*W
                v=g[d,r,j*W:(j+1)*W]
                if j<2:
                    v=v.astype(f32)
                    v=(v*cos-partner(v)*sin).astype(bf)
                dps[r,c:c+W]=v
                gbv[0:1,c:c+W]+=jnp.sum(v.astype(f32),0,keepdims=True)
        for j in range(3*D//512):
            dn+=dot(dps[r,j*512:(j+1)*512],w_ref[:,j*512:(j+1)*512],NT)
        n,rs=moments(x_ref[r,:].astype(f32))
        for k,x in ((0,dn),(1,dn*n)):
            a,b=sums(x,seg)
            gev[0:1,k*D:(k+1)*D]+=a; gev[1:2,k*D:(k+1)*D]+=b
        dn=dn*(1.0+pick(seg,emb_ref,1,D))
        gf_ref[r,:]=dm_ref[r,:]+(dn-jnp.mean(dn,-1,keepdims=True)-n*jnp.mean(dn*n,-1,keepdims=True))*rs
    def weight(j):
        B=D//nd
        for h in range(nd):
            v=dot(n1_ref[:,h*B:(h+1)*B],dps[:,j*D:(j+1)*D],TN).astype(bf)
            gw[j,h//2,h%2]=v.reshape(p.Z,p.Y,K,D)
        qkv[j].start()
    todo=[a.step for a in rest]+[a.step for a in rest]
    per=-(-len(todo)//NR)
    for i in range(NR):
        tile(i)
        if i<NR-1:
            for f in todo[i*per:(i+1)*per]: f()
    gev[0:2,2*D:]=gem_ref[0:2,:]
    for j in range(8):
        for t in range(2): hsum[p.h,2*j+t:2*j+t+1,:]=gev[t:t+1,j*E:(j+1)*E]
    hc=[remote(hsum.at[p.h],hsum.at[p.h],hs.at[d],hr.at[d],(lax.rem(p.h+d,nd),p.s)) for d in range(1,nd)]
    vec=jnp.concatenate([gbv[0:1,:],gbm_ref[0:1,0:D],gbm_ref[1:2,:],gbm_ref[2:3,0:D]],1)
    for q in range(vec.shape[1]//256):
        h,s=divmod(q,ns)
        bsc[h//2,h%2,s//p.Y,s%p.Y,0:1,:]=vec[:,q*256:(q+1)*256]
    bias.start()
    weight(0)
    weight(1)
    qkv[0].step(); bias.step()
    weight(2)
    qkv[1].step(); qkv[2].step()
    for f in todo[(NR-1)*per:]: f()
    bias.step()
    for c in hc: c.wait()
    tot=hsum[0]
    for i in range(1,nd): tot=tot+hsum[i]
    demb[p.s]=tot.astype(bf)
    qc=[remote(demb.at[p.s],demb.at[p.s],qs.at[d],qr.at[d],(p.h,lax.rem(p.s+d,ns))) for d in range(1,ns)]
    qkv[0].step(); bias.step()
    qkv[1].step()
    qkv[2].step()
    for j,a in enumerate(rest): a.last(rest_out,j*D)
    bias.last(bout)
    everyone(p,lambda dh,d,dev: remote(bout,bias_all.at[me],bs.at[dh,d],br.at[dh,d],dev))
    bias_all[me]=bout[...]
    for c in qc: c.wait()
    Q=ns*16
    flat=demb[...].reshape(Q,E)
    r0=lax.broadcasted_iota(jnp.int32,(Q,ns*8),0); c0=lax.broadcasted_iota(jnp.int32,(Q,ns*8),1)
    spread=dot(jnp.where((r0//16==c0//8)&(r0%2==c0%8),1.0,0.0).astype(bf),act[...])
    rr=lax.broadcasted_iota(jnp.int32,(Q,128),0)%16//2
    rk=lax.broadcasted_iota(jnp.int32,(Q,K),0)%16//2
    tot=jnp.zeros((Q,K),f32)
    for j in range(8):
        m=jnp.where(rr==j,spread,0.0).astype(bf)
        gada[:,j*E:(j+1)*E]=dot(m,flat,TN)[:K,:]
        tot=jnp.where(rk==j,dot(flat,wada[:,j*E:(j+1)*E],NT),tot)
    dscr[...]=jnp.concatenate([tot,jnp.zeros((Q,128-K),f32)],1).reshape(ns,16,128)
    dact[me]=dscr[p.s]
    everyone(p,lambda dh,d,dev: remote(dscr.at[dev[1]],dact.at[me],ds_.at[dh,d],dr.at[dh,d],dev))
    r8=lax.broadcasted_iota(jnp.int32,(8,Q),0); c8=lax.broadcasted_iota(jnp.int32,(8,Q),1)
    gbada[...]=dot(jnp.where(c8%16//2==r8,1.0,0.0).astype(bf),flat)
    for a in qkv: a.step()
    for j in range(3): qkv[j].last(qkv_out,j*D)
    for a in rest+qkv+[bias]: a.finish()
    for i in range(NR):
        for c in sends[i]: c.wait_send()
    everyone(p,lambda dh,d,dev: make_remote(bout,bias_all.at[me],bs.at[dh,d],br.at[dh,d],dev).wait())
    everyone(p,lambda dh,d,dev: make_remote(dscr.at[dev[1]],dact.at[me],ds_.at[dh,d],dr.at[dh,d],dev).wait())

def final(nd,ns,dqkv,rest,x,n1,dm,wq,cos,sin,seg,emb,gb,ge,act,wada,R=128):
    F,D=x.shape; K,E6=wada.shape; E=E6//8; H=gb.shape[1]; N=nd*ns; W=D//nd; NR=F//R
    X,Y,Z=sizes(nd,ns)
    S=jax.ShapeDtypeStruct; M=pltpu.VMEM; A=pltpu.SemaphoreType.DMA
    outs=[S((F,D),f32),S((K,2*H+D),f32),S((K,3*D),f32),S((N,8,256),f32),S((K,E6),f32),S((8,E),f32),S((N,16,128),f32)]
    scr=[M((nd,F,3*W),bf),M((F,D),bf),M((F,D),bf),M((F,D),f32),M((D,3*D),bf),M((F,3*D),bf),M((3,X,2,Z,Y,K,D),bf),M((8,3*D),f32),M((8,E6),f32),
         M((X,2,Z,Y,8,256),f32),M((8,256),f32),M((nd,16,E),f32),M((ns,16,E),bf),M((ns,16,128),f32),
         A((NR,nd)),A((NR,nd)),A((NR,)),A((4,)),A((nd,)),A((nd,)),A((ns,)),A((ns,)),A((nd,ns)),A((nd,ns)),A((nd,ns)),A((nd,ns))]
    for _ in range((2*H+D)//D): scr+=Reduce.scratch(nd,ns,K,D,bf,REST(D),False)
    for _ in range(3): scr+=Reduce.scratch(nd,ns,K,D,bf,QKV(D),True)
    scr+=Reduce.scratch(nd,ns,8,256,f32,QKV(256),True)
    def k(*refs): final_kernel(nd,ns,R,refs[:14+len(outs)],refs[14+len(outs):])
    return pl.pallas_call(k,out_shape=tuple(outs),in_specs=[ANY]*6+[V]*8,out_specs=(V,)*len(outs),scratch_shapes=scr,
        compiler_params=pltpu.CompilerParams(collective_id=1,has_side_effects=True,vmem_limit_bytes=63*2**20),name="final")(
        dqkv,rest,x,n1,dm,wq,cos,sin,seg,emb,gb,ge,act,wada)


def body(frames,time_embed,segment_ids,frame_mask,positions,w_ada,b_ada,w_qkv,b_qkv,w_out,b_out,w_up,b_up,w_down,b_down,cotangent):
    _,F,D=frames.shape
    nd=lax.axis_size("head"); ns=lax.axis_size("seq"); dev=lax.axis_index("head")*ns+lax.axis_index("seq")
    X,Y,Z=sizes(nd,ns); N=nd*ns
    W=D//nd
    E=b_ada.shape[0]; E6=w_ada.shape[1]; K=w_ada.shape[0]; H=w_up.shape[1]; nt=H//D
    x=frames[0]; cot=cotangent[0]
    def reorder(w): return w.reshape(-1,3,nd,W).transpose(0,2,1,3).reshape(-1,3*D)
    def restore(w): return w.reshape(-1,nd,3,W).transpose(0,2,1,3).reshape(-1,3*D)
    def hide(w): return w.reshape(-1,N,nt,K).transpose(0,2,1,3).reshape(-1,H)
    def unhide(w): return w.reshape(-1,nt,N,K).transpose(0,2,1,3).reshape(-1,H)
    rest=jnp.concatenate([hide(w_up),w_down.reshape(nt,K,D).transpose(1,0,2).reshape(K,H),w_out],axis=1)
    bs=(b_qkv,b_out,b_up,b_down,b_ada); ends=[0]
    for b in bs: ends.append(ends[-1]+b.shape[0])
    wide=-(-ends[-1]//256)*256
    bias=jnp.zeros((16,wide),bf).at[0,:ends[-1]].set(jnp.concatenate(bs))
    time8=jnp.zeros((8,D),f32).at[:2].set(time_embed[0].astype(f32))
    ids=jnp.zeros((8,F),jnp.int32).at[0].set(segment_ids[0]).at[1].set(frame_mask[0])
    wq,bias_all,ids_all,emb,act=entry(nd,ns,[reorder(w_qkv)],bias,time8,ids,w_ada)
    rest_all=lax.all_gather(rest,HS,axis=0,tiled=True)
    wq=wq.reshape(D,3*D)
    bias_all=bias_all[:,0,:].astype(f32)
    bq,bo,bu,bd,ba=[bias_all[:,ends[i]:ends[i+1]].reshape(1,-1) for i in range(5)]
    bq=reorder(bq); bu=hide(bu)
    emb=emb.reshape(8,2,-1).transpose(1,0,2).reshape(2,E6)+ba
    seg_row=ids_all[:,0,:].reshape(-1); msk_row=ids_all[:,1,:].reshape(-1)
    column=lax.iota(jnp.int32,128)
    pair=(column%HD//2).astype(f32)
    angles=positions[0].astype(f32)[:,None]*(10000.0**(-(2.0*pair)/HD))
    cos=jnp.cos(angles); sin=jnp.where(column%2==0,-jnp.sin(angles),jnp.sin(angles))
    segc=segment_ids[0][:,None]; mskc=frame_mask[0].astype(f32)[:,None]
    normed,packed=qkv_proj(x,segc,emb,wq,bq,cos,sin,nd)
    qkv=lax.all_to_all(packed,"head",split_axis=0,concat_axis=0,tiled=True).reshape(nd*F,3*W)
    T=256
    qlo,qhi,klo,khi=tables(seg_row,msk_row,T)
    aq,ak=aux(seg_row,msk_row)
    o,lse=attn_fwd(qkv,qlo,qhi,aq,ak,T)
    def back(a):
        return lax.all_to_all(a.reshape(nd,F,-1),"head",split_axis=0,concat_axis=0,tiled=True)
    att=back(o).transpose(1,0,2).reshape(F,D)
    out,dmid,datt,grest,gb,ge=mid(x,att,cot,segc,mskc,emb,rest_all,bo,bu,bd)
    do=lax.all_to_all(datt.reshape(F,nd,W).transpose(1,0,2),"head",split_axis=0,concat_axis=0,tiled=True).reshape(nd*F,W)
    dqkv=attn_bwd(qkv,o,do,lse,klo,khi,aq,ak,T)
    gx,grest,gqkv,gbias,gada,gbada,dact=final(nd,ns,dqkv.reshape(nd,F,3*W),grest.reshape(X,2,Z,Y,K,2*H+D),x,normed,dmid,wq,cos,sin,segc,emb,gb,ge,act,w_ada)
    dact=dact[:,:,:K].reshape(N,8,2,K).sum(1).transpose(1,0,2).reshape(2,D)
    _,pull=jax.vjp(jax.nn.silu,time_embed[0].astype(f32))
    gtime=pull(dact)[0][None]
    gbada=lax.dynamic_slice_in_dim(gbada.reshape(-1),dev*E,E,0)
    gbias=gbias[:,0,:].reshape(-1)
    gbs=[]; at=0
    for k,order in ((3*D,restore),(D,None),(H,unhide),(D,None)):
        v=gbias[at:at+k]; at+=k
        if order: v=order(v[None])[0]
        gbs.append(lax.dynamic_slice_in_dim(v,dev*(k//N),k//N,0))
    gdown=grest[:,H:2*H].reshape(K,nt,D).transpose(1,0,2).reshape(nt*K,D)
    return (out[None],gx[None],gtime,gada,gbada,restore(gqkv),gbs[0],grest[:,2*H:],gbs[1],unhide(grest[:,:H]),gbs[2],gdown,gbs[3])


def solution(mesh):
    row=P("seq","head",None); ids=P("seq","head"); mat=P(HS,None); vec=P(HS); tim=P("seq",None,None)
    in_specs=(row,tim,ids,ids,ids)+(mat,vec)*5+(row,)
    out_specs=(row,row,tim)+(mat,vec)*5
    return jax.shard_map(body,mesh=mesh,in_specs=in_specs,out_specs=out_specs,check_vma=False)
```

```python
import functools
import math

import jax
import jax.numpy as jnp
from jax import lax
from jax.experimental import pallas as pl
from jax.experimental.pallas import tpu as pltpu
from jax.sharding import PartitionSpec as P

bf = jnp.bfloat16
f32 = jnp.float32
HS = ("head", "seq")
ANY = pl.BlockSpec(memory_space=pl.ANY)
V = pl.BlockSpec(memory_space=pltpu.VMEM)
NN = (((1,), (0,)), ((), ()))
NT = (((1,), (1,)), ((), ()))
TN = (((0,), (0,)), ((), ()))


def dot(a, b, dims=NN):
    return lax.dot_general(a, b, dims, preferred_element_type=f32)


HD=64
LOG2E=math.log2(math.e)
NEG=-1e30

def fwd_kernel(lo_ref,hi_ref,qkv_ref,auxq_ref,auxk_ref,o_ref,lse_ref,k2,vx,q2,s_scr,m_scr,acc,*,T,nh):
    qt=pl.program_id(0)
    W=nh*HD
    L=qkv_ref.shape[0]
    nk=L//T
    lane=lax.broadcasted_iota(jnp.int32,(T,128),1)
    @pl.when(qt==0)
    def _():
        @pl.loop(0,nk)
        def _(t):
            r=pl.ds(pl.multiple_of(t*T,T),T)
            for h in range(nh):
                k=qkv_ref[r,W+h*HD:W+(h+1)*HD]
                k2[h,t]=jnp.concatenate([k,k],axis=1)
                v=qkv_ref[r,2*W+h*HD:2*W+(h+1)*HD]
                one=jnp.where(lax.broadcasted_iota(jnp.int32,(T,HD),1)==0,1.0,0.0).astype(bf)
                vx[h,t]=jnp.concatenate([v,one],axis=1)
    lo=lo_ref[qt]; hi=hi_ref[qt]
    r=pl.ds(pl.multiple_of(qt*T,T),T)
    for h in range(nh):
        q=qkv_ref[r,h*HD:(h+1)*HD].astype(f32)*(HD**-0.5*LOG2E)
        qh=q.astype(bf)
        ql=(q-qh.astype(f32)).astype(bf)
        q2[h]=jnp.concatenate([qh,ql],axis=1)
    auxq=auxq_ref[r,:]
    eye=lax.broadcasted_iota(jnp.int32,(T,T),0)==lax.broadcasted_iota(jnp.int32,(T,T),1)
    def mx(s):
        m=s[:,:128]
        for j in range(1,T//128): m=jnp.maximum(m,s[:,j*128:(j+1)*128])
        return m
    ak=auxk_ref[r,:]
    for h in range(nh):
        raw=dot(q2[h],k2[h,qt],NT)
        s=dot(jnp.concatenate([q2[h],auxq],axis=1),jnp.concatenate([k2[h,qt],ak],axis=1),NT)
        s=jnp.where(eye,raw,s)
        s_scr[h,qt]=s
        m_scr[h]=mx(s)
    @pl.loop(lo,hi-1)
    def _(t):
        kt=jnp.where(t>=qt,t+1,t)
        ak=auxk_ref[pl.ds(pl.multiple_of(kt*T,T),T),:]
        for h in range(nh):
            s=dot(jnp.concatenate([q2[h],auxq],axis=1),jnp.concatenate([k2[h,kt],ak],axis=1),NT)
            s_scr[h,kt]=s
            m_scr[h]=jnp.maximum(m_scr[h],mx(s))
    for h in range(nh):
        m_scr[h]=jnp.broadcast_to(jnp.max(m_scr[h],axis=1,keepdims=True),(T,128))
        acc[h]=jnp.zeros((T,128),f32)
    @pl.loop(lo,hi)
    def _(kt):
        for h in range(nh):
            s=s_scr[h,kt]; m=m_scr[h]
            p=jnp.exp2(s-jnp.concatenate([m]*(T//128),axis=1)).astype(bf)
            acc[h]+=dot(p,vx[h,kt])
    lse=jnp.zeros((T,128),f32)
    for h in range(nh):
        a=acc[h]
        l=a[:,HD:HD+1]
        o_ref[:,h*HD:(h+1)*HD]=(a[:,:HD]/l).astype(bf)
        lse=jnp.where(lane==h,m_scr[h]+jnp.log2(l),lse)
    lse_ref[...]=lse

def attn_fwd(qkv,lo,hi,auxq,auxk,T):
    L,W3=qkv.shape; W=W3//3; nh=W//HD; nk=L//T
    return pl.pallas_call(
        functools.partial(fwd_kernel,T=T,nh=nh),
        out_shape=(jax.ShapeDtypeStruct((L,W),bf),jax.ShapeDtypeStruct((L,128),f32)),
        grid_spec=pltpu.PrefetchScalarGridSpec(num_scalar_prefetch=2,grid=(nk,),
            in_specs=[pl.BlockSpec((L,W3),lambda i,*_:(0,0)),pl.BlockSpec((L,128),lambda i,*_:(0,0)),pl.BlockSpec((L,128),lambda i,*_:(0,0))],
            out_specs=[pl.BlockSpec((T,W),lambda i,*_:(i,0)),pl.BlockSpec((T,128),lambda i,*_:(i,0))],
            scratch_shapes=[pltpu.VMEM((nh,nk,T,128),bf),pltpu.VMEM((nh,nk,T,128),bf),pltpu.VMEM((nh,T,128),bf),
                pltpu.VMEM((nh,nk,T,T),f32),pltpu.VMEM((nh,T,128),f32),pltpu.VMEM((nh,T,128),f32)]),
        compiler_params=pltpu.CompilerParams(vmem_limit_bytes=60*2**20),
        name="attn_fwd",
    )(lo,hi,qkv,auxq,auxk)

def bwd_kernel(lo_ref,hi_ref,qkv_ref,o_ref,do_ref,lse_ref,auxq_ref,auxk_ref,dqkv_ref,q2,qa,k2,dox,vx,kT,dqT,dk,dv,*,T,nh):
    kt=pl.program_id(0)
    W=nh*HD
    L=qkv_ref.shape[0]
    nk=L//T
    lane=lax.broadcasted_iota(jnp.int32,(T,128),1)
    lane64=lax.broadcasted_iota(jnp.int32,(T,HD),1)
    @pl.when(kt==0)
    def _():
        dqT[...]=jnp.zeros_like(dqT)
        @pl.loop(0,nk)
        def _(t):
            r=pl.ds(pl.multiple_of(t*T,T),T)
            lse=lse_ref[r,:]
            aq=auxq_ref[r,:].astype(f32)
            kT[t]=qkv_ref[r,W:2*W].T
            for h in range(nh):
                q=qkv_ref[r,h*HD:(h+1)*HD].astype(f32)*(HD**-0.5*LOG2E)
                qh=q.astype(bf)
                ql=(q-qh.astype(f32)).astype(bf)
                q2[h,t]=jnp.concatenate([qh,ql],axis=1)
                k=qkv_ref[r,W+h*HD:W+(h+1)*HD]
                k2[h,t]=jnp.concatenate([k,k],axis=1)
                v=qkv_ref[r,2*W+h*HD:2*W+(h+1)*HD]
                vx[h,t]=jnp.concatenate([v,jnp.where(lane64<2,1.0,0.0).astype(bf)],axis=1)
                nl=-lse[:,h:h+1]
                l1=nl.astype(bf).astype(f32); l2=(nl-l1).astype(bf).astype(f32); l3=nl-l1-l2
                qa[h,t]=jnp.where(lane==0,l1,jnp.where(lane==1,l2,jnp.where(lane==2,l3,aq))).astype(bf)
                do=do_ref[r,h*HD:(h+1)*HD]
                nd=-jnp.sum(do.astype(f32)*o_ref[r,h*HD:(h+1)*HD].astype(f32),axis=1,keepdims=True)
                d1=nd.astype(bf).astype(f32); d2=nd-d1
                dox[h,t]=jnp.concatenate([do,jnp.where(lane64==0,d1,jnp.where(lane64==1,d2,0.0)).astype(bf)],axis=1)
    r=pl.ds(pl.multiple_of(kt*T,T),T)
    ak=auxk_ref[r,:]
    lo=lo_ref[kt]; hi=hi_ref[kt]
    def tile(qt,diag):
        rq=pl.ds(pl.multiple_of(qt*T,T),T)
        for h in range(nh):
            kx=jnp.concatenate([k2[h,kt],ak],axis=1)
            s=dot(kx,jnp.concatenate([q2[h,qt],qa[h,qt]],axis=1),NT)
            if diag:
                eye=lax.broadcasted_iota(jnp.int32,(T,T),0)==lax.broadcasted_iota(jnp.int32,(T,T),1)
                qr=jnp.where(lane<3,qa[h,qt].astype(f32),0.0).astype(bf)
                raw=dot(kx,jnp.concatenate([q2[h,qt],qr],axis=1),NT)
                s=jnp.where(eye,raw,s)
            p=jnp.exp2(s)
            dp=dot(vx[h,kt],dox[h,qt],NT)
            ds=(p*dp).astype(bf)
            pb=p.astype(bf)
            g=h//2
            rv=dot(pb,do_ref[rq,g*128:(g+1)*128])
            rk=dot(ds,qkv_ref[rq,g*128:(g+1)*128])
            dv[h]+=rv
            dk[h]+=rk
            dqT[qt,h*HD:(h+1)*HD,:]+=dot(kT[kt,h*HD:(h+1)*HD,:],ds)
    dk[...]=jnp.zeros_like(dk); dv[...]=jnp.zeros_like(dv)
    tile(kt,True)
    @pl.loop(lo,hi-1)
    def _(t):
        tile(jnp.where(t>=kt,t+1,t),False)
    for g in range(nh//2):
        dqkv_ref[r,W+g*128:W+(g+1)*128]=(jnp.where(lane<HD,dk[2*g],dk[2*g+1])*HD**-0.5).astype(bf)
        dqkv_ref[r,2*W+g*128:2*W+(g+1)*128]=jnp.where(lane<HD,dv[2*g],dv[2*g+1]).astype(bf)
    @pl.when(kt==nk-1)
    def _():
        @pl.loop(0,nk)
        def _(t):
            dqkv_ref[pl.ds(pl.multiple_of(t*T,T),T),0:W]=(dqT[t].T*HD**-0.5).astype(bf)

def attn_bwd(qkv,o,do,lse,lo,hi,auxq,auxk,T):
    L,W3=qkv.shape; W=W3//3; nh=W//HD; nk=L//T
    full=lambda w: pl.BlockSpec((L,w),lambda i,*_:(0,0))
    return pl.pallas_call(
        functools.partial(bwd_kernel,T=T,nh=nh),
        out_shape=jax.ShapeDtypeStruct((L,W3),bf),
        grid_spec=pltpu.PrefetchScalarGridSpec(num_scalar_prefetch=2,grid=(nk,),
            in_specs=[full(W3),full(W),full(W),full(128),full(128),full(128)],
            out_specs=full(W3),
            scratch_shapes=[pltpu.VMEM((nh,nk,T,128),bf)]*5+[pltpu.VMEM((nk,W,T),bf),pltpu.VMEM((nk,W,T),f32),
                pltpu.VMEM((nh,T,128),f32),pltpu.VMEM((nh,T,128),f32)]),
        compiler_params=pltpu.CompilerParams(vmem_limit_bytes=60*2**20),
        name="attn_bwd",
    )(lo,hi,qkv,o,do,lse,auxq,auxk)

def tables(seg,mask,T):
    L=seg.shape[0]; nk=L//T
    s=seg.reshape(nk,T); m=mask.reshape(nk,T)
    has=jnp.stack([jnp.any(s==c,axis=1) for c in (0,1)],1)
    real=jnp.stack([jnp.any((s==c)&(m==1),axis=1) for c in (0,1)],1)
    use=jnp.any(has[:,None,:]&real[None,:,:],axis=2)|jnp.eye(nk,dtype=bool)
    idx=jnp.arange(nk,dtype=jnp.int32)
    qlo=jnp.min(jnp.where(use,idx[None,:],nk),axis=1); qhi=jnp.max(jnp.where(use,idx[None,:],-1),axis=1)+1
    klo=jnp.min(jnp.where(use,idx[:,None],nk),axis=0); khi=jnp.max(jnp.where(use,idx[:,None],-1),axis=0)+1
    return [a.astype(jnp.int32) for a in (qlo,qhi,klo,khi)]
def aux(seg,mask):
    L=seg.shape[0]
    lane=lax.broadcasted_iota(jnp.int32,(L,128),1)
    sg=seg[:,None]; pad=(mask==0)[:,None]
    aq=jnp.where(lane==3,jnp.where(sg!=0,NEG,0.),jnp.where(lane==4,jnp.where(sg!=1,NEG,0.),jnp.where(lane==5,NEG,0.))).astype(bf)
    ak=jnp.where(lane<3,1.,jnp.where(lane==3,(sg==0).astype(f32),jnp.where(lane==4,(sg==1).astype(f32),jnp.where(lane==5,pad.astype(f32),0.)))).astype(bf)
    return aq,ak

EPS=1e-6

def moments(x):
    c=jnp.mean(x,-1,keepdims=True)
    xc=x-c
    rs=lax.rsqrt(jnp.mean(xc*xc,-1,keepdims=True)+EPS)
    return xc*rs, rs
def pick(seg,emb,i,D):
    return jnp.where(seg==0,emb[0:1,i*D:(i+1)*D],emb[1:2,i*D:(i+1)*D])
def sums(x,seg):
    a=jnp.sum(jnp.where(seg==0,x,0.0),0,keepdims=True); b=jnp.sum(jnp.where(seg==1,x,0.0),0,keepdims=True)
    return a,b
def partner(v):
    w=v.shape[1]
    lane=lax.broadcasted_iota(jnp.int32,v.shape,1)
    return jnp.where(lane%2==0,pltpu.roll(v,w-1,1),pltpu.roll(v,1,1))
def gelu_both(v):
    c=math.sqrt(2/math.pi)
    v2=v*v
    t=jnp.tanh(c*v*(1.0+0.044715*v2))
    h=0.5*(1.0+t)
    return v*h, h+0.5*v*(1.0-t*t)*(c*(1.0+3*0.044715*v2))

def qkv_kernel(x_ref,seg_ref,emb_ref,w_ref,b_ref,cos_ref,sin_ref,n_ref,p_ref,*,R,nd,W):
    F,D=x_ref.shape
    @pl.loop(0,F//R)
    def _(i):
        r=pl.ds(pl.multiple_of(i*R,R),R)
        seg=seg_ref[r,:]
        n,_=moments(x_ref[r,:].astype(f32))
        y=(n*(1.0+pick(seg,emb_ref,1,D))+pick(seg,emb_ref,0,D)).astype(bf)
        n_ref[r,:]=y
        cos=jnp.concatenate([cos_ref[r,:]]*(W//128),1); sin=jnp.concatenate([sin_ref[r,:]]*(W//128),1)
        for d in range(nd):
            for j in range(3):
                c=(d*3+j)*W
                v=dot(y,w_ref[:,c:c+W])+b_ref[0:1,c:c+W]
                if j<2: v=v*cos+partner(v)*sin
                p_ref[d,r,j*W:(j+1)*W]=v.astype(bf)

def qkv_proj(x,seg,emb,w,b,cos,sin,nd,R=128):
    F,D=x.shape; W=D//nd
    return pl.pallas_call(functools.partial(qkv_kernel,R=R,nd=nd,W=W),
        out_shape=(jax.ShapeDtypeStruct((F,D),bf),jax.ShapeDtypeStruct((nd,F,3*W),bf)),
        in_specs=[V]*7,out_specs=(V,V),
        compiler_params=pltpu.CompilerParams(vmem_limit_bytes=60*2**20),name="qkv_proj",
        cost_estimate=pl.CostEstimate(flops=2*F*D*3*D,bytes_accessed=14*2**20,transcendentals=0))(x,seg,emb,w,b,cos,sin)

def mid_kernel(x_ref,a_ref,c_ref,seg_ref,msk_ref,emb_ref,w_ref,bo_ref,bu_ref,bd_ref,
               out_ref,dm_ref,da_ref,gu_ref,gw_ref,gb_ref,ge_ref,
               wo_ref,wu_ref,wd_ref,n2s,acts,dhs,dfs,dps,dgelu,sem,*,R):
    F,D=x_ref.shape; H=bu_ref.shape[1]; CH=512
    loads=[pltpu.make_async_copy(w_ref.at[:,pl.ds(o,n)],r,sem.at[i]) for i,(o,n,r) in enumerate(((2*H,D,wo_ref),(0,H,wu_ref),(H,H,wd_ref)))]
    for l in loads: l.start()
    gb_ref[...]=jnp.zeros_like(gb_ref); ge_ref[...]=jnp.zeros_like(ge_ref)
    for l in loads: l.wait()
    def down(j):
        t,o=divmod(j*CH,D)
        return slice(o,o+CH),slice(t*D,(t+1)*D)
    @pl.loop(0,F//R)
    def _(i):
        r=pl.ds(pl.multiple_of(i*R,R),R)
        seg=seg_ref[r,:]; msk=msk_ref[r,:]
        def acc(k,x):
            a,b=sums(x,seg)
            ge_ref[0:1,k*D:(k+1)*D]+=a; ge_ref[1:2,k*D:(k+1)*D]+=b
        branch=(dot(a_ref[r,:],wo_ref[...])+bo_ref[0:1,:])*msk
        g1=pick(seg,emb_ref,2,D)
        middle=x_ref[r,:].astype(f32)+g1*branch
        n,rs=moments(middle)
        sc2=1.0+pick(seg,emb_ref,4,D)
        n2=(n*sc2+pick(seg,emb_ref,3,D)).astype(bf)
        n2s[r,:]=n2
        feed=jnp.broadcast_to(bd_ref[0:1,:],(R,D))
        for j in range(H//CH):
            c=slice(j*CH,(j+1)*CH)
            h=dot(n2,wu_ref[:,c])+bu_ref[0:1,c]
            a,g=gelu_both(h)
            a=a.astype(bf)
            acts[r,c]=a; dgelu[:,c]=g
            feed+=dot(a,wd_ref[down(j)])
        up=c_ref[r,:].astype(f32)
        g2=pick(seg,emb_ref,5,D)
        out_ref[r,:]=(middle+g2*feed).astype(bf)
        df=(up*g2).astype(bf)
        dfs[r,:]=df
        acc(3,up*feed)
        gb_ref[2:3,0:D]+=jnp.sum(df.astype(f32),0,keepdims=True)
        dn=jnp.zeros((R,D),f32)
        for j in range(H//CH):
            c=slice(j*CH,(j+1)*CH)
            dh=(dot(df,wd_ref[down(j)],NT)*dgelu[:,c]).astype(bf)
            dhs[r,c]=dh
            gb_ref[1:2,c]+=jnp.sum(dh.astype(f32),0,keepdims=True)
            dn+=dot(dh,wu_ref[:,c],NT)
        acc(1,dn); acc(2,dn*n)
        dn=dn*sc2
        dmid=up+(dn-jnp.mean(dn,-1,keepdims=True)-n*jnp.mean(dn*n,-1,keepdims=True))*rs
        dm_ref[r,:]=dmid
        acc(0,dmid*branch)
        dp=(dmid*g1*msk).astype(bf)
        dps[r,:]=dp
        gb_ref[0:1,0:D]+=jnp.sum(dp.astype(f32),0,keepdims=True)
        da_ref[r,:]=dot(dp,wo_ref[...],NT).astype(bf)
    @pl.loop(0,D//256)
    def _(i):
        c=pl.ds(pl.multiple_of(i*256,256),256)
        gw_ref[c,H:H+D]=dot(a_ref[:,c],dps[...],TN).astype(bf)
        gu_ref[c,:]=dot(n2s[:,c],dhs[...],TN).astype(bf)
        for t in range(H//D):
            e=pl.ds(pl.multiple_of(t*D+i*256,256),256)
            gw_ref[c,t*D:(t+1)*D]=dot(acts[:,e],dfs[...],TN).astype(bf)

def mid(x,a,c,seg,msk,emb,w,bo,bu,bd,R=128):
    F,D=x.shape; H=bu.shape[1]
    S=jax.ShapeDtypeStruct; M=pltpu.VMEM
    return pl.pallas_call(functools.partial(mid_kernel,R=R),
        out_shape=(S((F,D),bf),S((F,D),f32),S((F,D),bf),S((D,H),bf),S((D,H+D),bf),S((8,H),f32),S((8,4*D),f32)),
        in_specs=[V]*6+[ANY]+[V]*3,out_specs=(V,)*7,
        scratch_shapes=[M((D,D),bf),M((D,H),bf),M((D,H),bf),M((F,D),bf),M((F,H),bf),M((F,H),bf),M((F,D),bf),M((F,D),bf),M((R,H),f32),pltpu.SemaphoreType.DMA((3,))],
        compiler_params=pltpu.CompilerParams(vmem_limit_bytes=62*2**20),name="mid",
        cost_estimate=pl.CostEstimate(flops=6*F*D*(D+2*H),bytes_accessed=30*2**20,transcendentals=F*H))(x,a,c,seg,msk,emb,w,bo,bu,bd)

def tail_kernel(x_ref,n1_ref,dm_ref,g_ref,seg_ref,emb_ref,w_ref,cos_ref,sin_ref,gf_ref,gw_ref,gb_ref,ge_ref,dps,*,R,nd,W):
    F,D=x_ref.shape
    gb_ref[...]=jnp.zeros_like(gb_ref); ge_ref[...]=jnp.zeros_like(ge_ref)
    @pl.loop(0,F//R)
    def _(i):
        r=pl.ds(pl.multiple_of(i*R,R),R)
        seg=seg_ref[r,:]
        cos=jnp.concatenate([cos_ref[r,:]]*(W//128),1); sin=jnp.concatenate([sin_ref[r,:]]*(W//128),1)
        dn=jnp.zeros((R,D),f32)
        for d in range(nd):
            for j in range(3):
                c=(d*3+j)*W
                v=g_ref[d,r,j*W:(j+1)*W]
                if j<2:
                    v=v.astype(f32)
                    v=(v*cos-partner(v)*sin).astype(bf)
                dps[r,c:c+W]=v
                gb_ref[0:1,c:c+W]+=jnp.sum(v.astype(f32),0,keepdims=True)
        for j in range(3*D//512):
            dn+=dot(dps[r,j*512:(j+1)*512],w_ref[:,j*512:(j+1)*512],NT)
        n,rs=moments(x_ref[r,:].astype(f32))
        for k,x in ((0,dn),(1,dn*n)):
            a,b=sums(x,seg)
            ge_ref[0:1,k*D:(k+1)*D]+=a; ge_ref[1:2,k*D:(k+1)*D]+=b
        dn=dn*(1.0+pick(seg,emb_ref,1,D))
        gf_ref[r,:]=dm_ref[r,:]+(dn-jnp.mean(dn,-1,keepdims=True)-n*jnp.mean(dn*n,-1,keepdims=True))*rs
    @pl.loop(0,D//256)
    def _(i):
        c=pl.ds(pl.multiple_of(i*256,256),256)
        for j in range(3):
            gw_ref[c,j*D:(j+1)*D]=dot(n1_ref[:,c],dps[:,j*D:(j+1)*D],TN).astype(bf)

def tail(x,n1,dm,g,seg,emb,w,cos,sin,R=128):
    F,D=x.shape; nd=g.shape[0]; W=D//nd
    S=jax.ShapeDtypeStruct
    return pl.pallas_call(functools.partial(tail_kernel,R=R,nd=nd,W=W),
        out_shape=(S((F,D),f32),S((D,3*D),bf),S((8,3*D),f32),S((8,2*D),f32)),
        in_specs=[V]*9,out_specs=(V,)*4,
        scratch_shapes=[pltpu.VMEM((F,3*D),bf)],
        compiler_params=pltpu.CompilerParams(vmem_limit_bytes=60*2**20),name="tail",
        cost_estimate=pl.CostEstimate(flops=4*F*D*3*D,bytes_accessed=20*2**20,transcendentals=0))(x,n1,dm,g,seg,emb,w,cos,sin)

def sizes(nd,ns):
    Y=2**((ns.bit_length()-1)//2)
    return nd//2,Y,ns//Y

class Place:
    def __init__(self,nd,ns):
        self.nd,self.ns=nd,ns
        self.X,self.Y,self.Z=sizes(nd,ns)
        self.h=lax.axis_index("head"); self.s=lax.axis_index("seq")
        self.x,self.c=self.h//2,self.h%2
        self.z,self.y=self.s//self.Y,self.s%self.Y
    def at(self,x=None,c=None,z=None,y=None):
        x=self.x if x is None else x; c=self.c if c is None else c
        z=self.z if z is None else z; y=self.y if y is None else y
        return (x*2+c,z*self.Y+y)

def near_first(n):
    out=[]
    for d in range(1,n//2+1):
        out.append(d)
        if n-d!=d: out.append(n-d)
    return out

def remote(src,dst,ss,rs,dev):
    cp=pltpu.make_async_remote_copy(src_ref=src,dst_ref=dst,send_sem=ss,recv_sem=rs,device_id=dev,device_id_type=pl.DeviceIdType.MESH)
    cp.start()
    return cp

def greet_all(p):
    b=pltpu.get_barrier_semaphore()
    @pl.loop(0,p.nd)
    def _(dh):
        @pl.loop(0,p.ns)
        def _(ds):
            @pl.when(dh+ds>0)
            def _():
                pl.semaphore_signal(b,inc=1,device_id=(lax.rem(p.h+dh,p.nd),lax.rem(p.s+ds,p.ns)),device_id_type=pl.DeviceIdType.MESH)
    pl.semaphore_wait(b,p.nd*p.ns-1)

class Gather:
    @staticmethod
    def sems(nd,ns):
        X,Y,Z=sizes(nd,ns)
        D=pltpu.SemaphoreType.DMA
        one=[D((Z,)),D((Z,X)),D((Z,Y)),D((Z,X,Y)),D((Z,X,Y)),D((Z,)),D((2,Z,X,Y))]
        return one+one+[D(())]
    def __init__(self,p,shard,out,sems):
        self.p,self.shard,self.out=p,shard,out
        self.ss,self.rs,self.ls=sems[:7],sems[7:14],sems[14]
        self.all=[]; self.half=shard.shape[-1]//2
        self.two={}; self.three={}
    def send(self,k,idx,src,dst,dev):
        cp=remote(src,dst,self.ss[k].at[idx],self.rs[k].at[idx],dev)
        self.all.append(cp); return cp
    def cols(self,part): return pl.ds(part*self.half,self.half)
    def loc(self,x,z,y,part=None):
        r=self.out.at[x,self.p.c,z,y]
        return r if part is None else r.at[:,self.cols(part)]
    def start(self):
        p=self.p
        self.zc={}
        for dz in near_first(p.Z):
            self.zc[dz]=self.send(0,(dz,),self.shard,self.loc(p.x,p.z,p.y),p.at(z=lax.rem(p.z+dz,p.Z)))
        self.local=pltpu.make_async_copy(self.shard,self.loc(p.x,p.z,p.y),self.ls)
        self.local.start()
        self.second(0)
    def second(self,dz):
        p=self.p; zz=lax.rem(p.z+p.Z-dz,p.Z)
        if dz: self.zc[dz].wait_recv()
        def src(part=None):
            if dz: return self.loc(p.x,zz,p.y,part)
            return self.shard if part is None else self.shard.at[:,self.cols(part)]
        for dx in near_first(p.X):
            self.two[0,dz,dx]=self.send(1,(dz,dx),src(0),self.loc(p.x,zz,p.y,0),p.at(x=lax.rem(p.x+dx,p.X)))
        for dy in near_first(p.Y):
            self.two[1,dz,dy]=self.send(2,(dz,dy),src(1),self.loc(p.x,zz,p.y,1),p.at(y=lax.rem(p.y+dy,p.Y)))
        self.send(5,(dz,),src(),self.loc(p.x,zz,p.y),p.at(c=1-p.c))
        for dy in near_first(p.Y):
            self.three[0,dz,0,dy]=self.send(3,(dz,0,dy),src(0),self.loc(p.x,zz,p.y,0),p.at(y=lax.rem(p.y+dy,p.Y)))
        for dx in near_first(p.X):
            self.three[1,dz,dx,0]=self.send(4,(dz,dx,0),src(1),self.loc(p.x,zz,p.y,1),p.at(x=lax.rem(p.x+dx,p.X)))
    def third(self,dz):
        p=self.p; zz=lax.rem(p.z+p.Z-dz,p.Z)
        for dx in near_first(p.X):
            self.two[0,dz,dx].wait_recv()
            l=self.loc(lax.rem(p.x+p.X-dx,p.X),zz,p.y,0)
            for dy in near_first(p.Y):
                self.three[0,dz,dx,dy]=self.send(3,(dz,dx,dy),l,l,p.at(y=lax.rem(p.y+dy,p.Y)))
            self.send(6,(0,dz,dx,0),l,l,p.at(c=1-p.c))
        for dy in near_first(p.Y):
            self.two[1,dz,dy].wait_recv()
            l=self.loc(p.x,zz,lax.rem(p.y+p.Y-dy,p.Y),1)
            for dx in near_first(p.X):
                self.three[1,dz,dx,dy]=self.send(4,(dz,dx,dy),l,l,p.at(x=lax.rem(p.x+dx,p.X)))
            self.send(6,(1,dz,0,dy),l,l,p.at(c=1-p.c))
    def fourth(self,dz):
        p=self.p; zz=lax.rem(p.z+p.Z-dz,p.Z)
        for part in (0,1):
            for dx in range(p.X):
                for dy in range(p.Y):
                    if (part,dz,dx,dy) not in self.three: continue
                    self.three[part,dz,dx,dy].wait_recv()
                    l=self.loc(lax.rem(p.x+p.X-dx,p.X),zz,lax.rem(p.y+p.Y-dy,p.Y),part)
                    self.send(6,(part,dz,dx,dy),l,l,p.at(c=1-p.c))
    def finish(self):
        waited=set()
        for cp in self.zc.values(): waited.add(id(cp))
        for d in (self.two,self.three):
            for cp in d.values(): waited.add(id(cp))
        for cp in self.all:
            if id(cp) not in waited: cp.wait_recv()
            cp.wait_send()
        self.local.wait()

def entry_kernel(nd,ns,nw,*refs):
    shards=refs[:nw]; bias,time,ids,wada=refs[nw:nw+4]
    outs=refs[nw+4:2*nw+4]; bias_all,ids_all,emb,act=refs[2*nw+4:2*nw+8]
    time_all,part,r1,r2,bs,br,isd,ir,ts,tr,e1s,e1r,e2s,e2r=refs[2*nw+8:2*nw+22]
    gs=refs[2*nw+22:]
    p=Place(nd,ns); n=len(Gather.sems(nd,ns))
    greet_all(p)
    tail=[]
    first=[]
    for ds in range(1,ns):
        first.append(remote(time,time_all.at[p.s],ts.at[ds],tr.at[ds],(p.h,lax.rem(p.s+ds,ns))))
    g=[Gather(p,shards[i],outs[i],gs[i*n:(i+1)*n]) for i in range(nw)]
    for a in g: a.start()
    me=p.h*ns+p.s
    for dh in range(1,nd):
        tail.append(remote(ids,ids_all.at[p.h],isd.at[dh],ir.at[dh],(lax.rem(p.h+dh,nd),p.s)))
    @pl.loop(0,nd)
    def _(dh):
        @pl.loop(0,ns)
        def _(ds):
            @pl.when(dh+ds>0)
            def _():
                remote(bias,bias_all.at[me],bs.at[dh,ds],br.at[dh,ds],(lax.rem(p.h+dh,nd),lax.rem(p.s+ds,ns)))
    l1=pltpu.make_async_copy(bias,bias_all.at[me],bs.at[0,0]); l1.start()
    l2=pltpu.make_async_copy(ids,ids_all.at[p.h],isd.at[0]); l2.start()
    time_all[p.s]=time[...]
    for cp in first: cp.wait()
    D=time.shape[1]; K=wada.shape[0]; E=wada.shape[1]//8
    v=time_all[...].reshape(ns*8,D)
    low=(v/(1.0+jnp.exp(-v))).astype(bf)
    kk=D//(nd*ns)
    row=lax.broadcasted_iota(jnp.int32,(D,128),0); col=lax.broadcasted_iota(jnp.int32,(D,128),1)
    pickm=jnp.where((row==me*kk+col)&(col<kk),1.0,0.0).astype(bf)
    own=dot(low,pickm).astype(bf)
    act[...]=own
    for j in range(8):
        pj=dot(own[:,:K],wada[:,j*E:(j+1)*E])
        for s in range(ns):
            part[s,2*j:2*j+2,:]=pj[8*s:8*s+2,:]
    one=[remote(part.at[lax.rem(p.s+ds,ns)],r1.at[ds],e1s.at[ds],e1r.at[ds],(p.h,lax.rem(p.s+ds,ns))) for ds in range(1,ns)]
    order=[0]+near_first(p.Z)
    for a in g:
        for i,dz in enumerate(order):
            if dz: a.second(dz)
            if i: a.third(order[i-1])
        a.third(order[-1])
    tot=part[p.s]
    for ds in range(1,ns):
        one[ds-1].wait()
        tot=tot+r1[ds]
    r2[p.h]=tot
    two=[remote(r2.at[p.h],r2.at[p.h],e2s.at[dh],e2r.at[dh],(lax.rem(p.h+dh,nd),p.s)) for dh in range(1,nd)]
    for a in g:
        for dz in order: a.fourth(dz)
    for cp in two: cp.wait()
    tot=r2[0]
    for i in range(1,nd): tot=tot+r2[i]
    emb[...]=tot
    for a in g: a.finish()
    for cp in tail: cp.wait()
    l1.wait(); l2.wait()
    @pl.loop(0,nd)
    def _(dh):
        @pl.loop(0,ns)
        def _(ds):
            @pl.when(dh+ds>0)
            def _():
                pltpu.make_async_remote_copy(src_ref=bias,dst_ref=bias_all.at[me],send_sem=bs.at[dh,ds],recv_sem=br.at[dh,ds],device_id=(lax.rem(p.h+dh,nd),lax.rem(p.s+ds,ns)),device_id_type=pl.DeviceIdType.MESH).wait()

def entry(nd,ns,shards,bias,time,ids,wada):
    X,Y,Z=sizes(nd,ns)
    S=jax.ShapeDtypeStruct
    D=pltpu.SemaphoreType.DMA
    nw=len(shards); E=wada.shape[1]//8
    outs=[S((X,2,Z,Y)+a.shape,a.dtype) for a in shards]+[S((nd*ns,)+bias.shape,bias.dtype),S((nd,)+ids.shape,ids.dtype),S((16,E),f32),S((ns*8,128),bf)]
    scr=[pltpu.VMEM((ns,8,time.shape[1]),f32),pltpu.VMEM((ns,16,E),f32),pltpu.VMEM((ns,16,E),f32),pltpu.VMEM((nd,16,E),f32),
         D((nd,ns)),D((nd,ns)),D((nd,)),D((nd,)),D((ns,)),D((ns,)),D((ns,)),D((ns,)),D((nd,)),D((nd,))]
    for _ in shards: scr+=Gather.sems(nd,ns)
    return pl.pallas_call(functools.partial(entry_kernel,nd,ns,nw),out_shape=tuple(outs),
        in_specs=[ANY]*(nw+1)+[V,ANY,V],out_specs=tuple([ANY]*(nw+2)+[V,V]),scratch_shapes=scr,
        compiler_params=pltpu.CompilerParams(collective_id=0,has_side_effects=True,vmem_limit_bytes=40*2**20),name="entry")(*shards,bias,time,ids,wada)

ORD_X=-1
QW=512
class Reduce:
    def __init__(self,p,parts,scr,own=None,src=None,col=0):
        self.p,self.parts,self.src=p,parts,src
        it=iter(scr)
        self.own=own if own is not None else next(it)
        self.c=p.c if own is not None else 0
        self.w=self.own.shape[-1]; self.cs=pl.ds(col,self.w)
        self.cin=next(it); self.c1,self.c2,self.ls=next(it),next(it),next(it)
        self.bufs=[[(next(it),next(it),next(it)) for _ in o] for _,_,o in parts]
        self.sent=[]; self.stage=0
    @staticmethod
    def scratch(nd,ns,k,w,dt,parts,own):
        X,Y,Z=sizes(nd,ns); M=pltpu.VMEM; D=pltpu.SemaphoreType.DMA; n={"x":X,"y":Y,"z":Z}
        out=[] if own else [M((X,1,Z,Y,k,w),dt)]
        out+=[M((X,Z,Y,k,w),dt),D((X,)),D((X,)),D((X,))]
        for lo,hi,order in parts:
            for i,a in enumerate(order):
                left=tuple(n[b] for b in "xzy" if b in order[i+1:])
                out+=[M((max(n[a]-1,1),)+left+(k,hi-lo),dt),D((n[a],)),D((n[a],))]
        return out
    def start(self):
        p=self.p; self.l=[]; self.cc=[]
        for x in range(p.X):
            s=self.own.at[x,1-p.c] if self.src is None else self.src.at[x,1-p.c,:,:,:,self.cs]
            self.cc.append(remote(s,self.cin.at[x],self.c1.at[x],self.c2.at[x],p.at(c=1-p.c)))
            if self.src is not None:
                l=pltpu.make_async_copy(self.src.at[x,p.c,:,:,:,self.cs],self.own.at[x,0],self.ls.at[x]); l.start(); self.l.append(l)
        self.sent+=self.cc
    def place(self,order,i,v):
        p=self.p; mine={"x":p.x,"y":p.y,"z":p.z}
        ix={b:(mine[b] if b in order[:i] else v if b==order[i] else slice(None)) for b in "xyz"}
        return (ix["x"],self.c,ix["z"],ix["y"])
    def add(self,i,x,cols):
        i=i+(slice(None),slice(*cols))
        self.own[i]=(self.own[i].astype(f32)+x.astype(f32)).astype(self.own.dtype)
    def send(self,part,i):
        p=self.p; lo,hi,order=self.parts[part]; a=order[i]
        n={"x":p.X,"y":p.Y,"z":p.Z}[a]; me={"x":p.x,"y":p.y,"z":p.z}[a]
        buf,s1,s2=self.bufs[part][i]; out=[]
        for d in near_first(n):
            v=lax.rem(me+d,n)
            out.append((d,remote(self.own.at[self.place(order,i,v)+(slice(None),pl.ds(lo,hi-lo))],buf.at[d-1],s1.at[d],s2.at[d],p.at(**{a:v}))))
        self.sent+=[c for _,c in out]
        return out
    def step(self):
        p=self.p; st=self.stage; self.stage+=1
        if st==0:
            for x in range(p.X):
                if self.src is not None: self.l[x].wait()
                self.cc[x].wait_recv()
                @pl.loop(0,p.Z)
                def _(z):
                    for y in range(p.Y): self.add((x,self.c,z,y),self.cin[x,z,y],(0,self.w))
            self.go=[self.send(k,0) for k in range(len(self.parts))]
            return
        go=[]
        for k,(lo,hi,order) in enumerate(self.parts):
            buf=self.bufs[k][st-1][0]; left=[b for b in "xzy" if b in order[st:]]
            n={"x":p.X,"y":p.Y,"z":p.Z}; mine={"x":p.x,"y":p.y,"z":p.z}
            for d,c in self.go[k]:
                c.wait_recv()
                def one(at,d=d):
                    ix={**mine,**at}
                    self.add((ix["x"],self.c,ix["z"],ix["y"]),buf[(d-1,)+tuple(at[b] for b in left)],(lo,hi))
                if len(left)==2:
                    @pl.loop(0,n[left[0]])
                    def _(u):
                        for v in range(n[left[1]]): one({left[0]:u,left[1]:v})
                else:
                    @pl.loop(0,n[left[0]])
                    def _(u): one({left[0]:u})
            go.append(self.send(k,st))
        self.go=go
    def last(self,out,col=0):
        p=self.p
        for k,(lo,hi,order) in enumerate(self.parts):
            buf=self.bufs[k][2][0]
            t=self.own[p.x,self.c,p.z,p.y,:,lo:hi].astype(f32)
            for d,c in self.go[k]:
                c.wait_recv()
                t=t+buf[d-1].astype(f32)
            out[:,col+lo:col+hi]=t
    def finish(self):
        for c in self.sent: c.wait_send()

def greet(p):
    b=pltpu.get_barrier_semaphore()
    for d in range(1,p.nd): pl.semaphore_signal(b,inc=1,device_id=(lax.rem(p.h+d,p.nd),p.s),device_id_type=pl.DeviceIdType.MESH)
    for d in range(1,p.ns): pl.semaphore_signal(b,inc=1,device_id=(p.h,lax.rem(p.s+d,p.ns)),device_id_type=pl.DeviceIdType.MESH)
    pl.semaphore_wait(b,p.nd+p.ns-2)

def along_head(p,f): return [f(d,lax.rem(p.h+d,p.nd),(lax.rem(p.h+d,p.nd),p.s)) for d in range(1,p.nd)]
def along_seq(p,f): return [f(d,lax.rem(p.s+d,p.ns),(p.h,lax.rem(p.s+d,p.ns))) for d in range(1,p.ns)]

REST=(lambda w,j:((0,w,"xyz"),) if j==ORD_X else ((0,w,"yzx"),)); QKV=(lambda w:((0,w//2,"yxz"),(w//2,w,"xyz")))

def final_kernel(nd,ns,R,refs,scr):
    (g_ref,rest_ref,x_hbm,n1_hbm,dm_hbm,wq_hbm,cos_ref,sin_ref,seg_ref,emb_ref,gbm_ref,gem_ref,act,wada)=refs[:14]
    (gf_ref,rest_out,qkv_out,bias_all,gada,gbada,dact)=refs[14:]
    (g,x_ref,n1_ref,dm_ref,w_ref,dps,gw,gbv,gev,bsc,bout,hsum,demb,dscr)=scr[:14]
    (gs,gr,gl,ld,hs,hr,qs,qr,ds_,dr,bs,br)=scr[14:26]
    pools=scr[26:]
    p=Place(nd,ns); me=p.h*ns+p.s
    F,D=x_ref.shape; W=D//nd; E=D*6//8; K=wada.shape[0]; H=gbm_ref.shape[1]; NR=F//R
    nr=H//D; nq=3*D//QW
    greet(p)
    loads=[pltpu.make_async_copy(a,b,ld.at[i]) for i,(a,b) in enumerate(((x_hbm,x_ref),(wq_hbm,w_ref),(dm_hbm,dm_ref),(n1_hbm,n1_ref)))]
    sends=[]; own=[]
    def chunk(i):
        r=pl.ds(i*R,R)
        sends.append([remote(g_ref.at[lax.rem(p.h+d,nd),r],g.at[p.h,r],gs.at[i,d],gr.at[i,d],(lax.rem(p.h+d,nd),p.s)) for d in range(1,nd)])
    for i in range(NR):
        r=pl.ds(i*R,R)
        c=pltpu.make_async_copy(g_ref.at[p.h,r],g.at[p.h,r],gl.at[i]); c.start(); own.append(c)
    for i in range(min(2,NR)): chunk(i)
    for l in loads: l.start()
    it=iter(pools)
    take=lambda n: [next(it) for _ in range(n)]
    rest=[]
    for j in range(nr):
        rest.append(Reduce(p,REST(D,j),take(len(Reduce.scratch(nd,ns,K,D,bf,REST(D,j),False))),src=rest_ref,col=j*D))
        rest[-1].start()
    qkv=[Reduce(p,QKV(QW),take(len(Reduce.scratch(nd,ns,K,QW,bf,QKV(QW),True))),own=gw.at[j]) for j in range(nq)]
    bias=Reduce(p,QKV(256),take(len(Reduce.scratch(nd,ns,8,256,f32,QKV(256),True))),own=bsc)
    gbv[...]=jnp.zeros_like(gbv); gev[...]=jnp.zeros_like(gev); bsc[...]=jnp.zeros_like(bsc)
    for a in rest[:2]: a.step()
    for l in loads: l.wait()
    def turn(i):
        for c in sends[i]: c.wait_recv()
        own[i].wait()
        if i+2<NR: chunk(i+2)
        r=slice(i*R,(i+1)*R)
        cos=jnp.concatenate([cos_ref[r,:]]*(W//128),1); sin=jnp.concatenate([sin_ref[r,:]]*(W//128),1)
        @pl.loop(0,nd)
        def _(d):
            for j in range(3):
                c=pl.ds(pl.multiple_of((d*3+j)*W,W),W)
                v=g[d,r,j*W:(j+1)*W]
                if j<2:
                    v=v.astype(f32)
                    v=(v*cos-partner(v)*sin).astype(bf)
                dps[r,c]=v
                gbv[0:1,c]+=jnp.sum(v.astype(f32),0,keepdims=True)
    def norm(lo,hi):
        @pl.loop(lo,hi)
        def _(i):
            r=pl.ds(pl.multiple_of(i*R,R),R)
            seg=seg_ref[r,:]
            dn=jnp.zeros((R,D),f32)
            for j in range(3*D//512):
                dn+=dot(dps[r,j*512:(j+1)*512],w_ref[:,j*512:(j+1)*512],NT)
            n,rs=moments(x_ref[r,:].astype(f32))
            for k,x in ((0,dn),(1,dn*n)):
                a,b=sums(x,seg)
                gev[0:1,k*D:(k+1)*D]+=a; gev[1:2,k*D:(k+1)*D]+=b
            dn=dn*(1.0+pick(seg,emb_ref,1,D))
            gf_ref[r,:]=dm_ref[r,:]+(dn-jnp.mean(dn,-1,keepdims=True)-n*jnp.mean(dn*n,-1,keepdims=True))*rs
    def weight(j):
        B=D//nd
        for h in range(nd):
            v=dot(n1_ref[:,h*B:(h+1)*B],dps[:,j*QW:(j+1)*QW],TN).astype(bf)
            gw[j,h//2,h%2]=v.reshape(p.Z,p.Y,K,QW)
        qkv[j].start()
    steps=[a.step for _ in range(2) for a in rest]
    for i in range(NR):
        turn(i)
        if i:
            for f in steps[(i-1)*len(steps)//(NR-1):i*len(steps)//(NR-1)]: f()
    for j in range(nq):
        weight(j)
        if j: qkv[j-1].step()
    vec=jnp.concatenate([gbv[0:1,:],gbm_ref[0:1,0:D],gbm_ref[1:2,:],gbm_ref[2:3,0:D]],1)
    for q in range(vec.shape[1]//256):
        h,s=divmod(q,ns)
        bsc[h//2,h%2,s//p.Y,s%p.Y,0:1,:]=vec[:,q*256:(q+1)*256]
    bias.start()
    qkv[nq-1].step()
    norm(0,NR//2)
    bias.step()
    qkv[0].step()
    qkv[1].step()
    norm(NR//2,NR)
    gev[0:2,2*D:]=gem_ref[0:2,:]
    for j in range(8):
        for t in range(2): hsum[p.h,2*j+t:2*j+t+1,:]=gev[t:t+1,j*E:(j+1)*E]
    hc=[remote(hsum.at[p.h],hsum.at[p.h],hs.at[d],hr.at[d],(lax.rem(p.h+d,nd),p.s)) for d in range(1,nd)]
    qkv[0].step(); qkv[2].step(); qkv[1].step(); bias.step()
    for c in hc: c.wait()
    tot=hsum[0]
    for i in range(1,nd): tot=tot+hsum[i]
    demb[p.s]=tot.astype(bf)
    qc=[remote(demb.at[p.s],demb.at[p.s],qs.at[d],qr.at[d],(p.h,lax.rem(p.s+d,ns))) for d in range(1,ns)]
    qkv[3].step(); qkv[2].step(); bias.step()
    for j,a in enumerate(rest): a.last(rest_out,j*D)
    bias.last(bout)
    bias_all[p.h,p.s]=bout[...]
    bc=along_head(p,lambda d,h,dev: remote(bout,bias_all.at[p.h,p.s],bs.at[0,d],br.at[0,d],dev))
    qkv[4].step(); qkv[3].step()
    for c in qc: c.wait()
    Q=ns*16
    flat=demb[...].reshape(Q,E)
    r0=lax.broadcasted_iota(jnp.int32,(Q,ns*8),0); c0=lax.broadcasted_iota(jnp.int32,(Q,ns*8),1)
    spread=dot(jnp.where((r0//16==c0//8)&(r0%2==c0%8),1.0,0.0).astype(bf),act[...])
    rr=lax.broadcasted_iota(jnp.int32,(Q,128),0)%16//2
    rk=lax.broadcasted_iota(jnp.int32,(Q,K),0)%16//2
    tot=jnp.zeros((Q,K),f32)
    for j in range(8):
        m=jnp.where(rr==j,spread,0.0).astype(bf)
        gada[:,j*E:(j+1)*E]=dot(m,flat,TN)[:K,:]
        tot=jnp.where(rk==j,dot(flat,wada[:,j*E:(j+1)*E],NT),tot)
    dscr[...]=jnp.concatenate([tot,jnp.zeros((Q,128-K),f32)],1).reshape(ns,16,128)
    dact[p.h,p.s]=dscr[p.s]
    dc=along_seq(p,lambda d,s,dev: remote(dscr.at[s],dact.at[p.h,p.s],ds_.at[0,d],dr.at[0,d],dev))
    for c in bc: c.wait()
    bc=along_seq(p,lambda d,s,dev: remote(bias_all.at[:,p.s],bias_all.at[:,p.s],bs.at[1,d],br.at[1,d],dev))
    r8=lax.broadcasted_iota(jnp.int32,(8,Q),0); c8=lax.broadcasted_iota(jnp.int32,(8,Q),1)
    gbada[...]=dot(jnp.where(c8%16//2==r8,1.0,0.0).astype(bf),flat)
    qkv[5].step(); qkv[4].step()
    for c in dc: c.wait()
    dc=along_head(p,lambda d,h,dev: remote(dact.at[p.h],dact.at[p.h],ds_.at[1,d],dr.at[1,d],dev))
    for j in range(nq-1): qkv[j].last(qkv_out,j*QW)
    qkv[5].step()
    qkv[nq-1].last(qkv_out,(nq-1)*QW)
    for a in rest+qkv+[bias]: a.finish()
    for i in range(NR):
        for c in sends[i]: c.wait_send()
    for c in bc+dc: c.wait()

def final(nd,ns,dqkv,rest,x,n1,dm,wq,cos,sin,seg,emb,gb,ge,act,wada,R=128):
    F,D=x.shape; K,E6=wada.shape; E=E6//8; H=gb.shape[1]; N=nd*ns; W=D//nd; NR=F//R
    X,Y,Z=sizes(nd,ns)
    S=jax.ShapeDtypeStruct; M=pltpu.VMEM; A=pltpu.SemaphoreType.DMA
    outs=[S((F,D),f32),S((K,H),f32),S((K,3*D),f32),S((nd,ns,8,256),f32),S((K,E6),f32),S((8,E),f32),S((nd,ns,16,128),f32)]
    scr=[M((nd,F,3*W),bf),M((F,D),bf),M((F,D),bf),M((F,D),f32),M((D,3*D),bf),M((F,3*D),bf),M((3*D//QW,X,2,Z,Y,K,QW),bf),M((8,3*D),f32),M((8,E6),f32),
         M((X,2,Z,Y,8,256),f32),M((8,256),f32),M((nd,16,E),f32),M((ns,16,E),bf),M((ns,16,128),f32),
         A((NR,nd)),A((NR,nd)),A((NR,)),A((4,)),A((nd,)),A((nd,)),A((ns,)),A((ns,)),A((2,max(nd,ns))),A((2,max(nd,ns))),A((2,max(nd,ns))),A((2,max(nd,ns)))]
    for j in range(H//D): scr+=Reduce.scratch(nd,ns,K,D,bf,REST(D,j),False)
    for _ in range(3*D//QW): scr+=Reduce.scratch(nd,ns,K,QW,bf,QKV(QW),True)
    scr+=Reduce.scratch(nd,ns,8,256,f32,QKV(256),True)
    def k(*refs): final_kernel(nd,ns,R,refs[:14+len(outs)],refs[14+len(outs):])
    return pl.pallas_call(k,out_shape=tuple(outs),in_specs=[ANY]*6+[V]*8,out_specs=(V,)*len(outs),scratch_shapes=scr,
        compiler_params=pltpu.CompilerParams(collective_id=1,has_side_effects=True,vmem_limit_bytes=63*2**20),name="final")(
        dqkv,rest,x,n1,dm,wq,cos,sin,seg,emb,gb,ge,act,wada)


def body(frames,time_embed,segment_ids,frame_mask,positions,w_ada,b_ada,w_qkv,b_qkv,w_out,b_out,w_up,b_up,w_down,b_down,cotangent):
    _,F,D=frames.shape
    nd=lax.axis_size("head"); ns=lax.axis_size("seq"); dev=lax.axis_index("head")*ns+lax.axis_index("seq")
    X,Y,Z=sizes(nd,ns); N=nd*ns
    W=D//nd
    E=b_ada.shape[0]; E6=w_ada.shape[1]; K=w_ada.shape[0]; H=w_up.shape[1]; nt=H//D
    x=frames[0]; cot=cotangent[0]
    def reorder(w): return w.reshape(-1,3,nd,W).transpose(0,2,1,3).reshape(-1,3*D)
    def restore(w): return w.reshape(-1,nd,3,W).transpose(0,2,1,3).reshape(-1,3*D)
    def hide(w): return w.reshape(-1,N,nt,K).transpose(0,2,1,3).reshape(-1,H)
    def unhide(w): return w.reshape(-1,nt,N,K).transpose(0,2,1,3).reshape(-1,H)
    rest=jnp.concatenate([hide(w_up),w_down.reshape(nt,K,D).transpose(1,0,2).reshape(K,H),w_out],axis=1)
    bs=(b_qkv,b_out,b_up,b_down,b_ada); ends=[0]
    for b in bs: ends.append(ends[-1]+b.shape[0])
    wide=-(-ends[-1]//256)*256
    bias=jnp.zeros((16,wide),bf).at[0,:ends[-1]].set(jnp.concatenate(bs))
    time8=jnp.zeros((8,D),f32).at[:2].set(time_embed[0].astype(f32))
    ids=jnp.zeros((8,F),jnp.int32).at[0].set(segment_ids[0]).at[1].set(frame_mask[0])
    wq,bias_all,ids_all,emb,act=entry(nd,ns,[reorder(w_qkv)],bias,time8,ids,w_ada)
    rest_all=lax.all_gather(rest,HS,axis=0,tiled=True)
    wq=wq.reshape(D,3*D)
    bias_all=bias_all[:,0,:].astype(f32)
    bq,bo,bu,bd,ba=[bias_all[:,ends[i]:ends[i+1]].reshape(1,-1) for i in range(5)]
    bq=reorder(bq); bu=hide(bu)
    emb=emb.reshape(8,2,-1).transpose(1,0,2).reshape(2,E6)+ba
    seg_row=ids_all[:,0,:].reshape(-1); msk_row=ids_all[:,1,:].reshape(-1)
    column=lax.iota(jnp.int32,128)
    pair=(column%HD//2).astype(f32)
    angles=positions[0].astype(f32)[:,None]*(10000.0**(-(2.0*pair)/HD))
    cos=jnp.cos(angles); sin=jnp.where(column%2==0,-jnp.sin(angles),jnp.sin(angles))
    segc=segment_ids[0][:,None]; mskc=frame_mask[0].astype(f32)[:,None]
    normed,packed=qkv_proj(x,segc,emb,wq,bq,cos,sin,nd)
    qkv=lax.all_to_all(packed,"head",split_axis=0,concat_axis=0,tiled=True).reshape(nd*F,3*W)
    T=512
    qlo,qhi,klo,khi=tables(seg_row,msk_row,T)
    aq,ak=aux(seg_row,msk_row)
    o,lse=attn_fwd(qkv,qlo,qhi,aq,ak,T)
    def back(a):
        return lax.all_to_all(a.reshape(nd,F,-1),"head",split_axis=0,concat_axis=0,tiled=True)
    att=back(o).transpose(1,0,2).reshape(F,D)
    out,dmid,datt,gup,gdo,gb,ge=mid(x,att,cot,segc,mskc,emb,rest_all,bo,bu,bd)
    gdo=lax.psum_scatter(gdo,HS,scatter_dimension=0,tiled=True).astype(f32)
    do=lax.all_to_all(datt.reshape(F,nd,W).transpose(1,0,2),"head",split_axis=0,concat_axis=0,tiled=True).reshape(nd*F,W)
    dqkv=attn_bwd(qkv,o,do,lse,klo,khi,aq,ak,T)
    gx,gup,gqkv,gbias,gada,gbada,dact=final(nd,ns,dqkv.reshape(nd,F,3*W),gup.reshape(X,2,Z,Y,K,H),x,normed,dmid,wq,cos,sin,segc,emb,gb,ge,act,w_ada)
    dact=dact[:,:,:,:K].reshape(N,8,2,K).sum(1).transpose(1,0,2).reshape(2,D)
    _,pull=jax.vjp(jax.nn.silu,time_embed[0].astype(f32))
    gtime=pull(dact)[0][None]
    gbada=lax.dynamic_slice_in_dim(gbada.reshape(-1),dev*E,E,0)
    gbias=gbias[:,:,0,:].reshape(-1)
    gbs=[]; at=0
    for k,order in ((3*D,restore),(D,None),(H,unhide),(D,None)):
        v=gbias[at:at+k]; at+=k
        if order: v=order(v[None])[0]
        gbs.append(lax.dynamic_slice_in_dim(v,dev*(k//N),k//N,0))
    gdown=gdo[:,:H].reshape(K,nt,D).transpose(1,0,2).reshape(nt*K,D)
    return (out[None],gx[None],gtime,gada,gbada,restore(gqkv),gbs[0],gdo[:,H:],gbs[1],unhide(gup),gbs[2],gdown,gbs[3])


def solution(mesh):
    row=P("seq","head",None); ids=P("seq","head"); mat=P(HS,None); vec=P(HS); tim=P("seq",None,None)
    in_specs=(row,tim,ids,ids,ids)+(mat,vec)*5+(row,)
    out_specs=(row,row,tim)+(mat,vec)*5
    return jax.shard_map(body,mesh=mesh,in_specs=in_specs,out_specs=out_specs,check_vma=False)
```

```python
import functools
import math

import jax
import jax.numpy as jnp
import numpy as np
from jax import lax
from jax.experimental import pallas as pl
from jax.experimental.pallas import tpu as pltpu
from jax.sharding import PartitionSpec as P

bf = jnp.bfloat16
f32 = jnp.float32
HS = ("head", "seq")
ANY = pl.BlockSpec(memory_space=pl.ANY)
V = pl.BlockSpec(memory_space=pltpu.VMEM)
NN = (((1,), (0,)), ((), ()))
NT = (((1,), (1,)), ((), ()))
TN = (((0,), (0,)), ((), ()))


def dot(a, b, dims=NN):
    return lax.dot_general(a, b, dims, preferred_element_type=f32)


HD=64
LOG2E=math.log2(math.e)
NEG=-1e30

def only(x,h):
    lane=lax.broadcasted_iota(jnp.int32,x.shape,1)
    return jnp.where((lane<HD) if h%2==0 else (lane>=HD),x,jnp.zeros_like(x))

def fwd_kernel(lo_ref,hi_ref,qkv_ref,auxq_ref,auxk_ref,o_ref,lse_ref,qs,s_scr,m_scr,acc,*,T,nh):
    qt=pl.program_id(0)
    W=nh*HD
    lane=lax.broadcasted_iota(jnp.int32,(T,128),1)
    lo=lo_ref[qt]; hi=hi_ref[qt]
    rq=pl.ds(pl.multiple_of(qt*T,T),T)
    def key(kt,h): return qkv_ref[pl.ds(pl.multiple_of(kt*T,T),T),W+h//2*128:W+(h//2+1)*128]
    def value(kt,h): return qkv_ref[pl.ds(pl.multiple_of(kt*T,T),T),2*W+h//2*128:2*W+(h//2+1)*128]
    for h in range(nh):
        qs[h]=only(qkv_ref[rq,h//2*128:(h//2+1)*128],h)*jnp.asarray(HD**-0.5,bf)
    auxq=auxq_ref[rq,:]
    eye=lax.broadcasted_iota(jnp.int32,(T,T),0)==lax.broadcasted_iota(jnp.int32,(T,T),1)
    def mx(s):
        m=s[:,:128]
        for j in range(1,T//128): m=jnp.maximum(m,s[:,j*128:(j+1)*128])
        return m
    ak=auxk_ref[rq,:]
    for h in range(nh):
        raw=dot(qs[h],key(qt,h),NT)
        s=dot(jnp.concatenate([qs[h],auxq],axis=1),jnp.concatenate([key(qt,h),ak],axis=1),NT)
        s=jnp.where(eye,raw,s)
        s_scr[h,qt]=s
        m_scr[h]=mx(s)
    @pl.loop(lo,hi-1)
    def _(t):
        kt=jnp.where(t>=qt,t+1,t)
        ak=auxk_ref[pl.ds(pl.multiple_of(kt*T,T),T),:]
        for h in range(nh):
            s=dot(jnp.concatenate([qs[h],auxq],axis=1),jnp.concatenate([key(kt,h),ak],axis=1),NT)
            s_scr[h,kt]=s
            m_scr[h]=jnp.maximum(m_scr[h],mx(s))
    for h in range(nh):
        m_scr[h]=jnp.broadcast_to(jnp.max(m_scr[h],axis=1,keepdims=True),(T,128))
        acc[h]=jnp.zeros((T,256),f32)
    ones=jnp.ones((T,128),bf)
    @pl.loop(lo,hi)
    def _(kt):
        for h in range(nh):
            s=s_scr[h,kt]; m=m_scr[h]
            p=jnp.exp2((s-jnp.concatenate([m]*(T//128),axis=1))*LOG2E).astype(bf)
            acc[h]+=dot(p,jnp.concatenate([value(kt,h),ones],axis=1))
    lse=jnp.zeros((T,128),f32)
    for g in range(nh//2):
        o=[]
        for h in (2*g,2*g+1):
            l=acc[h,:,128:]
            o.append(acc[h,:,:128]/l)
            lse=jnp.where(lane==h,m_scr[h]+jnp.log(l),lse)
        o_ref[:,g*128:(g+1)*128]=jnp.where(lane<HD,o[0],o[1]).astype(bf)
    lse_ref[...]=lse

def attn_fwd(qkv,lo,hi,auxq,auxk,T):
    L,W3=qkv.shape; W=W3//3; nh=W//HD; nk=L//T
    return pl.pallas_call(
        functools.partial(fwd_kernel,T=T,nh=nh),
        out_shape=(jax.ShapeDtypeStruct((L,W),bf),jax.ShapeDtypeStruct((L,128),f32)),
        grid_spec=pltpu.PrefetchScalarGridSpec(num_scalar_prefetch=2,grid=(nk,),
            in_specs=[pl.BlockSpec((L,W3),lambda i,*_:(0,0)),pl.BlockSpec((L,128),lambda i,*_:(0,0)),pl.BlockSpec((L,128),lambda i,*_:(0,0))],
            out_specs=[pl.BlockSpec((T,W),lambda i,*_:(i,0)),pl.BlockSpec((T,128),lambda i,*_:(i,0))],
            scratch_shapes=[pltpu.VMEM((nh,T,128),bf),pltpu.VMEM((nh,nk,T,T),f32),pltpu.VMEM((nh,T,128),f32),pltpu.VMEM((nh,T,256),f32)]),
        compiler_params=pltpu.CompilerParams(vmem_limit_bytes=60*2**20),
        name="attn_fwd",
    )(lo,hi,qkv,auxq,auxk)

def bwd_kernel(lo_ref,hi_ref,qkv_ref,o_ref,do_ref,lse_ref,auxq_ref,auxk_ref,dqkv_ref,qs,qa,dos,dd,kT,dqT,dk,dv,*,T,nh):
    kt=pl.program_id(0)
    W=nh*HD
    L=qkv_ref.shape[0]
    nk=L//T
    lane=lax.broadcasted_iota(jnp.int32,(T,128),1)
    def pair(ref,t,h,at=0): return ref[pl.ds(pl.multiple_of(t*T,T),T),at+h//2*128:at+(h//2+1)*128]
    @pl.when(kt==0)
    def _():
        dqT[...]=jnp.zeros_like(dqT)
        @pl.loop(0,nk)
        def _(t):
            r=pl.ds(pl.multiple_of(t*T,T),T)
            lse=lse_ref[r,:]
            aq=auxq_ref[r,:].astype(f32)
            kT[t]=qkv_ref[r,W:2*W].T
            for h in range(nh):
                qs[h,t]=only(pair(qkv_ref,t,h),h)*jnp.asarray(HD**-0.5,bf)
                nl=-lse[:,h:h+1]
                l1=nl.astype(bf).astype(f32); l2=(nl-l1).astype(bf).astype(f32); l3=nl-l1-l2
                qa[h,t]=jnp.where(lane==0,l1,jnp.where(lane==1,l2,jnp.where(lane==2,l3,aq))).astype(bf)
                do=only(pair(do_ref,t,h),h)
                dos[h,t]=do
                nd=-jnp.sum(do.astype(f32)*pair(o_ref,t,h).astype(f32),axis=1,keepdims=True)
                d1=nd.astype(bf).astype(f32); d2=nd-d1
                dd[h,t]=jnp.where(lane==0,d1,jnp.where(lane==1,d2,0.0)).astype(bf)
    r=pl.ds(pl.multiple_of(kt*T,T),T)
    ak=auxk_ref[r,:]
    av=jnp.where(lane<2,1.0,0.0).astype(bf)
    lo=lo_ref[kt]; hi=hi_ref[kt]
    def tile(qt,diag):
        for h in range(nh):
            kx=jnp.concatenate([pair(qkv_ref,kt,h,W),ak],axis=1)
            s=dot(kx,jnp.concatenate([qs[h,qt],qa[h,qt]],axis=1),NT)
            if diag:
                eye=lax.broadcasted_iota(jnp.int32,(T,T),0)==lax.broadcasted_iota(jnp.int32,(T,T),1)
                qr=jnp.where(lane<3,qa[h,qt].astype(f32),0.0).astype(bf)
                raw=dot(kx,jnp.concatenate([qs[h,qt],qr],axis=1),NT)
                s=jnp.where(eye,raw,s)
            p=jnp.exp2(s*LOG2E)
            dp=dot(jnp.concatenate([pair(qkv_ref,kt,h,2*W),av],axis=1),jnp.concatenate([dos[h,qt],dd[h,qt]],axis=1),NT)
            ds=(p*dp).astype(bf)
            dv[h]+=dot(p.astype(bf),pair(do_ref,qt,h))
            dk[h]+=dot(ds,pair(qkv_ref,qt,h))
            dqT[qt,h*HD:(h+1)*HD,:]+=dot(kT[kt,h*HD:(h+1)*HD,:],ds)
    dk[...]=jnp.zeros_like(dk); dv[...]=jnp.zeros_like(dv)
    tile(kt,True)
    @pl.loop(lo,hi-1)
    def _(t):
        tile(jnp.where(t>=kt,t+1,t),False)
    for g in range(nh//2):
        dqkv_ref[r,W+g*128:W+(g+1)*128]=(jnp.where(lane<HD,dk[2*g],dk[2*g+1])*HD**-0.5).astype(bf)
        dqkv_ref[r,2*W+g*128:2*W+(g+1)*128]=jnp.where(lane<HD,dv[2*g],dv[2*g+1]).astype(bf)
    @pl.when(kt==nk-1)
    def _():
        @pl.loop(0,nk)
        def _(t):
            dqkv_ref[pl.ds(pl.multiple_of(t*T,T),T),0:W]=(dqT[t].T*HD**-0.5).astype(bf)

def attn_bwd(qkv,o,do,lse,lo,hi,auxq,auxk,T):
    L,W3=qkv.shape; W=W3//3; nh=W//HD; nk=L//T
    full=lambda w: pl.BlockSpec((L,w),lambda i,*_:(0,0))
    return pl.pallas_call(
        functools.partial(bwd_kernel,T=T,nh=nh),
        out_shape=jax.ShapeDtypeStruct((L,W3),bf),
        grid_spec=pltpu.PrefetchScalarGridSpec(num_scalar_prefetch=2,grid=(nk,),
            in_specs=[full(W3),full(W),full(W),full(128),full(128),full(128)],
            out_specs=full(W3),
            scratch_shapes=[pltpu.VMEM((nh,nk,T,128),bf)]*4+[pltpu.VMEM((nk,W,T),bf),pltpu.VMEM((nk,W,T),f32),
                pltpu.VMEM((nh,T,128),f32),pltpu.VMEM((nh,T,128),f32)]),
        compiler_params=pltpu.CompilerParams(vmem_limit_bytes=60*2**20),
        name="attn_bwd",
    )(lo,hi,qkv,o,do,lse,auxq,auxk)

def tables(seg,mask,T):
    L=seg.shape[0]; nk=L//T
    s=seg.reshape(nk,T); m=mask.reshape(nk,T)
    has=jnp.stack([jnp.any(s==c,axis=1) for c in (0,1)],1)
    real=jnp.stack([jnp.any((s==c)&(m==1),axis=1) for c in (0,1)],1)
    use=jnp.any(has[:,None,:]&real[None,:,:],axis=2)|jnp.eye(nk,dtype=bool)
    idx=jnp.arange(nk,dtype=jnp.int32)
    qlo=jnp.min(jnp.where(use,idx[None,:],nk),axis=1); qhi=jnp.max(jnp.where(use,idx[None,:],-1),axis=1)+1
    klo=jnp.min(jnp.where(use,idx[:,None],nk),axis=0); khi=jnp.max(jnp.where(use,idx[:,None],-1),axis=0)+1
    return [a.astype(jnp.int32) for a in (qlo,qhi,klo,khi)]
def aux(seg,mask):
    L=seg.shape[0]
    lane=lax.broadcasted_iota(jnp.int32,(L,128),1)
    sg=seg[:,None]; pad=(mask==0)[:,None]
    aq=jnp.where(lane==3,jnp.where(sg!=0,NEG,0.),jnp.where(lane==4,jnp.where(sg!=1,NEG,0.),jnp.where(lane==5,NEG,0.))).astype(bf)
    ak=jnp.where(lane<3,1.,jnp.where(lane==3,(sg==0).astype(f32),jnp.where(lane==4,(sg==1).astype(f32),jnp.where(lane==5,pad.astype(f32),0.)))).astype(bf)
    return aq,ak

EPS=1e-6

def moments(x):
    c=jnp.mean(x,-1,keepdims=True)
    xc=x-c
    rs=lax.rsqrt(jnp.mean(xc*xc,-1,keepdims=True)+EPS)
    return xc*rs, rs
def pick(seg,emb,i,D):
    return jnp.where(seg==0,emb[0:1,i*D:(i+1)*D],emb[1:2,i*D:(i+1)*D])
def sums(x,seg):
    a=jnp.sum(jnp.where(seg==0,x,0.0),0,keepdims=True); b=jnp.sum(jnp.where(seg==1,x,0.0),0,keepdims=True)
    return a,b
def partner(v):
    w=v.shape[1]
    lane=lax.broadcasted_iota(jnp.int32,v.shape,1)
    return jnp.where(lane%2==0,pltpu.roll(v,w-1,1),pltpu.roll(v,1,1))
def gelu_both(v):
    c=math.sqrt(2/math.pi)
    v2=v*v
    t=jnp.tanh(c*v*(1.0+0.044715*v2))
    h=0.5*(1.0+t)
    return v*h, h+0.5*v*(1.0-t*t)*(c*(1.0+3*0.044715*v2))

def qkv_kernel(x_ref,seg_ref,emb_ref,w_ref,b_ref,cos_ref,sin_ref,n_ref,p_ref,*,R,nd,W):
    F,D=x_ref.shape
    @pl.loop(0,F//R)
    def _(i):
        r=pl.ds(pl.multiple_of(i*R,R),R)
        seg=seg_ref[r,:]
        n,_=moments(x_ref[r,:].astype(f32))
        y=(n*(1.0+pick(seg,emb_ref,1,D))+pick(seg,emb_ref,0,D)).astype(bf)
        n_ref[r,:]=y
        cos=jnp.concatenate([cos_ref[r,:]]*(W//128),1); sin=jnp.concatenate([sin_ref[r,:]]*(W//128),1)
        for d in range(nd):
            for j in range(3):
                c=(d*3+j)*W
                v=dot(y,w_ref[:,c:c+W])+b_ref[0:1,c:c+W]
                if j<2: v=v*cos+partner(v)*sin
                p_ref[d,r,j*W:(j+1)*W]=v.astype(bf)

def qkv_proj(x,seg,emb,w,b,cos,sin,nd,R=128):
    F,D=x.shape; W=D//nd
    return pl.pallas_call(functools.partial(qkv_kernel,R=R,nd=nd,W=W),
        out_shape=(jax.ShapeDtypeStruct((F,D),bf),jax.ShapeDtypeStruct((nd,F,3*W),bf)),
        in_specs=[V]*7,out_specs=(V,V),
        compiler_params=pltpu.CompilerParams(vmem_limit_bytes=60*2**20),name="qkv_proj",
        cost_estimate=pl.CostEstimate(flops=2*F*D*3*D,bytes_accessed=14*2**20,transcendentals=0))(x,seg,emb,w,b,cos,sin)


def sizes(nd,ns):
    Y=2**((ns.bit_length()-1)//2)
    return nd//2,Y,ns//Y

class Place:
    def __init__(self,nd,ns):
        self.nd,self.ns=nd,ns
        self.X,self.Y,self.Z=sizes(nd,ns)
        self.h=lax.axis_index("head"); self.s=lax.axis_index("seq")
        self.x,self.c=self.h//2,self.h%2
        self.z,self.y=self.s//self.Y,self.s%self.Y
    def at(self,x=None,c=None,z=None,y=None):
        x=self.x if x is None else x; c=self.c if c is None else c
        z=self.z if z is None else z; y=self.y if y is None else y
        return (x*2+c,z*self.Y+y)

def near_first(n):
    out=[]
    for d in range(1,n//2+1):
        out.append(d)
        if n-d!=d: out.append(n-d)
    return out

def remote(src,dst,ss,rs,dev):
    cp=pltpu.make_async_remote_copy(src_ref=src,dst_ref=dst,send_sem=ss,recv_sem=rs,device_id=dev,device_id_type=pl.DeviceIdType.MESH)
    cp.start()
    return cp

def greet_all(p):
    b=pltpu.get_barrier_semaphore()
    @pl.loop(0,p.nd)
    def _(dh):
        @pl.loop(0,p.ns)
        def _(ds):
            @pl.when(dh+ds>0)
            def _():
                pl.semaphore_signal(b,inc=1,device_id=(lax.rem(p.h+dh,p.nd),lax.rem(p.s+ds,p.ns)),device_id_type=pl.DeviceIdType.MESH)
    pl.semaphore_wait(b,p.nd*p.ns-1)

class Gather:
    @staticmethod
    def sems(nd,ns):
        X,Y,Z=sizes(nd,ns)
        D=pltpu.SemaphoreType.DMA
        one=[D((Z,)),D((Z,X)),D((Z,Y)),D((Z,X,Y)),D((Z,X,Y)),D((Z,)),D((2,Z,X,Y))]
        return one+one+[D(())]
    def __init__(self,p,shard,out,sems):
        self.p,self.shard,self.out=p,shard,out
        self.ss,self.rs,self.ls=sems[:7],sems[7:14],sems[14]
        self.all=[]; self.half=shard.shape[-1]//2
        self.two={}; self.three={}
    def send(self,k,idx,src,dst,dev):
        cp=remote(src,dst,self.ss[k].at[idx],self.rs[k].at[idx],dev)
        self.all.append(cp); return cp
    def cols(self,part): return pl.ds(part*self.half,self.half)
    def loc(self,x,z,y,part=None):
        r=self.out.at[x,self.p.c,z,y]
        return r if part is None else r.at[:,self.cols(part)]
    def start(self):
        p=self.p
        self.zc={}
        for dz in near_first(p.Z):
            self.zc[dz]=self.send(0,(dz,),self.shard,self.loc(p.x,p.z,p.y),p.at(z=lax.rem(p.z+dz,p.Z)))
        self.local=pltpu.make_async_copy(self.shard,self.loc(p.x,p.z,p.y),self.ls)
        self.local.start()
        self.second(0)
    def second(self,dz):
        p=self.p; zz=lax.rem(p.z+p.Z-dz,p.Z)
        if dz: self.zc[dz].wait_recv()
        def src(part=None):
            if dz: return self.loc(p.x,zz,p.y,part)
            return self.shard if part is None else self.shard.at[:,self.cols(part)]
        for dx in near_first(p.X):
            self.two[0,dz,dx]=self.send(1,(dz,dx),src(0),self.loc(p.x,zz,p.y,0),p.at(x=lax.rem(p.x+dx,p.X)))
        for dy in near_first(p.Y):
            self.two[1,dz,dy]=self.send(2,(dz,dy),src(1),self.loc(p.x,zz,p.y,1),p.at(y=lax.rem(p.y+dy,p.Y)))
        self.send(5,(dz,),src(),self.loc(p.x,zz,p.y),p.at(c=1-p.c))
        for dy in near_first(p.Y):
            self.three[0,dz,0,dy]=self.send(3,(dz,0,dy),src(0),self.loc(p.x,zz,p.y,0),p.at(y=lax.rem(p.y+dy,p.Y)))
        for dx in near_first(p.X):
            self.three[1,dz,dx,0]=self.send(4,(dz,dx,0),src(1),self.loc(p.x,zz,p.y,1),p.at(x=lax.rem(p.x+dx,p.X)))
    def third(self,dz):
        p=self.p; zz=lax.rem(p.z+p.Z-dz,p.Z)
        for dx in near_first(p.X):
            self.two[0,dz,dx].wait_recv()
            l=self.loc(lax.rem(p.x+p.X-dx,p.X),zz,p.y,0)
            for dy in near_first(p.Y):
                self.three[0,dz,dx,dy]=self.send(3,(dz,dx,dy),l,l,p.at(y=lax.rem(p.y+dy,p.Y)))
            self.send(6,(0,dz,dx,0),l,l,p.at(c=1-p.c))
        for dy in near_first(p.Y):
            self.two[1,dz,dy].wait_recv()
            l=self.loc(p.x,zz,lax.rem(p.y+p.Y-dy,p.Y),1)
            for dx in near_first(p.X):
                self.three[1,dz,dx,dy]=self.send(4,(dz,dx,dy),l,l,p.at(x=lax.rem(p.x+dx,p.X)))
            self.send(6,(1,dz,0,dy),l,l,p.at(c=1-p.c))
    def fourth(self,dz):
        p=self.p; zz=lax.rem(p.z+p.Z-dz,p.Z)
        for part in (0,1):
            for dx in range(p.X):
                for dy in range(p.Y):
                    if (part,dz,dx,dy) not in self.three: continue
                    self.three[part,dz,dx,dy].wait_recv()
                    l=self.loc(lax.rem(p.x+p.X-dx,p.X),zz,lax.rem(p.y+p.Y-dy,p.Y),part)
                    self.send(6,(part,dz,dx,dy),l,l,p.at(c=1-p.c))
    def finish(self):
        waited=set()
        for cp in self.zc.values(): waited.add(id(cp))
        for d in (self.two,self.three):
            for cp in d.values(): waited.add(id(cp))
        for cp in self.all:
            if id(cp) not in waited: cp.wait_recv()
            cp.wait_send()
        self.local.wait()

def entry_kernel(nd,ns,nw,*refs):
    shards=refs[:nw]; bias,time,ids,wada=refs[nw:nw+4]
    outs=refs[nw+4:2*nw+4]; bias_all,ids_all,emb,act=refs[2*nw+4:2*nw+8]
    time_all,part,r1,r2,bs,br,isd,ir,ts,tr,e1s,e1r,e2s,e2r=refs[2*nw+8:2*nw+22]
    gs=refs[2*nw+22:]
    p=Place(nd,ns); n=len(Gather.sems(nd,ns))
    greet_all(p)
    tail=[]
    first=[]
    for ds in range(1,ns):
        first.append(remote(time,time_all.at[p.s],ts.at[ds],tr.at[ds],(p.h,lax.rem(p.s+ds,ns))))
    g=[Gather(p,shards[i],outs[i],gs[i*n:(i+1)*n]) for i in range(nw)]
    for a in g: a.start()
    me=p.h*ns+p.s
    for dh in range(1,nd):
        tail.append(remote(ids,ids_all.at[p.h],isd.at[dh],ir.at[dh],(lax.rem(p.h+dh,nd),p.s)))
    @pl.loop(0,nd)
    def _(dh):
        @pl.loop(0,ns)
        def _(ds):
            @pl.when(dh+ds>0)
            def _():
                remote(bias,bias_all.at[me],bs.at[dh,ds],br.at[dh,ds],(lax.rem(p.h+dh,nd),lax.rem(p.s+ds,ns)))
    l1=pltpu.make_async_copy(bias,bias_all.at[me],bs.at[0,0]); l1.start()
    l2=pltpu.make_async_copy(ids,ids_all.at[p.h],isd.at[0]); l2.start()
    time_all[p.s]=time[...]
    for cp in first: cp.wait()
    D=time.shape[1]; K=wada.shape[0]; E=wada.shape[1]//8
    v=time_all[...].reshape(ns*8,D)
    low=(v/(1.0+jnp.exp(-v))).astype(bf)
    kk=D//(nd*ns)
    row=lax.broadcasted_iota(jnp.int32,(D,128),0); col=lax.broadcasted_iota(jnp.int32,(D,128),1)
    pickm=jnp.where((row==me*kk+col)&(col<kk),1.0,0.0).astype(bf)
    own=dot(low,pickm).astype(bf)
    act[...]=own
    for j in range(8):
        pj=dot(own[:,:K],wada[:,j*E:(j+1)*E])
        for s in range(ns):
            part[s,2*j:2*j+2,:]=pj[8*s:8*s+2,:]
    one=[remote(part.at[lax.rem(p.s+ds,ns)],r1.at[ds],e1s.at[ds],e1r.at[ds],(p.h,lax.rem(p.s+ds,ns))) for ds in range(1,ns)]
    order=[0]+near_first(p.Z)
    for a in g:
        for i,dz in enumerate(order):
            if dz: a.second(dz)
            if i: a.third(order[i-1])
        a.third(order[-1])
    tot=part[p.s]
    for ds in range(1,ns):
        one[ds-1].wait()
        tot=tot+r1[ds]
    r2[p.h]=tot
    two=[remote(r2.at[p.h],r2.at[p.h],e2s.at[dh],e2r.at[dh],(lax.rem(p.h+dh,nd),p.s)) for dh in range(1,nd)]
    for a in g:
        for dz in order: a.fourth(dz)
    for cp in two: cp.wait()
    tot=r2[0]
    for i in range(1,nd): tot=tot+r2[i]
    emb[...]=tot
    for a in g: a.finish()
    for cp in tail: cp.wait()
    l1.wait(); l2.wait()
    @pl.loop(0,nd)
    def _(dh):
        @pl.loop(0,ns)
        def _(ds):
            @pl.when(dh+ds>0)
            def _():
                pltpu.make_async_remote_copy(src_ref=bias,dst_ref=bias_all.at[me],send_sem=bs.at[dh,ds],recv_sem=br.at[dh,ds],device_id=(lax.rem(p.h+dh,nd),lax.rem(p.s+ds,ns)),device_id_type=pl.DeviceIdType.MESH).wait()

def entry(nd,ns,shards,bias,time,ids,wada):
    X,Y,Z=sizes(nd,ns)
    S=jax.ShapeDtypeStruct
    D=pltpu.SemaphoreType.DMA
    nw=len(shards); E=wada.shape[1]//8
    outs=[S((X,2,Z,Y)+a.shape,a.dtype) for a in shards]+[S((nd*ns,)+bias.shape,bias.dtype),S((nd,)+ids.shape,ids.dtype),S((16,E),f32),S((ns*8,128),bf)]
    scr=[pltpu.VMEM((ns,8,time.shape[1]),f32),pltpu.VMEM((ns,16,E),f32),pltpu.VMEM((ns,16,E),f32),pltpu.VMEM((nd,16,E),f32),
         D((nd,ns)),D((nd,ns)),D((nd,)),D((nd,)),D((ns,)),D((ns,)),D((ns,)),D((ns,)),D((nd,)),D((nd,))]
    for _ in shards: scr+=Gather.sems(nd,ns)
    return pl.pallas_call(functools.partial(entry_kernel,nd,ns,nw),out_shape=tuple(outs),
        in_specs=[ANY]*(nw+1)+[V,ANY,V],out_specs=tuple([ANY]*(nw+2)+[V,V]),scratch_shapes=scr,
        compiler_params=pltpu.CompilerParams(collective_id=0,has_side_effects=True,vmem_limit_bytes=40*2**20),name="entry")(*shards,bias,time,ids,wada)

def make_remote(src,dst,ss,rs,dev):
    return pltpu.make_async_remote_copy(src_ref=src,dst_ref=dst,send_sem=ss,recv_sem=rs,device_id=dev,device_id_type=pl.DeviceIdType.MESH)

def mid_kernel(o_ref,x_ref,c_ref,seg_ref,msk_ref,emb_ref,w_ref,bo_ref,bu_ref,bd_ref,
               out_ref,dm_ref,do_ref,gu_ref,gw_ref,gb_ref,ge_ref,
               wo_ref,wu_ref,wd_ref,n2s,acts,dhs,dfs,dps,dgelu,a_ref,da_ref,sem,s1,s2,s3,t1,t2,t3,*,R,nd,ns):
    F,D=x_ref.shape; H=bu_ref.shape[1]; CH=512
    loads=[pltpu.make_async_copy(w_ref.at[:,pl.ds(o,n)],r,sem.at[i]) for i,(o,n,r) in enumerate(((2*H,D,wo_ref),(0,H,wu_ref),(H,H,wd_ref)))]
    p=Place(nd,ns); W=D//nd; NR=F//R
    b=pltpu.get_barrier_semaphore()
    for d in range(1,nd): pl.semaphore_signal(b,inc=1,device_id=(lax.rem(p.h+d,nd),p.s),device_id_type=pl.DeviceIdType.MESH)
    pl.semaphore_wait(b,nd-1)
    def rows(i): return pl.ds(pl.multiple_of(i*R,R),R)
    def cols(h): return pl.ds(pl.multiple_of(h*W,W),W)
    def arrive(i):
        return [make_remote(o_ref.at[lax.rem(p.h+d,nd),rows(i)],a_ref.at[rows(i),cols(p.h)],s1.at[i,d],s2.at[i,d],(lax.rem(p.h+d,nd),p.s)) for d in range(1,nd)]
    def kept(i): return pltpu.make_async_copy(o_ref.at[p.h,rows(i)],a_ref.at[rows(i),cols(p.h)],s3.at[i])
    def leave(i):
        return [make_remote(da_ref.at[rows(i),cols(lax.rem(p.h+d,nd))],do_ref.at[p.h,rows(i)],t1.at[i,d],t2.at[i,d],(lax.rem(p.h+d,nd),p.s)) for d in range(1,nd)]
    def stays(i): return pltpu.make_async_copy(da_ref.at[rows(i),cols(p.h)],do_ref.at[p.h,rows(i)],t3.at[i])
    for c in arrive(0)+[kept(0)]: c.start()
    for l in loads: l.start()
    gb_ref[...]=jnp.zeros_like(gb_ref); ge_ref[...]=jnp.zeros_like(ge_ref)
    for l in loads: l.wait()
    def down(j):
        t,o=divmod(j*CH,D)
        return slice(o,o+CH),slice(t*D,(t+1)*D)
    @pl.loop(0,F//R)
    def _(i):
        r=rows(i)
        for c in arrive(i): c.wait_recv()
        kept(i).wait()
        @pl.when(i+1<NR)
        def _():
            for c in arrive(i+1)+[kept(i+1)]: c.start()
        seg=seg_ref[r,:]; msk=msk_ref[r,:]
        def acc(k,x):
            a,b=sums(x,seg)
            ge_ref[0:1,k*D:(k+1)*D]+=a; ge_ref[1:2,k*D:(k+1)*D]+=b
        branch=(dot(a_ref[r,:],wo_ref[...])+bo_ref[0:1,:])*msk
        g1=pick(seg,emb_ref,2,D)
        middle=x_ref[r,:].astype(f32)+g1*branch
        n,rs=moments(middle)
        sc2=1.0+pick(seg,emb_ref,4,D)
        n2=(n*sc2+pick(seg,emb_ref,3,D)).astype(bf)
        n2s[r,:]=n2
        feed=jnp.broadcast_to(bd_ref[0:1,:],(R,D))
        for j in range(H//CH):
            c=slice(j*CH,(j+1)*CH)
            h=dot(n2,wu_ref[:,c])+bu_ref[0:1,c]
            a,g=gelu_both(h)
            a=a.astype(bf)
            acts[r,c]=a; dgelu[:,c]=g
            feed+=dot(a,wd_ref[down(j)])
        up=c_ref[r,:].astype(f32)
        g2=pick(seg,emb_ref,5,D)
        out_ref[r,:]=(middle+g2*feed).astype(bf)
        df=(up*g2).astype(bf)
        dfs[r,:]=df
        acc(3,up*feed)
        gb_ref[2:3,0:D]+=jnp.sum(df.astype(f32),0,keepdims=True)
        dn=jnp.zeros((R,D),f32)
        for j in range(H//CH):
            c=slice(j*CH,(j+1)*CH)
            dh=(dot(df,wd_ref[down(j)],NT)*dgelu[:,c]).astype(bf)
            dhs[r,c]=dh
            gb_ref[1:2,c]+=jnp.sum(dh.astype(f32),0,keepdims=True)
            dn+=dot(dh,wu_ref[:,c],NT)
        acc(1,dn); acc(2,dn*n)
        dn=dn*sc2
        dmid=up+(dn-jnp.mean(dn,-1,keepdims=True)-n*jnp.mean(dn*n,-1,keepdims=True))*rs
        dm_ref[r,:]=dmid
        acc(0,dmid*branch)
        dp=(dmid*g1*msk).astype(bf)
        dps[r,:]=dp
        gb_ref[0:1,0:D]+=jnp.sum(dp.astype(f32),0,keepdims=True)
        da_ref[r,:]=dot(dp,wo_ref[...],NT).astype(bf)
        for c in leave(i)+[stays(i)]: c.start()
    @pl.loop(0,D//256)
    def _(i):
        c=pl.ds(pl.multiple_of(i*256,256),256)
        gw_ref[c,H:H+D]=dot(a_ref[:,c],dps[...],TN).astype(bf)
        gu_ref[c,:]=dot(n2s[:,c],dhs[...],TN).astype(bf)
        for t in range(H//D):
            e=pl.ds(pl.multiple_of(t*D+i*256,256),256)
            gw_ref[c,t*D:(t+1)*D]=dot(acts[:,e],dfs[...],TN).astype(bf)
    for i in range(NR):
        for c in arrive(i): c.wait_send()
        for c in leave(i)+[stays(i)]: c.wait()

def mid(nd,ns,o,x,c,seg,msk,emb,w,bo,bu,bd,R=256):
    F,D=x.shape; H=bu.shape[1]; NR=F//R; A=pltpu.SemaphoreType.DMA
    S=jax.ShapeDtypeStruct; M=pltpu.VMEM
    return pl.pallas_call(functools.partial(mid_kernel,R=R,nd=nd,ns=ns),
        out_shape=(S((F,D),bf),S((F,D),f32),S((nd,F,D//nd),bf),S((D,H),bf),S((D,H+D),bf),S((8,H),f32),S((8,4*D),f32)),
        in_specs=[ANY]+[V]*5+[ANY]+[V]*3,out_specs=(V,V,ANY)+(V,)*4,
        scratch_shapes=[M((D,D),bf),M((D,H),bf),M((D,H),bf),M((F,D),bf),M((F,H),bf),M((F,H),bf),M((F,D),bf),M((F,D),bf),M((R,H),f32),M((F,D),bf),M((F,D),bf),A((3,)),A((NR,nd)),A((NR,nd)),A((NR,)),A((NR,nd)),A((NR,nd)),A((NR,))],
        compiler_params=pltpu.CompilerParams(collective_id=2,has_side_effects=True,vmem_limit_bytes=62*2**20),name="mid",
        cost_estimate=pl.CostEstimate(flops=6*F*D*(D+2*H),bytes_accessed=30*2**20,transcendentals=F*H))(o,x,c,seg,msk,emb,w,bo,bu,bd)


ORD_X=-1
QW=512
class Reduce:
    def __init__(self,p,parts,scr,own=None,src=None,col=0):
        self.p,self.parts,self.src=p,parts,src
        it=iter(scr)
        self.own=own if own is not None else next(it)
        self.c=p.c if own is not None else 0
        self.w=self.own.shape[-1]; self.cs=pl.ds(col,self.w)
        self.cin=next(it); self.c1,self.c2,self.ls=next(it),next(it),next(it)
        self.bufs=[[(next(it),next(it),next(it)) for _ in o] for _,_,o in parts]
        self.sent=[]; self.stage=0
    @staticmethod
    def scratch(nd,ns,k,w,dt,parts,own):
        X,Y,Z=sizes(nd,ns); M=pltpu.VMEM; D=pltpu.SemaphoreType.DMA; n={"x":X,"y":Y,"z":Z}
        out=[] if own else [M((X,1,Z,Y,k,w),dt)]
        out+=[M((X,Z,Y,k,w),dt),D((X,)),D((X,)),D((X,))]
        for lo,hi,order in parts:
            for i,a in enumerate(order):
                left=tuple(n[b] for b in "xzy" if b in order[i+1:])
                out+=[M((max(n[a]-1,1),)+left+(k,hi-lo),dt),D((n[a],)),D((n[a],))]
        return out
    def start(self):
        p=self.p; self.l=[]; self.cc=[]
        for x in range(p.X):
            s=self.own.at[x,1-p.c] if self.src is None else self.src.at[x,1-p.c,:,:,:,self.cs]
            self.cc.append(remote(s,self.cin.at[x],self.c1.at[x],self.c2.at[x],p.at(c=1-p.c)))
            if self.src is not None:
                l=pltpu.make_async_copy(self.src.at[x,p.c,:,:,:,self.cs],self.own.at[x,0],self.ls.at[x]); l.start(); self.l.append(l)
        self.sent+=self.cc
    def place(self,order,i,v):
        p=self.p; mine={"x":p.x,"y":p.y,"z":p.z}
        ix={b:(mine[b] if b in order[:i] else v if b==order[i] else slice(None)) for b in "xyz"}
        return (ix["x"],self.c,ix["z"],ix["y"])
    def add(self,i,x,cols):
        i=i+(slice(None),slice(*cols))
        self.own[i]=(self.own[i].astype(f32)+x.astype(f32)).astype(self.own.dtype)
    def send(self,part,i):
        p=self.p; lo,hi,order=self.parts[part]; a=order[i]
        n={"x":p.X,"y":p.Y,"z":p.Z}[a]; me={"x":p.x,"y":p.y,"z":p.z}[a]
        buf,s1,s2=self.bufs[part][i]; out=[]
        for d in near_first(n):
            v=lax.rem(me+d,n)
            out.append((d,remote(self.own.at[self.place(order,i,v)+(slice(None),pl.ds(lo,hi-lo))],buf.at[d-1],s1.at[d],s2.at[d],p.at(**{a:v}))))
        self.sent+=[c for _,c in out]
        return out
    def step(self):
        p=self.p; st=self.stage; self.stage+=1
        if st==0:
            for x in range(p.X):
                if self.src is not None: self.l[x].wait()
                self.cc[x].wait_recv()
                @pl.loop(0,p.Z)
                def _(z):
                    for y in range(p.Y): self.add((x,self.c,z,y),self.cin[x,z,y],(0,self.w))
            self.go=[self.send(k,0) for k in range(len(self.parts))]
            return
        go=[]
        for k,(lo,hi,order) in enumerate(self.parts):
            buf=self.bufs[k][st-1][0]; left=[b for b in "xzy" if b in order[st:]]
            n={"x":p.X,"y":p.Y,"z":p.Z}; mine={"x":p.x,"y":p.y,"z":p.z}
            for d,c in self.go[k]:
                c.wait_recv()
                def one(at,d=d):
                    ix={**mine,**at}
                    self.add((ix["x"],self.c,ix["z"],ix["y"]),buf[(d-1,)+tuple(at[b] for b in left)],(lo,hi))
                if len(left)==2:
                    @pl.loop(0,n[left[0]])
                    def _(u):
                        for v in range(n[left[1]]): one({left[0]:u,left[1]:v})
                else:
                    @pl.loop(0,n[left[0]])
                    def _(u): one({left[0]:u})
            go.append(self.send(k,st))
        self.go=go
    def last(self,out,col=0):
        p=self.p
        for k,(lo,hi,order) in enumerate(self.parts):
            buf=self.bufs[k][2][0]
            t=self.own[p.x,self.c,p.z,p.y,:,lo:hi].astype(f32)
            for d,c in self.go[k]:
                c.wait_recv()
                t=t+buf[d-1].astype(f32)
            out[:,col+lo:col+hi]=t
    def finish(self):
        for c in self.sent: c.wait_send()

def greet(p):
    b=pltpu.get_barrier_semaphore()
    for d in range(1,p.nd): pl.semaphore_signal(b,inc=1,device_id=(lax.rem(p.h+d,p.nd),p.s),device_id_type=pl.DeviceIdType.MESH)
    for d in range(1,p.ns): pl.semaphore_signal(b,inc=1,device_id=(p.h,lax.rem(p.s+d,p.ns)),device_id_type=pl.DeviceIdType.MESH)
    pl.semaphore_wait(b,p.nd+p.ns-2)

def along_head(p,f): return [f(d,lax.rem(p.h+d,p.nd),(lax.rem(p.h+d,p.nd),p.s)) for d in range(1,p.nd)]
def along_seq(p,f): return [f(d,lax.rem(p.s+d,p.ns),(p.h,lax.rem(p.s+d,p.ns))) for d in range(1,p.ns)]

REST=(lambda w,j:((0,w,"xyz"),) if j==ORD_X else ((0,w,"yzx"),)); QKV=(lambda w:((0,w//2,"yxz"),(w//2,w,"xyz")))

def final_kernel(nd,ns,R,refs,scr):
    (g_ref,rest_ref,x_hbm,n1_hbm,dm_hbm,wq_hbm,cos_ref,sin_ref,seg_ref,emb_ref,gbm_ref,gem_ref,act,wada)=refs[:14]
    (gf_ref,rest_out,qkv_out,bias_all,gada,gbada,dact)=refs[14:]
    (g,x_ref,n1_ref,dm_ref,w_ref,dps,gw,gbv,gev,bsc,bout,hsum,demb,dscr)=scr[:14]
    (gs,gr,gl,ld,hs,hr,qs,qr,ds_,dr,bs,br)=scr[14:26]
    pools=scr[26:]
    p=Place(nd,ns); me=p.h*ns+p.s
    F,D=x_ref.shape; W=D//nd; E=D*6//8; K=wada.shape[0]; H=gbm_ref.shape[1]; NR=F//R
    nr=H//D; nq=3*D//QW
    greet(p)
    loads=[pltpu.make_async_copy(a,b,ld.at[i]) for i,(a,b) in enumerate(((x_hbm,x_ref),(wq_hbm,w_ref),(dm_hbm,dm_ref),(n1_hbm,n1_ref)))]
    sends=[]; own=[]
    def chunk(i):
        r=pl.ds(i*R,R)
        sends.append([remote(g_ref.at[lax.rem(p.h+d,nd),r],g.at[p.h,r],gs.at[i,d],gr.at[i,d],(lax.rem(p.h+d,nd),p.s)) for d in range(1,nd)])
    for i in range(NR):
        r=pl.ds(i*R,R)
        c=pltpu.make_async_copy(g_ref.at[p.h,r],g.at[p.h,r],gl.at[i]); c.start(); own.append(c)
    for i in range(min(2,NR)): chunk(i)
    for l in loads: l.start()
    it=iter(pools)
    take=lambda n: [next(it) for _ in range(n)]
    rest=[]
    for j in range(nr):
        rest.append(Reduce(p,REST(D,j),take(len(Reduce.scratch(nd,ns,K,D,bf,REST(D,j),False))),src=rest_ref,col=j*D))
        rest[-1].start()
    qkv=[Reduce(p,QKV(QW),take(len(Reduce.scratch(nd,ns,K,QW,bf,QKV(QW),True))),own=gw.at[j]) for j in range(nq)]
    bias=Reduce(p,QKV(256),take(len(Reduce.scratch(nd,ns,8,256,f32,QKV(256),True))),own=bsc)
    gbv[...]=jnp.zeros_like(gbv); gev[...]=jnp.zeros_like(gev); bsc[...]=jnp.zeros_like(bsc)
    for a in rest[:2]: a.step()
    for l in loads: l.wait()
    def turn(i):
        for c in sends[i]: c.wait_recv()
        own[i].wait()
        if i+2<NR: chunk(i+2)
        r=slice(i*R,(i+1)*R)
        cos=jnp.concatenate([cos_ref[r,:]]*(W//128),1); sin=jnp.concatenate([sin_ref[r,:]]*(W//128),1)
        @pl.loop(0,nd)
        def _(d):
            for j in range(3):
                c=pl.ds(pl.multiple_of((d*3+j)*W,W),W)
                v=g[d,r,j*W:(j+1)*W]
                if j<2:
                    v=v.astype(f32)
                    v=(v*cos-partner(v)*sin).astype(bf)
                dps[r,c]=v
                gbv[0:1,c]+=jnp.sum(v.astype(f32),0,keepdims=True)
    def norm(lo,hi):
        @pl.loop(lo,hi)
        def _(i):
            r=pl.ds(pl.multiple_of(i*R,R),R)
            seg=seg_ref[r,:]
            dn=jnp.zeros((R,D),f32)
            for j in range(3*D//512):
                dn+=dot(dps[r,j*512:(j+1)*512],w_ref[:,j*512:(j+1)*512],NT)
            n,rs=moments(x_ref[r,:].astype(f32))
            for k,x in ((0,dn),(1,dn*n)):
                a,b=sums(x,seg)
                gev[0:1,k*D:(k+1)*D]+=a; gev[1:2,k*D:(k+1)*D]+=b
            dn=dn*(1.0+pick(seg,emb_ref,1,D))
            gf_ref[r,:]=dm_ref[r,:]+(dn-jnp.mean(dn,-1,keepdims=True)-n*jnp.mean(dn*n,-1,keepdims=True))*rs
    def weight(j):
        B=D//nd
        for h in range(nd):
            v=dot(n1_ref[:,h*B:(h+1)*B],dps[:,j*QW:(j+1)*QW],TN).astype(bf)
            gw[j,h//2,h%2]=v.reshape(p.Z,p.Y,K,QW)
        qkv[j].start()
    steps=[a.step for _ in range(2) for a in rest]
    for i in range(NR):
        turn(i)
        if i:
            for f in steps[(i-1)*len(steps)//(NR-1):i*len(steps)//(NR-1)]: f()
    for j in range(nq):
        weight(j)
        if j: qkv[j-1].step()
    vec=jnp.concatenate([gbv[0:1,:],gbm_ref[0:1,0:D],gbm_ref[1:2,:],gbm_ref[2:3,0:D]],1)
    for q in range(vec.shape[1]//256):
        h,s=divmod(q,ns)
        bsc[h//2,h%2,s//p.Y,s%p.Y,0:1,:]=vec[:,q*256:(q+1)*256]
    bias.start()
    qkv[nq-1].step()
    norm(0,NR//2)
    bias.step()
    qkv[0].step()
    qkv[1].step()
    norm(NR//2,NR)
    gev[0:2,2*D:]=gem_ref[0:2,:]
    for j in range(8):
        for t in range(2): hsum[p.h,2*j+t:2*j+t+1,:]=gev[t:t+1,j*E:(j+1)*E]
    hc=[remote(hsum.at[p.h],hsum.at[p.h],hs.at[d],hr.at[d],(lax.rem(p.h+d,nd),p.s)) for d in range(1,nd)]
    qkv[0].step(); qkv[2].step(); qkv[1].step(); bias.step()
    for c in hc: c.wait()
    tot=hsum[0]
    for i in range(1,nd): tot=tot+hsum[i]
    demb[p.s]=tot.astype(bf)
    qc=[remote(demb.at[p.s],demb.at[p.s],qs.at[d],qr.at[d],(p.h,lax.rem(p.s+d,ns))) for d in range(1,ns)]
    qkv[3].step(); qkv[2].step(); bias.step()
    for j,a in enumerate(rest): a.last(rest_out,j*D)
    bias.last(bout)
    bias_all[p.h,p.s]=bout[...]
    bc=along_head(p,lambda d,h,dev: remote(bout,bias_all.at[p.h,p.s],bs.at[0,d],br.at[0,d],dev))
    qkv[4].step(); qkv[3].step()
    for c in qc: c.wait()
    Q=ns*16
    flat=demb[...].reshape(Q,E)
    r0=lax.broadcasted_iota(jnp.int32,(Q,ns*8),0); c0=lax.broadcasted_iota(jnp.int32,(Q,ns*8),1)
    spread=dot(jnp.where((r0//16==c0//8)&(r0%2==c0%8),1.0,0.0).astype(bf),act[...])
    rr=lax.broadcasted_iota(jnp.int32,(Q,128),0)%16//2
    rk=lax.broadcasted_iota(jnp.int32,(Q,K),0)%16//2
    tot=jnp.zeros((Q,K),f32)
    for j in range(8):
        m=jnp.where(rr==j,spread,0.0).astype(bf)
        gada[:,j*E:(j+1)*E]=dot(m,flat,TN)[:K,:]
        tot=jnp.where(rk==j,dot(flat,wada[:,j*E:(j+1)*E],NT),tot)
    dscr[...]=jnp.concatenate([tot,jnp.zeros((Q,128-K),f32)],1).reshape(ns,16,128)
    dact[p.h,p.s]=dscr[p.s]
    dc=along_seq(p,lambda d,s,dev: remote(dscr.at[s],dact.at[p.h,p.s],ds_.at[0,d],dr.at[0,d],dev))
    for c in bc: c.wait()
    bc=along_seq(p,lambda d,s,dev: remote(bias_all.at[:,p.s],bias_all.at[:,p.s],bs.at[1,d],br.at[1,d],dev))
    r8=lax.broadcasted_iota(jnp.int32,(8,Q),0); c8=lax.broadcasted_iota(jnp.int32,(8,Q),1)
    gbada[...]=dot(jnp.where(c8%16//2==r8,1.0,0.0).astype(bf),flat)
    qkv[5].step(); qkv[4].step()
    for c in dc: c.wait()
    dc=along_head(p,lambda d,h,dev: remote(dact.at[p.h],dact.at[p.h],ds_.at[1,d],dr.at[1,d],dev))
    for j in range(nq-1): qkv[j].last(qkv_out,j*QW)
    qkv[5].step()
    qkv[nq-1].last(qkv_out,(nq-1)*QW)
    for a in rest+qkv+[bias]: a.finish()
    for i in range(NR):
        for c in sends[i]: c.wait_send()
    for c in bc+dc: c.wait()

def final(nd,ns,dqkv,rest,x,n1,dm,wq,cos,sin,seg,emb,gb,ge,act,wada,R=128):
    F,D=x.shape; K,E6=wada.shape; E=E6//8; H=gb.shape[1]; N=nd*ns; W=D//nd; NR=F//R
    X,Y,Z=sizes(nd,ns)
    S=jax.ShapeDtypeStruct; M=pltpu.VMEM; A=pltpu.SemaphoreType.DMA
    outs=[S((F,D),f32),S((K,H),f32),S((K,3*D),f32),S((nd,ns,8,256),f32),S((K,E6),f32),S((8,E),f32),S((nd,ns,16,128),f32)]
    scr=[M((nd,F,3*W),bf),M((F,D),bf),M((F,D),bf),M((F,D),f32),M((D,3*D),bf),M((F,3*D),bf),M((3*D//QW,X,2,Z,Y,K,QW),bf),M((8,3*D),f32),M((8,E6),f32),
         M((X,2,Z,Y,8,256),f32),M((8,256),f32),M((nd,16,E),f32),M((ns,16,E),bf),M((ns,16,128),f32),
         A((NR,nd)),A((NR,nd)),A((NR,)),A((4,)),A((nd,)),A((nd,)),A((ns,)),A((ns,)),A((2,max(nd,ns))),A((2,max(nd,ns))),A((2,max(nd,ns))),A((2,max(nd,ns)))]
    for j in range(H//D): scr+=Reduce.scratch(nd,ns,K,D,bf,REST(D,j),False)
    for _ in range(3*D//QW): scr+=Reduce.scratch(nd,ns,K,QW,bf,QKV(QW),True)
    scr+=Reduce.scratch(nd,ns,8,256,f32,QKV(256),True)
    def k(*refs): final_kernel(nd,ns,R,refs[:14+len(outs)],refs[14+len(outs):])
    return pl.pallas_call(k,out_shape=tuple(outs),in_specs=[ANY]*6+[V]*8,out_specs=(V,)*len(outs),scratch_shapes=scr,
        compiler_params=pltpu.CompilerParams(collective_id=1,has_side_effects=True,vmem_limit_bytes=63*2**20),name="final")(
        dqkv,rest,x,n1,dm,wq,cos,sin,seg,emb,gb,ge,act,wada)


def body(frames,time_embed,segment_ids,frame_mask,positions,w_ada,b_ada,w_qkv,b_qkv,w_out,b_out,w_up,b_up,w_down,b_down,cotangent):
    _,F,D=frames.shape
    nd=lax.axis_size("head"); ns=lax.axis_size("seq"); dev=lax.axis_index("head")*ns+lax.axis_index("seq")
    X,Y,Z=sizes(nd,ns); N=nd*ns
    W=D//nd
    E=b_ada.shape[0]; E6=w_ada.shape[1]; K=w_ada.shape[0]; H=w_up.shape[1]; nt=H//D
    x=frames[0]; cot=cotangent[0]
    def reorder(w): return w.reshape(-1,3,nd,W).transpose(0,2,1,3).reshape(-1,3*D)
    def restore(w): return w.reshape(-1,nd,3,W).transpose(0,2,1,3).reshape(-1,3*D)
    def hide(w): return w.reshape(-1,N,nt,K).transpose(0,2,1,3).reshape(-1,H)
    def unhide(w): return w.reshape(-1,nt,N,K).transpose(0,2,1,3).reshape(-1,H)
    rest=jnp.concatenate([hide(w_up),w_down.reshape(nt,K,D).transpose(1,0,2).reshape(K,H),w_out],axis=1)
    bs=(b_qkv,b_out,b_up,b_down,b_ada); ends=[0]
    for b in bs: ends.append(ends[-1]+b.shape[0])
    wide=-(-ends[-1]//256)*256
    bias=jnp.zeros((16,wide),bf).at[0,:ends[-1]].set(jnp.concatenate(bs))
    time8=jnp.zeros((8,D),f32).at[:2].set(time_embed[0].astype(f32))
    ids=jnp.zeros((8,F),jnp.int32).at[0].set(segment_ids[0]).at[1].set(frame_mask[0])
    wq,bias_all,ids_all,emb,act=entry(nd,ns,[reorder(w_qkv)],bias,time8,ids,w_ada)
    rest_all=lax.all_gather(rest,HS,axis=0,tiled=True)
    wq=wq.reshape(D,3*D)
    bias_all=bias_all[:,0,:].astype(f32)
    bq,bo,bu,bd,ba=[bias_all[:,ends[i]:ends[i+1]].reshape(1,-1) for i in range(5)]
    bq=reorder(bq); bu=hide(bu)
    emb=emb.reshape(8,2,-1).transpose(1,0,2).reshape(2,E6)+ba
    seg_row=ids_all[:,0,:].reshape(-1); msk_row=ids_all[:,1,:].reshape(-1)
    column=lax.iota(jnp.int32,128)
    pair=(column%HD//2).astype(f32)
    angles=positions[0].astype(f32)[:,None]*(10000.0**(-(2.0*pair)/HD))
    cos=jnp.cos(angles); sin=jnp.where(column%2==0,-jnp.sin(angles),jnp.sin(angles))
    segc=segment_ids[0][:,None]; mskc=frame_mask[0].astype(f32)[:,None]
    normed,packed=qkv_proj(x,segc,emb,wq,bq,cos,sin,nd)
    qkv=lax.all_to_all(packed,"head",split_axis=0,concat_axis=0,tiled=True).reshape(nd*F,3*W)
    T=512
    qlo,qhi,klo,khi=tables(seg_row,msk_row,T)
    aq,ak=aux(seg_row,msk_row)
    o,lse=attn_fwd(qkv,qlo,qhi,aq,ak,T)
    out,dmid,do,gup,gdo,gb,ge=mid(nd,ns,o.reshape(nd,F,W),x,cot,segc,mskc,emb,rest_all,bo,bu,bd)
    do=do.reshape(nd*F,W)
    gdo=lax.psum_scatter(gdo,HS,scatter_dimension=0,tiled=True).astype(f32)
    dqkv=attn_bwd(qkv,o,do,lse,klo,khi,aq,ak,T)
    gx,gup,gqkv,gbias,gada,gbada,dact=final(nd,ns,dqkv.reshape(nd,F,3*W),gup.reshape(X,2,Z,Y,K,H),x,normed,dmid,wq,cos,sin,segc,emb,gb,ge,act,w_ada)
    dact=dact[:,:,:,:K].reshape(N,8,2,K).sum(1).transpose(1,0,2).reshape(2,D)
    _,pull=jax.vjp(jax.nn.silu,time_embed[0].astype(f32))
    gtime=pull(dact)[0][None]
    gbada=lax.dynamic_slice_in_dim(gbada.reshape(-1),dev*E,E,0)
    gbias=gbias[:,:,0,:].reshape(-1)
    gbs=[]; at=0
    for k,order in ((3*D,restore),(D,None),(H,unhide),(D,None)):
        v=gbias[at:at+k]; at+=k
        if order: v=order(v[None])[0]
        gbs.append(lax.dynamic_slice_in_dim(v,dev*(k//N),k//N,0))
    gdown=gdo[:,:H].reshape(K,nt,D).transpose(1,0,2).reshape(nt*K,D)
    return (out[None],gx[None],gtime,gada,gbada,restore(gqkv),gbs[0],gdo[:,H:],gbs[1],unhide(gup),gbs[2],gdown,gbs[3])


def solution(mesh):
    row=P("seq","head",None); ids=P("seq","head"); mat=P(HS,None); vec=P(HS); tim=P("seq",None,None)
    in_specs=(row,tim,ids,ids,ids)+(mat,vec)*5+(row,)
    out_specs=(row,row,tim)+(mat,vec)*5
    return jax.shard_map(body,mesh=mesh,in_specs=in_specs,out_specs=out_specs,check_vma=False)
```

```python
import functools
import math

import jax
import jax.numpy as jnp
import numpy as np
from jax import lax
from jax.experimental import pallas as pl
from jax.experimental.pallas import tpu as pltpu
from jax.sharding import PartitionSpec as P

bf = jnp.bfloat16
f32 = jnp.float32
HS = ("head", "seq")
ANY = pl.BlockSpec(memory_space=pl.ANY)
V = pl.BlockSpec(memory_space=pltpu.VMEM)
NN = (((1,), (0,)), ((), ()))
NT = (((1,), (1,)), ((), ()))
TN = (((0,), (0,)), ((), ()))


def dot(a, b, dims=NN):
    return lax.dot_general(a, b, dims, preferred_element_type=f32)


HD=64
LOG2E=math.log2(math.e)
NEG=-1e30

def only(x,h):
    lane=lax.broadcasted_iota(jnp.int32,x.shape,1)
    return jnp.where((lane<HD) if h%2==0 else (lane>=HD),x,jnp.zeros_like(x))

def fwd_kernel(lo_ref,hi_ref,qkv_ref,auxq_ref,auxk_ref,o_ref,lse_ref,qs,s_scr,m_scr,acc,*,T,nh):
    qt=pl.program_id(0)
    W=nh*HD
    lane=lax.broadcasted_iota(jnp.int32,(T,128),1)
    lo=lo_ref[qt]; hi=hi_ref[qt]
    rq=pl.ds(pl.multiple_of(qt*T,T),T)
    def key(kt,h): return qkv_ref[pl.ds(pl.multiple_of(kt*T,T),T),W+h//2*128:W+(h//2+1)*128]
    def value(kt,h): return qkv_ref[pl.ds(pl.multiple_of(kt*T,T),T),2*W+h//2*128:2*W+(h//2+1)*128]
    for h in range(nh):
        qs[h]=only(qkv_ref[rq,h//2*128:(h//2+1)*128],h)*jnp.asarray(HD**-0.5,bf)
    auxq=auxq_ref[rq,:]
    eye=lax.broadcasted_iota(jnp.int32,(T,T),0)==lax.broadcasted_iota(jnp.int32,(T,T),1)
    def mx(s):
        m=s[:,:128]
        for j in range(1,T//128): m=jnp.maximum(m,s[:,j*128:(j+1)*128])
        return m
    ak=auxk_ref[rq,:]
    for h in range(nh):
        raw=dot(qs[h],key(qt,h),NT)
        s=dot(jnp.concatenate([qs[h],auxq],axis=1),jnp.concatenate([key(qt,h),ak],axis=1),NT)
        s=jnp.where(eye,raw,s)
        s_scr[h,qt]=s
        m_scr[h]=mx(s)
    @pl.loop(lo,hi-1)
    def _(t):
        kt=jnp.where(t>=qt,t+1,t)
        ak=auxk_ref[pl.ds(pl.multiple_of(kt*T,T),T),:]
        for h in range(nh):
            s=dot(jnp.concatenate([qs[h],auxq],axis=1),jnp.concatenate([key(kt,h),ak],axis=1),NT)
            s_scr[h,kt]=s
            m_scr[h]=jnp.maximum(m_scr[h],mx(s))
    for h in range(nh):
        m_scr[h]=jnp.broadcast_to(jnp.max(m_scr[h],axis=1,keepdims=True),(T,128))
        acc[h]=jnp.zeros((T,256),f32)
    ones=jnp.ones((T,128),bf)
    @pl.loop(lo,hi)
    def _(kt):
        for h in range(nh):
            s=s_scr[h,kt]; m=m_scr[h]
            p=jnp.exp2((s-jnp.concatenate([m]*(T//128),axis=1))*LOG2E).astype(bf)
            acc[h]+=dot(p,jnp.concatenate([value(kt,h),ones],axis=1))
    lse=jnp.zeros((T,128),f32)
    for g in range(nh//2):
        o=[]
        for h in (2*g,2*g+1):
            l=acc[h,:,128:]
            o.append(acc[h,:,:128]/l)
            lse=jnp.where(lane==h,m_scr[h]+jnp.log(l),lse)
        o_ref[:,g*128:(g+1)*128]=jnp.where(lane<HD,o[0],o[1]).astype(bf)
    lse_ref[...]=lse

def attn_fwd(qkv,lo,hi,auxq,auxk,T):
    L,W3=qkv.shape; W=W3//3; nh=W//HD; nk=L//T
    return pl.pallas_call(
        functools.partial(fwd_kernel,T=T,nh=nh),
        out_shape=(jax.ShapeDtypeStruct((L,W),bf),jax.ShapeDtypeStruct((L,128),f32)),
        grid_spec=pltpu.PrefetchScalarGridSpec(num_scalar_prefetch=2,grid=(nk,),
            in_specs=[pl.BlockSpec((L,W3),lambda i,*_:(0,0)),pl.BlockSpec((L,128),lambda i,*_:(0,0)),pl.BlockSpec((L,128),lambda i,*_:(0,0))],
            out_specs=[pl.BlockSpec((T,W),lambda i,*_:(i,0)),pl.BlockSpec((T,128),lambda i,*_:(i,0))],
            scratch_shapes=[pltpu.VMEM((nh,T,128),bf),pltpu.VMEM((nh,nk,T,T),f32),pltpu.VMEM((nh,T,128),f32),pltpu.VMEM((nh,T,256),f32)]),
        compiler_params=pltpu.CompilerParams(vmem_limit_bytes=60*2**20),
        name="attn_fwd",cost_estimate=pl.CostEstimate(flops=16*nh*L*L*HD,bytes_accessed=4*2**20,transcendentals=nh*L*L),
    )(lo,hi,qkv,auxq,auxk)

def bwd_kernel(lo_ref,hi_ref,qkv_ref,o_ref,do_ref,lse_ref,auxq_ref,auxk_ref,dqkv_ref,qs,qa,dos,dd,kT,dqT,dk,dv,*,T,nh):
    kt=pl.program_id(0)
    W=nh*HD
    L=qkv_ref.shape[0]
    nk=L//T
    lane=lax.broadcasted_iota(jnp.int32,(T,128),1)
    def pair(ref,t,h,at=0): return ref[pl.ds(pl.multiple_of(t*T,T),T),at+h//2*128:at+(h//2+1)*128]
    @pl.when(kt==0)
    def _():
        dqT[...]=jnp.zeros_like(dqT)
        @pl.loop(0,nk)
        def _(t):
            r=pl.ds(pl.multiple_of(t*T,T),T)
            lse=lse_ref[r,:]
            aq=auxq_ref[r,:].astype(f32)
            kT[t]=qkv_ref[r,W:2*W].T
            for h in range(nh):
                qs[h,t]=only(pair(qkv_ref,t,h),h)*jnp.asarray(HD**-0.5,bf)
                nl=-lse[:,h:h+1]
                l1=nl.astype(bf).astype(f32); l2=(nl-l1).astype(bf).astype(f32); l3=nl-l1-l2
                qa[h,t]=jnp.where(lane==0,l1,jnp.where(lane==1,l2,jnp.where(lane==2,l3,aq))).astype(bf)
                do=only(pair(do_ref,t,h),h)
                dos[h,t]=do
                nd=-jnp.sum(do.astype(f32)*pair(o_ref,t,h).astype(f32),axis=1,keepdims=True)
                d1=nd.astype(bf).astype(f32); d2=nd-d1
                dd[h,t]=jnp.where(lane==0,d1,jnp.where(lane==1,d2,0.0)).astype(bf)
    r=pl.ds(pl.multiple_of(kt*T,T),T)
    ak=auxk_ref[r,:]
    av=jnp.where(lane<2,1.0,0.0).astype(bf)
    lo=lo_ref[kt]; hi=hi_ref[kt]
    def tile(qt,diag):
        for h in range(nh):
            kx=jnp.concatenate([pair(qkv_ref,kt,h,W),ak],axis=1)
            s=dot(kx,jnp.concatenate([qs[h,qt],qa[h,qt]],axis=1),NT)
            if diag:
                eye=lax.broadcasted_iota(jnp.int32,(T,T),0)==lax.broadcasted_iota(jnp.int32,(T,T),1)
                qr=jnp.where(lane<3,qa[h,qt].astype(f32),0.0).astype(bf)
                raw=dot(kx,jnp.concatenate([qs[h,qt],qr],axis=1),NT)
                s=jnp.where(eye,raw,s)
            p=jnp.exp2(s*LOG2E)
            dp=dot(jnp.concatenate([pair(qkv_ref,kt,h,2*W),av],axis=1),jnp.concatenate([dos[h,qt],dd[h,qt]],axis=1),NT)
            ds=(p*dp).astype(bf)
            dv[h]+=dot(p.astype(bf),pair(do_ref,qt,h))
            dk[h]+=dot(ds,pair(qkv_ref,qt,h))
            dqT[qt,h*HD:(h+1)*HD,:]+=dot(kT[kt,h*HD:(h+1)*HD,:],ds)
    dk[...]=jnp.zeros_like(dk); dv[...]=jnp.zeros_like(dv)
    tile(kt,True)
    @pl.loop(lo,hi-1)
    def _(t):
        tile(jnp.where(t>=kt,t+1,t),False)
    for g in range(nh//2):
        dqkv_ref[r,W+g*128:W+(g+1)*128]=(jnp.where(lane<HD,dk[2*g],dk[2*g+1])*HD**-0.5).astype(bf)
        dqkv_ref[r,2*W+g*128:2*W+(g+1)*128]=jnp.where(lane<HD,dv[2*g],dv[2*g+1]).astype(bf)
    @pl.when(kt==nk-1)
    def _():
        @pl.loop(0,nk)
        def _(t):
            dqkv_ref[pl.ds(pl.multiple_of(t*T,T),T),0:W]=(dqT[t].T*HD**-0.5).astype(bf)

def attn_bwd(qkv,o,do,lse,lo,hi,auxq,auxk,T):
    L,W3=qkv.shape; W=W3//3; nh=W//HD; nk=L//T
    full=lambda w: pl.BlockSpec((L,w),lambda i,*_:(0,0))
    return pl.pallas_call(
        functools.partial(bwd_kernel,T=T,nh=nh),
        out_shape=jax.ShapeDtypeStruct((L,W3),bf),
        grid_spec=pltpu.PrefetchScalarGridSpec(num_scalar_prefetch=2,grid=(nk,),
            in_specs=[full(W3),full(W),full(W),full(128),full(128),full(128)],
            out_specs=full(W3),
            scratch_shapes=[pltpu.VMEM((nh,nk,T,128),bf)]*4+[pltpu.VMEM((nk,W,T),bf),pltpu.VMEM((nk,W,T),f32),
                pltpu.VMEM((nh,T,128),f32),pltpu.VMEM((nh,T,128),f32)]),
        compiler_params=pltpu.CompilerParams(vmem_limit_bytes=60*2**20),
        name="attn_bwd",cost_estimate=pl.CostEstimate(flops=40*nh*L*L*HD,bytes_accessed=8*2**20,transcendentals=nh*L*L),
    )(lo,hi,qkv,o,do,lse,auxq,auxk)

def tables(seg,mask,T):
    L=seg.shape[0]; nk=L//T
    s=seg.reshape(nk,T); m=mask.reshape(nk,T)
    has=jnp.stack([jnp.any(s==c,axis=1) for c in (0,1)],1)
    real=jnp.stack([jnp.any((s==c)&(m==1),axis=1) for c in (0,1)],1)
    use=jnp.any(has[:,None,:]&real[None,:,:],axis=2)|jnp.eye(nk,dtype=bool)
    idx=jnp.arange(nk,dtype=jnp.int32)
    qlo=jnp.min(jnp.where(use,idx[None,:],nk),axis=1); qhi=jnp.max(jnp.where(use,idx[None,:],-1),axis=1)+1
    klo=jnp.min(jnp.where(use,idx[:,None],nk),axis=0); khi=jnp.max(jnp.where(use,idx[:,None],-1),axis=0)+1
    return [a.astype(jnp.int32) for a in (qlo,qhi,klo,khi)]
def aux(seg,mask):
    L=seg.shape[0]
    lane=lax.broadcasted_iota(jnp.int32,(L,128),1)
    sg=seg[:,None]; pad=(mask==0)[:,None]
    aq=jnp.where(lane==3,jnp.where(sg!=0,NEG,0.),jnp.where(lane==4,jnp.where(sg!=1,NEG,0.),jnp.where(lane==5,NEG,0.))).astype(bf)
    ak=jnp.where(lane<3,1.,jnp.where(lane==3,(sg==0).astype(f32),jnp.where(lane==4,(sg==1).astype(f32),jnp.where(lane==5,pad.astype(f32),0.)))).astype(bf)
    return aq,ak

EPS=1e-6

def moments(x):
    c=jnp.mean(x,-1,keepdims=True)
    xc=x-c
    rs=lax.rsqrt(jnp.mean(xc*xc,-1,keepdims=True)+EPS)
    return xc*rs, rs
def pick(seg,emb,i,D):
    return jnp.where(seg==0,emb[0:1,i*D:(i+1)*D],emb[1:2,i*D:(i+1)*D])
def sums(x,seg):
    a=jnp.sum(jnp.where(seg==0,x,0.0),0,keepdims=True); b=jnp.sum(jnp.where(seg==1,x,0.0),0,keepdims=True)
    return a,b
def partner(v):
    w=v.shape[1]
    lane=lax.broadcasted_iota(jnp.int32,v.shape,1)
    return jnp.where(lane%2==0,pltpu.roll(v,w-1,1),pltpu.roll(v,1,1))
def gelu_both(v):
    c=math.sqrt(2/math.pi)
    v2=v*v
    t=jnp.tanh(c*v*(1.0+0.044715*v2))
    h=0.5*(1.0+t)
    return v*h, h+0.5*v*(1.0-t*t)*(c*(1.0+3*0.044715*v2))

def qkv_kernel(x_ref,seg_ref,emb_ref,w_ref,b_ref,cos_ref,sin_ref,n_ref,*p_refs,R,nd):
    F,D=x_ref.shape
    @pl.loop(0,F//R)
    def _(i):
        r=pl.ds(pl.multiple_of(i*R,R),R)
        seg=seg_ref[r,:]
        n,_=moments(x_ref[r,:].astype(f32))
        n_ref[r,:]=(n*(1.0+pick(seg,emb_ref,1,D))+pick(seg,emb_ref,0,D)).astype(bf)
    for q,p_ref in enumerate(p_refs):
        @pl.loop(0,F//R)
        def _(i):
            r=pl.ds(pl.multiple_of(i*R,R),R)
            cos=cos_ref[r,:]; sin=sin_ref[r,:]
            for d in range(0,nd,2):
                c=(q*nd+d)*384
                v=dot(n_ref[r,:],w_ref[:,c:c+768])+b_ref[0:1,c:c+768]
                for k in range(6):
                    a=v[:,k*128:(k+1)*128]
                    if k%3<2: a=a*cos+partner(a)*sin
                    p_ref[d+k//3,r,k%3*128:(k%3+1)*128]=a.astype(bf)

def qkv_proj(x,seg,emb,w,b,cos,sin,nd,R=256):
    F,D=x.shape; PP=D//nd//128
    return pl.pallas_call(functools.partial(qkv_kernel,R=R,nd=nd),
        out_shape=(jax.ShapeDtypeStruct((F,D),bf),)+(jax.ShapeDtypeStruct((nd,F,384),bf),)*PP,
        in_specs=[V]*7,out_specs=(V,)*(1+PP),
        compiler_params=pltpu.CompilerParams(vmem_limit_bytes=40*2**20),name="qkv_proj",
        cost_estimate=pl.CostEstimate(flops=2*F*D*3*D,bytes_accessed=14*2**20,transcendentals=0))(x,seg,emb,w,b,cos,sin)


def sizes(nd,ns):
    Y=2**((ns.bit_length()-1)//2)
    return nd//2,Y,ns//Y

class Place:
    def __init__(self,nd,ns):
        self.nd,self.ns=nd,ns
        self.X,self.Y,self.Z=sizes(nd,ns)
        self.h=lax.axis_index("head"); self.s=lax.axis_index("seq")
        self.x,self.c=self.h//2,self.h%2
        self.z,self.y=self.s//self.Y,self.s%self.Y
    def at(self,x=None,c=None,z=None,y=None):
        x=self.x if x is None else x; c=self.c if c is None else c
        z=self.z if z is None else z; y=self.y if y is None else y
        return (x*2+c,z*self.Y+y)

def near_first(n):
    out=[]
    for d in range(1,n//2+1):
        out.append(d)
        if n-d!=d: out.append(n-d)
    return out

def remote(src,dst,ss,rs,dev):
    cp=pltpu.make_async_remote_copy(src_ref=src,dst_ref=dst,send_sem=ss,recv_sem=rs,device_id=dev,device_id_type=pl.DeviceIdType.MESH)
    cp.start()
    return cp

def greet(p):
    b=pltpu.get_barrier_semaphore()
    for d in range(1,p.nd): pl.semaphore_signal(b,inc=1,device_id=(lax.rem(p.h+d,p.nd),p.s),device_id_type=pl.DeviceIdType.MESH)
    for d in range(1,p.ns): pl.semaphore_signal(b,inc=1,device_id=(p.h,lax.rem(p.s+d,p.ns)),device_id_type=pl.DeviceIdType.MESH)
    pl.semaphore_wait(b,p.nd+p.ns-2)

def along_head(p,f): return [f(d,lax.rem(p.h+d,p.nd),(lax.rem(p.h+d,p.nd),p.s)) for d in range(1,p.nd)]
def along_seq(p,f): return [f(d,lax.rem(p.s+d,p.ns),(p.h,lax.rem(p.s+d,p.ns))) for d in range(1,p.ns)]

class Gather:
    @staticmethod
    def sems(nd,ns):
        X,Y,Z=sizes(nd,ns)
        D=pltpu.SemaphoreType.DMA
        one=[D((Z,)),D((Z,X)),D((Z,Y)),D((Z,X,Y)),D((Z,X,Y)),D((Z,)),D((2,Z,X,Y))]
        return one+one+[D(())]
    def __init__(self,p,shard,out,sems):
        self.p,self.shard,self.out=p,shard,out
        self.ss,self.rs,self.ls=sems[:7],sems[7:14],sems[14]
        self.all=[]; self.half=shard.shape[-1]//2
        self.two={}; self.three={}
    def send(self,k,idx,src,dst,dev):
        cp=remote(src,dst,self.ss[k].at[idx],self.rs[k].at[idx],dev)
        self.all.append(cp); return cp
    def cols(self,part): return pl.ds(part*self.half,self.half)
    def loc(self,x,z,y,part=None):
        r=self.out.at[x,self.p.c,z,y]
        return r if part is None else r.at[:,self.cols(part)]
    def start(self):
        p=self.p
        self.zc={}
        for dz in near_first(p.Z):
            self.zc[dz]=self.send(0,(dz,),self.shard,self.loc(p.x,p.z,p.y),p.at(z=lax.rem(p.z+dz,p.Z)))
        self.local=pltpu.make_async_copy(self.shard,self.loc(p.x,p.z,p.y),self.ls)
        self.local.start()
        self.second(0)
    def second(self,dz):
        p=self.p; zz=lax.rem(p.z+p.Z-dz,p.Z)
        if dz: self.zc[dz].wait_recv()
        def src(part=None):
            if dz: return self.loc(p.x,zz,p.y,part)
            return self.shard if part is None else self.shard.at[:,self.cols(part)]
        for dx in near_first(p.X):
            self.two[0,dz,dx]=self.send(1,(dz,dx),src(0),self.loc(p.x,zz,p.y,0),p.at(x=lax.rem(p.x+dx,p.X)))
        for dy in near_first(p.Y):
            self.two[1,dz,dy]=self.send(2,(dz,dy),src(1),self.loc(p.x,zz,p.y,1),p.at(y=lax.rem(p.y+dy,p.Y)))
        self.send(5,(dz,),src(),self.loc(p.x,zz,p.y),p.at(c=1-p.c))
        for dy in near_first(p.Y):
            self.three[0,dz,0,dy]=self.send(3,(dz,0,dy),src(0),self.loc(p.x,zz,p.y,0),p.at(y=lax.rem(p.y+dy,p.Y)))
        for dx in near_first(p.X):
            self.three[1,dz,dx,0]=self.send(4,(dz,dx,0),src(1),self.loc(p.x,zz,p.y,1),p.at(x=lax.rem(p.x+dx,p.X)))
    def third(self,dz):
        p=self.p; zz=lax.rem(p.z+p.Z-dz,p.Z)
        for dx in near_first(p.X):
            self.two[0,dz,dx].wait_recv()
            l=self.loc(lax.rem(p.x+p.X-dx,p.X),zz,p.y,0)
            for dy in near_first(p.Y):
                self.three[0,dz,dx,dy]=self.send(3,(dz,dx,dy),l,l,p.at(y=lax.rem(p.y+dy,p.Y)))
            self.send(6,(0,dz,dx,0),l,l,p.at(c=1-p.c))
        for dy in near_first(p.Y):
            self.two[1,dz,dy].wait_recv()
            l=self.loc(p.x,zz,lax.rem(p.y+p.Y-dy,p.Y),1)
            for dx in near_first(p.X):
                self.three[1,dz,dx,dy]=self.send(4,(dz,dx,dy),l,l,p.at(x=lax.rem(p.x+dx,p.X)))
            self.send(6,(1,dz,0,dy),l,l,p.at(c=1-p.c))
    def fourth(self,dz):
        p=self.p; zz=lax.rem(p.z+p.Z-dz,p.Z)
        for part in (0,1):
            for dx in range(p.X):
                for dy in range(p.Y):
                    if (part,dz,dx,dy) not in self.three: continue
                    self.three[part,dz,dx,dy].wait_recv()
                    l=self.loc(lax.rem(p.x+p.X-dx,p.X),zz,lax.rem(p.y+p.Y-dy,p.Y),part)
                    self.send(6,(part,dz,dx,dy),l,l,p.at(c=1-p.c))
    def finish(self):
        waited=set()
        for cp in self.zc.values(): waited.add(id(cp))
        for d in (self.two,self.three):
            for cp in d.values(): waited.add(id(cp))
        for cp in self.all:
            if id(cp) not in waited: cp.wait_recv()
            cp.wait_send()
        self.local.wait()

def entry_kernel(nd,ns,nw,*refs):
    shards=refs[:nw]; bias,time,ids,wada=refs[nw:nw+4]
    outs=refs[nw+4:2*nw+4]; bias_all,ids_all,emb,act=refs[2*nw+4:2*nw+8]
    time_all,part,r1,r2,bs,br,isd,ir,ts,tr,e1s,e1r,e2s,e2r=refs[2*nw+8:2*nw+22]
    gs=refs[2*nw+22:]
    p=Place(nd,ns); n=len(Gather.sems(nd,ns))
    greet(p)
    tail=[]
    first=[]
    for ds in range(1,ns):
        first.append(remote(time,time_all.at[p.s],ts.at[ds],tr.at[ds],(p.h,lax.rem(p.s+ds,ns))))
    g=[Gather(p,shards[i],outs[i],gs[i*n:(i+1)*n]) for i in range(nw)]
    for a in g: a.start()
    me=p.h*ns+p.s
    for dh in range(1,nd):
        tail.append(remote(ids,ids_all.at[p.h],isd.at[dh],ir.at[dh],(lax.rem(p.h+dh,nd),p.s)))
    bc=along_head(p,lambda d,h,dev: remote(bias,bias_all.at[p.h,p.s],bs.at[0,d],br.at[0,d],dev))
    l1=pltpu.make_async_copy(bias,bias_all.at[p.h,p.s],bs.at[0,0]); l1.start()
    l2=pltpu.make_async_copy(ids,ids_all.at[p.h],isd.at[0]); l2.start()
    time_all[p.s]=time[...]
    for cp in first: cp.wait()
    D=time.shape[1]; K=wada.shape[0]; E=wada.shape[1]//8
    v=time_all[...].reshape(ns*8,D)
    low=(v/(1.0+jnp.exp(-v))).astype(bf)
    kk=D//(nd*ns)
    row=lax.broadcasted_iota(jnp.int32,(D,128),0); col=lax.broadcasted_iota(jnp.int32,(D,128),1)
    pickm=jnp.where((row==me*kk+col)&(col<kk),1.0,0.0).astype(bf)
    own=dot(low,pickm).astype(bf)
    act[...]=own
    for j in range(8):
        pj=dot(own[:,:K],wada[:,j*E:(j+1)*E])
        for s in range(ns):
            part[s,2*j:2*j+2,:]=pj[8*s:8*s+2,:]
    one=[remote(part.at[lax.rem(p.s+ds,ns)],r1.at[ds],e1s.at[ds],e1r.at[ds],(p.h,lax.rem(p.s+ds,ns))) for ds in range(1,ns)]
    l1.wait()
    for cp in bc: cp.wait()
    tail+=along_seq(p,lambda d,s,dev: remote(bias_all.at[:,p.s],bias_all.at[:,p.s],bs.at[1,d],br.at[1,d],dev))
    order=[0]+near_first(p.Z)
    for a in g:
        for i,dz in enumerate(order):
            if dz: a.second(dz)
            if i: a.third(order[i-1])
        a.third(order[-1])
    tot=part[p.s]
    for ds in range(1,ns):
        one[ds-1].wait()
        tot=tot+r1[ds]
    r2[p.h]=tot
    two=[remote(r2.at[p.h],r2.at[p.h],e2s.at[dh],e2r.at[dh],(lax.rem(p.h+dh,nd),p.s)) for dh in range(1,nd)]
    for a in g:
        for dz in order: a.fourth(dz)
    for cp in two: cp.wait()
    tot=r2[0]
    for i in range(1,nd): tot=tot+r2[i]
    emb[...]=tot
    for a in g: a.finish()
    for cp in tail: cp.wait()
    l2.wait()

def entry(nd,ns,shards,bias,time,ids,wada):
    X,Y,Z=sizes(nd,ns)
    S=jax.ShapeDtypeStruct
    D=pltpu.SemaphoreType.DMA
    nw=len(shards); E=wada.shape[1]//8
    outs=[S((X,2,Z,Y)+a.shape,a.dtype) for a in shards]+[S((nd,ns)+bias.shape,bias.dtype),S((nd,)+ids.shape,ids.dtype),S((16,E),f32),S((ns*8,128),bf)]
    scr=[pltpu.VMEM((ns,8,time.shape[1]),f32),pltpu.VMEM((ns,16,E),f32),pltpu.VMEM((ns,16,E),f32),pltpu.VMEM((nd,16,E),f32),
         D((2,max(nd,ns))),D((2,max(nd,ns))),D((nd,)),D((nd,)),D((ns,)),D((ns,)),D((ns,)),D((ns,)),D((nd,)),D((nd,))]
    for _ in shards: scr+=Gather.sems(nd,ns)
    return pl.pallas_call(functools.partial(entry_kernel,nd,ns,nw),out_shape=tuple(outs),
        in_specs=[ANY]*(nw+1)+[V,ANY,V],out_specs=tuple([ANY]*(nw+2)+[V,V]),scratch_shapes=scr,
        compiler_params=pltpu.CompilerParams(collective_id=0,has_side_effects=True,vmem_limit_bytes=40*2**20),name="entry")(*shards,bias,time,ids,wada)

def make_remote(src,dst,ss,rs,dev):
    return pltpu.make_async_remote_copy(src_ref=src,dst_ref=dst,send_sem=ss,recv_sem=rs,device_id=dev,device_id_type=pl.DeviceIdType.MESH)

def mid_kernel(PP,*refs,R,nd,ns):
    mid_body(refs[:PP],refs[PP+9:2*PP+9],*refs[PP:PP+9],*refs[2*PP+9:],R=R,nd=nd,ns=ns)

def mid_body(o_refs,do_refs,x_ref,c_ref,seg_ref,msk_ref,emb_ref,w_ref,bo_ref,bu_ref,bd_ref,
               out_ref,dm_ref,gu_ref,gw_ref,gb_ref,ge_ref,
               wo_ref,wu_ref,wd_ref,n2s,acts,dhs,dfs,dps,dgelu,a_ref,da_ref,sem,s1,s2,s3,t1,t2,t3,*,R,nd,ns):
    F,D=x_ref.shape; H=bu_ref.shape[1]; CH=512
    loads=[pltpu.make_async_copy(w_ref.at[:,pl.ds(o,n)],r,sem.at[i]) for i,(o,n,r) in enumerate(((2*H,D,wo_ref),(0,H,wu_ref),(H,H,wd_ref)))]
    p=Place(nd,ns); W=D//nd; NR=F//R
    b=pltpu.get_barrier_semaphore()
    for d in range(1,nd): pl.semaphore_signal(b,inc=1,device_id=(lax.rem(p.h+d,nd),p.s),device_id_type=pl.DeviceIdType.MESH)
    pl.semaphore_wait(b,nd-1)
    def rows(i): return pl.ds(pl.multiple_of(i*R,R),R)
    def cols(h,q): return pl.ds(pl.multiple_of(h*W+q*128,128),128)
    def arrive(i):
        return [make_remote(o.at[lax.rem(p.h+d,nd),rows(i)],a_ref.at[rows(i),cols(p.h,q)],s1.at[i,d,q],s2.at[i,d,q],(lax.rem(p.h+d,nd),p.s)) for d in range(1,nd) for q,o in enumerate(o_refs)]
    def kept(i): return [pltpu.make_async_copy(o.at[p.h,rows(i)],a_ref.at[rows(i),cols(p.h,q)],s3.at[i,q]) for q,o in enumerate(o_refs)]
    def leave(i):
        return [make_remote(da_ref.at[rows(i),cols(lax.rem(p.h+d,nd),q)],o.at[p.h,rows(i)],t1.at[i,d,q],t2.at[i,d,q],(lax.rem(p.h+d,nd),p.s)) for q,o in enumerate(do_refs) for d in range(1,nd)]
    def stays(i): return [pltpu.make_async_copy(da_ref.at[rows(i),cols(p.h,q)],o.at[p.h,rows(i)],t3.at[i,q]) for q,o in enumerate(do_refs)]
    for c in arrive(0)+kept(0): c.start()
    for l in loads: l.start()
    gb_ref[...]=jnp.zeros_like(gb_ref); ge_ref[...]=jnp.zeros_like(ge_ref)
    for l in loads: l.wait()
    def down(j):
        t,o=divmod(j*CH,D)
        return slice(o,o+CH),slice(t*D,(t+1)*D)
    @pl.loop(0,F//R)
    def _(i):
        r=rows(i)
        for c in arrive(i): c.wait_recv()
        for c in kept(i): c.wait()
        @pl.when(i+1<NR)
        def _():
            for c in arrive(i+1)+kept(i+1): c.start()
        seg=seg_ref[r,:]; msk=msk_ref[r,:]
        def acc(k,x):
            a,b=sums(x,seg)
            ge_ref[0:1,k*D:(k+1)*D]+=a; ge_ref[1:2,k*D:(k+1)*D]+=b
        branch=(dot(a_ref[r,:],wo_ref[...])+bo_ref[0:1,:])*msk
        g1=pick(seg,emb_ref,2,D)
        middle=x_ref[r,:].astype(f32)+g1*branch
        n,rs=moments(middle)
        sc2=1.0+pick(seg,emb_ref,4,D)
        n2=(n*sc2+pick(seg,emb_ref,3,D)).astype(bf)
        n2s[r,:]=n2
        feed=jnp.broadcast_to(bd_ref[0:1,:],(R,D))
        for j in range(H//CH):
            c=slice(j*CH,(j+1)*CH)
            h=dot(n2,wu_ref[:,c])+bu_ref[0:1,c]
            a,g=gelu_both(h)
            a=a.astype(bf)
            acts[r,c]=a; dgelu[:,c]=g
            feed+=dot(a,wd_ref[down(j)])
        up=c_ref[r,:].astype(f32)
        g2=pick(seg,emb_ref,5,D)
        out_ref[r,:]=(middle+g2*feed).astype(bf)
        df=(up*g2).astype(bf)
        dfs[r,:]=df
        acc(3,up*feed)
        gb_ref[2:3,0:D]+=jnp.sum(df.astype(f32),0,keepdims=True)
        dn=jnp.zeros((R,D),f32)
        for j in range(H//CH):
            c=slice(j*CH,(j+1)*CH)
            dh=(dot(df,wd_ref[down(j)],NT)*dgelu[:,c]).astype(bf)
            dhs[r,c]=dh
            gb_ref[1:2,c]+=jnp.sum(dh.astype(f32),0,keepdims=True)
            dn+=dot(dh,wu_ref[:,c],NT)
        acc(1,dn); acc(2,dn*n)
        dn=dn*sc2
        dmid=up+(dn-jnp.mean(dn,-1,keepdims=True)-n*jnp.mean(dn*n,-1,keepdims=True))*rs
        dm_ref[r,:]=dmid
        acc(0,dmid*branch)
        dp=(dmid*g1*msk).astype(bf)
        dps[r,:]=dp
        gb_ref[0:1,0:D]+=jnp.sum(dp.astype(f32),0,keepdims=True)
        da_ref[r,:]=dot(dp,wo_ref[...],NT).astype(bf)
        for c in leave(i)+stays(i): c.start()
    @pl.loop(0,D//256)
    def _(i):
        c=pl.ds(pl.multiple_of(i*256,256),256)
        gw_ref[c,H:H+D]=dot(a_ref[:,c],dps[...],TN).astype(bf)
        gu_ref[c,:]=dot(n2s[:,c],dhs[...],TN).astype(bf)
        for t in range(H//D):
            e=pl.ds(pl.multiple_of(t*D+i*256,256),256)
            gw_ref[c,t*D:(t+1)*D]=dot(acts[:,e],dfs[...],TN).astype(bf)
    for i in range(NR):
        for c in arrive(i): c.wait_send()
        for c in leave(i)+stays(i): c.wait()

def mid(nd,ns,os,x,c,seg,msk,emb,w,bo,bu,bd,R=256):
    F,D=x.shape; H=bu.shape[1]; NR=F//R; PP=len(os); A=pltpu.SemaphoreType.DMA
    S=jax.ShapeDtypeStruct; M=pltpu.VMEM
    return pl.pallas_call(functools.partial(mid_kernel,PP,R=R,nd=nd,ns=ns),
        out_shape=(S((nd,F,128),bf),)*PP+(S((F,D),bf),S((F,D),f32),S((D,H),bf),S((D,H+D),bf),S((8,H),f32),S((8,4*D),f32)),
        in_specs=[ANY]*PP+[V]*5+[ANY]+[V]*3,out_specs=(ANY,)*PP+(V,)*6,
        scratch_shapes=[M((D,D),bf),M((D,H),bf),M((D,H),bf),M((F,D),bf),M((F,H),bf),M((F,H),bf),M((F,D),bf),M((F,D),bf),M((R,H),f32),M((F,D),bf),M((F,D),bf),A((3,)),A((NR,nd,PP)),A((NR,nd,PP)),A((NR,PP)),A((NR,nd,PP)),A((NR,nd,PP)),A((NR,PP))],
        compiler_params=pltpu.CompilerParams(collective_id=2,has_side_effects=True,vmem_limit_bytes=62*2**20),name="mid",
        cost_estimate=pl.CostEstimate(flops=6*F*D*(D+2*H),bytes_accessed=30*2**20,transcendentals=F*H))(*os,x,c,seg,msk,emb,w,bo,bu,bd)


ORD_X=-1
QW=512
class Reduce:
    def __init__(self,p,parts,scr,own=None,src=None,col=0):
        self.p,self.parts,self.src=p,parts,src
        it=iter(scr)
        self.own=own if own is not None else next(it)
        self.c=p.c if own is not None else 0
        self.w=self.own.shape[-1]; self.cs=pl.ds(col,self.w)
        self.cin=next(it); self.c1,self.c2,self.ls=next(it),next(it),next(it)
        self.bufs=[[(next(it),next(it),next(it)) for _ in o] for _,_,o in parts]
        self.sent=[]; self.stage=0
    @staticmethod
    def scratch(nd,ns,k,w,dt,parts,own):
        X,Y,Z=sizes(nd,ns); M=pltpu.VMEM; D=pltpu.SemaphoreType.DMA; n={"x":X,"y":Y,"z":Z}
        out=[] if own else [M((X,1,Z,Y,k,w),dt)]
        out+=[M((X,Z,Y,k,w),dt),D((X,)),D((X,)),D((X,))]
        for lo,hi,order in parts:
            for i,a in enumerate(order):
                left=tuple(n[b] for b in "xzy" if b in order[i+1:])
                out+=[M((max(n[a]-1,1),)+left+(k,hi-lo),dt),D((n[a],)),D((n[a],))]
        return out
    def start(self):
        p=self.p; self.l=[]; self.cc=[]
        for x in range(p.X):
            s=self.own.at[x,1-p.c] if self.src is None else self.src.at[x,1-p.c,:,:,:,self.cs]
            self.cc.append(remote(s,self.cin.at[x],self.c1.at[x],self.c2.at[x],p.at(c=1-p.c)))
            if self.src is not None:
                l=pltpu.make_async_copy(self.src.at[x,p.c,:,:,:,self.cs],self.own.at[x,0],self.ls.at[x]); l.start(); self.l.append(l)
        self.sent+=self.cc
    def place(self,order,i,v):
        p=self.p; mine={"x":p.x,"y":p.y,"z":p.z}
        ix={b:(mine[b] if b in order[:i] else v if b==order[i] else slice(None)) for b in "xyz"}
        return (ix["x"],self.c,ix["z"],ix["y"])
    def add(self,i,x,cols):
        i=i+(slice(None),slice(*cols))
        self.own[i]=(self.own[i].astype(f32)+x.astype(f32)).astype(self.own.dtype)
    def send(self,part,i):
        p=self.p; lo,hi,order=self.parts[part]; a=order[i]
        n={"x":p.X,"y":p.Y,"z":p.Z}[a]; me={"x":p.x,"y":p.y,"z":p.z}[a]
        buf,s1,s2=self.bufs[part][i]; out=[]
        for d in near_first(n):
            v=lax.rem(me+d,n)
            out.append((d,remote(self.own.at[self.place(order,i,v)+(slice(None),pl.ds(lo,hi-lo))],buf.at[d-1],s1.at[d],s2.at[d],p.at(**{a:v}))))
        self.sent+=[c for _,c in out]
        return out
    def step(self):
        p=self.p; st=self.stage; self.stage+=1
        if st==0:
            for x in range(p.X):
                if self.src is not None: self.l[x].wait()
                self.cc[x].wait_recv()
                @pl.loop(0,p.Z)
                def _(z):
                    for y in range(p.Y): self.add((x,self.c,z,y),self.cin[x,z,y],(0,self.w))
            self.go=[self.send(k,0) for k in range(len(self.parts))]
            return
        go=[]
        for k,(lo,hi,order) in enumerate(self.parts):
            buf=self.bufs[k][st-1][0]; left=[b for b in "xzy" if b in order[st:]]
            n={"x":p.X,"y":p.Y,"z":p.Z}; mine={"x":p.x,"y":p.y,"z":p.z}
            for d,c in self.go[k]:
                c.wait_recv()
                def one(at,d=d):
                    ix={**mine,**at}
                    self.add((ix["x"],self.c,ix["z"],ix["y"]),buf[(d-1,)+tuple(at[b] for b in left)],(lo,hi))
                if len(left)==2:
                    @pl.loop(0,n[left[0]])
                    def _(u):
                        for v in range(n[left[1]]): one({left[0]:u,left[1]:v})
                else:
                    @pl.loop(0,n[left[0]])
                    def _(u): one({left[0]:u})
            go.append(self.send(k,st))
        self.go=go
    def last(self,out,col=0):
        p=self.p
        for k,(lo,hi,order) in enumerate(self.parts):
            buf=self.bufs[k][2][0]
            t=self.own[p.x,self.c,p.z,p.y,:,lo:hi].astype(f32)
            for d,c in self.go[k]:
                c.wait_recv()
                t=t+buf[d-1].astype(f32)
            out[:,col+lo:col+hi]=t
    def finish(self):
        for c in self.sent: c.wait_send()

REST=(lambda w,j:((0,w,"xyz"),) if j==ORD_X else ((0,w,"yzx"),)); QKV=(lambda w:((0,w//2,"yxz"),(w//2,w,"xyz")))

def final_kernel(nd,ns,R,here,refs,scr):
    (g_ref,rest_ref,x_hbm,n1_hbm,dm_hbm,wq_hbm,cos_ref,sin_ref,seg_ref,emb_ref,gbm_ref,gem_ref,act,wada)=refs[:14]
    (gf_ref,rest_out,qkv_out,bias_all,gada,gbada,dact)=refs[14:]
    (g,x_ref,n1_ref,dm_ref,w_ref,dps,gw,gbv,gev,bsc,bout,hsum,demb,dscr)=scr[:14]
    (gs,gr,gl,gh,ld,hs,hr,qs,qr,ds_,dr,bs,br)=scr[14:27]
    pools=scr[27:]
    p=Place(nd,ns); me=p.h*ns+p.s
    F,D=x_ref.shape; W=D//nd; E=D*6//8; K=wada.shape[0]; H=gbm_ref.shape[1]; NR=F//R
    nr=H//D; nq=3*D//QW; PP=W//128; C=3*D//PP; ne=nq//PP*(PP-1)
    come=[pltpu.make_async_copy(a,g.at[q],gh.at[q]) for q,a in enumerate(here)]
    for c in come: c.start()
    greet(p)
    loads=[pltpu.make_async_copy(a,b,ld.at[i]) for i,(a,b) in enumerate(((x_hbm,x_ref),(wq_hbm,w_ref),(dm_hbm,dm_ref),(n1_hbm,n1_ref)))]
    sends=[]; own=[]
    def chunk(i):
        r=pl.ds(i*R,R)
        sends.append([remote(g_ref.at[lax.rem(p.h+d,nd),r],g.at[PP-1,p.h,r],gs.at[i,d],gr.at[i,d],(lax.rem(p.h+d,nd),p.s)) for d in range(1,nd)])
    for i in range(NR):
        r=pl.ds(i*R,R)
        c=pltpu.make_async_copy(g_ref.at[p.h,r],g.at[PP-1,p.h,r],gl.at[i]); c.start(); own.append(c)
    for i in range(min(2,NR)): chunk(i)
    for l in loads: l.start()
    it=iter(pools)
    take=lambda n: [next(it) for _ in range(n)]
    rest=[]
    for j in range(nr):
        rest.append(Reduce(p,REST(D,j),take(len(Reduce.scratch(nd,ns,K,D,bf,REST(D,j),False))),src=rest_ref,col=j*D))
        rest[-1].start()
    qkv=[Reduce(p,QKV(QW),take(len(Reduce.scratch(nd,ns,K,QW,bf,QKV(QW),True))),own=gw.at[j]) for j in range(nq)]
    bias=Reduce(p,QKV(256),take(len(Reduce.scratch(nd,ns,8,256,f32,QKV(256),True))),own=bsc)
    gbv[...]=jnp.zeros_like(gbv); gev[...]=jnp.zeros_like(gev); bsc[...]=jnp.zeros_like(bsc)
    for a in rest[:2]: a.step()
    for l in loads: l.wait()
    def unturn(q,r):
        cos=cos_ref[r,:]; sin=sin_ref[r,:]
        @pl.loop(0,nd)
        def _(d):
            for j in range(3):
                c=pl.ds(pl.multiple_of(((q*nd+d)*3+j)*128,128),128)
                v=g[q,d,r,j*128:(j+1)*128]
                if j<2:
                    v=v.astype(f32)
                    v=(v*cos-partner(v)*sin).astype(bf)
                dps[r,c]=v
                gbv[0:1,c]+=jnp.sum(v.astype(f32),0,keepdims=True)
    def turn(i):
        for c in sends[i]: c.wait_recv()
        own[i].wait()
        if i+2<NR: chunk(i+2)
        r=slice(i*R,(i+1)*R)
        unturn(PP-1,r)
    def norm(lo,hi):
        @pl.loop(lo,hi)
        def _(i):
            r=pl.ds(pl.multiple_of(i*R,R),R)
            seg=seg_ref[r,:]
            dn=jnp.zeros((R,D),f32)
            for j in range(3*D//512):
                dn+=dot(dps[r,j*512:(j+1)*512],w_ref[:,j*512:(j+1)*512],NT)
            n,rs=moments(x_ref[r,:].astype(f32))
            for k,x in ((0,dn),(1,dn*n)):
                a,b=sums(x,seg)
                gev[0:1,k*D:(k+1)*D]+=a; gev[1:2,k*D:(k+1)*D]+=b
            dn=dn*(1.0+pick(seg,emb_ref,1,D))
            gf_ref[r,:]=dm_ref[r,:]+(dn-jnp.mean(dn,-1,keepdims=True)-n*jnp.mean(dn*n,-1,keepdims=True))*rs
    def weight(j):
        B=D//nd
        for h in range(nd):
            v=dot(n1_ref[:,h*B:(h+1)*B],dps[:,j*QW:(j+1)*QW],TN).astype(bf)
            gw[j,h//2,h%2]=v.reshape(p.Z,p.Y,K,QW)
        qkv[j].start()
    for q,c in enumerate(come):
        c.wait()
        @pl.loop(0,NR)
        def _(i,q=q): unturn(q,pl.ds(pl.multiple_of(i*R,R),R))
    for j in range(ne):
        weight(j)
        if j: qkv[j-1].step()
    for a in qkv[:ne][-1:]: a.step()
    steps=[]
    for k in range(max(ne,nr)): steps+=[a.step for a in qkv[:ne][k:k+1]]+[a.step for a in rest[k:k+1]]
    for i in range(NR):
        turn(i)
        for f in steps[i*len(steps)//NR:(i+1)*len(steps)//NR]: f()
    for j in range(ne,nq):
        weight(j)
        if j>ne: qkv[j-1].step()
        if j-ne<nr: rest[j-ne].step()
    vec=jnp.concatenate([gbv[0:1,:],gbm_ref[0:1,0:D],gbm_ref[1:2,:],gbm_ref[2:3,0:D]],1)
    for q in range(vec.shape[1]//256):
        h,s=divmod(q,ns)
        bsc[h//2,h%2,s//p.Y,s%p.Y,0:1,:]=vec[:,q*256:(q+1)*256]
    bias.start()
    qkv[nq-1].step()
    for a in qkv[:ne]: a.step()
    norm(0,NR//2)
    bias.step()
    qkv[ne].step()
    norm(NR//2,NR)
    gev[0:2,2*D:]=gem_ref[0:2,:]
    for j in range(8):
        for t in range(2): hsum[p.h,2*j+t:2*j+t+1,:]=gev[t:t+1,j*E:(j+1)*E]
    hc=[remote(hsum.at[p.h],hsum.at[p.h],hs.at[d],hr.at[d],(lax.rem(p.h+d,nd),p.s)) for d in range(1,nd)]
    qkv[ne+1].step(); qkv[ne].step(); bias.step()
    for c in hc: c.wait()
    tot=hsum[0]
    for i in range(1,nd): tot=tot+hsum[i]
    demb[p.s]=tot.astype(bf)
    qc=[remote(demb.at[p.s],demb.at[p.s],qs.at[d],qr.at[d],(p.h,lax.rem(p.s+d,ns))) for d in range(1,ns)]
    qkv[ne+2].step(); qkv[ne+1].step(); bias.step()
    for j in range(ne+3,nq): qkv[j].step(); qkv[j-1].step()
    for j,a in enumerate(rest): a.last(rest_out,j*D)
    bias.last(bout)
    bias_all[p.h,p.s]=bout[...]
    bc=along_head(p,lambda d,h,dev: remote(bout,bias_all.at[p.h,p.s],bs.at[0,d],br.at[0,d],dev))
    for j in range(ne): qkv[j].last(qkv_out,j*QW)
    for c in qc: c.wait()
    qkv[nq-1].step()
    Q=ns*16
    flat=demb[...].reshape(Q,E)
    r0=lax.broadcasted_iota(jnp.int32,(Q,ns*8),0); c0=lax.broadcasted_iota(jnp.int32,(Q,ns*8),1)
    spread=dot(jnp.where((r0//16==c0//8)&(r0%2==c0%8),1.0,0.0).astype(bf),act[...])
    rr=lax.broadcasted_iota(jnp.int32,(Q,128),0)%16//2
    rk=lax.broadcasted_iota(jnp.int32,(Q,K),0)%16//2
    tot=jnp.zeros((Q,K),f32)
    for j in range(8):
        m=jnp.where(rr==j,spread,0.0).astype(bf)
        gada[:,j*E:(j+1)*E]=dot(m,flat,TN)[:K,:]
        tot=jnp.where(rk==j,dot(flat,wada[:,j*E:(j+1)*E],NT),tot)
    dscr[...]=jnp.concatenate([tot,jnp.zeros((Q,128-K),f32)],1).reshape(ns,16,128)
    dact[p.h,p.s]=dscr[p.s]
    dc=along_seq(p,lambda d,s,dev: remote(dscr.at[s],dact.at[p.h,p.s],ds_.at[0,d],dr.at[0,d],dev))
    for c in bc: c.wait()
    bc=along_seq(p,lambda d,s,dev: remote(bias_all.at[:,p.s],bias_all.at[:,p.s],bs.at[1,d],br.at[1,d],dev))
    r8=lax.broadcasted_iota(jnp.int32,(8,Q),0); c8=lax.broadcasted_iota(jnp.int32,(8,Q),1)
    gbada[...]=dot(jnp.where(c8%16//2==r8,1.0,0.0).astype(bf),flat)
    for c in dc: c.wait()
    dc=along_head(p,lambda d,h,dev: remote(dact.at[p.h],dact.at[p.h],ds_.at[1,d],dr.at[1,d],dev))
    for j in range(ne,nq): qkv[j].last(qkv_out,j*QW)
    for a in rest+qkv+[bias]: a.finish()
    for i in range(NR):
        for c in sends[i]: c.wait_send()
    for c in bc+dc: c.wait()

def final(nd,ns,here,dqkv,rest,x,n1,dm,wq,cos,sin,seg,emb,gb,ge,act,wada,R=128):
    F,D=x.shape; K,E6=wada.shape; E=E6//8; H=gb.shape[1]; N=nd*ns; W=D//nd; NR=F//R
    X,Y,Z=sizes(nd,ns)
    S=jax.ShapeDtypeStruct; M=pltpu.VMEM; A=pltpu.SemaphoreType.DMA
    outs=[S((F,D),f32),S((K,H),f32),S((K,3*D),f32),S((nd,ns,8,256),f32),S((K,E6),f32),S((8,E),f32),S((nd,ns,16,128),f32)]
    scr=[M((W//128,nd,F,384),bf),M((F,D),bf),M((F,D),bf),M((F,D),f32),M((D,3*D),bf),M((F,3*D),bf),M((3*D//QW,X,2,Z,Y,K,QW),bf),M((8,3*D),f32),M((8,E6),f32),
         M((X,2,Z,Y,8,256),f32),M((8,256),f32),M((nd,16,E),f32),M((ns,16,E),bf),M((ns,16,128),f32),
         A((NR,nd)),A((NR,nd)),A((NR,)),A((W//128,)),A((4,)),A((nd,)),A((nd,)),A((ns,)),A((ns,)),A((2,max(nd,ns))),A((2,max(nd,ns))),A((2,max(nd,ns))),A((2,max(nd,ns)))]
    for j in range(H//D): scr+=Reduce.scratch(nd,ns,K,D,bf,REST(D,j),False)
    for _ in range(3*D//QW): scr+=Reduce.scratch(nd,ns,K,QW,bf,QKV(QW),True)
    scr+=Reduce.scratch(nd,ns,8,256,f32,QKV(256),True)
    m=len(here)
    def k(*refs): final_kernel(nd,ns,R,refs[:m],refs[m:m+14+len(outs)],refs[m+14+len(outs):])
    return pl.pallas_call(k,out_shape=tuple(outs),in_specs=[ANY]*(6+m)+[V]*8,out_specs=(V,)*len(outs),scratch_shapes=scr,
        compiler_params=pltpu.CompilerParams(collective_id=1,has_side_effects=True,vmem_limit_bytes=63*2**20),name="final")(
        *here,dqkv,rest,x,n1,dm,wq,cos,sin,seg,emb,gb,ge,act,wada)


def body(frames,time_embed,segment_ids,frame_mask,positions,w_ada,b_ada,w_qkv,b_qkv,w_out,b_out,w_up,b_up,w_down,b_down,cotangent):
    _,F,D=frames.shape
    nd=lax.axis_size("head"); ns=lax.axis_size("seq"); dev=lax.axis_index("head")*ns+lax.axis_index("seq")
    X,Y,Z=sizes(nd,ns); N=nd*ns
    W=D//nd
    E=b_ada.shape[0]; E6=w_ada.shape[1]; K=w_ada.shape[0]; H=w_up.shape[1]; nt=H//D
    x=frames[0]; cot=cotangent[0]
    PP=W//128
    def reorder(w): return w.reshape(-1,3,nd,PP,128).transpose(0,3,2,1,4).reshape(-1,3*D)
    def restore(w): return w.reshape(-1,PP,nd,3,128).transpose(0,3,2,1,4).reshape(-1,3*D)
    def hide(w): return w.reshape(-1,N,nt,K).transpose(0,2,1,3).reshape(-1,H)
    def unhide(w): return w.reshape(-1,nt,N,K).transpose(0,2,1,3).reshape(-1,H)
    rest=jnp.concatenate([hide(w_up),w_down.reshape(nt,K,D).transpose(1,0,2).reshape(K,H),w_out],axis=1)
    bs=(b_qkv,b_out,b_up,b_down,b_ada); ends=[0]
    for b in bs: ends.append(ends[-1]+b.shape[0])
    wide=-(-ends[-1]//256)*256
    bias=jnp.zeros((16,wide),bf).at[0,:ends[-1]].set(jnp.concatenate(bs))
    time8=jnp.zeros((8,D),f32).at[:2].set(time_embed[0].astype(f32))
    ids=jnp.zeros((8,F),jnp.int32).at[0].set(segment_ids[0]).at[1].set(frame_mask[0])
    wq,bias_all,ids_all,emb,act=entry(nd,ns,[reorder(w_qkv)],bias,time8,ids,w_ada)
    rest_all=lax.all_gather(rest,HS,axis=0,tiled=True)
    wq=wq.reshape(D,3*D)
    bias_all=bias_all[:,:,0,:].reshape(N,-1).astype(f32)
    bq,bo,bu,bd,ba=[bias_all[:,ends[i]:ends[i+1]].reshape(1,-1) for i in range(5)]
    bq=reorder(bq); bu=hide(bu)
    emb=emb.reshape(8,2,-1).transpose(1,0,2).reshape(2,E6)+ba
    seg_row=ids_all[:,0,:].reshape(-1); msk_row=ids_all[:,1,:].reshape(-1)
    column=lax.iota(jnp.int32,128)
    pair=(column%HD//2).astype(f32)
    angles=positions[0].astype(f32)[:,None]*(10000.0**(-(2.0*pair)/HD))
    cos=jnp.cos(angles); sin=jnp.where(column%2==0,-jnp.sin(angles),jnp.sin(angles))
    segc=segment_ids[0][:,None]; mskc=frame_mask[0].astype(f32)[:,None]
    normed,*packed=qkv_proj(x,segc,emb,wq,bq,cos,sin,nd)
    def swap(a): return lax.all_to_all(a,"head",split_axis=0,concat_axis=0,tiled=True)
    qkv=[]
    for a in packed:
        if qkv: a,qkv[-1]=lax.optimization_barrier((a,qkv[-1]))
        qkv.append(swap(a))
    qkv=[a.reshape(nd*F,384) for a in qkv]
    T=512
    qlo,qhi,klo,khi=tables(seg_row,msk_row,T)
    aq,ak=aux(seg_row,msk_row)
    os=[attn_fwd(a,qlo,qhi,aq,ak,T) for a in qkv]
    *dos,out,dmid,gup,gdo,gb,ge=mid(nd,ns,[o.reshape(nd,F,128) for o,_ in os],x,cot,segc,mskc,emb,rest_all,bo,bu,bd)
    gdo=lax.psum_scatter(gdo,HS,scatter_dimension=0,tiled=True).astype(f32)
    dqkv=[attn_bwd(a,o,do.reshape(nd*F,128),lse,klo,khi,aq,ak,T).reshape(nd,F,384) for a,(o,lse),do in zip(qkv,os,dos)]
    gx,gup,gqkv,gbias,gada,gbada,dact=final(nd,ns,[swap(a) for a in dqkv[:-1]],dqkv[-1],gup.reshape(X,2,Z,Y,K,H),x,normed,dmid,
        wq,cos,sin,segc,emb,gb,ge,act,w_ada)
    dact=dact[:,:,:,:K].reshape(N,8,2,K).sum(1).transpose(1,0,2).reshape(2,D)
    _,pull=jax.vjp(jax.nn.silu,time_embed[0].astype(f32))
    gtime=pull(dact)[0][None]
    gbada=lax.dynamic_slice_in_dim(gbada.reshape(-1),dev*E,E,0)
    gbias=gbias[:,:,0,:].reshape(-1)
    gbs=[]; at=0
    for k,order in ((3*D,restore),(D,None),(H,unhide),(D,None)):
        v=gbias[at:at+k]; at+=k
        if order: v=order(v[None])[0]
        gbs.append(lax.dynamic_slice_in_dim(v,dev*(k//N),k//N,0))
    gdown=gdo[:,:H].reshape(K,nt,D).transpose(1,0,2).reshape(nt*K,D)
    return (out[None],gx[None],gtime,gada,gbada,restore(gqkv),gbs[0],gdo[:,H:],gbs[1],unhide(gup),gbs[2],gdown,gbs[3])


def solution(mesh):
    row=P("seq","head",None); ids=P("seq","head"); mat=P(HS,None); vec=P(HS); tim=P("seq",None,None)
    in_specs=(row,tim,ids,ids,ids)+(mat,vec)*5+(row,)
    out_specs=(row,row,tim)+(mat,vec)*5
    return jax.shard_map(body,mesh=mesh,in_specs=in_specs,out_specs=out_specs,check_vma=False)
```

```python
import functools
import math

import jax
import jax.numpy as jnp
import numpy as np
from jax import lax
from jax.experimental import pallas as pl
from jax.experimental.pallas import tpu as pltpu
from jax.sharding import PartitionSpec as P

bf = jnp.bfloat16
f32 = jnp.float32
HS = ("head", "seq")
ANY = pl.BlockSpec(memory_space=pl.ANY)
V = pl.BlockSpec(memory_space=pltpu.VMEM)
NN = (((1,), (0,)), ((), ()))
NT = (((1,), (1,)), ((), ()))
TN = (((0,), (0,)), ((), ()))


def dot(a, b, dims=NN):
    return lax.dot_general(a, b, dims, preferred_element_type=f32)


HD=64
LOG2E=math.log2(math.e)
NEG=-1e30

def only(x,h):
    lane=lax.broadcasted_iota(jnp.int32,x.shape,1)
    return jnp.where((lane<HD) if h%2==0 else (lane>=HD),x,jnp.zeros_like(x))

def fwd_kernel(lo_ref,hi_ref,qkv_ref,auxq_ref,auxk_ref,o_ref,lse_ref,qs,s_scr,m_scr,acc,*,T,nh):
    qt=pl.program_id(0)
    W=nh*HD
    lane=lax.broadcasted_iota(jnp.int32,(T,128),1)
    lo=lo_ref[qt]; hi=hi_ref[qt]
    rq=pl.ds(pl.multiple_of(qt*T,T),T)
    def key(kt,h): return qkv_ref[pl.ds(pl.multiple_of(kt*T,T),T),W+h//2*128:W+(h//2+1)*128]
    def value(kt,h): return qkv_ref[pl.ds(pl.multiple_of(kt*T,T),T),2*W+h//2*128:2*W+(h//2+1)*128]
    for h in range(nh):
        qs[h]=only(qkv_ref[rq,h//2*128:(h//2+1)*128],h)*jnp.asarray(HD**-0.5,bf)
    auxq=auxq_ref[rq,:]
    eye=lax.broadcasted_iota(jnp.int32,(T,T),0)==lax.broadcasted_iota(jnp.int32,(T,T),1)
    def mx(s):
        m=s[:,:128]
        for j in range(1,T//128): m=jnp.maximum(m,s[:,j*128:(j+1)*128])
        return m
    ak=auxk_ref[rq,:]
    for h in range(nh):
        raw=dot(qs[h],key(qt,h),NT)
        s=dot(jnp.concatenate([qs[h],auxq],axis=1),jnp.concatenate([key(qt,h),ak],axis=1),NT)
        s=jnp.where(eye,raw,s)
        s_scr[h,qt]=s
        m_scr[h]=mx(s)
    @pl.loop(lo,hi-1)
    def _(t):
        kt=jnp.where(t>=qt,t+1,t)
        ak=auxk_ref[pl.ds(pl.multiple_of(kt*T,T),T),:]
        for h in range(nh):
            s=dot(jnp.concatenate([qs[h],auxq],axis=1),jnp.concatenate([key(kt,h),ak],axis=1),NT)
            s_scr[h,kt]=s
            m_scr[h]=jnp.maximum(m_scr[h],mx(s))
    for h in range(nh):
        m_scr[h]=jnp.broadcast_to(jnp.max(m_scr[h],axis=1,keepdims=True),(T,128))
        acc[h]=jnp.zeros((T,256),f32)
    ones=jnp.ones((T,128),bf)
    @pl.loop(lo,hi)
    def _(kt):
        for h in range(nh):
            s=s_scr[h,kt]; m=m_scr[h]
            p=jnp.exp2((s-jnp.concatenate([m]*(T//128),axis=1))*LOG2E).astype(bf)
            acc[h]+=dot(p,jnp.concatenate([value(kt,h),ones],axis=1))
    lse=jnp.zeros((T,128),f32)
    for g in range(nh//2):
        o=[]
        for h in (2*g,2*g+1):
            l=acc[h,:,128:]
            o.append(acc[h,:,:128]/l)
            lse=jnp.where(lane==h,m_scr[h]+jnp.log(l),lse)
        o_ref[:,g*128:(g+1)*128]=jnp.where(lane<HD,o[0],o[1]).astype(bf)
    lse_ref[...]=lse

def attn_fwd(qkv,lo,hi,auxq,auxk,T):
    L,W3=qkv.shape; W=W3//3; nh=W//HD; nk=L//T
    return pl.pallas_call(
        functools.partial(fwd_kernel,T=T,nh=nh),
        out_shape=(jax.ShapeDtypeStruct((L,W),bf),jax.ShapeDtypeStruct((L,128),f32)),
        grid_spec=pltpu.PrefetchScalarGridSpec(num_scalar_prefetch=2,grid=(nk,),
            in_specs=[pl.BlockSpec((L,W3),lambda i,*_:(0,0)),pl.BlockSpec((L,128),lambda i,*_:(0,0)),pl.BlockSpec((L,128),lambda i,*_:(0,0))],
            out_specs=[pl.BlockSpec((T,W),lambda i,*_:(i,0)),pl.BlockSpec((T,128),lambda i,*_:(i,0))],
            scratch_shapes=[pltpu.VMEM((nh,T,128),bf),pltpu.VMEM((nh,nk,T,T),f32),pltpu.VMEM((nh,T,128),f32),pltpu.VMEM((nh,T,256),f32)]),
        compiler_params=pltpu.CompilerParams(vmem_limit_bytes=60*2**20),
        name="attn_fwd",cost_estimate=pl.CostEstimate(flops=16*nh*L*L*HD,bytes_accessed=4*2**20,transcendentals=nh*L*L),
    )(lo,hi,qkv,auxq,auxk)

def bwd_kernel(lo_ref,hi_ref,qkv_ref,o_ref,do_ref,lse_ref,auxq_ref,auxk_ref,dqkv_ref,qs,qa,dos,dd,kT,dqT,dk,dv,*,T,nh):
    kt=pl.program_id(0)
    W=nh*HD
    L=qkv_ref.shape[0]
    nk=L//T
    lane=lax.broadcasted_iota(jnp.int32,(T,128),1)
    def pair(ref,t,h,at=0): return ref[pl.ds(pl.multiple_of(t*T,T),T),at+h//2*128:at+(h//2+1)*128]
    @pl.when(kt==0)
    def _():
        dqT[...]=jnp.zeros_like(dqT)
        @pl.loop(0,nk)
        def _(t):
            r=pl.ds(pl.multiple_of(t*T,T),T)
            lse=lse_ref[r,:]
            aq=auxq_ref[r,:].astype(f32)
            kT[t]=qkv_ref[r,W:2*W].T
            for h in range(nh):
                qs[h,t]=only(pair(qkv_ref,t,h),h)*jnp.asarray(HD**-0.5,bf)
                nl=-lse[:,h:h+1]
                l1=nl.astype(bf).astype(f32); l2=(nl-l1).astype(bf).astype(f32); l3=nl-l1-l2
                qa[h,t]=jnp.where(lane==0,l1,jnp.where(lane==1,l2,jnp.where(lane==2,l3,aq))).astype(bf)
                do=only(pair(do_ref,t,h),h)
                dos[h,t]=do
                nd=-jnp.sum(do.astype(f32)*pair(o_ref,t,h).astype(f32),axis=1,keepdims=True)
                d1=nd.astype(bf).astype(f32); d2=nd-d1
                dd[h,t]=jnp.where(lane==0,d1,jnp.where(lane==1,d2,0.0)).astype(bf)
    r=pl.ds(pl.multiple_of(kt*T,T),T)
    ak=auxk_ref[r,:]
    av=jnp.where(lane<2,1.0,0.0).astype(bf)
    lo=lo_ref[kt]; hi=hi_ref[kt]
    def tile(qt,diag):
        for h in range(nh):
            kx=jnp.concatenate([pair(qkv_ref,kt,h,W),ak],axis=1)
            s=dot(kx,jnp.concatenate([qs[h,qt],qa[h,qt]],axis=1),NT)
            if diag:
                eye=lax.broadcasted_iota(jnp.int32,(T,T),0)==lax.broadcasted_iota(jnp.int32,(T,T),1)
                qr=jnp.where(lane<3,qa[h,qt].astype(f32),0.0).astype(bf)
                raw=dot(kx,jnp.concatenate([qs[h,qt],qr],axis=1),NT)
                s=jnp.where(eye,raw,s)
            p=jnp.exp2(s*LOG2E)
            dp=dot(jnp.concatenate([pair(qkv_ref,kt,h,2*W),av],axis=1),jnp.concatenate([dos[h,qt],dd[h,qt]],axis=1),NT)
            ds=(p*dp).astype(bf)
            dv[h]+=dot(p.astype(bf),pair(do_ref,qt,h))
            dk[h]+=dot(ds,pair(qkv_ref,qt,h))
            dqT[qt,h*HD:(h+1)*HD,:]+=dot(kT[kt,h*HD:(h+1)*HD,:],ds)
    dk[...]=jnp.zeros_like(dk); dv[...]=jnp.zeros_like(dv)
    tile(kt,True)
    @pl.loop(lo,hi-1)
    def _(t):
        tile(jnp.where(t>=kt,t+1,t),False)
    for g in range(nh//2):
        dqkv_ref[r,W+g*128:W+(g+1)*128]=(jnp.where(lane<HD,dk[2*g],dk[2*g+1])*HD**-0.5).astype(bf)
        dqkv_ref[r,2*W+g*128:2*W+(g+1)*128]=jnp.where(lane<HD,dv[2*g],dv[2*g+1]).astype(bf)
    @pl.when(kt==nk-1)
    def _():
        @pl.loop(0,nk)
        def _(t):
            dqkv_ref[pl.ds(pl.multiple_of(t*T,T),T),0:W]=(dqT[t].T*HD**-0.5).astype(bf)

def attn_bwd(qkv,o,do,lse,lo,hi,auxq,auxk,T):
    L,W3=qkv.shape; W=W3//3; nh=W//HD; nk=L//T
    full=lambda w: pl.BlockSpec((L,w),lambda i,*_:(0,0))
    return pl.pallas_call(
        functools.partial(bwd_kernel,T=T,nh=nh),
        out_shape=jax.ShapeDtypeStruct((L,W3),bf),
        grid_spec=pltpu.PrefetchScalarGridSpec(num_scalar_prefetch=2,grid=(nk,),
            in_specs=[full(W3),full(W),full(W),full(128),full(128),full(128)],
            out_specs=full(W3),
            scratch_shapes=[pltpu.VMEM((nh,nk,T,128),bf)]*4+[pltpu.VMEM((nk,W,T),bf),pltpu.VMEM((nk,W,T),f32),
                pltpu.VMEM((nh,T,128),f32),pltpu.VMEM((nh,T,128),f32)]),
        compiler_params=pltpu.CompilerParams(vmem_limit_bytes=60*2**20),
        name="attn_bwd",cost_estimate=pl.CostEstimate(flops=40*nh*L*L*HD,bytes_accessed=8*2**20,transcendentals=nh*L*L),
    )(lo,hi,qkv,o,do,lse,auxq,auxk)

def tables(seg,mask,T):
    L=seg.shape[0]; nk=L//T
    s=seg.reshape(nk,T); m=mask.reshape(nk,T)
    has=jnp.stack([jnp.any(s==c,axis=1) for c in (0,1)],1)
    real=jnp.stack([jnp.any((s==c)&(m==1),axis=1) for c in (0,1)],1)
    use=jnp.any(has[:,None,:]&real[None,:,:],axis=2)|jnp.eye(nk,dtype=bool)
    idx=jnp.arange(nk,dtype=jnp.int32)
    qlo=jnp.min(jnp.where(use,idx[None,:],nk),axis=1); qhi=jnp.max(jnp.where(use,idx[None,:],-1),axis=1)+1
    klo=jnp.min(jnp.where(use,idx[:,None],nk),axis=0); khi=jnp.max(jnp.where(use,idx[:,None],-1),axis=0)+1
    return [a.astype(jnp.int32) for a in (qlo,qhi,klo,khi)]
def aux(seg,mask):
    L=seg.shape[0]
    lane=lax.broadcasted_iota(jnp.int32,(L,128),1)
    sg=seg[:,None]; pad=(mask==0)[:,None]
    aq=jnp.where(lane==3,jnp.where(sg!=0,NEG,0.),jnp.where(lane==4,jnp.where(sg!=1,NEG,0.),jnp.where(lane==5,NEG,0.))).astype(bf)
    ak=jnp.where(lane<3,1.,jnp.where(lane==3,(sg==0).astype(f32),jnp.where(lane==4,(sg==1).astype(f32),jnp.where(lane==5,pad.astype(f32),0.)))).astype(bf)
    return aq,ak

EPS=1e-6

def moments(x):
    c=jnp.mean(x,-1,keepdims=True)
    xc=x-c
    rs=lax.rsqrt(jnp.mean(xc*xc,-1,keepdims=True)+EPS)
    return xc*rs, rs
def pick(seg,emb,i,D):
    return jnp.where(seg==0,emb[0:1,i*D:(i+1)*D],emb[1:2,i*D:(i+1)*D])
def sums(x,seg):
    a=jnp.sum(jnp.where(seg==0,x,0.0),0,keepdims=True); b=jnp.sum(jnp.where(seg==1,x,0.0),0,keepdims=True)
    return a,b
def partner(v):
    w=v.shape[1]
    lane=lax.broadcasted_iota(jnp.int32,v.shape,1)
    return jnp.where(lane%2==0,pltpu.roll(v,w-1,1),pltpu.roll(v,1,1))
def gelu_both(v):
    c=math.sqrt(2/math.pi)
    v2=v*v
    t=jnp.tanh(c*v*(1.0+0.044715*v2))
    h=0.5*(1.0+t)
    return v*h, h+0.5*v*(1.0-t*t)*(c*(1.0+3*0.044715*v2))

def qkv_kernel(x_ref,seg_ref,emb_ref,w_ref,b_ref,cos_ref,sin_ref,n_ref,*p_refs,R,nd):
    F,D=x_ref.shape
    @pl.loop(0,F//R)
    def _(i):
        r=pl.ds(pl.multiple_of(i*R,R),R)
        seg=seg_ref[r,:]
        n,_=moments(x_ref[r,:].astype(f32))
        n_ref[r,:]=(n*(1.0+pick(seg,emb_ref,1,D))+pick(seg,emb_ref,0,D)).astype(bf)
    for q,p_ref in enumerate(p_refs):
        @pl.loop(0,F//R)
        def _(i):
            r=pl.ds(pl.multiple_of(i*R,R),R)
            cos=cos_ref[r,:]; sin=sin_ref[r,:]
            for d in range(0,nd,2):
                c=(q*nd+d)*384
                v=dot(n_ref[r,:],w_ref[:,c:c+768])+b_ref[0:1,c:c+768]
                for k in range(6):
                    a=v[:,k*128:(k+1)*128]
                    if k%3<2: a=a*cos+partner(a)*sin
                    p_ref[d+k//3,r,k%3*128:(k%3+1)*128]=a.astype(bf)

def qkv_proj(x,seg,emb,w,b,cos,sin,nd,R=256):
    F,D=x.shape; PP=D//nd//128
    return pl.pallas_call(functools.partial(qkv_kernel,R=R,nd=nd),
        out_shape=(jax.ShapeDtypeStruct((F,D),bf),)+(jax.ShapeDtypeStruct((nd,F,384),bf),)*PP,
        in_specs=[V]*7,out_specs=(V,)*(1+PP),
        compiler_params=pltpu.CompilerParams(vmem_limit_bytes=40*2**20),name="qkv_proj",
        cost_estimate=pl.CostEstimate(flops=2*F*D*3*D,bytes_accessed=14*2**20,transcendentals=0))(x,seg,emb,w,b,cos,sin)


def sizes(nd,ns):
    Y=2**((ns.bit_length()-1)//2)
    return nd//2,Y,ns//Y

class Place:
    def __init__(self,nd,ns):
        self.nd,self.ns=nd,ns
        self.X,self.Y,self.Z=sizes(nd,ns)
        self.h=lax.axis_index("head"); self.s=lax.axis_index("seq")
        self.x,self.c=self.h//2,self.h%2
        self.z,self.y=self.s//self.Y,self.s%self.Y
    def at(self,x=None,c=None,z=None,y=None):
        x=self.x if x is None else x; c=self.c if c is None else c
        z=self.z if z is None else z; y=self.y if y is None else y
        return (x*2+c,z*self.Y+y)

def near_first(n):
    out=[]
    for d in range(1,n//2+1):
        out.append(d)
        if n-d!=d: out.append(n-d)
    return out

def remote(src,dst,ss,rs,dev):
    cp=pltpu.make_async_remote_copy(src_ref=src,dst_ref=dst,send_sem=ss,recv_sem=rs,device_id=dev,device_id_type=pl.DeviceIdType.MESH)
    cp.start()
    return cp

def greet(p):
    b=pltpu.get_barrier_semaphore()
    for d in range(1,p.nd): pl.semaphore_signal(b,inc=1,device_id=(lax.rem(p.h+d,p.nd),p.s),device_id_type=pl.DeviceIdType.MESH)
    for d in range(1,p.ns): pl.semaphore_signal(b,inc=1,device_id=(p.h,lax.rem(p.s+d,p.ns)),device_id_type=pl.DeviceIdType.MESH)
    pl.semaphore_wait(b,p.nd+p.ns-2)

def along_head(p,f): return [f(d,lax.rem(p.h+d,p.nd),(lax.rem(p.h+d,p.nd),p.s)) for d in range(1,p.nd)]
def along_seq(p,f): return [f(d,lax.rem(p.s+d,p.ns),(p.h,lax.rem(p.s+d,p.ns))) for d in range(1,p.ns)]

class Gather:
    @staticmethod
    def sems(nd,ns):
        X,Y,Z=sizes(nd,ns)
        D=pltpu.SemaphoreType.DMA
        one=[D((Z,)),D((Z,X)),D((Z,Y)),D((Z,X,Y)),D((Z,X,Y)),D((Z,)),D((2,Z,X,Y))]
        return one+one+[D(())]
    def __init__(self,p,shard,out,sems):
        self.p,self.shard,self.out=p,shard,out
        self.ss,self.rs,self.ls=sems[:7],sems[7:14],sems[14]
        self.all=[]; self.half=shard.shape[-1]//2
        self.two={}; self.three={}
    def send(self,k,idx,src,dst,dev):
        cp=remote(src,dst,self.ss[k].at[idx],self.rs[k].at[idx],dev)
        self.all.append(cp); return cp
    def cols(self,part): return pl.ds(part*self.half,self.half)
    def loc(self,x,z,y,part=None):
        r=self.out.at[x,self.p.c,z,y]
        return r if part is None else r.at[:,self.cols(part)]
    def start(self):
        p=self.p
        self.zc={}
        for dz in near_first(p.Z):
            self.zc[dz]=self.send(0,(dz,),self.shard,self.loc(p.x,p.z,p.y),p.at(z=lax.rem(p.z+dz,p.Z)))
        self.local=pltpu.make_async_copy(self.shard,self.loc(p.x,p.z,p.y),self.ls)
        self.local.start()
        self.second(0)
    def second(self,dz):
        p=self.p; zz=lax.rem(p.z+p.Z-dz,p.Z)
        if dz: self.zc[dz].wait_recv()
        def src(part=None):
            if dz: return self.loc(p.x,zz,p.y,part)
            return self.shard if part is None else self.shard.at[:,self.cols(part)]
        for dx in near_first(p.X):
            self.two[0,dz,dx]=self.send(1,(dz,dx),src(0),self.loc(p.x,zz,p.y,0),p.at(x=lax.rem(p.x+dx,p.X)))
        for dy in near_first(p.Y):
            self.two[1,dz,dy]=self.send(2,(dz,dy),src(1),self.loc(p.x,zz,p.y,1),p.at(y=lax.rem(p.y+dy,p.Y)))
        self.send(5,(dz,),src(),self.loc(p.x,zz,p.y),p.at(c=1-p.c))
        for dy in near_first(p.Y):
            self.three[0,dz,0,dy]=self.send(3,(dz,0,dy),src(0),self.loc(p.x,zz,p.y,0),p.at(y=lax.rem(p.y+dy,p.Y)))
        for dx in near_first(p.X):
            self.three[1,dz,dx,0]=self.send(4,(dz,dx,0),src(1),self.loc(p.x,zz,p.y,1),p.at(x=lax.rem(p.x+dx,p.X)))
    def third(self,dz):
        p=self.p; zz=lax.rem(p.z+p.Z-dz,p.Z)
        for dx in near_first(p.X):
            self.two[0,dz,dx].wait_recv()
            l=self.loc(lax.rem(p.x+p.X-dx,p.X),zz,p.y,0)
            for dy in near_first(p.Y):
                self.three[0,dz,dx,dy]=self.send(3,(dz,dx,dy),l,l,p.at(y=lax.rem(p.y+dy,p.Y)))
            self.send(6,(0,dz,dx,0),l,l,p.at(c=1-p.c))
        for dy in near_first(p.Y):
            self.two[1,dz,dy].wait_recv()
            l=self.loc(p.x,zz,lax.rem(p.y+p.Y-dy,p.Y),1)
            for dx in near_first(p.X):
                self.three[1,dz,dx,dy]=self.send(4,(dz,dx,dy),l,l,p.at(x=lax.rem(p.x+dx,p.X)))
            self.send(6,(1,dz,0,dy),l,l,p.at(c=1-p.c))
    def fourth(self,dz):
        p=self.p; zz=lax.rem(p.z+p.Z-dz,p.Z)
        for part in (0,1):
            for dx in range(p.X):
                for dy in range(p.Y):
                    if (part,dz,dx,dy) not in self.three: continue
                    self.three[part,dz,dx,dy].wait_recv()
                    l=self.loc(lax.rem(p.x+p.X-dx,p.X),zz,lax.rem(p.y+p.Y-dy,p.Y),part)
                    self.send(6,(part,dz,dx,dy),l,l,p.at(c=1-p.c))
    def finish(self):
        waited=set()
        for cp in self.zc.values(): waited.add(id(cp))
        for d in (self.two,self.three):
            for cp in d.values(): waited.add(id(cp))
        for cp in self.all:
            if id(cp) not in waited: cp.wait_recv()
            cp.wait_send()
        self.local.wait()

def entry_kernel(nd,ns,nw,*refs):
    shards=refs[:nw]; bias,time,ids,wada=refs[nw:nw+4]
    outs=refs[nw+4:2*nw+4]; bias_all,ids_all,emb,act=refs[2*nw+4:2*nw+8]
    time_all,part,r1,r2,bs,br,isd,ir,ts,tr,e1s,e1r,e2s,e2r=refs[2*nw+8:2*nw+22]
    gs=refs[2*nw+22:]
    p=Place(nd,ns); n=len(Gather.sems(nd,ns))
    greet(p)
    tail=[]
    first=[]
    for ds in range(1,ns):
        first.append(remote(time,time_all.at[p.s],ts.at[ds],tr.at[ds],(p.h,lax.rem(p.s+ds,ns))))
    g=[Gather(p,shards[i],outs[i],gs[i*n:(i+1)*n]) for i in range(nw)]
    for a in g: a.start()
    me=p.h*ns+p.s
    for dh in range(1,nd):
        tail.append(remote(ids,ids_all.at[p.h],isd.at[dh],ir.at[dh],(lax.rem(p.h+dh,nd),p.s)))
    bc=along_head(p,lambda d,h,dev: remote(bias,bias_all.at[p.h,p.s],bs.at[0,d],br.at[0,d],dev))
    l1=pltpu.make_async_copy(bias,bias_all.at[p.h,p.s],bs.at[0,0]); l1.start()
    l2=pltpu.make_async_copy(ids,ids_all.at[p.h],isd.at[0]); l2.start()
    time_all[p.s]=time[...]
    for cp in first: cp.wait()
    D=time.shape[1]; K=wada.shape[0]; E=wada.shape[1]//8
    v=time_all[...].reshape(ns*8,D)
    low=(v/(1.0+jnp.exp(-v))).astype(bf)
    kk=D//(nd*ns)
    row=lax.broadcasted_iota(jnp.int32,(D,128),0); col=lax.broadcasted_iota(jnp.int32,(D,128),1)
    pickm=jnp.where((row==me*kk+col)&(col<kk),1.0,0.0).astype(bf)
    own=dot(low,pickm).astype(bf)
    act[...]=own
    for j in range(8):
        pj=dot(own[:,:K],wada[:,j*E:(j+1)*E])
        for s in range(ns):
            part[s,2*j:2*j+2,:]=pj[8*s:8*s+2,:]
    one=[remote(part.at[lax.rem(p.s+ds,ns)],r1.at[ds],e1s.at[ds],e1r.at[ds],(p.h,lax.rem(p.s+ds,ns))) for ds in range(1,ns)]
    l1.wait()
    for cp in bc: cp.wait()
    tail+=along_seq(p,lambda d,s,dev: remote(bias_all.at[:,p.s],bias_all.at[:,p.s],bs.at[1,d],br.at[1,d],dev))
    order=[0]+near_first(p.Z)
    for a in g:
        for i,dz in enumerate(order):
            if dz: a.second(dz)
            if i: a.third(order[i-1])
        a.third(order[-1])
    tot=part[p.s]
    for ds in range(1,ns):
        one[ds-1].wait()
        tot=tot+r1[ds]
    r2[p.h]=tot
    two=[remote(r2.at[p.h],r2.at[p.h],e2s.at[dh],e2r.at[dh],(lax.rem(p.h+dh,nd),p.s)) for dh in range(1,nd)]
    for a in g:
        for dz in order: a.fourth(dz)
    for cp in two: cp.wait()
    tot=r2[0]
    for i in range(1,nd): tot=tot+r2[i]
    emb[...]=tot
    for a in g: a.finish()
    for cp in tail: cp.wait()
    l2.wait()

def entry(nd,ns,shards,bias,time,ids,wada):
    X,Y,Z=sizes(nd,ns)
    S=jax.ShapeDtypeStruct
    D=pltpu.SemaphoreType.DMA
    nw=len(shards); E=wada.shape[1]//8
    outs=[S((X,2,Z,Y)+a.shape,a.dtype) for a in shards]+[S((nd,ns)+bias.shape,bias.dtype),S((nd,)+ids.shape,ids.dtype),S((16,E),f32),S((ns*8,128),bf)]
    scr=[pltpu.VMEM((ns,8,time.shape[1]),f32),pltpu.VMEM((ns,16,E),f32),pltpu.VMEM((ns,16,E),f32),pltpu.VMEM((nd,16,E),f32),
         D((2,max(nd,ns))),D((2,max(nd,ns))),D((nd,)),D((nd,)),D((ns,)),D((ns,)),D((ns,)),D((ns,)),D((nd,)),D((nd,))]
    for _ in shards: scr+=Gather.sems(nd,ns)
    return pl.pallas_call(functools.partial(entry_kernel,nd,ns,nw),out_shape=tuple(outs),
        in_specs=[ANY]*(nw+1)+[V,ANY,V],out_specs=tuple([ANY]*(nw+2)+[V,V]),scratch_shapes=scr,
        compiler_params=pltpu.CompilerParams(collective_id=0,has_side_effects=True,vmem_limit_bytes=40*2**20),name="entry")(*shards,bias,time,ids,wada)

def make_remote(src,dst,ss,rs,dev):
    return pltpu.make_async_remote_copy(src_ref=src,dst_ref=dst,send_sem=ss,recv_sem=rs,device_id=dev,device_id_type=pl.DeviceIdType.MESH)

def mid_kernel(PP,*refs,R,nd,ns):
    mid_body(refs[:PP],refs[PP+9:2*PP+9],*refs[PP:PP+9],*refs[2*PP+9:],R=R,nd=nd,ns=ns)

def mid_body(o_refs,do_refs,x_ref,c_ref,seg_ref,msk_ref,emb_ref,w_ref,bo_ref,bu_ref,bd_ref,
               out_ref,dm_ref,gu_ref,gw_ref,gb_ref,ge_ref,
               wo_ref,wu_ref,wd_ref,n2s,acts,dhs,dfs,dps,dgelu,a_ref,da_ref,sem,s1,s2,s3,t1,t2,t3,*,R,nd,ns):
    F,D=x_ref.shape; H=bu_ref.shape[1]; CH=512
    loads=[pltpu.make_async_copy(w_ref.at[:,pl.ds(o,n)],r,sem.at[i]) for i,(o,n,r) in enumerate(((2*H,D,wo_ref),(0,H,wu_ref),(H,H,wd_ref)))]
    p=Place(nd,ns); W=D//nd; NR=F//R
    b=pltpu.get_barrier_semaphore()
    for d in range(1,nd): pl.semaphore_signal(b,inc=1,device_id=(lax.rem(p.h+d,nd),p.s),device_id_type=pl.DeviceIdType.MESH)
    pl.semaphore_wait(b,nd-1)
    def rows(i): return pl.ds(pl.multiple_of(i*R,R),R)
    def cols(h,q): return pl.ds(pl.multiple_of(h*W+q*128,128),128)
    def arrive(i):
        return [make_remote(o.at[lax.rem(p.h+d,nd),rows(i)],a_ref.at[rows(i),cols(p.h,q)],s1.at[i,d,q],s2.at[i,d,q],(lax.rem(p.h+d,nd),p.s)) for d in range(1,nd) for q,o in enumerate(o_refs)]
    def kept(i): return [pltpu.make_async_copy(o.at[p.h,rows(i)],a_ref.at[rows(i),cols(p.h,q)],s3.at[i,q]) for q,o in enumerate(o_refs)]
    def leave(i):
        return [make_remote(da_ref.at[rows(i),cols(lax.rem(p.h+d,nd),q)],o.at[p.h,rows(i)],t1.at[i,d,q],t2.at[i,d,q],(lax.rem(p.h+d,nd),p.s)) for q,o in enumerate(do_refs) for d in range(1,nd)]
    def stays(i): return [pltpu.make_async_copy(da_ref.at[rows(i),cols(p.h,q)],o.at[p.h,rows(i)],t3.at[i,q]) for q,o in enumerate(do_refs)]
    for c in arrive(0)+kept(0): c.start()
    for l in loads: l.start()
    gb_ref[...]=jnp.zeros_like(gb_ref); ge_ref[...]=jnp.zeros_like(ge_ref)
    for l in loads: l.wait()
    def down(j):
        t,o=divmod(j*CH,D)
        return slice(o,o+CH),slice(t*D,(t+1)*D)
    @pl.loop(0,F//R)
    def _(i):
        r=rows(i)
        for c in arrive(i): c.wait_recv()
        for c in kept(i): c.wait()
        @pl.when(i+1<NR)
        def _():
            for c in arrive(i+1)+kept(i+1): c.start()
        seg=seg_ref[r,:]; msk=msk_ref[r,:]
        def acc(k,x):
            a,b=sums(x,seg)
            ge_ref[0:1,k*D:(k+1)*D]+=a; ge_ref[1:2,k*D:(k+1)*D]+=b
        branch=(dot(a_ref[r,:],wo_ref[...])+bo_ref[0:1,:])*msk
        g1=pick(seg,emb_ref,2,D)
        middle=x_ref[r,:].astype(f32)+g1*branch
        n,rs=moments(middle)
        sc2=1.0+pick(seg,emb_ref,4,D)
        n2=(n*sc2+pick(seg,emb_ref,3,D)).astype(bf)
        n2s[r,:]=n2
        feed=jnp.broadcast_to(bd_ref[0:1,:],(R,D))
        for j in range(H//CH):
            c=slice(j*CH,(j+1)*CH)
            h=dot(n2,wu_ref[:,c])+bu_ref[0:1,c]
            a,g=gelu_both(h)
            a=a.astype(bf)
            acts[r,c]=a; dgelu[:,c]=g
            feed+=dot(a,wd_ref[down(j)])
        up=c_ref[r,:].astype(f32)
        g2=pick(seg,emb_ref,5,D)
        out_ref[r,:]=(middle+g2*feed).astype(bf)
        df=(up*g2).astype(bf)
        dfs[r,:]=df
        acc(3,up*feed)
        gb_ref[2:3,0:D]+=jnp.sum(df.astype(f32),0,keepdims=True)
        dn=jnp.zeros((R,D),f32)
        for j in range(H//CH):
            c=slice(j*CH,(j+1)*CH)
            dh=(dot(df,wd_ref[down(j)],NT)*dgelu[:,c]).astype(bf)
            dhs[r,c]=dh
            gb_ref[1:2,c]+=jnp.sum(dh.astype(f32),0,keepdims=True)
            dn+=dot(dh,wu_ref[:,c],NT)
        acc(1,dn); acc(2,dn*n)
        dn=dn*sc2
        dmid=up+(dn-jnp.mean(dn,-1,keepdims=True)-n*jnp.mean(dn*n,-1,keepdims=True))*rs
        dm_ref[r,:]=dmid
        acc(0,dmid*branch)
        dp=(dmid*g1*msk).astype(bf)
        dps[r,:]=dp
        gb_ref[0:1,0:D]+=jnp.sum(dp.astype(f32),0,keepdims=True)
        da_ref[r,:]=dot(dp,wo_ref[...],NT).astype(bf)
        for c in leave(i)+stays(i): c.start()
    @pl.loop(0,D//256)
    def _(i):
        c=pl.ds(pl.multiple_of(i*256,256),256)
        gw_ref[c,H:H+D]=dot(a_ref[:,c],dps[...],TN).astype(bf)
        gu_ref[c,:]=dot(n2s[:,c],dhs[...],TN).astype(bf)
        for t in range(H//D):
            e=pl.ds(pl.multiple_of(t*D+i*256,256),256)
            gw_ref[c,t*D:(t+1)*D]=dot(acts[:,e],dfs[...],TN).astype(bf)
    for i in range(NR):
        for c in arrive(i): c.wait_send()
        for c in leave(i)+stays(i): c.wait()

def mid(nd,ns,os,x,c,seg,msk,emb,w,bo,bu,bd,R=256):
    F,D=x.shape; H=bu.shape[1]; NR=F//R; PP=len(os); A=pltpu.SemaphoreType.DMA
    S=jax.ShapeDtypeStruct; M=pltpu.VMEM
    return pl.pallas_call(functools.partial(mid_kernel,PP,R=R,nd=nd,ns=ns),
        out_shape=(S((nd,F,128),bf),)*PP+(S((F,D),bf),S((F,D),f32),S((D,H),bf),S((D,H+D),bf),S((8,H),f32),S((8,4*D),f32)),
        in_specs=[ANY]*PP+[V]*5+[ANY]+[V]*3,out_specs=(ANY,)*PP+(V,)*6,
        scratch_shapes=[M((D,D),bf),M((D,H),bf),M((D,H),bf),M((F,D),bf),M((F,H),bf),M((F,H),bf),M((F,D),bf),M((F,D),bf),M((R,H),f32),M((F,D),bf),M((F,D),bf),A((3,)),A((NR,nd,PP)),A((NR,nd,PP)),A((NR,PP)),A((NR,nd,PP)),A((NR,nd,PP)),A((NR,PP))],
        compiler_params=pltpu.CompilerParams(collective_id=2,has_side_effects=True,vmem_limit_bytes=62*2**20),name="mid",
        cost_estimate=pl.CostEstimate(flops=6*F*D*(D+2*H),bytes_accessed=30*2**20,transcendentals=F*H))(*os,x,c,seg,msk,emb,w,bo,bu,bd)


ORD_X=-1
QW=512
class Reduce:
    def __init__(self,p,parts,scr,own=None,src=None,col=0):
        self.p,self.parts,self.src=p,parts,src
        it=iter(scr)
        self.own=own if own is not None else next(it)
        self.c=p.c if own is not None else 0
        self.w=self.own.shape[-1]; self.cs=pl.ds(col,self.w)
        self.cin=next(it); self.c1,self.c2,self.ls=next(it),next(it),next(it)
        self.bufs=[[(next(it),next(it),next(it)) for _ in o] for _,_,o in parts]
        self.sent=[]; self.stage=0
    @staticmethod
    def scratch(nd,ns,k,w,dt,parts,own):
        X,Y,Z=sizes(nd,ns); M=pltpu.VMEM; D=pltpu.SemaphoreType.DMA; n={"x":X,"y":Y,"z":Z}
        out=[] if own else [M((X,1,Z,Y,k,w),dt)]
        out+=[M((X,Z,Y,k,w),dt),D((X,)),D((X,)),D((X,))]
        for lo,hi,order in parts:
            for i,a in enumerate(order):
                left=tuple(n[b] for b in "xzy" if b in order[i+1:])
                out+=[M((max(n[a]-1,1),)+left+(k,hi-lo),dt),D((n[a],)),D((n[a],))]
        return out
    def start(self):
        p=self.p; self.l=[]; self.cc=[]
        for x in range(p.X):
            s=self.own.at[x,1-p.c] if self.src is None else self.src.at[x,1-p.c,:,:,:,self.cs]
            self.cc.append(remote(s,self.cin.at[x],self.c1.at[x],self.c2.at[x],p.at(c=1-p.c)))
            if self.src is not None:
                l=pltpu.make_async_copy(self.src.at[x,p.c,:,:,:,self.cs],self.own.at[x,0],self.ls.at[x]); l.start(); self.l.append(l)
        self.sent+=self.cc
    def place(self,order,i,v):
        p=self.p; mine={"x":p.x,"y":p.y,"z":p.z}
        ix={b:(mine[b] if b in order[:i] else v if b==order[i] else slice(None)) for b in "xyz"}
        return (ix["x"],self.c,ix["z"],ix["y"])
    def add(self,i,x,cols):
        i=i+(slice(None),slice(*cols))
        self.own[i]=(self.own[i].astype(f32)+x.astype(f32)).astype(self.own.dtype)
    def send(self,part,i):
        p=self.p; lo,hi,order=self.parts[part]; a=order[i]
        n={"x":p.X,"y":p.Y,"z":p.Z}[a]; me={"x":p.x,"y":p.y,"z":p.z}[a]
        buf,s1,s2=self.bufs[part][i]; out=[]
        for d in near_first(n):
            v=lax.rem(me+d,n)
            out.append((d,remote(self.own.at[self.place(order,i,v)+(slice(None),pl.ds(lo,hi-lo))],buf.at[d-1],s1.at[d],s2.at[d],p.at(**{a:v}))))
        self.sent+=[c for _,c in out]
        return out
    def step(self):
        p=self.p; st=self.stage; self.stage+=1
        if st==0:
            for x in range(p.X):
                if self.src is not None: self.l[x].wait()
                self.cc[x].wait_recv()
                @pl.loop(0,p.Z)
                def _(z):
                    for y in range(p.Y): self.add((x,self.c,z,y),self.cin[x,z,y],(0,self.w))
            self.go=[self.send(k,0) for k in range(len(self.parts))]
            return
        go=[]
        for k,(lo,hi,order) in enumerate(self.parts):
            buf=self.bufs[k][st-1][0]; left=[b for b in "xzy" if b in order[st:]]
            n={"x":p.X,"y":p.Y,"z":p.Z}; mine={"x":p.x,"y":p.y,"z":p.z}
            for d,c in self.go[k]:
                c.wait_recv()
                def one(at,d=d):
                    ix={**mine,**at}
                    self.add((ix["x"],self.c,ix["z"],ix["y"]),buf[(d-1,)+tuple(at[b] for b in left)],(lo,hi))
                if len(left)==2:
                    @pl.loop(0,n[left[0]])
                    def _(u):
                        for v in range(n[left[1]]): one({left[0]:u,left[1]:v})
                else:
                    @pl.loop(0,n[left[0]])
                    def _(u): one({left[0]:u})
            go.append(self.send(k,st))
        self.go=go
    def last(self,put):
        p=self.p
        for k,(lo,hi,order) in enumerate(self.parts):
            buf=self.bufs[k][2][0]
            t=self.own[p.x,self.c,p.z,p.y,:,lo:hi].astype(f32)
            for d,c in self.go[k]:
                c.wait_recv()
                t=t+buf[d-1].astype(f32)
            put(lo,t)
    def finish(self):
        for c in self.sent: c.wait_send()

REST=(lambda w,j:((0,w//2,"yxz"),(w//2,w,"xyz"))); QKV=(lambda w:((0,w//2,"yzx"),(w//2,w,"xyz")))

def final_kernel(nd,ns,R,here,refs,scr):
    (g_ref,rest_ref,x_hbm,n1_hbm,dm_hbm,wq_hbm,cos_ref,sin_ref,seg_ref,emb_ref,gbm_ref,gem_ref,act,wada)=refs[:14]
    (gf_ref,rest_out,qkv_out,bias_all,gada,gbada,dact)=refs[14:]
    (g,x_ref,n1_ref,dm_ref,w_ref,dps,gw,gbv,gev,bsc,bout,hsum,demb,dscr)=scr[:14]; rtmp=scr[-1]; scr=scr[:-1]
    (gs,gr,gl,gh,ld,hs,hr,qs,qr,ds_,dr,bs,br)=scr[14:27]
    pools=scr[27:]
    p=Place(nd,ns); me=p.h*ns+p.s
    F,D=x_ref.shape; W=D//nd; E=D*6//8; K=wada.shape[0]; H=gbm_ref.shape[1]; NR=F//R
    nr=H//D; nq=3*D//QW; PP=W//128; C=3*D//PP; ne=nq//PP*(PP-1)
    come=[pltpu.make_async_copy(a,g.at[q],gh.at[q]) for q,a in enumerate(here)]
    for c in come: c.start()
    greet(p)
    loads=[pltpu.make_async_copy(a,b,ld.at[i]) for i,(a,b) in enumerate(((x_hbm,x_ref),(wq_hbm,w_ref),(dm_hbm,dm_ref),(n1_hbm,n1_ref)))]
    sends=[]; own=[]
    def chunk(i):
        r=pl.ds(i*R,R)
        sends.append([remote(g_ref.at[lax.rem(p.h+d,nd),r],g.at[PP-1,p.h,r],gs.at[i,d],gr.at[i,d],(lax.rem(p.h+d,nd),p.s)) for d in range(1,nd)])
    for i in range(NR):
        r=pl.ds(i*R,R)
        c=pltpu.make_async_copy(g_ref.at[p.h,r],g.at[PP-1,p.h,r],gl.at[i]); c.start(); own.append(c)
    for i in range(min(2,NR)): chunk(i)
    for l in loads: l.start()
    it=iter(pools)
    take=lambda n: [next(it) for _ in range(n)]
    rest=[]
    for j in range(nr):
        rest.append(Reduce(p,REST(D,j),take(len(Reduce.scratch(nd,ns,K,D,bf,REST(D,j),False))),src=rest_ref,col=j*D))
        rest[-1].start()
    qkv=[Reduce(p,QKV(QW),take(len(Reduce.scratch(nd,ns,K,QW,bf,QKV(QW),True))),own=gw.at[j]) for j in range(nq)]
    bias=Reduce(p,QKV(256),take(len(Reduce.scratch(nd,ns,8,256,f32,QKV(256),True))),own=bsc)
    gbv[...]=jnp.zeros_like(gbv); gev[...]=jnp.zeros_like(gev); bsc[...]=jnp.zeros_like(bsc)
    for a in rest[:2]: a.step()
    for l in loads: l.wait()
    def unturn(q,r):
        cos=cos_ref[r,:]; sin=sin_ref[r,:]
        @pl.loop(0,nd)
        def _(d):
            for j in range(3):
                c=pl.ds(pl.multiple_of(((q*nd+d)*3+j)*128,128),128)
                v=g[q,d,r,j*128:(j+1)*128]
                if j<2:
                    v=v.astype(f32)
                    v=(v*cos-partner(v)*sin).astype(bf)
                dps[r,c]=v
                gbv[0:1,c]+=jnp.sum(v.astype(f32),0,keepdims=True)
    def turn(i):
        for c in sends[i]: c.wait_recv()
        own[i].wait()
        if i+2<NR: chunk(i+2)
        r=slice(i*R,(i+1)*R)
        unturn(PP-1,r)
    def norm(lo,hi):
        @pl.loop(lo,hi)
        def _(i):
            r=pl.ds(pl.multiple_of(i*R,R),R)
            seg=seg_ref[r,:]
            dn=jnp.zeros((R,D),f32)
            for j in range(3*D//512):
                dn+=dot(dps[r,j*512:(j+1)*512],w_ref[:,j*512:(j+1)*512],NT)
            n,rs=moments(x_ref[r,:].astype(f32))
            for k,x in ((0,dn),(1,dn*n)):
                a,b=sums(x,seg)
                gev[0:1,k*D:(k+1)*D]+=a; gev[1:2,k*D:(k+1)*D]+=b
            dn=dn*(1.0+pick(seg,emb_ref,1,D))
            gf_ref[r,:]=dm_ref[r,:]+(dn-jnp.mean(dn,-1,keepdims=True)-n*jnp.mean(dn*n,-1,keepdims=True))*rs
    def weight(j):
        B=D//nd
        for h in range(nd):
            v=dot(n1_ref[:,h*B:(h+1)*B],dps[:,j*QW:(j+1)*QW],TN).astype(bf)
            gw[j,h//2,h%2]=v.reshape(p.Z,p.Y,K,QW)
        qkv[j].start()
    for q,c in enumerate(come):
        c.wait()
        @pl.loop(0,NR)
        def _(i,q=q): unturn(q,pl.ds(pl.multiple_of(i*R,R),R))
    for j in range(ne):
        weight(j)
        if j: qkv[j-1].step()
    for a in qkv[:ne][-1:]: a.step()
    steps=[]
    for k in range(max(ne,nr)): steps+=[a.step for a in qkv[:ne][k:k+1]]+[a.step for a in rest[k:k+1]]
    for i in range(NR):
        turn(i)
        for f in steps[i*len(steps)//NR:(i+1)*len(steps)//NR]: f()
    for j in range(ne,nq):
        weight(j)
        if j>ne: qkv[j-1].step()
        if j-ne<nr: rest[j-ne].step()
    vec=jnp.concatenate([gbv[0:1,:],gbm_ref[0:1,0:D],gbm_ref[1:2,:],gbm_ref[2:3,0:D]],1)
    for q in range(vec.shape[1]//256):
        h,s=divmod(q,ns)
        bsc[h//2,h%2,s//p.Y,s%p.Y,0:1,:]=vec[:,q*256:(q+1)*256]
    bias.start()
    qkv[nq-1].step()
    for a in qkv[:ne]: a.step()
    norm(0,NR//2)
    bias.step()
    qkv[ne].step()
    norm(NR//2,NR)
    gev[0:2,2*D:]=gem_ref[0:2,:]
    for j in range(8):
        for t in range(2): hsum[p.h,2*j+t:2*j+t+1,:]=gev[t:t+1,j*E:(j+1)*E]
    hc=[remote(hsum.at[p.h],hsum.at[p.h],hs.at[d],hr.at[d],(lax.rem(p.h+d,nd),p.s)) for d in range(1,nd)]
    qkv[ne+1].step(); qkv[ne].step(); bias.step()
    for c in hc: c.wait()
    tot=hsum[0]
    for i in range(1,nd): tot=tot+hsum[i]
    demb[p.s]=tot.astype(bf)
    qc=[remote(demb.at[p.s],demb.at[p.s],qs.at[d],qr.at[d],(p.h,lax.rem(p.s+d,ns))) for d in range(1,ns)]
    qkv[ne+2].step(); qkv[ne+1].step(); bias.step()
    for j in range(ne+3,nq): qkv[j].step(); qkv[j-1].step()
    for j,a in enumerate(rest):
        def put(c,t,j=j): rtmp[j,:,c:c+t.shape[1]]=t
        a.last(put)
    wide=128*nr
    r0=lax.broadcasted_iota(jnp.int32,(wide,wide),0); c0=lax.broadcasted_iota(jnp.int32,(wide,wide),1)
    perm=jnp.where((r0//128==c0//K%nr)&(r0%128//K==c0//(K*nr))&(r0%K==c0%K),1.0,0.0)
    for b in range(D//128):
        v=jnp.concatenate([rtmp[j,:,b*128:(b+1)*128] for j in range(nr)],1)
        rest_out[:,b*wide:(b+1)*wide]=lax.dot_general(v,perm,NN,precision=lax.Precision.HIGHEST,preferred_element_type=f32)
    def keep(c,t): bout[:,c:c+t.shape[1]]=t
    bias.last(keep)
    def home(j):
        def put(c,t):
            for k in range(t.shape[1]//128):
                s=(j*QW+c)//128+k
                at=(s%3*nd+s//3%nd)*PP+s//3//nd
                qkv_out[:,at*128:(at+1)*128]=t[:,k*128:(k+1)*128]
        return put
    bias_all[p.h,p.s]=bout[...]
    bc=along_head(p,lambda d,h,dev: remote(bout,bias_all.at[p.h,p.s],bs.at[0,d],br.at[0,d],dev))
    for j in range(ne): qkv[j].last(home(j))
    for c in qc: c.wait()
    qkv[nq-1].step()
    Q=ns*16
    flat=demb[...].reshape(Q,E)
    r0=lax.broadcasted_iota(jnp.int32,(Q,ns*8),0); c0=lax.broadcasted_iota(jnp.int32,(Q,ns*8),1)
    spread=dot(jnp.where((r0//16==c0//8)&(r0%2==c0%8),1.0,0.0).astype(bf),act[...])
    rr=lax.broadcasted_iota(jnp.int32,(Q,128),0)%16//2
    rk=lax.broadcasted_iota(jnp.int32,(Q,K),0)%16//2
    tot=jnp.zeros((Q,K),f32)
    for j in range(8):
        m=jnp.where(rr==j,spread,0.0).astype(bf)
        gada[:,j*E:(j+1)*E]=dot(m,flat,TN)[:K,:]
        tot=jnp.where(rk==j,dot(flat,wada[:,j*E:(j+1)*E],NT),tot)
    dscr[...]=jnp.concatenate([tot,jnp.zeros((Q,128-K),f32)],1).reshape(ns,16,128)
    dact[p.h,p.s]=dscr[p.s]
    dc=along_seq(p,lambda d,s,dev: remote(dscr.at[s],dact.at[p.h,p.s],ds_.at[0,d],dr.at[0,d],dev))
    for c in bc: c.wait()
    bc=along_seq(p,lambda d,s,dev: remote(bias_all.at[:,p.s],bias_all.at[:,p.s],bs.at[1,d],br.at[1,d],dev))
    r8=lax.broadcasted_iota(jnp.int32,(8,Q),0); c8=lax.broadcasted_iota(jnp.int32,(8,Q),1)
    gbada[...]=dot(jnp.where(c8%16//2==r8,1.0,0.0).astype(bf),flat)
    for c in dc: c.wait()
    dc=along_head(p,lambda d,h,dev: remote(dact.at[p.h],dact.at[p.h],ds_.at[1,d],dr.at[1,d],dev))
    for j in range(ne,nq): qkv[j].last(home(j))
    for a in rest+qkv+[bias]: a.finish()
    for i in range(NR):
        for c in sends[i]: c.wait_send()
    for c in bc+dc: c.wait()

def final(nd,ns,here,dqkv,rest,x,n1,dm,wq,cos,sin,seg,emb,gb,ge,act,wada,R=128):
    F,D=x.shape; K,E6=wada.shape; E=E6//8; H=gb.shape[1]; N=nd*ns; W=D//nd; NR=F//R
    X,Y,Z=sizes(nd,ns)
    S=jax.ShapeDtypeStruct; M=pltpu.VMEM; A=pltpu.SemaphoreType.DMA
    outs=[S((F,D),f32),S((K,H),f32),S((K,3*D),f32),S((nd,ns,8,256),f32),S((K,E6),f32),S((8,E),f32),S((nd,ns,16,128),f32)]
    scr=[M((W//128,nd,F,384),bf),M((F,D),bf),M((F,D),bf),M((F,D),f32),M((D,3*D),bf),M((F,3*D),bf),M((3*D//QW,X,2,Z,Y,K,QW),bf),M((8,3*D),f32),M((8,E6),f32),
         M((X,2,Z,Y,8,256),f32),M((8,256),f32),M((nd,16,E),f32),M((ns,16,E),bf),M((ns,16,128),f32),
         A((NR,nd)),A((NR,nd)),A((NR,)),A((W//128,)),A((4,)),A((nd,)),A((nd,)),A((ns,)),A((ns,)),A((2,max(nd,ns))),A((2,max(nd,ns))),A((2,max(nd,ns))),A((2,max(nd,ns)))]
    for j in range(H//D): scr+=Reduce.scratch(nd,ns,K,D,bf,REST(D,j),False)
    for _ in range(3*D//QW): scr+=Reduce.scratch(nd,ns,K,QW,bf,QKV(QW),True)
    scr+=Reduce.scratch(nd,ns,8,256,f32,QKV(256),True)
    scr+=[M((H//D,K,D),f32)]
    m=len(here)
    def k(*refs): final_kernel(nd,ns,R,refs[:m],refs[m:m+14+len(outs)],refs[m+14+len(outs):])
    return pl.pallas_call(k,out_shape=tuple(outs),in_specs=[ANY]*(6+m)+[V]*8,out_specs=(V,)*len(outs),scratch_shapes=scr,
        compiler_params=pltpu.CompilerParams(collective_id=1,has_side_effects=True,vmem_limit_bytes=63*2**20),name="final")(
        *here,dqkv,rest,x,n1,dm,wq,cos,sin,seg,emb,gb,ge,act,wada)


def body(frames,time_embed,segment_ids,frame_mask,positions,w_ada,b_ada,w_qkv,b_qkv,w_out,b_out,w_up,b_up,w_down,b_down,cotangent):
    _,F,D=frames.shape
    nd=lax.axis_size("head"); ns=lax.axis_size("seq"); dev=lax.axis_index("head")*ns+lax.axis_index("seq")
    X,Y,Z=sizes(nd,ns); N=nd*ns
    W=D//nd
    E=b_ada.shape[0]; E6=w_ada.shape[1]; K=w_ada.shape[0]; H=w_up.shape[1]; nt=H//D
    x=frames[0]; cot=cotangent[0]
    PP=W//128
    def reorder(w): return w.reshape(-1,3,nd,PP,128).transpose(0,3,2,1,4).reshape(-1,3*D)
    def restore(w): return w.reshape(-1,PP,nd,3,128).transpose(0,3,2,1,4).reshape(-1,3*D)
    def hide(w): return w.reshape(-1,N,nt,K).transpose(0,2,1,3).reshape(-1,H)
    def unhide(w): return w.reshape(-1,nt,N,K).transpose(0,2,1,3).reshape(-1,H)
    rest=jnp.concatenate([hide(w_up),w_down.reshape(nt,K,D).transpose(1,0,2).reshape(K,H),w_out],axis=1)
    bs=(b_qkv,b_out,b_up,b_down,b_ada); ends=[0]
    for b in bs: ends.append(ends[-1]+b.shape[0])
    wide=-(-ends[-1]//256)*256
    bias=jnp.zeros((16,wide),bf).at[0,:ends[-1]].set(jnp.concatenate(bs))
    time8=jnp.zeros((8,D),f32).at[:2].set(time_embed[0].astype(f32))
    ids=jnp.zeros((8,F),jnp.int32).at[0].set(segment_ids[0]).at[1].set(frame_mask[0])
    wq,bias_all,ids_all,emb,act=entry(nd,ns,[reorder(w_qkv)],bias,time8,ids,w_ada)
    rest_all=lax.all_gather(rest,HS,axis=0,tiled=True)
    wq=wq.reshape(D,3*D)
    bias_all=bias_all[:,:,0,:].reshape(N,-1).astype(f32)
    bq,bo,bu,bd,ba=[bias_all[:,ends[i]:ends[i+1]].reshape(1,-1) for i in range(5)]
    bq=reorder(bq); bu=hide(bu)
    emb=emb.reshape(8,2,-1).transpose(1,0,2).reshape(2,E6)+ba
    seg_row=ids_all[:,0,:].reshape(-1); msk_row=ids_all[:,1,:].reshape(-1)
    column=lax.iota(jnp.int32,128)
    pair=(column%HD//2).astype(f32)
    angles=positions[0].astype(f32)[:,None]*(10000.0**(-(2.0*pair)/HD))
    cos=jnp.cos(angles); sin=jnp.where(column%2==0,-jnp.sin(angles),jnp.sin(angles))
    segc=segment_ids[0][:,None]; mskc=frame_mask[0].astype(f32)[:,None]
    normed,*packed=qkv_proj(x,segc,emb,wq,bq,cos,sin,nd)
    def swap(a): return lax.all_to_all(a,"head",split_axis=0,concat_axis=0,tiled=True)
    qkv=[]
    for a in packed:
        if qkv: a,qkv[-1]=lax.optimization_barrier((a,qkv[-1]))
        qkv.append(swap(a))
    qkv=[a.reshape(nd*F,384) for a in qkv]
    T=512
    qlo,qhi,klo,khi=tables(seg_row,msk_row,T)
    aq,ak=aux(seg_row,msk_row)
    os=[attn_fwd(a,qlo,qhi,aq,ak,T) for a in qkv]
    *dos,out,dmid,gup,gdo,gb,ge=mid(nd,ns,[o.reshape(nd,F,128) for o,_ in os],x,cot,segc,mskc,emb,rest_all,bo,bu,bd)
    gdo=lax.psum_scatter(gdo,HS,scatter_dimension=0,tiled=True).astype(f32)
    dqkv=[attn_bwd(a,o,do.reshape(nd*F,128),lse,klo,khi,aq,ak,T).reshape(nd,F,384) for a,(o,lse),do in zip(qkv,os,dos)]
    gx,gup,gqkv,gbias,gada,gbada,dact=final(nd,ns,[swap(a) for a in dqkv[:-1]],dqkv[-1],gup.reshape(X,2,Z,Y,K,H),x,normed,dmid,
        wq,cos,sin,segc,emb,gb,ge,act,w_ada)
    dact=dact[:,:,:,:K].reshape(N,8,2,K).sum(1).transpose(1,0,2).reshape(2,D)
    _,pull=jax.vjp(jax.nn.silu,time_embed[0].astype(f32))
    gtime=pull(dact)[0][None]
    gbada=lax.dynamic_slice_in_dim(gbada.reshape(-1),dev*E,E,0)
    gbias=gbias[:,:,0,:].reshape(-1)
    gbs=[]; at=0
    for k,order in ((3*D,restore),(D,None),(H,unhide),(D,None)):
        v=gbias[at:at+k]; at+=k
        if order: v=order(v[None])[0]
        gbs.append(lax.dynamic_slice_in_dim(v,dev*(k//N),k//N,0))
    gdown=gdo[:,:H].reshape(K,nt,D).transpose(1,0,2).reshape(nt*K,D)
    return (out[None],gx[None],gtime,gada,gbada,gqkv,gbs[0],gdo[:,H:],gbs[1],gup,gbs[2],gdown,gbs[3])


def solution(mesh):
    row=P("seq","head",None); ids=P("seq","head"); mat=P(HS,None); vec=P(HS); tim=P("seq",None,None)
    in_specs=(row,tim,ids,ids,ids)+(mat,vec)*5+(row,)
    out_specs=(row,row,tim)+(mat,vec)*5
    return jax.shard_map(body,mesh=mesh,in_specs=in_specs,out_specs=out_specs,check_vma=False)
```

```python
import functools
import math

import jax
import jax.numpy as jnp
import numpy as np
from jax import lax
from jax.experimental import pallas as pl
from jax.experimental.pallas import tpu as pltpu
from jax.sharding import PartitionSpec as P

bf = jnp.bfloat16
f32 = jnp.float32
HS = ("head", "seq")
ANY = pl.BlockSpec(memory_space=pl.ANY)
V = pl.BlockSpec(memory_space=pltpu.VMEM)
NN = (((1,), (0,)), ((), ()))
NT = (((1,), (1,)), ((), ()))
TN = (((0,), (0,)), ((), ()))


def dot(a, b, dims=NN):
    return lax.dot_general(a, b, dims, preferred_element_type=f32)


HD=64
LOG2E=math.log2(math.e)
NEG=-1e30

def only(x,h):
    lane=lax.broadcasted_iota(jnp.int32,x.shape,1)
    return jnp.where((lane<HD) if h%2==0 else (lane>=HD),x,jnp.zeros_like(x))

def fwd_kernel(lo_ref,hi_ref,qkv_ref,auxq_ref,auxk_ref,o_ref,lse_ref,qs,s_scr,m_scr,acc,*,T,nh):
    qt=pl.program_id(0)
    W=nh*HD
    lane=lax.broadcasted_iota(jnp.int32,(T,128),1)
    lo=lo_ref[qt]; hi=hi_ref[qt]
    rq=pl.ds(pl.multiple_of(qt*T,T),T)
    def key(kt,h): return qkv_ref[pl.ds(pl.multiple_of(kt*T,T),T),W+h//2*128:W+(h//2+1)*128]
    def value(kt,h): return qkv_ref[pl.ds(pl.multiple_of(kt*T,T),T),2*W+h//2*128:2*W+(h//2+1)*128]
    for h in range(nh):
        qs[h]=only(qkv_ref[rq,h//2*128:(h//2+1)*128],h)*jnp.asarray(HD**-0.5,bf)
    auxq=auxq_ref[rq,:]
    eye=lax.broadcasted_iota(jnp.int32,(T,T),0)==lax.broadcasted_iota(jnp.int32,(T,T),1)
    def mx(s):
        m=s[:,:128]
        for j in range(1,T//128): m=jnp.maximum(m,s[:,j*128:(j+1)*128])
        return m
    ak=auxk_ref[rq,:]
    for h in range(nh):
        raw=dot(qs[h],key(qt,h),NT)
        s=dot(jnp.concatenate([qs[h],auxq],axis=1),jnp.concatenate([key(qt,h),ak],axis=1),NT)
        s=jnp.where(eye,raw,s)
        s_scr[h,qt]=s
        m_scr[h]=mx(s)
    @pl.loop(lo,hi-1)
    def _(t):
        kt=jnp.where(t>=qt,t+1,t)
        ak=auxk_ref[pl.ds(pl.multiple_of(kt*T,T),T),:]
        for h in range(nh):
            s=dot(jnp.concatenate([qs[h],auxq],axis=1),jnp.concatenate([key(kt,h),ak],axis=1),NT)
            s_scr[h,kt]=s
            m_scr[h]=jnp.maximum(m_scr[h],mx(s))
    for h in range(nh):
        m_scr[h]=jnp.broadcast_to(jnp.max(m_scr[h],axis=1,keepdims=True),(T,128))
        acc[h]=jnp.zeros((T,256),f32)
    ones=jnp.ones((T,128),bf)
    @pl.loop(lo,hi)
    def _(kt):
        for h in range(nh):
            s=s_scr[h,kt]; m=m_scr[h]
            p=jnp.exp2((s-jnp.concatenate([m]*(T//128),axis=1))*LOG2E).astype(bf)
            acc[h]+=dot(p,jnp.concatenate([value(kt,h),ones],axis=1))
    lse=jnp.zeros((T,128),f32)
    for g in range(nh//2):
        o=[]
        for h in (2*g,2*g+1):
            l=acc[h,:,128:]
            o.append(acc[h,:,:128]/l)
            lse=jnp.where(lane==h,m_scr[h]+jnp.log(l),lse)
        o_ref[:,g*128:(g+1)*128]=jnp.where(lane<HD,o[0],o[1]).astype(bf)
    lse_ref[...]=lse

def attn_fwd(qkv,lo,hi,auxq,auxk,T):
    L,W3=qkv.shape; W=W3//3; nh=W//HD; nk=L//T
    return pl.pallas_call(
        functools.partial(fwd_kernel,T=T,nh=nh),
        out_shape=(jax.ShapeDtypeStruct((L,W),bf),jax.ShapeDtypeStruct((L,128),f32)),
        grid_spec=pltpu.PrefetchScalarGridSpec(num_scalar_prefetch=2,grid=(nk,),
            in_specs=[pl.BlockSpec((L,W3),lambda i,*_:(0,0)),pl.BlockSpec((L,128),lambda i,*_:(0,0)),pl.BlockSpec((L,128),lambda i,*_:(0,0))],
            out_specs=[pl.BlockSpec((T,W),lambda i,*_:(i,0)),pl.BlockSpec((T,128),lambda i,*_:(i,0))],
            scratch_shapes=[pltpu.VMEM((nh,T,128),bf),pltpu.VMEM((nh,nk,T,T),f32),pltpu.VMEM((nh,T,128),f32),pltpu.VMEM((nh,T,256),f32)]),
        compiler_params=pltpu.CompilerParams(vmem_limit_bytes=60*2**20),
        name="attn_fwd",cost_estimate=pl.CostEstimate(flops=16*nh*L*L*HD,bytes_accessed=4*2**20,transcendentals=nh*L*L),
    )(lo,hi,qkv,auxq,auxk)

def bwd_kernel(lo_ref,hi_ref,qkv_ref,o_ref,do_ref,lse_ref,auxq_ref,auxk_ref,dqkv_ref,qs,qa,dos,dd,kT,dqT,dk,dv,*,T,nh):
    kt=pl.program_id(0)
    W=nh*HD
    L=qkv_ref.shape[0]
    nk=L//T
    lane=lax.broadcasted_iota(jnp.int32,(T,128),1)
    def pair(ref,t,h,at=0): return ref[pl.ds(pl.multiple_of(t*T,T),T),at+h//2*128:at+(h//2+1)*128]
    @pl.when(kt==0)
    def _():
        dqT[...]=jnp.zeros_like(dqT)
        @pl.loop(0,nk)
        def _(t):
            r=pl.ds(pl.multiple_of(t*T,T),T)
            lse=lse_ref[r,:]
            aq=auxq_ref[r,:].astype(f32)
            kT[t]=qkv_ref[r,W:2*W].T
            for h in range(nh):
                qs[h,t]=only(pair(qkv_ref,t,h),h)*jnp.asarray(HD**-0.5,bf)
                nl=-lse[:,h:h+1]
                l1=nl.astype(bf).astype(f32); l2=(nl-l1).astype(bf).astype(f32); l3=nl-l1-l2
                qa[h,t]=jnp.where(lane==0,l1,jnp.where(lane==1,l2,jnp.where(lane==2,l3,aq))).astype(bf)
                do=only(pair(do_ref,t,h),h)
                dos[h,t]=do
                nd=-jnp.sum(do.astype(f32)*pair(o_ref,t,h).astype(f32),axis=1,keepdims=True)
                d1=nd.astype(bf).astype(f32); d2=nd-d1
                dd[h,t]=jnp.where(lane==0,d1,jnp.where(lane==1,d2,0.0)).astype(bf)
    r=pl.ds(pl.multiple_of(kt*T,T),T)
    ak=auxk_ref[r,:]
    av=jnp.where(lane<2,1.0,0.0).astype(bf)
    lo=lo_ref[kt]; hi=hi_ref[kt]
    def tile(qt,diag):
        for h in range(nh):
            kx=jnp.concatenate([pair(qkv_ref,kt,h,W),ak],axis=1)
            s=dot(kx,jnp.concatenate([qs[h,qt],qa[h,qt]],axis=1),NT)
            if diag:
                eye=lax.broadcasted_iota(jnp.int32,(T,T),0)==lax.broadcasted_iota(jnp.int32,(T,T),1)
                qr=jnp.where(lane<3,qa[h,qt].astype(f32),0.0).astype(bf)
                raw=dot(kx,jnp.concatenate([qs[h,qt],qr],axis=1),NT)
                s=jnp.where(eye,raw,s)
            p=jnp.exp2(s*LOG2E)
            dp=dot(jnp.concatenate([pair(qkv_ref,kt,h,2*W),av],axis=1),jnp.concatenate([dos[h,qt],dd[h,qt]],axis=1),NT)
            ds=(p*dp).astype(bf)
            dv[h]+=dot(p.astype(bf),pair(do_ref,qt,h))
            dk[h]+=dot(ds,pair(qkv_ref,qt,h))
            dqT[qt,h*HD:(h+1)*HD,:]+=dot(kT[kt,h*HD:(h+1)*HD,:],ds)
    dk[...]=jnp.zeros_like(dk); dv[...]=jnp.zeros_like(dv)
    tile(kt,True)
    @pl.loop(lo,hi-1)
    def _(t):
        tile(jnp.where(t>=kt,t+1,t),False)
    for g in range(nh//2):
        dqkv_ref[r,W+g*128:W+(g+1)*128]=(jnp.where(lane<HD,dk[2*g],dk[2*g+1])*HD**-0.5).astype(bf)
        dqkv_ref[r,2*W+g*128:2*W+(g+1)*128]=jnp.where(lane<HD,dv[2*g],dv[2*g+1]).astype(bf)
    @pl.when(kt==nk-1)
    def _():
        @pl.loop(0,nk)
        def _(t):
            dqkv_ref[pl.ds(pl.multiple_of(t*T,T),T),0:W]=(dqT[t].T*HD**-0.5).astype(bf)

def attn_bwd(qkv,o,do,lse,lo,hi,auxq,auxk,T):
    L,W3=qkv.shape; W=W3//3; nh=W//HD; nk=L//T
    full=lambda w: pl.BlockSpec((L,w),lambda i,*_:(0,0))
    return pl.pallas_call(
        functools.partial(bwd_kernel,T=T,nh=nh),
        out_shape=jax.ShapeDtypeStruct((L,W3),bf),
        grid_spec=pltpu.PrefetchScalarGridSpec(num_scalar_prefetch=2,grid=(nk,),
            in_specs=[full(W3),full(W),full(W),full(128),full(128),full(128)],
            out_specs=full(W3),
            scratch_shapes=[pltpu.VMEM((nh,nk,T,128),bf)]*4+[pltpu.VMEM((nk,W,T),bf),pltpu.VMEM((nk,W,T),f32),
                pltpu.VMEM((nh,T,128),f32),pltpu.VMEM((nh,T,128),f32)]),
        compiler_params=pltpu.CompilerParams(vmem_limit_bytes=60*2**20),
        name="attn_bwd",cost_estimate=pl.CostEstimate(flops=40*nh*L*L*HD,bytes_accessed=8*2**20,transcendentals=nh*L*L),
    )(lo,hi,qkv,o,do,lse,auxq,auxk)

def tables(seg,mask,T):
    L=seg.shape[0]; nk=L//T
    s=seg.reshape(nk,T); m=mask.reshape(nk,T)
    has=jnp.stack([jnp.any(s==c,axis=1) for c in (0,1)],1)
    real=jnp.stack([jnp.any((s==c)&(m==1),axis=1) for c in (0,1)],1)
    use=jnp.any(has[:,None,:]&real[None,:,:],axis=2)|jnp.eye(nk,dtype=bool)
    idx=jnp.arange(nk,dtype=jnp.int32)
    qlo=jnp.min(jnp.where(use,idx[None,:],nk),axis=1); qhi=jnp.max(jnp.where(use,idx[None,:],-1),axis=1)+1
    klo=jnp.min(jnp.where(use,idx[:,None],nk),axis=0); khi=jnp.max(jnp.where(use,idx[:,None],-1),axis=0)+1
    return [a.astype(jnp.int32) for a in (qlo,qhi,klo,khi)]
def aux(seg,mask):
    L=seg.shape[0]
    lane=lax.broadcasted_iota(jnp.int32,(L,128),1)
    sg=seg[:,None]; pad=(mask==0)[:,None]
    aq=jnp.where(lane==3,jnp.where(sg!=0,NEG,0.),jnp.where(lane==4,jnp.where(sg!=1,NEG,0.),jnp.where(lane==5,NEG,0.))).astype(bf)
    ak=jnp.where(lane<3,1.,jnp.where(lane==3,(sg==0).astype(f32),jnp.where(lane==4,(sg==1).astype(f32),jnp.where(lane==5,pad.astype(f32),0.)))).astype(bf)
    return aq,ak

EPS=1e-6

def moments(x):
    c=jnp.mean(x,-1,keepdims=True)
    xc=x-c
    rs=lax.rsqrt(jnp.mean(xc*xc,-1,keepdims=True)+EPS)
    return xc*rs, rs
def pick(seg,emb,i,D):
    return jnp.where(seg==0,emb[0:1,i*D:(i+1)*D],emb[1:2,i*D:(i+1)*D])
def sums(x,seg):
    a=jnp.sum(jnp.where(seg==0,x,0.0),0,keepdims=True); b=jnp.sum(jnp.where(seg==1,x,0.0),0,keepdims=True)
    return a,b
def partner(v):
    w=v.shape[1]
    lane=lax.broadcasted_iota(jnp.int32,v.shape,1)
    return jnp.where(lane%2==0,pltpu.roll(v,w-1,1),pltpu.roll(v,1,1))
def gelu_both(v):
    c=math.sqrt(2/math.pi)
    v2=v*v
    t=jnp.tanh(c*v*(1.0+0.044715*v2))
    h=0.5*(1.0+t)
    return v*h, h+0.5*v*(1.0-t*t)*(c*(1.0+3*0.044715*v2))

def qkv_kernel(x_ref,seg_ref,emb_ref,w_ref,b_ref,cos_ref,sin_ref,n_ref,*p_refs,R,nd):
    F,D=x_ref.shape
    @pl.loop(0,F//R)
    def _(i):
        r=pl.ds(pl.multiple_of(i*R,R),R)
        seg=seg_ref[r,:]
        n,_=moments(x_ref[r,:].astype(f32))
        n_ref[r,:]=(n*(1.0+pick(seg,emb_ref,1,D))+pick(seg,emb_ref,0,D)).astype(bf)
    for q,p_ref in enumerate(p_refs):
        @pl.loop(0,F//R)
        def _(i):
            r=pl.ds(pl.multiple_of(i*R,R),R)
            cos=cos_ref[r,:]; sin=sin_ref[r,:]
            for d in range(0,nd,2):
                c=(q*nd+d)*384
                v=dot(n_ref[r,:],w_ref[:,c:c+768])+b_ref[0:1,c:c+768]
                for k in range(6):
                    a=v[:,k*128:(k+1)*128]
                    if k%3<2: a=a*cos+partner(a)*sin
                    p_ref[d+k//3,r,k%3*128:(k%3+1)*128]=a.astype(bf)

def qkv_proj(x,seg,emb,w,b,cos,sin,nd,R=256):
    F,D=x.shape; PP=D//nd//128
    return pl.pallas_call(functools.partial(qkv_kernel,R=R,nd=nd),
        out_shape=(jax.ShapeDtypeStruct((F,D),bf),)+(jax.ShapeDtypeStruct((nd,F,384),bf),)*PP,
        in_specs=[V]*7,out_specs=(V,)*(1+PP),
        compiler_params=pltpu.CompilerParams(vmem_limit_bytes=40*2**20),name="qkv_proj",
        cost_estimate=pl.CostEstimate(flops=2*F*D*3*D,bytes_accessed=14*2**20,transcendentals=0))(x,seg,emb,w,b,cos,sin)


def sizes(nd,ns):
    Y=2**((ns.bit_length()-1)//2)
    return nd//2,Y,ns//Y

class Place:
    def __init__(self,nd,ns):
        self.nd,self.ns=nd,ns
        self.X,self.Y,self.Z=sizes(nd,ns)
        self.h=lax.axis_index("head"); self.s=lax.axis_index("seq")
        self.x,self.c=self.h//2,self.h%2
        self.z,self.y=self.s//self.Y,self.s%self.Y
    def at(self,x=None,c=None,z=None,y=None):
        x=self.x if x is None else x; c=self.c if c is None else c
        z=self.z if z is None else z; y=self.y if y is None else y
        return (x*2+c,z*self.Y+y)

def near_first(n):
    out=[]
    for d in range(1,n//2+1):
        out.append(d)
        if n-d!=d: out.append(n-d)
    return out

def remote(src,dst,ss,rs,dev):
    cp=pltpu.make_async_remote_copy(src_ref=src,dst_ref=dst,send_sem=ss,recv_sem=rs,device_id=dev,device_id_type=pl.DeviceIdType.MESH)
    cp.start()
    return cp

def greet(p):
    b=pltpu.get_barrier_semaphore()
    for d in range(1,p.nd): pl.semaphore_signal(b,inc=1,device_id=(lax.rem(p.h+d,p.nd),p.s),device_id_type=pl.DeviceIdType.MESH)
    for d in range(1,p.ns): pl.semaphore_signal(b,inc=1,device_id=(p.h,lax.rem(p.s+d,p.ns)),device_id_type=pl.DeviceIdType.MESH)
    pl.semaphore_wait(b,p.nd+p.ns-2)

def along_head(p,f): return [f(d,lax.rem(p.h+d,p.nd),(lax.rem(p.h+d,p.nd),p.s)) for d in range(1,p.nd)]
def along_seq(p,f): return [f(d,lax.rem(p.s+d,p.ns),(p.h,lax.rem(p.s+d,p.ns))) for d in range(1,p.ns)]

class Gather:
    @staticmethod
    def sems(nd,ns):
        X,Y,Z=sizes(nd,ns)
        D=pltpu.SemaphoreType.DMA
        one=[D((Z,)),D((Z,X)),D((Z,Y)),D((Z,X,Y)),D((Z,X,Y)),D((Z,)),D((2,Z,X,Y))]
        return one+one+[D(())]
    def __init__(self,p,shard,out,sems):
        self.p,self.shard,self.out=p,shard,out
        self.ss,self.rs,self.ls=sems[:7],sems[7:14],sems[14]
        self.all=[]; self.half=shard.shape[-1]//2
        self.two={}; self.three={}
    def send(self,k,idx,src,dst,dev):
        cp=remote(src,dst,self.ss[k].at[idx],self.rs[k].at[idx],dev)
        self.all.append(cp); return cp
    def cols(self,part): return pl.ds(part*self.half,self.half)
    def loc(self,x,z,y,part=None):
        r=self.out.at[x,self.p.c,z,y]
        return r if part is None else r.at[:,self.cols(part)]
    def start(self):
        p=self.p
        self.zc={}
        for dz in near_first(p.Z):
            self.zc[dz]=self.send(0,(dz,),self.shard,self.loc(p.x,p.z,p.y),p.at(z=lax.rem(p.z+dz,p.Z)))
        self.local=pltpu.make_async_copy(self.shard,self.loc(p.x,p.z,p.y),self.ls)
        self.local.start()
        self.second(0)
    def second(self,dz):
        p=self.p; zz=lax.rem(p.z+p.Z-dz,p.Z)
        if dz: self.zc[dz].wait_recv()
        def src(part=None):
            if dz: return self.loc(p.x,zz,p.y,part)
            return self.shard if part is None else self.shard.at[:,self.cols(part)]
        for dx in near_first(p.X):
            self.two[0,dz,dx]=self.send(1,(dz,dx),src(0),self.loc(p.x,zz,p.y,0),p.at(x=lax.rem(p.x+dx,p.X)))
        for dy in near_first(p.Y):
            self.two[1,dz,dy]=self.send(2,(dz,dy),src(1),self.loc(p.x,zz,p.y,1),p.at(y=lax.rem(p.y+dy,p.Y)))
        self.send(5,(dz,),src(),self.loc(p.x,zz,p.y),p.at(c=1-p.c))
        for dy in near_first(p.Y):
            self.three[0,dz,0,dy]=self.send(3,(dz,0,dy),src(0),self.loc(p.x,zz,p.y,0),p.at(y=lax.rem(p.y+dy,p.Y)))
        for dx in near_first(p.X):
            self.three[1,dz,dx,0]=self.send(4,(dz,dx,0),src(1),self.loc(p.x,zz,p.y,1),p.at(x=lax.rem(p.x+dx,p.X)))
    def third(self,dz):
        p=self.p; zz=lax.rem(p.z+p.Z-dz,p.Z)
        for dx in near_first(p.X):
            self.two[0,dz,dx].wait_recv()
            l=self.loc(lax.rem(p.x+p.X-dx,p.X),zz,p.y,0)
            for dy in near_first(p.Y):
                self.three[0,dz,dx,dy]=self.send(3,(dz,dx,dy),l,l,p.at(y=lax.rem(p.y+dy,p.Y)))
            self.send(6,(0,dz,dx,0),l,l,p.at(c=1-p.c))
        for dy in near_first(p.Y):
            self.two[1,dz,dy].wait_recv()
            l=self.loc(p.x,zz,lax.rem(p.y+p.Y-dy,p.Y),1)
            for dx in near_first(p.X):
                self.three[1,dz,dx,dy]=self.send(4,(dz,dx,dy),l,l,p.at(x=lax.rem(p.x+dx,p.X)))
            self.send(6,(1,dz,0,dy),l,l,p.at(c=1-p.c))
    def fourth(self,dz):
        p=self.p; zz=lax.rem(p.z+p.Z-dz,p.Z)
        for part in (0,1):
            for dx in range(p.X):
                for dy in range(p.Y):
                    if (part,dz,dx,dy) not in self.three: continue
                    self.three[part,dz,dx,dy].wait_recv()
                    l=self.loc(lax.rem(p.x+p.X-dx,p.X),zz,lax.rem(p.y+p.Y-dy,p.Y),part)
                    self.send(6,(part,dz,dx,dy),l,l,p.at(c=1-p.c))
    def finish(self):
        waited=set()
        for cp in self.zc.values(): waited.add(id(cp))
        for d in (self.two,self.three):
            for cp in d.values(): waited.add(id(cp))
        for cp in self.all:
            if id(cp) not in waited: cp.wait_recv()
            cp.wait_send()
        self.local.wait()

def entry_kernel(nd,ns,nw,*refs):
    shards=refs[:nw]; bias,time,ids,wada=refs[nw:nw+4]
    outs=refs[nw+4:2*nw+4]; bias_all,ids_all,emb,act=refs[2*nw+4:2*nw+8]
    time_all,part,r1,r2,bs,br,isd,ir,ts,tr,e1s,e1r,e2s,e2r=refs[2*nw+8:2*nw+22]
    gs=refs[2*nw+22:]
    p=Place(nd,ns); n=len(Gather.sems(nd,ns))
    greet(p)
    tail=[]
    first=[]
    for ds in range(1,ns):
        first.append(remote(time,time_all.at[p.s],ts.at[ds],tr.at[ds],(p.h,lax.rem(p.s+ds,ns))))
    g=[Gather(p,shards[i],outs[i],gs[i*n:(i+1)*n]) for i in range(nw)]
    for a in g: a.start()
    me=p.h*ns+p.s
    for dh in range(1,nd):
        tail.append(remote(ids,ids_all.at[p.h],isd.at[dh],ir.at[dh],(lax.rem(p.h+dh,nd),p.s)))
    bc=along_head(p,lambda d,h,dev: remote(bias,bias_all.at[p.h,p.s],bs.at[0,d],br.at[0,d],dev))
    l1=pltpu.make_async_copy(bias,bias_all.at[p.h,p.s],bs.at[0,0]); l1.start()
    l2=pltpu.make_async_copy(ids,ids_all.at[p.h],isd.at[0]); l2.start()
    time_all[p.s]=time[...]
    for cp in first: cp.wait()
    D=time.shape[1]; K=wada.shape[0]; E=wada.shape[1]//8
    v=time_all[...].reshape(ns*8,D)
    low=(v/(1.0+jnp.exp(-v))).astype(bf)
    kk=D//(nd*ns)
    row=lax.broadcasted_iota(jnp.int32,(D,128),0); col=lax.broadcasted_iota(jnp.int32,(D,128),1)
    pickm=jnp.where((row==me*kk+col)&(col<kk),1.0,0.0).astype(bf)
    own=dot(low,pickm).astype(bf)
    act[...]=own
    for j in range(8):
        pj=dot(own[:,:K],wada[:,j*E:(j+1)*E])
        for s in range(ns):
            part[s,2*j:2*j+2,:]=pj[8*s:8*s+2,:]
    one=[remote(part.at[lax.rem(p.s+ds,ns)],r1.at[ds],e1s.at[ds],e1r.at[ds],(p.h,lax.rem(p.s+ds,ns))) for ds in range(1,ns)]
    l1.wait()
    for cp in bc: cp.wait()
    tail+=along_seq(p,lambda d,s,dev: remote(bias_all.at[:,p.s],bias_all.at[:,p.s],bs.at[1,d],br.at[1,d],dev))
    order=[0]+near_first(p.Z)
    for a in g:
        for i,dz in enumerate(order):
            if dz: a.second(dz)
            if i: a.third(order[i-1])
        a.third(order[-1])
    tot=part[p.s]
    for ds in range(1,ns):
        one[ds-1].wait()
        tot=tot+r1[ds]
    r2[p.h]=tot
    two=[remote(r2.at[p.h],r2.at[p.h],e2s.at[dh],e2r.at[dh],(lax.rem(p.h+dh,nd),p.s)) for dh in range(1,nd)]
    for a in g:
        for dz in order: a.fourth(dz)
    for cp in two: cp.wait()
    tot=r2[0]
    for i in range(1,nd): tot=tot+r2[i]
    emb[...]=tot
    for a in g: a.finish()
    for cp in tail: cp.wait()
    l2.wait()

def entry(nd,ns,shards,bias,time,ids,wada):
    X,Y,Z=sizes(nd,ns)
    S=jax.ShapeDtypeStruct
    D=pltpu.SemaphoreType.DMA
    nw=len(shards); E=wada.shape[1]//8
    outs=[S((X,2,Z,Y)+a.shape,a.dtype) for a in shards]+[S((nd,ns)+bias.shape,bias.dtype),S((nd,)+ids.shape,ids.dtype),S((16,E),f32),S((ns*8,128),bf)]
    scr=[pltpu.VMEM((ns,8,time.shape[1]),f32),pltpu.VMEM((ns,16,E),f32),pltpu.VMEM((ns,16,E),f32),pltpu.VMEM((nd,16,E),f32),
         D((2,max(nd,ns))),D((2,max(nd,ns))),D((nd,)),D((nd,)),D((ns,)),D((ns,)),D((ns,)),D((ns,)),D((nd,)),D((nd,))]
    for _ in shards: scr+=Gather.sems(nd,ns)
    return pl.pallas_call(functools.partial(entry_kernel,nd,ns,nw),out_shape=tuple(outs),
        in_specs=[ANY]*(nw+1)+[V,ANY,V],out_specs=tuple([ANY]*(nw+2)+[V,V]),scratch_shapes=scr,
        compiler_params=pltpu.CompilerParams(collective_id=0,has_side_effects=True,vmem_limit_bytes=60*2**20),name="entry")(*shards,bias,time,ids,wada)

def make_remote(src,dst,ss,rs,dev):
    return pltpu.make_async_remote_copy(src_ref=src,dst_ref=dst,send_sem=ss,recv_sem=rs,device_id=dev,device_id_type=pl.DeviceIdType.MESH)

def mid_kernel(PP,*refs,R,nd,ns):
    mid_body(refs[:PP],refs[PP+9:2*PP+9],*refs[PP:PP+9],*refs[2*PP+9:],R=R,nd=nd,ns=ns)

def mid_body(o_refs,do_refs,x_ref,c_ref,seg_ref,msk_ref,emb_ref,w_ref,bo_ref,bu_ref,bd_ref,
               out_ref,dm_ref,gu_ref,gw_ref,gb_ref,ge_ref,
               wo_ref,wu_ref,wd_ref,n2s,acts,dhs,dfs,dps,dgelu,a_ref,da_ref,sem,s1,s2,s3,t1,t2,t3,*,R,nd,ns):
    F,D=x_ref.shape; H=bu_ref.shape[1]; CH=512
    loads=[pltpu.make_async_copy(w_ref.at[:,pl.ds(o,n)],r,sem.at[i]) for i,(o,n,r) in enumerate(((2*H,D,wo_ref),(0,H,wu_ref),(H,H,wd_ref)))]
    p=Place(nd,ns); W=D//nd; NR=F//R
    b=pltpu.get_barrier_semaphore()
    for d in range(1,nd): pl.semaphore_signal(b,inc=1,device_id=(lax.rem(p.h+d,nd),p.s),device_id_type=pl.DeviceIdType.MESH)
    pl.semaphore_wait(b,nd-1)
    def rows(i): return pl.ds(pl.multiple_of(i*R,R),R)
    def cols(h,q): return pl.ds(pl.multiple_of(h*W+q*128,128),128)
    def arrive(i):
        return [make_remote(o.at[lax.rem(p.h+d,nd),rows(i)],a_ref.at[rows(i),cols(p.h,q)],s1.at[i,d,q],s2.at[i,d,q],(lax.rem(p.h+d,nd),p.s)) for d in range(1,nd) for q,o in enumerate(o_refs)]
    def kept(i): return [pltpu.make_async_copy(o.at[p.h,rows(i)],a_ref.at[rows(i),cols(p.h,q)],s3.at[i,q]) for q,o in enumerate(o_refs)]
    def leave(i):
        return [make_remote(da_ref.at[rows(i),cols(lax.rem(p.h+d,nd),q)],o.at[p.h,rows(i)],t1.at[i,d,q],t2.at[i,d,q],(lax.rem(p.h+d,nd),p.s)) for q,o in enumerate(do_refs) for d in range(1,nd)]
    def stays(i): return [pltpu.make_async_copy(da_ref.at[rows(i),cols(p.h,q)],o.at[p.h,rows(i)],t3.at[i,q]) for q,o in enumerate(do_refs)]
    for c in arrive(0)+kept(0): c.start()
    for l in loads: l.start()
    gb_ref[...]=jnp.zeros_like(gb_ref); ge_ref[...]=jnp.zeros_like(ge_ref)
    for l in loads: l.wait()
    def down(j):
        t,o=divmod(j*CH,D)
        return slice(o,o+CH),slice(t*D,(t+1)*D)
    @pl.loop(0,F//R)
    def _(i):
        r=rows(i)
        for c in arrive(i): c.wait_recv()
        for c in kept(i): c.wait()
        @pl.when(i+1<NR)
        def _():
            for c in arrive(i+1)+kept(i+1): c.start()
        seg=seg_ref[r,:]; msk=msk_ref[r,:]
        def acc(k,x):
            a,b=sums(x,seg)
            ge_ref[0:1,k*D:(k+1)*D]+=a; ge_ref[1:2,k*D:(k+1)*D]+=b
        branch=(dot(a_ref[r,:],wo_ref[...])+bo_ref[0:1,:])*msk
        g1=pick(seg,emb_ref,2,D)
        middle=x_ref[r,:].astype(f32)+g1*branch
        n,rs=moments(middle)
        sc2=1.0+pick(seg,emb_ref,4,D)
        n2=(n*sc2+pick(seg,emb_ref,3,D)).astype(bf)
        n2s[r,:]=n2
        feed=jnp.broadcast_to(bd_ref[0:1,:],(R,D))
        for j in range(H//CH):
            c=slice(j*CH,(j+1)*CH)
            h=dot(n2,wu_ref[:,c])+bu_ref[0:1,c]
            a,g=gelu_both(h)
            a=a.astype(bf)
            acts[r,c]=a; dgelu[:,c]=g
            feed+=dot(a,wd_ref[down(j)])
        up=c_ref[r,:].astype(f32)
        g2=pick(seg,emb_ref,5,D)
        out_ref[r,:]=(middle+g2*feed).astype(bf)
        df=(up*g2).astype(bf)
        dfs[r,:]=df
        acc(3,up*feed)
        gb_ref[2:3,0:D]+=jnp.sum(df.astype(f32),0,keepdims=True)
        dn=jnp.zeros((R,D),f32)
        for j in range(H//CH):
            c=slice(j*CH,(j+1)*CH)
            dh=(dot(df,wd_ref[down(j)],NT)*dgelu[:,c]).astype(bf)
            dhs[r,c]=dh
            gb_ref[1:2,c]+=jnp.sum(dh.astype(f32),0,keepdims=True)
            dn+=dot(dh,wu_ref[:,c],NT)
        acc(1,dn); acc(2,dn*n)
        dn=dn*sc2
        dmid=up+(dn-jnp.mean(dn,-1,keepdims=True)-n*jnp.mean(dn*n,-1,keepdims=True))*rs
        dm_ref[r,:]=dmid
        acc(0,dmid*branch)
        dp=(dmid*g1*msk).astype(bf)
        dps[r,:]=dp
        gb_ref[0:1,0:D]+=jnp.sum(dp.astype(f32),0,keepdims=True)
        da_ref[r,:]=dot(dp,wo_ref[...],NT).astype(bf)
        for c in leave(i)+stays(i): c.start()
    @pl.loop(0,D//256)
    def _(i):
        c=pl.ds(pl.multiple_of(i*256,256),256)
        gw_ref[c,H:H+D]=dot(a_ref[:,c],dps[...],TN).astype(bf)
        gu_ref[c,:]=dot(n2s[:,c],dhs[...],TN).astype(bf)
        for t in range(H//D):
            e=pl.ds(pl.multiple_of(t*D+i*256,256),256)
            gw_ref[c,t*D:(t+1)*D]=dot(acts[:,e],dfs[...],TN).astype(bf)
    for i in range(NR):
        for c in arrive(i): c.wait_send()
        for c in leave(i)+stays(i): c.wait()

def mid(nd,ns,os,x,c,seg,msk,emb,w,bo,bu,bd,R=256):
    F,D=x.shape; H=bu.shape[1]; NR=F//R; PP=len(os); A=pltpu.SemaphoreType.DMA
    S=jax.ShapeDtypeStruct; M=pltpu.VMEM
    return pl.pallas_call(functools.partial(mid_kernel,PP,R=R,nd=nd,ns=ns),
        out_shape=(S((nd,F,128),bf),)*PP+(S((F,D),bf),S((F,D),f32),S((D,H),bf),S((D,H+D),bf),S((8,H),f32),S((8,4*D),f32)),
        in_specs=[ANY]*PP+[V]*5+[ANY]+[V]*3,out_specs=(ANY,)*PP+(V,)*6,
        scratch_shapes=[M((D,D),bf),M((D,H),bf),M((D,H),bf),M((F,D),bf),M((F,H),bf),M((F,H),bf),M((F,D),bf),M((F,D),bf),M((R,H),f32),M((F,D),bf),M((F,D),bf),A((3,)),A((NR,nd,PP)),A((NR,nd,PP)),A((NR,PP)),A((NR,nd,PP)),A((NR,nd,PP)),A((NR,PP))],
        compiler_params=pltpu.CompilerParams(collective_id=2,has_side_effects=True,vmem_limit_bytes=62*2**20),name="mid",
        cost_estimate=pl.CostEstimate(flops=6*F*D*(D+2*H),bytes_accessed=30*2**20,transcendentals=F*H))(*os,x,c,seg,msk,emb,w,bo,bu,bd)


ORD_X=-1
QW=512
class Reduce:
    def __init__(self,p,parts,scr,own=None,src=None,col=0):
        self.p,self.parts,self.src=p,parts,src
        it=iter(scr)
        self.own=own if own is not None else next(it)
        self.c=p.c if own is not None else 0
        self.w=self.own.shape[-1]; self.cs=pl.ds(col,self.w)
        self.cin=next(it); self.c1,self.c2,self.ls=next(it),next(it),next(it)
        self.bufs=[[(next(it),next(it),next(it)) for _ in o] for _,_,o in parts]
        self.sent=[]; self.stage=0
    @staticmethod
    def scratch(nd,ns,k,w,dt,parts,own):
        X,Y,Z=sizes(nd,ns); M=pltpu.VMEM; D=pltpu.SemaphoreType.DMA; n={"x":X,"y":Y,"z":Z}
        out=[] if own else [M((X,1,Z,Y,k,w),dt)]
        out+=[M((X,Z,Y,k,w),dt),D((X,)),D((X,)),D((X,))]
        for lo,hi,order in parts:
            for i,a in enumerate(order):
                left=tuple(n[b] for b in "xzy" if b in order[i+1:])
                out+=[M((max(n[a]-1,1),)+left+(k,hi-lo),dt),D((n[a],)),D((n[a],))]
        return out
    def start(self):
        p=self.p; self.l=[]; self.cc=[]
        for x in range(p.X):
            s=self.own.at[x,1-p.c] if self.src is None else self.src.at[x,1-p.c,:,:,:,self.cs]
            self.cc.append(remote(s,self.cin.at[x],self.c1.at[x],self.c2.at[x],p.at(c=1-p.c)))
            if self.src is not None:
                l=pltpu.make_async_copy(self.src.at[x,p.c,:,:,:,self.cs],self.own.at[x,0],self.ls.at[x]); l.start(); self.l.append(l)
        self.sent+=self.cc
    def place(self,order,i,v):
        p=self.p; mine={"x":p.x,"y":p.y,"z":p.z}
        ix={b:(mine[b] if b in order[:i] else v if b==order[i] else slice(None)) for b in "xyz"}
        return (ix["x"],self.c,ix["z"],ix["y"])
    def add(self,i,x,cols):
        i=i+(slice(None),slice(*cols))
        self.own[i]=(self.own[i].astype(f32)+x.astype(f32)).astype(self.own.dtype)
    def send(self,part,i):
        p=self.p; lo,hi,order=self.parts[part]; a=order[i]
        n={"x":p.X,"y":p.Y,"z":p.Z}[a]; me={"x":p.x,"y":p.y,"z":p.z}[a]
        buf,s1,s2=self.bufs[part][i]; out=[]
        for d in near_first(n):
            v=lax.rem(me+d,n)
            out.append((d,remote(self.own.at[self.place(order,i,v)+(slice(None),pl.ds(lo,hi-lo))],buf.at[d-1],s1.at[d],s2.at[d],p.at(**{a:v}))))
        self.sent+=[c for _,c in out]
        return out
    def step(self):
        p=self.p; st=self.stage; self.stage+=1
        if st==0:
            for x in range(p.X):
                if self.src is not None: self.l[x].wait()
                self.cc[x].wait_recv()
                @pl.loop(0,p.Z)
                def _(z):
                    for y in range(p.Y): self.add((x,self.c,z,y),self.cin[x,z,y],(0,self.w))
            self.go=[self.send(k,0) for k in range(len(self.parts))]
            return
        go=[]
        for k,(lo,hi,order) in enumerate(self.parts):
            buf=self.bufs[k][st-1][0]; left=[b for b in "xzy" if b in order[st:]]
            n={"x":p.X,"y":p.Y,"z":p.Z}; mine={"x":p.x,"y":p.y,"z":p.z}
            for d,c in self.go[k]:
                c.wait_recv()
                def one(at,d=d):
                    ix={**mine,**at}
                    self.add((ix["x"],self.c,ix["z"],ix["y"]),buf[(d-1,)+tuple(at[b] for b in left)],(lo,hi))
                if len(left)==2:
                    @pl.loop(0,n[left[0]])
                    def _(u):
                        for v in range(n[left[1]]): one({left[0]:u,left[1]:v})
                else:
                    @pl.loop(0,n[left[0]])
                    def _(u): one({left[0]:u})
            go.append(self.send(k,st))
        self.go=go
    def last(self,put):
        p=self.p
        for k,(lo,hi,order) in enumerate(self.parts):
            buf=self.bufs[k][2][0]
            t=self.own[p.x,self.c,p.z,p.y,:,lo:hi].astype(f32)
            for d,c in self.go[k]:
                c.wait_recv()
                t=t+buf[d-1].astype(f32)
            put(lo,t)
    def finish(self):
        for c in self.sent: c.wait_send()

REST=(lambda w,j:((0,w//2,"yxz"),(w//2,w,"xyz"))); QKV=(lambda w:((0,w//2,"yzx"),(w//2,w,"xyz")))

def final_kernel(nd,ns,R,here,refs,scr):
    (g_ref,rest_ref,x_hbm,n1_hbm,dm_hbm,wq_hbm,cos_ref,sin_ref,seg_ref,emb_ref,gbm_ref,gem_ref,act,wada)=refs[:14]
    (gf_ref,rest_out,qkv_out,bias_all,gada,gbada,dact)=refs[14:]
    (g,x_ref,n1_ref,dm_ref,w_ref,dps,gw,gbv,gev,bsc,bout,hsum,demb,dscr)=scr[:14]; rtmp=scr[-1]; scr=scr[:-1]
    (gs,gr,gl,gh,ld,hs,hr,qs,qr,ds_,dr,bs,br)=scr[14:27]
    pools=scr[27:]
    p=Place(nd,ns); me=p.h*ns+p.s
    F,D=x_ref.shape; W=D//nd; E=D*6//8; K=wada.shape[0]; H=gbm_ref.shape[1]; NR=F//R
    nr=H//D; nq=3*D//QW; PP=W//128; C=3*D//PP; ne=nq//PP*(PP-1)
    come=[pltpu.make_async_copy(a,g.at[q],gh.at[q]) for q,a in enumerate(here)]
    for c in come: c.start()
    greet(p)
    loads=[pltpu.make_async_copy(a,b,ld.at[i]) for i,(a,b) in enumerate(((x_hbm,x_ref),(wq_hbm,w_ref),(dm_hbm,dm_ref),(n1_hbm,n1_ref)))]
    sends=[]; own=[]
    def chunk(i):
        r=pl.ds(i*R,R)
        sends.append([remote(g_ref.at[lax.rem(p.h+d,nd),r],g.at[PP-1,p.h,r],gs.at[i,d],gr.at[i,d],(lax.rem(p.h+d,nd),p.s)) for d in range(1,nd)])
    for i in range(NR):
        r=pl.ds(i*R,R)
        c=pltpu.make_async_copy(g_ref.at[p.h,r],g.at[PP-1,p.h,r],gl.at[i]); c.start(); own.append(c)
    for i in range(min(2,NR)): chunk(i)
    for l in loads: l.start()
    it=iter(pools)
    take=lambda n: [next(it) for _ in range(n)]
    rest=[]
    for j in range(nr):
        rest.append(Reduce(p,REST(D,j),take(len(Reduce.scratch(nd,ns,K,D,bf,REST(D,j),False))),src=rest_ref,col=j*D))
        rest[-1].start()
    qkv=[Reduce(p,QKV(QW),take(len(Reduce.scratch(nd,ns,K,QW,bf,QKV(QW),True))),own=gw.at[j]) for j in range(nq)]
    bias=Reduce(p,QKV(256),take(len(Reduce.scratch(nd,ns,8,256,f32,QKV(256),True))),own=bsc)
    gbv[...]=jnp.zeros_like(gbv); gev[...]=jnp.zeros_like(gev); bsc[...]=jnp.zeros_like(bsc)
    for a in rest[:2]: a.step()
    for l in loads: l.wait()
    def unturn(q,r):
        cos=cos_ref[r,:]; sin=sin_ref[r,:]
        @pl.loop(0,nd)
        def _(d):
            for j in range(3):
                c=pl.ds(pl.multiple_of(((q*nd+d)*3+j)*128,128),128)
                v=g[q,d,r,j*128:(j+1)*128]
                if j<2:
                    v=v.astype(f32)
                    v=(v*cos-partner(v)*sin).astype(bf)
                dps[r,c]=v
                gbv[0:1,c]+=jnp.sum(v.astype(f32),0,keepdims=True)
    def turn(i):
        for c in sends[i]: c.wait_recv()
        own[i].wait()
        if i+2<NR: chunk(i+2)
        r=slice(i*R,(i+1)*R)
        unturn(PP-1,r)
    def norm(lo,hi):
        @pl.loop(lo,hi)
        def _(i):
            r=pl.ds(pl.multiple_of(i*R,R),R)
            seg=seg_ref[r,:]
            dn=jnp.zeros((R,D),f32)
            for j in range(3*D//512):
                dn+=dot(dps[r,j*512:(j+1)*512],w_ref[:,j*512:(j+1)*512],NT)
            n,rs=moments(x_ref[r,:].astype(f32))
            for k,x in ((0,dn),(1,dn*n)):
                a,b=sums(x,seg)
                gev[0:1,k*D:(k+1)*D]+=a; gev[1:2,k*D:(k+1)*D]+=b
            dn=dn*(1.0+pick(seg,emb_ref,1,D))
            gf_ref[r,:]=dm_ref[r,:]+(dn-jnp.mean(dn,-1,keepdims=True)-n*jnp.mean(dn*n,-1,keepdims=True))*rs
    def weight(j):
        B=D//nd
        for h in range(nd):
            v=dot(n1_ref[:,h*B:(h+1)*B],dps[:,j*QW:(j+1)*QW],TN).astype(bf)
            gw[j,h//2,h%2]=v.reshape(p.Z,p.Y,K,QW)
        qkv[j].start()
    for q,c in enumerate(come):
        c.wait()
        @pl.loop(0,NR)
        def _(i,q=q): unturn(q,pl.ds(pl.multiple_of(i*R,R),R))
    for j in range(ne):
        weight(j)
        if j: qkv[j-1].step()
    for a in qkv[:ne][-1:]: a.step()
    steps=[]
    for k in range(max(ne,nr)): steps+=[a.step for a in qkv[:ne][k:k+1]]+[a.step for a in rest[k:k+1]]
    for i in range(NR):
        turn(i)
        for f in steps[i*len(steps)//NR:(i+1)*len(steps)//NR]: f()
    for j in range(ne,nq):
        weight(j)
        if j>ne: qkv[j-1].step()
        if j-ne<nr: rest[j-ne].step()
    vec=jnp.concatenate([gbv[0:1,:],gbm_ref[0:1,0:D],gbm_ref[1:2,:],gbm_ref[2:3,0:D]],1)
    for q in range(vec.shape[1]//256):
        h,s=divmod(q,ns)
        bsc[h//2,h%2,s//p.Y,s%p.Y,0:1,:]=vec[:,q*256:(q+1)*256]
    bias.start()
    qkv[nq-1].step()
    for a in qkv[:ne]: a.step()
    norm(0,NR//2)
    bias.step()
    qkv[ne].step()
    norm(NR//2,NR)
    gev[0:2,2*D:]=gem_ref[0:2,:]
    for j in range(8):
        for t in range(2): hsum[p.h,2*j+t:2*j+t+1,:]=gev[t:t+1,j*E:(j+1)*E]
    hc=[remote(hsum.at[p.h],hsum.at[p.h],hs.at[d],hr.at[d],(lax.rem(p.h+d,nd),p.s)) for d in range(1,nd)]
    qkv[ne+1].step(); qkv[ne].step(); bias.step()
    for c in hc: c.wait()
    tot=hsum[0]
    for i in range(1,nd): tot=tot+hsum[i]
    demb[p.s]=tot.astype(bf)
    qc=[remote(demb.at[p.s],demb.at[p.s],qs.at[d],qr.at[d],(p.h,lax.rem(p.s+d,ns))) for d in range(1,ns)]
    qkv[ne+2].step(); qkv[ne+1].step(); bias.step()
    for j in range(ne+3,nq): qkv[j].step(); qkv[j-1].step()
    for j,a in enumerate(rest):
        def put(c,t,j=j): rtmp[j,:,c:c+t.shape[1]]=t
        a.last(put)
    wide=128*nr
    r0=lax.broadcasted_iota(jnp.int32,(wide,wide),0); c0=lax.broadcasted_iota(jnp.int32,(wide,wide),1)
    perm=jnp.where((r0//128==c0//K%nr)&(r0%128//K==c0//(K*nr))&(r0%K==c0%K),1.0,0.0)
    for b in range(D//128):
        v=jnp.concatenate([rtmp[j,:,b*128:(b+1)*128] for j in range(nr)],1)
        rest_out[:,b*wide:(b+1)*wide]=lax.dot_general(v,perm,NN,precision=lax.Precision.HIGHEST,preferred_element_type=f32)
    def keep(c,t): bout[:,c:c+t.shape[1]]=t
    bias.last(keep)
    def home(j):
        def put(c,t):
            for k in range(t.shape[1]//128):
                s=(j*QW+c)//128+k
                at=(s%3*nd+s//3%nd)*PP+s//3//nd
                qkv_out[:,at*128:(at+1)*128]=t[:,k*128:(k+1)*128]
        return put
    bias_all[p.h,p.s]=bout[...]
    bc=along_head(p,lambda d,h,dev: remote(bout,bias_all.at[p.h,p.s],bs.at[0,d],br.at[0,d],dev))
    for j in range(ne): qkv[j].last(home(j))
    for c in qc: c.wait()
    qkv[nq-1].step()
    Q=ns*16
    flat=demb[...].reshape(Q,E)
    r0=lax.broadcasted_iota(jnp.int32,(Q,ns*8),0); c0=lax.broadcasted_iota(jnp.int32,(Q,ns*8),1)
    spread=dot(jnp.where((r0//16==c0//8)&(r0%2==c0%8),1.0,0.0).astype(bf),act[...])
    rr=lax.broadcasted_iota(jnp.int32,(Q,128),0)%16//2
    rk=lax.broadcasted_iota(jnp.int32,(Q,K),0)%16//2
    tot=jnp.zeros((Q,K),f32)
    for j in range(8):
        m=jnp.where(rr==j,spread,0.0).astype(bf)
        gada[:,j*E:(j+1)*E]=dot(m,flat,TN)[:K,:]
        tot=jnp.where(rk==j,dot(flat,wada[:,j*E:(j+1)*E],NT),tot)
    dscr[...]=jnp.concatenate([tot,jnp.zeros((Q,128-K),f32)],1).reshape(ns,16,128)
    dact[p.h,p.s]=dscr[p.s]
    dc=along_seq(p,lambda d,s,dev: remote(dscr.at[s],dact.at[p.h,p.s],ds_.at[0,d],dr.at[0,d],dev))
    for c in bc: c.wait()
    bc=along_seq(p,lambda d,s,dev: remote(bias_all.at[:,p.s],bias_all.at[:,p.s],bs.at[1,d],br.at[1,d],dev))
    r8=lax.broadcasted_iota(jnp.int32,(8,Q),0); c8=lax.broadcasted_iota(jnp.int32,(8,Q),1)
    gbada[...]=dot(jnp.where(c8%16//2==r8,1.0,0.0).astype(bf),flat)
    for c in dc: c.wait()
    dc=along_head(p,lambda d,h,dev: remote(dact.at[p.h],dact.at[p.h],ds_.at[1,d],dr.at[1,d],dev))
    for j in range(ne,nq): qkv[j].last(home(j))
    for a in rest+qkv+[bias]: a.finish()
    for i in range(NR):
        for c in sends[i]: c.wait_send()
    for c in bc+dc: c.wait()

def final(nd,ns,here,dqkv,rest,x,n1,dm,wq,cos,sin,seg,emb,gb,ge,act,wada,R=128):
    F,D=x.shape; K,E6=wada.shape; E=E6//8; H=gb.shape[1]; N=nd*ns; W=D//nd; NR=F//R
    X,Y,Z=sizes(nd,ns)
    S=jax.ShapeDtypeStruct; M=pltpu.VMEM; A=pltpu.SemaphoreType.DMA
    outs=[S((F,D),f32),S((K,H),f32),S((K,3*D),f32),S((nd,ns,8,256),f32),S((K,E6),f32),S((8,E),f32),S((nd,ns,16,128),f32)]
    scr=[M((W//128,nd,F,384),bf),M((F,D),bf),M((F,D),bf),M((F,D),f32),M((D,3*D),bf),M((F,3*D),bf),M((3*D//QW,X,2,Z,Y,K,QW),bf),M((8,3*D),f32),M((8,E6),f32),
         M((X,2,Z,Y,8,256),f32),M((8,256),f32),M((nd,16,E),f32),M((ns,16,E),bf),M((ns,16,128),f32),
         A((NR,nd)),A((NR,nd)),A((NR,)),A((W//128,)),A((4,)),A((nd,)),A((nd,)),A((ns,)),A((ns,)),A((2,max(nd,ns))),A((2,max(nd,ns))),A((2,max(nd,ns))),A((2,max(nd,ns)))]
    for j in range(H//D): scr+=Reduce.scratch(nd,ns,K,D,bf,REST(D,j),False)
    for _ in range(3*D//QW): scr+=Reduce.scratch(nd,ns,K,QW,bf,QKV(QW),True)
    scr+=Reduce.scratch(nd,ns,8,256,f32,QKV(256),True)
    scr+=[M((H//D,K,D),f32)]
    m=len(here)
    def k(*refs): final_kernel(nd,ns,R,refs[:m],refs[m:m+14+len(outs)],refs[m+14+len(outs):])
    return pl.pallas_call(k,out_shape=tuple(outs),in_specs=[ANY]*(6+m)+[V]*8,out_specs=(V,)*len(outs),scratch_shapes=scr,
        compiler_params=pltpu.CompilerParams(collective_id=1,has_side_effects=True,vmem_limit_bytes=63*2**20),name="final")(
        *here,dqkv,rest,x,n1,dm,wq,cos,sin,seg,emb,gb,ge,act,wada)


def body(frames,time_embed,segment_ids,frame_mask,positions,w_ada,b_ada,w_qkv,b_qkv,w_out,b_out,w_up,b_up,w_down,b_down,cotangent):
    _,F,D=frames.shape
    nd=lax.axis_size("head"); ns=lax.axis_size("seq"); dev=lax.axis_index("head")*ns+lax.axis_index("seq")
    X,Y,Z=sizes(nd,ns); N=nd*ns
    W=D//nd
    E=b_ada.shape[0]; E6=w_ada.shape[1]; K=w_ada.shape[0]; H=w_up.shape[1]; nt=H//D
    x=frames[0]; cot=cotangent[0]
    PP=W//128
    def reorder(w): return w.reshape(-1,3,nd,PP,128).transpose(0,3,2,1,4).reshape(-1,3*D)
    def restore(w): return w.reshape(-1,PP,nd,3,128).transpose(0,3,2,1,4).reshape(-1,3*D)
    def hide(w): return w.reshape(-1,N,nt,K).transpose(0,2,1,3).reshape(-1,H)
    def unhide(w): return w.reshape(-1,nt,N,K).transpose(0,2,1,3).reshape(-1,H)
    rest=jnp.concatenate([hide(w_up),w_down.reshape(nt,K,D).transpose(1,0,2).reshape(K,H),w_out],axis=1)
    bs=(b_qkv,b_out,b_up,b_down,b_ada); ends=[0]
    for b in bs: ends.append(ends[-1]+b.shape[0])
    wide=-(-ends[-1]//256)*256
    bias=jnp.zeros((16,wide),bf).at[0,:ends[-1]].set(jnp.concatenate(bs))
    time8=jnp.zeros((8,D),f32).at[:2].set(time_embed[0].astype(f32))
    ids=jnp.zeros((8,F),jnp.int32).at[0].set(segment_ids[0]).at[1].set(frame_mask[0])
    wq,bias_all,ids_all,emb,act=entry(nd,ns,[reorder(w_qkv)],bias,time8,ids,w_ada)
    rest_all=lax.all_gather(rest,HS,axis=0,tiled=True)
    wq=wq.reshape(D,3*D)
    bias_all=bias_all[:,:,0,:].reshape(N,-1).astype(f32)
    bq,bo,bu,bd,ba=[bias_all[:,ends[i]:ends[i+1]].reshape(1,-1) for i in range(5)]
    bq=reorder(bq); bu=hide(bu)
    emb=emb.reshape(8,2,-1).transpose(1,0,2).reshape(2,E6)+ba
    seg_row=ids_all[:,0,:].reshape(-1); msk_row=ids_all[:,1,:].reshape(-1)
    column=lax.iota(jnp.int32,128)
    pair=(column%HD//2).astype(f32)
    angles=positions[0].astype(f32)[:,None]*(10000.0**(-(2.0*pair)/HD))
    cos=jnp.cos(angles); sin=jnp.where(column%2==0,-jnp.sin(angles),jnp.sin(angles))
    segc=segment_ids[0][:,None]; mskc=frame_mask[0].astype(f32)[:,None]
    normed,*packed=qkv_proj(x,segc,emb,wq,bq,cos,sin,nd)
    def swap(a): return lax.all_to_all(a,"head",split_axis=0,concat_axis=0,tiled=True)
    qkv=[]
    for a in packed:
        if qkv: a,qkv[-1]=lax.optimization_barrier((a,qkv[-1]))
        qkv.append(swap(a))
    qkv=[a.reshape(nd*F,384) for a in qkv]
    T=512
    qlo,qhi,klo,khi=tables(seg_row,msk_row,T)
    aq,ak=aux(seg_row,msk_row)
    os=[attn_fwd(a,qlo,qhi,aq,ak,T) for a in qkv]
    *dos,out,dmid,gup,gdo,gb,ge=mid(nd,ns,[o.reshape(nd,F,128) for o,_ in os],x,cot,segc,mskc,emb,rest_all,bo,bu,bd)
    gdo=lax.psum_scatter(gdo,HS,scatter_dimension=0,tiled=True).astype(f32)
    dqkv=[attn_bwd(a,o,do.reshape(nd*F,128),lse,klo,khi,aq,ak,T).reshape(nd,F,384) for a,(o,lse),do in zip(qkv,os,dos)]
    gx,gup,gqkv,gbias,gada,gbada,dact=final(nd,ns,[swap(a) for a in dqkv[:-1]],dqkv[-1],gup.reshape(X,2,Z,Y,K,H),x,normed,dmid,
        wq,cos,sin,segc,emb,gb,ge,act,w_ada)
    dact=dact[:,:,:,:K].reshape(N,8,2,K).sum(1).transpose(1,0,2).reshape(2,D)
    _,pull=jax.vjp(jax.nn.silu,time_embed[0].astype(f32))
    gtime=pull(dact)[0][None]
    gbada=lax.dynamic_slice_in_dim(gbada.reshape(-1),dev*E,E,0)
    gbias=gbias[:,:,0,:].reshape(-1)
    gbs=[]; at=0
    for k,order in ((3*D,restore),(D,None),(H,unhide),(D,None)):
        v=gbias[at:at+k]; at+=k
        if order: v=order(v[None])[0]
        gbs.append(lax.dynamic_slice_in_dim(v,dev*(k//N),k//N,0))
    gdown=gdo[:,:H].reshape(K,nt,D).transpose(1,0,2).reshape(nt*K,D)
    return (out[None],gx[None],gtime,gada,gbada,gqkv,gbs[0],gdo[:,H:],gbs[1],gup,gbs[2],gdown,gbs[3])


def solution(mesh):
    row=P("seq","head",None); ids=P("seq","head"); mat=P(HS,None); vec=P(HS); tim=P("seq",None,None)
    in_specs=(row,tim,ids,ids,ids)+(mat,vec)*5+(row,)
    out_specs=(row,row,tim)+(mat,vec)*5
    return jax.shard_map(body,mesh=mesh,in_specs=in_specs,out_specs=out_specs,check_vma=False)
```
